32 devices in a mesh: dp: 8 (over y, x, core), shard: 4 (over z).
Axes of the slice: x: 2, y: 2, z: 4, core: 2. Of those that a mesh axis runs over, the one named last changes fastest.
Arguments:
- tokens: bfloat16 [32768, 768], P(('dp', 'shard')), may hold values from -6 to 6
- cotangent: bfloat16 [32768, 768], P(('dp', 'shard')), may hold values from -6 to 6
- seq_lengths: int32 [64], replicated, may hold values from 128 to 512, as said below
- seq_owner: int32 [64], replicated, may hold values from 0 to 31, as said below
- attend_master: float32 [768, 3072], P('shard')
- expand_master: float32 [768, 3072], P('shard'), may hold values from -0.21875 to 0.21875
- project_master: float32 [3072, 768], P('shard'), may hold values from -0.21875 to 0.21875
- vector_master: float32 [768, 12], P('shard')
- attend_mean: float32 [768, 3072], P('shard'), may hold values from -40 to 40
- expand_mean: float32 [768, 3072], P('shard'), may hold values from -56 to 56
- project_mean: float32 [3072, 768], P('shard'), may hold values from -56 to 56
- vector_mean: float32 [768, 12], P('shard'), may hold values from -64 to 64
- attend_square: float32 [768, 3072], P('shard'), may hold values from 3.2768 to 13.1072
- expand_square: float32 [768, 3072], P('shard'), may hold values from 6.5536 to 26.2144
- project_square: float32 [3072, 768], P('shard'), may hold values from 6.5536 to 26.2144
- vector_square: float32 [768, 12], P('shard'), may hold values from 9.8304 to 39.3216
Outputs:
- layer_output: bfloat16 [32768, 768], P(('dp', 'shard'))
- input_grad: float32 [32768, 768], P(('dp', 'shard'))
- attend_means: float32 [768, 3072], P('shard')
- expand_means: float32 [768, 3072], P('shard')
- project_means: float32 [3072, 768], P('shard')
- vector_means: float32 [768, 12], P('shard')
- attend_squares: float32 [768, 3072], P('shard')
- expand_squares: float32 [768, 3072], P('shard')
- project_squares: float32 [3072, 768], P('shard')
- vector_squares: float32 [768, 12], P('shard')
- attend_weights: float32 [768, 3072], P('shard')
- expand_weights: float32 [768, 3072], P('shard')
- project_weights: float32 [3072, 768], P('shard')
- vector_weights: float32 [768, 12], P('shard')
The draws below stay inside these ranges and needn't reach their ends.
Inputs may be any that keep to these rules, and one draw needn't show every extreme that they name: `seq_lengths`: the sequences of one slot group, packed, fit its 1024 rows; each sequence has at least 128 tokens; the longest sequence has exactly 512 tokens. `seq_owner`: every slot group holds one to three sequences.
All inputs are finite; a program needn't handle non-finite values.
Results may differ from the reference program's by a relative error of at most 0.01.
The reference program's roundings to bfloat16 on the way count: a program that leaves them out, or rounds other values in their place, can miss the bound.
Values may be sent and summed in bfloat16 or wider, within the bound.
No kernel may reach another device: no remote copies, remote signals or barrier semaphores. Data moves between devices by JAX's collectives and lax.ppermute only.
A program may use at most 256 MiB of HBM per device.

```python
import math
import jax
import jax.numpy as jnp
from jax import lax

D = 768
HEADS = 12
HEAD_DIM = 64
FF = 3072
TOK_DEV = 1024
SEQ_LEN = 512
STEP = 10
SEQS = 64
TOKENS = 32768
N_DP = 8
N_SHARD = 4


def deal_sequences(key):
    order_key, length_key, shuffle_key = jax.random.split(key, 3)
    devices = SEQS // 2
    order = jax.random.permutation(order_key, devices).astype(jnp.int32)
    pattern = jnp.array([1, 2, 3, 2], dtype=jnp.int32)
    per_device = pattern[order % 4]
    ends = jnp.cumsum(per_device).astype(jnp.int32)
    base = jnp.arange(SEQS, dtype=jnp.int32)
    base_owner = jnp.sum((ends[None, :] <= base[:, None]).astype(jnp.int32), axis=1).astype(jnp.int32)
    limit = jnp.minimum(SEQ_LEN, TOK_DEV // per_device[base_owner])
    lowest = max(1, SEQ_LEN // 4)
    base_len = jax.random.randint(length_key, (SEQS,), lowest, limit + 1).astype(jnp.int32)
    first_slot = ends - per_device
    forced = jnp.sum(jnp.where(order == 0, first_slot, 0))
    base_len = jnp.where(base == forced, SEQ_LEN, base_len).astype(jnp.int32)
    shuffle = jax.random.permutation(shuffle_key, SEQS)
    return (base_owner[shuffle], base_len[shuffle])


def draw_seq_lengths(key, part):
    return deal_sequences(key)[1]


def draw_seq_owner(key, part):
    return deal_sequences(key)[0]


def draw_attend_master(key, part):
    key = jax.random.fold_in(key, 11)
    base = jax.random.normal(key, (D, 4 * D), jnp.float32)
    column = jnp.arange(4 * D)
    factor = jnp.where(column >= 3 * D, 3.0, 1.0) * D ** (-0.5)
    return base * factor[None, :]


def draw_vector_master(key, part):
    key = jax.random.fold_in(key, 12)
    gain_key, shift_key = jax.random.split(key)
    gains = jax.random.uniform(gain_key, (D, 12), jnp.float32, 0.5, 1.5)
    shifts = 0.3 * jax.random.normal(shift_key, (D, 12), jnp.float32)
    column = jnp.arange(12)
    is_gain = (column == 0) | (column == 2)
    return jnp.where(is_gain[None, :], gains, shifts)


def raised(drawn, own_key, source, target, parts, factor):
    owner, partner = [(jnp.arange(drawn.shape[axis_at]) // (drawn.shape[axis_at] // parts)).reshape([-1 if axis == axis_at else 1 for axis in range(drawn.ndim)]) for axis_at in (source, target)]
    chosen = jax.random.permutation(own_key, parts)[partner]
    strong = (owner == chosen) | (owner == (partner + parts // 2) % parts)
    return jnp.where(strong, factor * drawn, drawn)


def block_levels(own_key, dims, cuts, least, top_value):
    factor_of, own = 1.0, jax.random.fold_in(own_key, 6)
    for position, shards_of in cuts:
        heights = jnp.exp(jax.random.uniform(jax.random.fold_in(own, position), (shards_of,), jnp.float32, least / len(cuts), top_value / len(cuts)))
        factor_of = factor_of * jnp.repeat(heights, dims[position] // shards_of).reshape([-1 if axis == position else 1 for axis in range(len(dims))])
    return factor_of


def scatter_about(key, shape, scale, most, pieces=(), kind=jnp.bfloat16):
    factor_of = block_levels(key, shape, pieces, -0.22, 0.18) if pieces else 1.0
    entries = jax.random.normal(key, shape, jnp.float32) * scale * factor_of
    return jnp.minimum(jnp.maximum(entries, -most), most).astype(kind)


def gaussian_with(rng, shape, scale, most, cuts, heavy, kind=jnp.bfloat16):
    values = scale * jax.random.normal(rng, shape, jnp.float32)
    if cuts:
        values = values * block_levels(rng, shape, cuts, -0.22, 0.18)
    return jnp.clip(raised(values, jax.random.fold_in(rng, 3), *heavy), -most, most).astype(kind)


def setup_inputs(seed: int = 0) -> dict:
    key_of = jax.random.split(jax.random.key(seed), 17)
    tokens = scatter_about(key_of[0], (TOKENS, D), 1.0, 6.0, ((0, 32),))
    cotangent = gaussian_with(key_of[1], (TOKENS, D), 1.0, 6.0, ((0, 32),), (0, 1, 32, 2.75))
    seq_lengths = draw_seq_lengths(jax.random.fold_in(key_of[16], 71), 0)
    seq_owner = draw_seq_owner(jax.random.fold_in(key_of[16], 71), 0)
    attend_master = draw_attend_master(jax.random.fold_in(key_of[16], 71), 0)
    expand_master = scatter_about(key_of[5], (D, FF), D ** -0.5, 0.21875, ((0, 4),), jnp.float32)
    project_master = scatter_about(key_of[6], (FF, D), (FF // 4) ** -0.5, 0.21875, ((0, 4),), jnp.float32)
    vector_master = draw_vector_master(jax.random.fold_in(key_of[16], 71), 0)
    attend_mean = scatter_about(key_of[8], (D, 4 * D), (0.035 * TOKENS ** 0.5), 40.0, ((0, 4),), jnp.float32)
    expand_mean = scatter_about(key_of[9], (D, FF), (0.05 * TOKENS ** 0.5), 56.0, ((0, 4),), jnp.float32)
    project_mean = scatter_about(key_of[10], (FF, D), (0.05 * TOKENS ** 0.5), 56.0, ((0, 4),), jnp.float32)
    vector_mean = scatter_about(key_of[11], (D, 12), (0.06 * TOKENS ** 0.5), 64.0, ((0, 4),), jnp.float32)
    attend_square = jnp.clip(jnp.exp(math.log(13.1072) - 1.3862944 * jax.random.uniform(key_of[12], (D, 4 * D), jnp.float32) ** block_levels(key_of[12], (D, 4 * D), ((0, 4),), -0.2, 0.2)), 3.2768, 13.1072)
    expand_square = jnp.clip(jnp.exp(math.log(26.2144) - 1.3862944 * jax.random.uniform(key_of[13], (D, FF), jnp.float32) ** block_levels(key_of[13], (D, FF), ((0, 4),), -0.2, 0.2)), 6.5536, 26.2144)
    project_square = jnp.clip(jnp.exp(math.log(26.2144) - 1.3862944 * jax.random.uniform(key_of[14], (FF, D), jnp.float32) ** block_levels(key_of[14], (FF, D), ((0, 4),), -0.2, 0.2)), 6.5536, 26.2144)
    vector_square = jnp.clip(jnp.exp(math.log(39.3216) - 1.3862944 * jax.random.uniform(key_of[15], (D, 12), jnp.float32) ** block_levels(key_of[15], (D, 12), ((0, 4),), -0.2, 0.2)), 9.8304, 39.3216)
    return {"tokens": tokens, "cotangent": cotangent, "seq_lengths": seq_lengths, "seq_owner": seq_owner, "attend_master": attend_master, "expand_master": expand_master, "project_master": project_master, "vector_master": vector_master, "attend_mean": attend_mean, "expand_mean": expand_mean, "project_mean": project_mean, "vector_mean": vector_mean, "attend_square": attend_square, "expand_square": expand_square, "project_square": project_square, "vector_square": vector_square}


@jax.custom_vjp
def low(v):
    return lax.optimization_barrier(v.astype(jnp.bfloat16)).astype(jnp.float32)

@jax.custom_vjp
def low_back(v):
    return v

def low_keep(v):
    return (low(v), None)

def low_pass(kept, grad):
    return (grad,)

def back_keep(v):
    return (v, None)

def back_low(kept, grad):
    return (low(grad),)
low.defvjp(low_keep, low_pass)
low_back.defvjp(back_keep, back_low)
HIGH = lax.Precision.HIGHEST
NORM_EPS = 1e-05
MASK_FILL = -1e+30
BETA_ONE = 0.9
BETA_TWO = 0.999
ADAM_EPS = 1e-08
RATE_MATRIX = 0.05
RATE_VECTOR = 0.3
DECAY_MATRIX = 0.01

def layer_norm(values, gain, shift):
    centre = lax.optimization_barrier(jnp.mean(values, axis=-1, keepdims=True))
    centred = values - centre
    spread = lax.optimization_barrier(jnp.mean(centred * centred, axis=-1, keepdims=True))
    return centred * lax.rsqrt(spread + NORM_EPS) * gain + shift

def slot_segments(seq_lengths, seq_owner, device, slots):
    mine = seq_owner == device
    owned = jnp.where(mine, seq_lengths, 0).astype(jnp.int32)
    starts = (jnp.cumsum(owned) - owned).astype(jnp.int32)
    place = jnp.arange(slots, dtype=jnp.int32)[:, None]
    inside = mine[None, :] & (place >= starts[None, :]) & (place < (starts + owned)[None, :])
    labels = jnp.arange(seq_lengths.shape[0], dtype=jnp.int32)[None, :] + 1
    return (lax.optimization_barrier(jnp.sum(jnp.where(inside, labels, 0), axis=1)) - 1).astype(jnp.int32)

def device_block(rows, segment, attend, expand, project, vector):
    slots = rows.shape[0]
    normed_one = low(layer_norm(rows, vector[:, 0], vector[:, 1]))
    query = low_back(low(jnp.dot(normed_one, attend[:, :D], precision=HIGH) + vector[:, 4]))
    keyrows = low_back(low(jnp.dot(normed_one, attend[:, D:2 * D], precision=HIGH)))
    value = low_back(low(jnp.dot(normed_one, attend[:, 2 * D:3 * D], precision=HIGH) + vector[:, 5]))
    q_heads = query.reshape(slots, HEADS, HEAD_DIM)
    k_heads = keyrows.reshape(slots, HEADS, HEAD_DIM)
    v_heads = value.reshape(slots, HEADS, HEAD_DIM)
    scores = low_back(jnp.einsum('qhd,khd->hqk', q_heads, k_heads, precision=HIGH) * HEAD_DIM ** (-0.5))
    place = jnp.arange(slots, dtype=jnp.int32)
    permit = (segment[:, None] == segment[None, :]) & (place[None, :] <= place[:, None])
    probs = low(jax.nn.softmax(jnp.where(permit[None], scores, MASK_FILL), axis=-1))
    mixed = low_back(low(jnp.einsum('hqk,khd->qhd', probs, v_heads, precision=HIGH).reshape(slots, D)))
    resid = rows + low_back(jnp.dot(mixed, attend[:, 3 * D:], precision=HIGH) + vector[:, 6])
    normed_two = low(layer_norm(resid, vector[:, 2], vector[:, 3]))
    pre = low_back(jnp.dot(normed_two, expand, precision=HIGH) + vector[:, 8:].reshape(FF))
    act = low(jax.nn.gelu(pre, approximate=False))
    live = (segment >= 0).astype(jnp.float32)[:, None]
    return (resid + jnp.dot(act, project, precision=HIGH) + vector[:, 7]) * live

def layer(rows, attend, expand, project, vector, segments):
    count = segments.shape[0]
    stacked = rows.reshape(count, TOK_DEV, D)
    checked = jax.checkpoint(device_block)

    def one_group(pair):
        return checked(pair[0], pair[1], attend, expand, project, vector)
    return lax.map(one_group, (stacked, segments)).reshape(count * TOK_DEV, D)

def adam(master, mean, square, grad, rate, decay):
    mean_new = BETA_ONE * mean + (1.0 - BETA_ONE) * grad
    square_new = BETA_TWO * square + (1.0 - BETA_TWO) * grad * grad
    mean_hat = mean_new / (1.0 - BETA_ONE ** STEP)
    square_hat = square_new / (1.0 - BETA_TWO ** STEP)
    master_new = master - rate * (mean_hat / (jnp.sqrt(square_hat) + ADAM_EPS) + decay * master)
    return (mean_new, square_new, master_new)

def reference(tokens, cotangent, seq_lengths, seq_owner, attend_master, expand_master, project_master, vector_master, attend_mean, expand_mean, project_mean, vector_mean, attend_square, expand_square, project_square, vector_square):
    count = N_DP * N_SHARD
    segments = jax.vmap(lambda device: slot_segments(seq_lengths, seq_owner, device, TOK_DEV))(jnp.arange(count, dtype=jnp.int32))
    rows = tokens.astype(jnp.float32)
    attend = low(attend_master)
    expand = low(expand_master)
    project = low(project_master)
    vector = low(vector_master)

    def forward(rows_in, attend_in, expand_in, project_in, vector_in):
        return layer(rows_in, attend_in, expand_in, project_in, vector_in, segments)
    result, pullback = jax.vjp(forward, rows, attend, expand, project, vector)
    input_grad, attend_grad, expand_grad, project_grad, vector_grad = pullback(cotangent.astype(jnp.float32))
    attend_state = adam(attend_master, attend_mean, attend_square, attend_grad, RATE_MATRIX, DECAY_MATRIX)
    expand_state = adam(expand_master, expand_mean, expand_square, expand_grad, RATE_MATRIX, DECAY_MATRIX)
    project_state = adam(project_master, project_mean, project_square, project_grad, RATE_MATRIX, DECAY_MATRIX)
    vector_state = adam(vector_master, vector_mean, vector_square, vector_grad, RATE_VECTOR, 0.0)
    return (result.astype(jnp.bfloat16), input_grad, attend_state[0], expand_state[0], project_state[0], vector_state[0], attend_state[1], expand_state[1], project_state[1], vector_state[1], attend_state[2], expand_state[2], project_state[2], vector_state[2])
```

```python
import math

import jax
import jax.numpy as jnp
from jax import lax
from jax.experimental import pallas as pl
from jax.experimental.pallas import tpu as pltpu
from jax.sharding import PartitionSpec as P

HEADS = 12
HEAD_DIM = 64
STEP = 10


NORM_EPS = 1e-05
MASK_FILL = -1e30
BETA_ONE = 0.9
BETA_TWO = 0.999
ADAM_EPS = 1e-08
RATE_MATRIX = 0.05
RATE_VECTOR = 0.3
DECAY_MATRIX = 0.01


def layer_norm(values, gain, shift):
    centre = jnp.mean(values, axis=-1, keepdims=True)
    centred = values - centre
    spread = jnp.mean(centred * centred, axis=-1, keepdims=True)
    return centred * lax.rsqrt(spread + NORM_EPS) * gain + shift


def exact_gelu(values):
    return jax.nn.gelu(values, approximate=False)


def slot_segments(seq_lengths, seq_owner, device, slots):
    mine = seq_owner == device
    owned = jnp.where(mine, seq_lengths, 0)
    starts = jnp.cumsum(owned) - owned
    place = jnp.arange(slots, dtype=jnp.int32)[:, None]
    inside = mine[None, :] & (place >= starts[None, :]) & (place < (starts + owned)[None, :])
    labels = jnp.arange(seq_lengths.shape[0], dtype=jnp.int32)[None, :] + 1
    return jnp.sum(jnp.where(inside, labels, 0), axis=1) - 1


def allowed(segment, first, end):
    later = jnp.arange(first, end, dtype=jnp.int32)[:, None]
    earlier = jnp.arange(end, dtype=jnp.int32)[None, :]
    same = segment[first:end, None] == segment[None, :end]
    return same & (earlier <= later)


def block_scores(query, keyrows, segment, first, end, scale):
    scores = (
        jnp.einsum(
            "qhd,khd->hqk", query[first:end], keyrows[:end], preferred_element_type=jnp.float32
        )
        * scale
    )
    return jnp.where(allowed(segment, first, end)[None], scores, MASK_FILL)


def attention_forward(query, keyrows, value, segment, block, scale):
    slots = query.shape[0]
    mixed_parts = []
    log_parts = []
    for first in range(0, slots, block):
        end = first + block
        masked = block_scores(query, keyrows, segment, first, end, scale)
        top = jnp.max(masked, axis=-1, keepdims=True)
        expo = jnp.exp(masked - top)
        total = jnp.sum(expo, axis=-1, keepdims=True)
        probs = (expo / total).astype(jnp.bfloat16)
        mixed_parts.append(
            jnp.einsum(
                "hqk,khd->qhd", probs, value[:end], preferred_element_type=jnp.float32
            ).astype(jnp.bfloat16)
        )
        log_parts.append(top + jnp.log(total))
    return (jnp.concatenate(mixed_parts, axis=0), log_parts)


def attention_backward(query, keyrows, value, grad_mixed, segment, log_parts, block, scale):
    slots = query.shape[0]
    grad_keys = jnp.zeros(keyrows.shape, jnp.float32)
    grad_values = jnp.zeros(value.shape, jnp.float32)
    query_parts = []
    for number, first in enumerate(range(0, slots, block)):
        end = first + block
        masked = block_scores(query, keyrows, segment, first, end, scale)
        probs = jnp.exp(masked - log_parts[number])
        probs_low = probs.astype(jnp.bfloat16)
        grad_part = grad_mixed[first:end]
        grad_values = grad_values.at[:end].add(
            jnp.einsum("hqk,qhd->khd", probs_low, grad_part, preferred_element_type=jnp.float32)
        )
        grad_probs = jnp.einsum(
            "qhd,khd->hqk", grad_part, value[:end], preferred_element_type=jnp.float32
        )
        grad_scores = probs * (grad_probs - jnp.sum(probs * grad_probs, axis=-1, keepdims=True))
        grad_low = grad_scores.astype(jnp.bfloat16)
        query_parts.append(
            jnp.einsum("hqk,khd->qhd", grad_low, keyrows[:end], preferred_element_type=jnp.float32)
            * scale
        )
        grad_keys = grad_keys.at[:end].add(
            jnp.einsum(
                "hqk,qhd->khd", grad_low, query[first:end], preferred_element_type=jnp.float32
            )
            * scale
        )
    return (jnp.concatenate(query_parts, axis=0), grad_keys, grad_values)


def adam(master, mean, square, grad, rate, decay):
    mean_new = BETA_ONE * mean + (1.0 - BETA_ONE) * grad
    square_new = BETA_TWO * square + (1.0 - BETA_TWO) * grad * grad
    mean_hat = mean_new / (1.0 - BETA_ONE**STEP)
    square_hat = square_new / (1.0 - BETA_TWO**STEP)
    master_new = master - rate * (mean_hat / (jnp.sqrt(square_hat) + ADAM_EPS) + decay * master)
    return (mean_new, square_new, master_new)


class Ring:
    def __init__(self):
        self.group = lax.axis_size("shard")
        self.data = lax.axis_size("dp")
        self.plane = self.data // 2
        self.side = math.isqrt(self.plane)
        self.square = self.data == 2 * self.side * self.side
        self.z = lax.axis_index("shard")
        device = lax.axis_index("dp")
        self.core = device % 2
        chip = device // 2
        high, low = chip // self.side, chip % self.side
        straight = low * self.side + high
        crossed = high * self.side + low
        self.block = jnp.where(self.core == 0, straight, crossed)
        self.block_other = jnp.where(self.core == 0, crossed, straight)

    def fits(self, rows, columns):
        return self.square and rows % (16 * self.plane) == 0 and columns % 256 == 0

    def send_core(self, value):
        return lax.ppermute(value, "dp", [(i, i ^ 1) for i in range(self.data)])

    def send_plane(self, value, step):
        side = self.side
        first, second = step // side, step % side
        pairs = []
        for device in range(self.data):
            core, chip = device % 2, device // 2
            high, low = chip // side, chip % side
            if core == 0:
                low, high = (low + first) % side, (high + second) % side
            else:
                high, low = (high + first) % side, (low + second) % side
            pairs.append((device, (high * side + low) * 2 + core))
        return lax.ppermute(value, "dp", pairs)

    def shifted(self, block, step):
        side = self.side
        first, second = step // side, step % side
        return (block // side + first) % side * side + (block % side + second) % side

    def back(self, block, step):
        side = self.side
        first, second = step // side, step % side
        return (block // side - first) % side * side + (block % side - second) % side

    def send_shard(self, value, step):
        group = self.group
        return lax.ppermute(value, "shard", [(i, (i + step) % group) for i in range(group)])


def place_pieces(own, mine, other, ring):
    group, plane = ring.group, ring.plane
    rows, columns = own.shape
    piece, half = rows // plane, columns // 2
    scalars = [ring.z, ring.core]
    scalars += [ring.back(ring.block, step) for step in range(plane)]
    scalars += [ring.back(ring.block_other, step) for step in range(plane)]
    where = jnp.stack([jnp.asarray(v, jnp.int32) for v in scalars])
    count = 1 + 2 * plane * (group - 1)

    def kernel(where_ref, own_ref, *refs):
        pieces, out_ref, sems = refs[: 2 * plane], refs[-2], refs[-1]
        z, core = where_ref[0], where_ref[1]
        copies = []

        def begin(source, first_row, height, first_column, width):
            target = out_ref.at[pl.ds(first_row, height), pl.ds(first_column, width)]
            copy = pltpu.make_async_copy(source, target, sems.at[len(copies)])
            copy.start()
            copies.append(copy)

        begin(own_ref, pl.multiple_of(z * rows, 16), rows, 0, columns)
        for number, ref in enumerate(pieces):
            block = where_ref[2 + number]
            column = pl.multiple_of((core if number < plane else 1 - core) * half, 128)
            for step in range(1, group):
                source = lax.rem(z - step + group, group)
                row = pl.multiple_of(source * rows + block * piece, 16)
                begin(ref.at[step - 1], row, piece, column, half)
        for copy in copies:
            copy.wait()

    return pl.pallas_call(
        kernel,
        out_shape=jax.ShapeDtypeStruct((rows * group, columns), own.dtype),
        in_specs=[pl.BlockSpec(memory_space=pltpu.SMEM)]
        + [pl.BlockSpec(memory_space=pl.ANY)] * (1 + 2 * plane),
        out_specs=pl.BlockSpec(memory_space=pl.ANY),
        scratch_shapes=[pltpu.SemaphoreType.DMA((count,))],
        name="place_pieces",
    )(where, own, *mine, *other)


def gather_weight(master, ring):
    rows, columns = master.shape
    own = master.astype(jnp.bfloat16)
    if not ring.fits(rows, columns):
        return lax.all_gather(own, "shard", axis=0, tiled=True)
    piece, half = rows // ring.plane, columns // 2
    chunk = lax.dynamic_slice(
        master, (ring.block * piece, ring.core * half), (piece, half)
    ).astype(jnp.bfloat16)
    foreign = jnp.stack([ring.send_shard(chunk, step) for step in range(1, ring.group)])
    mine = [foreign] + [ring.send_plane(foreign, step) for step in range(1, ring.plane)]
    other = [ring.send_core(value) for value in mine]
    return place_pieces(own, mine, other, ring)


def sum_gradient(grad, ring):
    total, columns = grad.shape
    group, plane = ring.group, ring.plane
    rows = total // group
    if not ring.fits(rows, columns):
        whole = lax.psum_scatter(
            grad.astype(jnp.float32), "shard", scatter_dimension=0, tiled=True
        )
        return lax.psum(whole, "dp")
    piece, half = rows // plane, columns // 2
    kept = lax.dynamic_slice(grad, (0, ring.core * half), (total, half))
    sent = lax.dynamic_slice(grad, (0, (1 - ring.core) * half), (total, half))
    got = ring.send_core(sent)
    chip = (kept.astype(jnp.float32) + got.astype(jnp.float32)).astype(jnp.bfloat16)
    chip = chip.reshape(group, plane, piece, half)

    def block_of(step):
        block = ring.shifted(ring.block, step)
        return lax.dynamic_index_in_dim(chip, block, 1, keepdims=False)

    arrived = [ring.send_plane(block_of(step), step) for step in range(1, plane)]
    level = block_of(0).astype(jnp.float32)
    for value in arrived:
        level = level + value.astype(jnp.float32)
    level = level.astype(jnp.bfloat16)

    def shard_of(step):
        return lax.dynamic_index_in_dim(level, (ring.z + step) % group, 0, keepdims=False)

    arrived = [ring.send_shard(shard_of(step), step) for step in range(1, group)]
    done = shard_of(0).astype(jnp.float32)
    for value in arrived:
        done = done + value.astype(jnp.float32)
    done = done.astype(jnp.bfloat16)
    blocks = [done] + [ring.send_plane(done, step) for step in range(1, plane)]
    column = in_order(blocks, ring, ring.block)
    other = ring.send_core(column)
    low = jnp.where(ring.core == 0, column, other)
    high = jnp.where(ring.core == 0, other, column)
    return jnp.concatenate([low, high], axis=1).astype(jnp.float32)


def in_order(blocks, ring, block):
    side, plane = ring.side, ring.plane
    parts = []
    for target in range(plane):
        value = blocks[0]
        for step in range(1, plane):
            value = jnp.where(ring.back(block, step) == target, blocks[step], value)
        parts.append(value)
    return jnp.concatenate(parts, axis=0)


def gather_vector(master, ring):
    own = master.astype(jnp.bfloat16)
    group = ring.group
    parts = [own] + [ring.send_shard(own, step) for step in range(1, group)]
    stacked = jnp.stack(parts)
    order = (ring.z - jnp.arange(group)) % group
    return jnp.take(stacked, order, axis=0).reshape(group * own.shape[0], own.shape[1])


def sum_vector(grad, ring):
    group = ring.group
    if not ring.square or ring.side != 2:
        whole = lax.psum_scatter(grad, "shard", scatter_dimension=0, tiled=True)
        return lax.psum(whole, "dp")
    flat = grad.reshape(group, -1, 128)
    flat = flat + ring.send_core(flat)
    for bit in (2, 4):
        flat = flat + lax.ppermute(flat, "dp", [(i, i ^ bit) for i in range(ring.data)])

    def shard_of(step):
        return lax.dynamic_index_in_dim(flat, (ring.z + step) % group, 0, keepdims=False)

    done = shard_of(0)
    for step in range(1, group):
        done = done + ring.send_shard(shard_of(step), step)
    return done.reshape(grad.shape[0] // group, grad.shape[1])


def on_device(
    tokens,
    cotangent,
    seq_lengths,
    seq_owner,
    attend_master,
    expand_master,
    project_master,
    vector_master,
    attend_mean,
    expand_mean,
    project_mean,
    vector_mean,
    attend_square,
    expand_square,
    project_square,
    vector_square,
):
    ring = Ring()
    width = tokens.shape[1]
    vector = gather_vector(vector_master, ring)
    inner = gather_weight(attend_master[:, : 3 * width], ring)
    outer = gather_weight(attend_master[:, 3 * width :], ring)
    expand = gather_weight(expand_master, ring)
    project = gather_weight(project_master, ring)
    slots, width = tokens.shape
    heads = HEADS
    head_width = HEAD_DIM
    scale = head_width ** (-0.5)
    block = min(512, slots)
    device = lax.axis_index("dp") * ring.group + ring.z
    segment = slot_segments(seq_lengths, seq_owner, device, slots)
    live = (segment >= 0).astype(jnp.float32)[:, None]
    params = vector.astype(jnp.float32)
    rows = tokens.astype(jnp.float32)
    normed_one, pull_one = jax.vjp(layer_norm, rows, params[:, 0], params[:, 1])
    normed_one_low = normed_one.astype(jnp.bfloat16)
    bias_inner = jnp.concatenate([params[:, 4], jnp.zeros((width,), jnp.float32), params[:, 5]])
    projected = (
        jnp.dot(normed_one_low, inner, preferred_element_type=jnp.float32) + bias_inner
    ).astype(jnp.bfloat16)
    query = projected[:, :width].reshape(slots, heads, head_width)
    keyrows = projected[:, width : 2 * width].reshape(slots, heads, head_width)
    value = projected[:, 2 * width :].reshape(slots, heads, head_width)
    mixed, log_parts = attention_forward(query, keyrows, value, segment, block, scale)
    mixed_flat = mixed.reshape(slots, width)
    resid = rows + (jnp.dot(mixed_flat, outer, preferred_element_type=jnp.float32) + params[:, 6])
    normed_two, pull_two = jax.vjp(layer_norm, resid, params[:, 2], params[:, 3])
    normed_two_low = normed_two.astype(jnp.bfloat16)
    pre = jnp.dot(normed_two_low, expand, preferred_element_type=jnp.float32) + params[
        :, 8:
    ].reshape(-1)
    act, pull_gelu = jax.vjp(exact_gelu, pre)
    act_low = act.astype(jnp.bfloat16)
    layer_output = (
        (resid + jnp.dot(act_low, project, preferred_element_type=jnp.float32) + params[:, 7])
        * live
    ).astype(jnp.bfloat16)
    back = cotangent.astype(jnp.float32) * live
    back_low = back.astype(jnp.bfloat16)
    project_grad = jnp.einsum("tf,td->fd", act_low, back_low, preferred_element_type=jnp.float32)
    grad_act = jnp.einsum("td,fd->tf", back_low, project, preferred_element_type=jnp.float32)
    grad_pre = pull_gelu(grad_act)[0]
    grad_pre_low = grad_pre.astype(jnp.bfloat16)
    expand_grad = jnp.einsum(
        "td,tf->df", normed_two_low, grad_pre_low, preferred_element_type=jnp.float32
    )
    grad_two = jnp.einsum("tf,df->td", grad_pre_low, expand, preferred_element_type=jnp.float32)
    grad_resid_norm, gain_two, shift_two = pull_two(grad_two)
    grad_resid = back + grad_resid_norm
    grad_attn_low = grad_resid.astype(jnp.bfloat16)
    outer_grad = jnp.einsum(
        "td,te->de", mixed_flat, grad_attn_low, preferred_element_type=jnp.float32
    )
    grad_mixed = jnp.einsum("te,de->td", grad_attn_low, outer, preferred_element_type=jnp.float32)
    grad_mixed_low = grad_mixed.astype(jnp.bfloat16).reshape(slots, heads, head_width)
    grad_query, grad_keys, grad_values = attention_backward(
        query, keyrows, value, grad_mixed_low, segment, log_parts, block, scale
    )
    grad_inner_low = jnp.concatenate(
        [
            grad_query.reshape(slots, width),
            grad_keys.reshape(slots, width),
            grad_values.reshape(slots, width),
        ],
        axis=1,
    ).astype(jnp.bfloat16)
    inner_grad = jnp.einsum(
        "td,te->de", normed_one_low, grad_inner_low, preferred_element_type=jnp.float32
    )
    grad_one = jnp.einsum("te,de->td", grad_inner_low, inner, preferred_element_type=jnp.float32)
    grad_rows_norm, gain_one, shift_one = pull_one(grad_one)
    input_grad = grad_resid + grad_rows_norm
    inner_sums = jnp.sum(grad_inner_low, axis=0, dtype=jnp.float32)
    columns = jnp.stack(
        [
            gain_one,
            shift_one,
            gain_two,
            shift_two,
            inner_sums[:width],
            inner_sums[2 * width :],
            jnp.sum(grad_attn_low, axis=0, dtype=jnp.float32),
            jnp.sum(back, axis=0),
        ],
        axis=1,
    )
    vector_grad = jnp.concatenate(
        [columns, jnp.sum(grad_pre_low, axis=0, dtype=jnp.float32).reshape(width, 4)], axis=1
    )
    attend_sum = jnp.concatenate(
        [
            sum_gradient(inner_grad.astype(jnp.bfloat16), ring),
            sum_gradient(outer_grad.astype(jnp.bfloat16), ring),
        ],
        axis=1,
    )
    expand_sum = sum_gradient(expand_grad.astype(jnp.bfloat16), ring)
    project_sum = sum_gradient(project_grad.astype(jnp.bfloat16), ring)
    vector_sum = sum_vector(vector_grad, ring)
    attend_state = adam(
        attend_master, attend_mean, attend_square, attend_sum, RATE_MATRIX, DECAY_MATRIX
    )
    expand_state = adam(
        expand_master, expand_mean, expand_square, expand_sum, RATE_MATRIX, DECAY_MATRIX
    )
    project_state = adam(
        project_master, project_mean, project_square, project_sum, RATE_MATRIX, DECAY_MATRIX
    )
    vector_state = adam(vector_master, vector_mean, vector_square, vector_sum, RATE_VECTOR, 0.0)
    return (
        layer_output,
        input_grad,
        attend_state[0],
        expand_state[0],
        project_state[0],
        vector_state[0],
        attend_state[1],
        expand_state[1],
        project_state[1],
        vector_state[1],
        attend_state[2],
        expand_state[2],
        project_state[2],
        vector_state[2],
    )


def solution(mesh):
    return jax.shard_map(
        on_device,
        mesh=mesh,
        in_specs=(
            P(("dp", "shard"), None),
            P(("dp", "shard"), None),
            P(),
            P(),
            P("shard", None),
            P("shard", None),
            P("shard", None),
            P("shard", None),
            P("shard", None),
            P("shard", None),
            P("shard", None),
            P("shard", None),
            P("shard", None),
            P("shard", None),
            P("shard", None),
            P("shard", None),
        ),
        out_specs=(
            P(("dp", "shard"), None),
            P(("dp", "shard"), None),
            P("shard", None),
            P("shard", None),
            P("shard", None),
            P("shard", None),
            P("shard", None),
            P("shard", None),
            P("shard", None),
            P("shard", None),
            P("shard", None),
            P("shard", None),
            P("shard", None),
            P("shard", None),
        ),
        check_vma=False,
    )
```

```python
import math

import jax
import jax.numpy as jnp
from jax import lax
from jax.experimental import pallas as pl
from jax.experimental.pallas import tpu as pltpu
from jax.sharding import PartitionSpec as P

HEADS = 12
HEAD_DIM = 64
STEP = 10


NORM_EPS = 1e-05
MASK_FILL = -1e30
BETA_ONE = 0.9
BETA_TWO = 0.999
ADAM_EPS = 1e-08
RATE_MATRIX = 0.05
RATE_VECTOR = 0.3
DECAY_MATRIX = 0.01


def layer_norm(values, gain, shift):
    centre = jnp.mean(values, axis=-1, keepdims=True)
    centred = values - centre
    spread = jnp.mean(centred * centred, axis=-1, keepdims=True)
    return centred * lax.rsqrt(spread + NORM_EPS) * gain + shift


def exact_gelu(values):
    return jax.nn.gelu(values, approximate=False)


def slot_segments(seq_lengths, seq_owner, device, slots):
    mine = seq_owner == device
    owned = jnp.where(mine, seq_lengths, 0)
    starts = jnp.cumsum(owned) - owned
    place = jnp.arange(slots, dtype=jnp.int32)[:, None]
    inside = mine[None, :] & (place >= starts[None, :]) & (place < (starts + owned)[None, :])
    labels = jnp.arange(seq_lengths.shape[0], dtype=jnp.int32)[None, :] + 1
    return jnp.sum(jnp.where(inside, labels, 0), axis=1) - 1


def allowed(segment, first, end):
    later = jnp.arange(first, end, dtype=jnp.int32)[:, None]
    earlier = jnp.arange(end, dtype=jnp.int32)[None, :]
    same = segment[first:end, None] == segment[None, :end]
    return same & (earlier <= later)


def block_scores(query, keyrows, segment, first, end, scale):
    scores = (
        jnp.einsum(
            "qhd,khd->hqk", query[first:end], keyrows[:end], preferred_element_type=jnp.float32
        )
        * scale
    )
    return jnp.where(allowed(segment, first, end)[None], scores, MASK_FILL)


def attention_forward(query, keyrows, value, segment, block, scale):
    slots = query.shape[0]
    mixed_parts = []
    log_parts = []
    for first in range(0, slots, block):
        end = first + block
        masked = block_scores(query, keyrows, segment, first, end, scale)
        top = jnp.max(masked, axis=-1, keepdims=True)
        expo = jnp.exp(masked - top)
        total = jnp.sum(expo, axis=-1, keepdims=True)
        probs = (expo / total).astype(jnp.bfloat16)
        mixed_parts.append(
            jnp.einsum(
                "hqk,khd->qhd", probs, value[:end], preferred_element_type=jnp.float32
            ).astype(jnp.bfloat16)
        )
        log_parts.append(top + jnp.log(total))
    return (jnp.concatenate(mixed_parts, axis=0), log_parts)


def attention_backward(query, keyrows, value, grad_mixed, segment, log_parts, block, scale):
    slots = query.shape[0]
    grad_keys = jnp.zeros(keyrows.shape, jnp.float32)
    grad_values = jnp.zeros(value.shape, jnp.float32)
    query_parts = []
    for number, first in enumerate(range(0, slots, block)):
        end = first + block
        masked = block_scores(query, keyrows, segment, first, end, scale)
        probs = jnp.exp(masked - log_parts[number])
        probs_low = probs.astype(jnp.bfloat16)
        grad_part = grad_mixed[first:end]
        grad_values = grad_values.at[:end].add(
            jnp.einsum("hqk,qhd->khd", probs_low, grad_part, preferred_element_type=jnp.float32)
        )
        grad_probs = jnp.einsum(
            "qhd,khd->hqk", grad_part, value[:end], preferred_element_type=jnp.float32
        )
        grad_scores = probs * (grad_probs - jnp.sum(probs * grad_probs, axis=-1, keepdims=True))
        grad_low = grad_scores.astype(jnp.bfloat16)
        query_parts.append(
            jnp.einsum("hqk,khd->qhd", grad_low, keyrows[:end], preferred_element_type=jnp.float32)
            * scale
        )
        grad_keys = grad_keys.at[:end].add(
            jnp.einsum(
                "hqk,qhd->khd", grad_low, query[first:end], preferred_element_type=jnp.float32
            )
            * scale
        )
    return (jnp.concatenate(query_parts, axis=0), grad_keys, grad_values)


def adam(master, mean, square, grad, rate, decay):
    mean_new = BETA_ONE * mean + (1.0 - BETA_ONE) * grad
    square_new = BETA_TWO * square + (1.0 - BETA_TWO) * grad * grad
    mean_hat = mean_new / (1.0 - BETA_ONE**STEP)
    square_hat = square_new / (1.0 - BETA_TWO**STEP)
    master_new = master - rate * (mean_hat / (jnp.sqrt(square_hat) + ADAM_EPS) + decay * master)
    return (mean_new, square_new, master_new)


class Ring:
    def __init__(self):
        self.group = lax.axis_size("shard")
        self.data = lax.axis_size("dp")
        self.plane = self.data // 2
        self.side = math.isqrt(self.plane)
        self.square = self.data == 2 * self.side * self.side
        self.z = lax.axis_index("shard")
        device = lax.axis_index("dp")
        self.core = device % 2
        chip = device // 2
        high, low = chip // self.side, chip % self.side
        straight = low * self.side + high
        crossed = high * self.side + low
        self.block = jnp.where(self.core == 0, straight, crossed)
        self.block_other = jnp.where(self.core == 0, crossed, straight)

    def fits(self, rows, columns):
        return self.square and rows % (16 * self.plane) == 0 and columns % 256 == 0

    def send_core(self, value):
        return lax.ppermute(value, "dp", [(i, i ^ 1) for i in range(self.data)])

    def send_plane(self, value, step):
        side = self.side
        first, second = step // side, step % side
        pairs = []
        for device in range(self.data):
            core, chip = device % 2, device // 2
            high, low = chip // side, chip % side
            if core == 0:
                low, high = (low + first) % side, (high + second) % side
            else:
                high, low = (high + first) % side, (low + second) % side
            pairs.append((device, (high * side + low) * 2 + core))
        return lax.ppermute(value, "dp", pairs)

    def shifted(self, block, step):
        side = self.side
        first, second = step // side, step % side
        return (block // side + first) % side * side + (block % side + second) % side

    def back(self, block, step):
        side = self.side
        first, second = step // side, step % side
        return (block // side - first) % side * side + (block % side - second) % side

    def send_shard(self, value, step):
        group = self.group
        return lax.ppermute(value, "shard", [(i, (i + step) % group) for i in range(group)])


def place_pieces(own, mine, other, ring):
    group, plane = ring.group, ring.plane
    rows, columns = own.shape
    piece, half = rows // plane, columns // 2
    scalars = [ring.z, ring.core]
    scalars += [ring.back(ring.block, step) for step in range(plane)]
    scalars += [ring.back(ring.block_other, step) for step in range(plane)]
    where = jnp.stack([jnp.asarray(v, jnp.int32) for v in scalars])
    count = 1 + 2 * plane * (group - 1)

    def kernel(where_ref, own_ref, *refs):
        pieces, out_ref, sems = refs[: 2 * plane], refs[-2], refs[-1]
        z, core = where_ref[0], where_ref[1]
        copies = []

        def begin(source, first_row, height, first_column, width):
            target = out_ref.at[pl.ds(first_row, height), pl.ds(first_column, width)]
            copy = pltpu.make_async_copy(source, target, sems.at[len(copies)])
            copy.start()
            copies.append(copy)

        begin(own_ref, pl.multiple_of(z * rows, 16), rows, 0, columns)
        for number, ref in enumerate(pieces):
            block = where_ref[2 + number]
            column = pl.multiple_of((core if number < plane else 1 - core) * half, 128)
            for step in range(1, group):
                source = lax.rem(z - step + group, group)
                row = pl.multiple_of(source * rows + block * piece, 16)
                begin(ref.at[step - 1], row, piece, column, half)
        for copy in copies:
            copy.wait()

    return pl.pallas_call(
        kernel,
        out_shape=jax.ShapeDtypeStruct((rows * group, columns), own.dtype),
        in_specs=[pl.BlockSpec(memory_space=pltpu.SMEM)]
        + [pl.BlockSpec(memory_space=pl.ANY)] * (1 + 2 * plane),
        out_specs=pl.BlockSpec(memory_space=pltpu.VMEM),
        scratch_shapes=[pltpu.SemaphoreType.DMA((count,))],
        compiler_params=pltpu.CompilerParams(vmem_limit_bytes=16 * 1024 * 1024),
        name="place_pieces",
    )(where, own, *mine, *other)


def gather_weight(master, ring):
    rows, columns = master.shape
    own = master.astype(jnp.bfloat16)
    if not ring.fits(rows, columns):
        return lax.all_gather(own, "shard", axis=0, tiled=True)
    piece, half = rows // ring.plane, columns // 2
    chunk = lax.dynamic_slice(
        master, (ring.block * piece, ring.core * half), (piece, half)
    ).astype(jnp.bfloat16)
    foreign = jnp.stack([ring.send_shard(chunk, step) for step in range(1, ring.group)])
    mine = [foreign] + [ring.send_plane(foreign, step) for step in range(1, ring.plane)]
    other = [ring.send_core(value) for value in mine]
    return place_pieces(own, mine, other, ring)


def sum_gradient(grad, ring):
    total, columns = grad.shape
    group, plane = ring.group, ring.plane
    rows = total // group
    if not ring.fits(rows, columns):
        whole = lax.psum_scatter(
            grad.astype(jnp.float32), "shard", scatter_dimension=0, tiled=True
        )
        return lax.psum(whole, "dp")
    piece, half = rows // plane, columns // 2
    kept = lax.dynamic_slice(grad, (0, ring.core * half), (total, half))
    sent = lax.dynamic_slice(grad, (0, (1 - ring.core) * half), (total, half))
    got = ring.send_core(sent)
    chip = (kept.astype(jnp.float32) + got.astype(jnp.float32)).astype(jnp.bfloat16)
    chip = chip.reshape(group, plane, piece, half)

    def block_of(step):
        block = ring.shifted(ring.block, step)
        return lax.dynamic_index_in_dim(chip, block, 1, keepdims=False)

    arrived = [ring.send_plane(block_of(step), step) for step in range(1, plane)]
    level = block_of(0).astype(jnp.float32)
    for value in arrived:
        level = level + value.astype(jnp.float32)
    level = level.astype(jnp.bfloat16)

    def shard_of(step):
        return lax.dynamic_index_in_dim(level, (ring.z + step) % group, 0, keepdims=False)

    arrived = [ring.send_shard(shard_of(step), step) for step in range(1, group)]
    done = shard_of(0).astype(jnp.float32)
    for value in arrived:
        done = done + value.astype(jnp.float32)
    done = done.astype(jnp.bfloat16)
    blocks = [done] + [ring.send_plane(done, step) for step in range(1, plane)]
    column = in_order(blocks, ring, ring.block)
    other = ring.send_core(column)
    low = jnp.where(ring.core == 0, column, other)
    high = jnp.where(ring.core == 0, other, column)
    return jnp.concatenate([low, high], axis=1).astype(jnp.float32)


def in_order(blocks, ring, block):
    side, plane = ring.side, ring.plane
    parts = []
    for target in range(plane):
        value = blocks[0]
        for step in range(1, plane):
            value = jnp.where(ring.back(block, step) == target, blocks[step], value)
        parts.append(value)
    return jnp.concatenate(parts, axis=0)


def gather_vector(master, ring):
    own = master.astype(jnp.bfloat16)
    group = ring.group
    parts = [own] + [ring.send_shard(own, step) for step in range(1, group)]
    stacked = jnp.stack(parts)
    order = (ring.z - jnp.arange(group)) % group
    return jnp.take(stacked, order, axis=0).reshape(group * own.shape[0], own.shape[1])


def sum_vector(grad, ring):
    group = ring.group
    if not ring.square or ring.side != 2:
        whole = lax.psum_scatter(grad, "shard", scatter_dimension=0, tiled=True)
        return lax.psum(whole, "dp")
    flat = grad.reshape(group, -1, 128)
    flat = flat + ring.send_core(flat)
    for bit in (2, 4):
        flat = flat + lax.ppermute(flat, "dp", [(i, i ^ bit) for i in range(ring.data)])

    def shard_of(step):
        return lax.dynamic_index_in_dim(flat, (ring.z + step) % group, 0, keepdims=False)

    done = shard_of(0)
    for step in range(1, group):
        done = done + ring.send_shard(shard_of(step), step)
    return done.reshape(grad.shape[0] // group, grad.shape[1])


def on_device(
    tokens,
    cotangent,
    seq_lengths,
    seq_owner,
    attend_master,
    expand_master,
    project_master,
    vector_master,
    attend_mean,
    expand_mean,
    project_mean,
    vector_mean,
    attend_square,
    expand_square,
    project_square,
    vector_square,
):
    ring = Ring()
    width = tokens.shape[1]
    vector = gather_vector(vector_master, ring)
    inner = gather_weight(attend_master[:, : 3 * width], ring)
    outer = gather_weight(attend_master[:, 3 * width :], ring)
    expand = gather_weight(expand_master, ring)
    project = gather_weight(project_master, ring)
    slots, width = tokens.shape
    heads = HEADS
    head_width = HEAD_DIM
    scale = head_width ** (-0.5)
    block = min(512, slots)
    device = lax.axis_index("dp") * ring.group + ring.z
    segment = slot_segments(seq_lengths, seq_owner, device, slots)
    live = (segment >= 0).astype(jnp.float32)[:, None]
    params = vector.astype(jnp.float32)
    rows = tokens.astype(jnp.float32)
    normed_one, pull_one = jax.vjp(layer_norm, rows, params[:, 0], params[:, 1])
    normed_one_low = normed_one.astype(jnp.bfloat16)
    bias_inner = jnp.concatenate([params[:, 4], jnp.zeros((width,), jnp.float32), params[:, 5]])
    projected = (
        jnp.dot(normed_one_low, inner, preferred_element_type=jnp.float32) + bias_inner
    ).astype(jnp.bfloat16)
    query = projected[:, :width].reshape(slots, heads, head_width)
    keyrows = projected[:, width : 2 * width].reshape(slots, heads, head_width)
    value = projected[:, 2 * width :].reshape(slots, heads, head_width)
    mixed, log_parts = attention_forward(query, keyrows, value, segment, block, scale)
    mixed_flat = mixed.reshape(slots, width)
    resid = rows + (jnp.dot(mixed_flat, outer, preferred_element_type=jnp.float32) + params[:, 6])
    normed_two, pull_two = jax.vjp(layer_norm, resid, params[:, 2], params[:, 3])
    normed_two_low = normed_two.astype(jnp.bfloat16)
    pre = jnp.dot(normed_two_low, expand, preferred_element_type=jnp.float32) + params[
        :, 8:
    ].reshape(-1)
    act, pull_gelu = jax.vjp(exact_gelu, pre)
    act_low = act.astype(jnp.bfloat16)
    layer_output = (
        (resid + jnp.dot(act_low, project, preferred_element_type=jnp.float32) + params[:, 7])
        * live
    ).astype(jnp.bfloat16)
    back = cotangent.astype(jnp.float32) * live
    back_low = back.astype(jnp.bfloat16)
    project_grad = jnp.einsum("tf,td->fd", act_low, back_low, preferred_element_type=jnp.float32)
    grad_act = jnp.einsum("td,fd->tf", back_low, project, preferred_element_type=jnp.float32)
    grad_pre = pull_gelu(grad_act)[0]
    grad_pre_low = grad_pre.astype(jnp.bfloat16)
    expand_grad = jnp.einsum(
        "td,tf->df", normed_two_low, grad_pre_low, preferred_element_type=jnp.float32
    )
    grad_two = jnp.einsum("tf,df->td", grad_pre_low, expand, preferred_element_type=jnp.float32)
    grad_resid_norm, gain_two, shift_two = pull_two(grad_two)
    grad_resid = back + grad_resid_norm
    grad_attn_low = grad_resid.astype(jnp.bfloat16)
    outer_grad = jnp.einsum(
        "td,te->de", mixed_flat, grad_attn_low, preferred_element_type=jnp.float32
    )
    grad_mixed = jnp.einsum("te,de->td", grad_attn_low, outer, preferred_element_type=jnp.float32)
    grad_mixed_low = grad_mixed.astype(jnp.bfloat16).reshape(slots, heads, head_width)
    grad_query, grad_keys, grad_values = attention_backward(
        query, keyrows, value, grad_mixed_low, segment, log_parts, block, scale
    )
    grad_inner_low = jnp.concatenate(
        [
            grad_query.reshape(slots, width),
            grad_keys.reshape(slots, width),
            grad_values.reshape(slots, width),
        ],
        axis=1,
    ).astype(jnp.bfloat16)
    inner_grad = jnp.einsum(
        "td,te->de", normed_one_low, grad_inner_low, preferred_element_type=jnp.float32
    )
    grad_one = jnp.einsum("te,de->td", grad_inner_low, inner, preferred_element_type=jnp.float32)
    grad_rows_norm, gain_one, shift_one = pull_one(grad_one)
    input_grad = grad_resid + grad_rows_norm
    inner_sums = jnp.sum(grad_inner_low, axis=0, dtype=jnp.float32)
    columns = jnp.stack(
        [
            gain_one,
            shift_one,
            gain_two,
            shift_two,
            inner_sums[:width],
            inner_sums[2 * width :],
            jnp.sum(grad_attn_low, axis=0, dtype=jnp.float32),
            jnp.sum(back, axis=0),
        ],
        axis=1,
    )
    vector_grad = jnp.concatenate(
        [columns, jnp.sum(grad_pre_low, axis=0, dtype=jnp.float32).reshape(width, 4)], axis=1
    )
    attend_sum = jnp.concatenate(
        [
            sum_gradient(inner_grad.astype(jnp.bfloat16), ring),
            sum_gradient(outer_grad.astype(jnp.bfloat16), ring),
        ],
        axis=1,
    )
    expand_sum = sum_gradient(expand_grad.astype(jnp.bfloat16), ring)
    project_sum = sum_gradient(project_grad.astype(jnp.bfloat16), ring)
    vector_sum = sum_vector(vector_grad, ring)
    attend_state = adam(
        attend_master, attend_mean, attend_square, attend_sum, RATE_MATRIX, DECAY_MATRIX
    )
    expand_state = adam(
        expand_master, expand_mean, expand_square, expand_sum, RATE_MATRIX, DECAY_MATRIX
    )
    project_state = adam(
        project_master, project_mean, project_square, project_sum, RATE_MATRIX, DECAY_MATRIX
    )
    vector_state = adam(vector_master, vector_mean, vector_square, vector_sum, RATE_VECTOR, 0.0)
    return (
        layer_output,
        input_grad,
        attend_state[0],
        expand_state[0],
        project_state[0],
        vector_state[0],
        attend_state[1],
        expand_state[1],
        project_state[1],
        vector_state[1],
        attend_state[2],
        expand_state[2],
        project_state[2],
        vector_state[2],
    )


def solution(mesh):
    return jax.shard_map(
        on_device,
        mesh=mesh,
        in_specs=(
            P(("dp", "shard"), None),
            P(("dp", "shard"), None),
            P(),
            P(),
            P("shard", None),
            P("shard", None),
            P("shard", None),
            P("shard", None),
            P("shard", None),
            P("shard", None),
            P("shard", None),
            P("shard", None),
            P("shard", None),
            P("shard", None),
            P("shard", None),
            P("shard", None),
        ),
        out_specs=(
            P(("dp", "shard"), None),
            P(("dp", "shard"), None),
            P("shard", None),
            P("shard", None),
            P("shard", None),
            P("shard", None),
            P("shard", None),
            P("shard", None),
            P("shard", None),
            P("shard", None),
            P("shard", None),
            P("shard", None),
            P("shard", None),
            P("shard", None),
        ),
        check_vma=False,
    )
```

```python
import math

import jax
import jax.numpy as jnp
from jax import lax
from jax.experimental import pallas as pl
from jax.experimental.pallas import tpu as pltpu
from jax.sharding import PartitionSpec as P

HEADS = 12
HEAD_DIM = 64
STEP = 10


NORM_EPS = 1e-05
MASK_FILL = -1e30
BETA_ONE = 0.9
BETA_TWO = 0.999
ADAM_EPS = 1e-08
RATE_MATRIX = 0.05
RATE_VECTOR = 0.3
DECAY_MATRIX = 0.01
BLOCK = 256
NT = (((1,), (1,)), ((), ()))
TN = (((0,), (0,)), ((), ()))


def layer_norm(values, gain, shift):
    centre = jnp.mean(values, axis=-1, keepdims=True)
    centred = values - centre
    spread = jnp.mean(centred * centred, axis=-1, keepdims=True)
    return centred * lax.rsqrt(spread + NORM_EPS) * gain + shift


def exact_gelu(values):
    return jax.nn.gelu(values, approximate=False)


def slot_segments(seq_lengths, seq_owner, device, slots):
    mine = seq_owner == device
    owned = jnp.where(mine, seq_lengths, 0)
    starts = jnp.cumsum(owned) - owned
    place = jnp.arange(slots, dtype=jnp.int32)[:, None]
    inside = mine[None, :] & (place >= starts[None, :]) & (place < (starts + owned)[None, :])
    labels = jnp.arange(seq_lengths.shape[0], dtype=jnp.int32)[None, :] + 1
    return jnp.sum(jnp.where(inside, labels, 0), axis=1) - 1


def dot(a, b, dims=(((1,), (0,)), ((), ()))):
    return lax.dot_general(a, b, dims, preferred_element_type=jnp.float32)


def mask_of(column, row, first, end, start):
    later = lax.broadcasted_iota(jnp.int32, (end - first, end - start), 0) + first
    earlier = lax.broadcasted_iota(jnp.int32, (end - first, end - start), 1) + start
    return (column == row) & (earlier <= later)


def forward_kernel(column_ref, row_ref, q_ref, k_ref, v_ref, mixed_ref, log_ref):
    slots = q_ref.shape[0]
    scale = HEAD_DIM**-0.5
    low = lax.broadcasted_iota(jnp.int32, (1, 128), 1) < HEAD_DIM
    for index in range(slots // BLOCK):
        first, end = index * BLOCK, (index + 1) * BLOCK
        start = max(0, first - 512)
        ok = mask_of(column_ref[first:end, :], row_ref[:, start:end], first, end, start)
        q = q_ref[first:end, :]
        k = k_ref[start:end, :]
        v = v_ref[start:end, :]
        mixed, logs = [], []
        for head in range(2):
            mine = low if head == 0 else ~low
            s = dot(jnp.where(mine, q, jnp.zeros_like(q)), k, NT) * scale
            s = jnp.where(ok, s, MASK_FILL)
            top = jnp.max(s, axis=1, keepdims=True)
            e = jnp.exp(s - top)
            total = jnp.sum(e, axis=1, keepdims=True)
            p = (e * (1.0 / total)).astype(jnp.bfloat16)
            mixed.append(dot(p, v))
            logs.append(top + jnp.log(total))
        mixed_ref[first:end, :] = jnp.where(low, mixed[0], mixed[1]).astype(jnp.bfloat16)
        log_ref[0, first:end, :] = jnp.concatenate(logs, axis=1)


def backward_kernel(column_ref, row_ref, q_ref, k_ref, v_ref, g_ref, log_ref, dq_ref, dk_ref, dv_ref, ka, va):
    slots = q_ref.shape[0]
    scale = HEAD_DIM**-0.5
    low = lax.broadcasted_iota(jnp.int32, (1, 128), 1) < HEAD_DIM
    ka[...] = jnp.zeros_like(ka)
    va[...] = jnp.zeros_like(va)
    for index in range(slots // BLOCK):
        first, end = index * BLOCK, (index + 1) * BLOCK
        start = max(0, first - 512)
        ok = mask_of(column_ref[first:end, :], row_ref[:, start:end], first, end, start)
        q = q_ref[first:end, :]
        g = g_ref[first:end, :]
        k = k_ref[start:end, :]
        v = v_ref[start:end, :]
        dq, dk, dv = [], [], []
        for head in range(2):
            mine = low if head == 0 else ~low
            s = dot(jnp.where(mine, q, jnp.zeros_like(q)), k, NT) * scale
            p = jnp.exp(jnp.where(ok, s - log_ref[0, first:end, head : head + 1], MASK_FILL))
            dp = dot(jnp.where(mine, g, jnp.zeros_like(g)), v, NT)
            w = p * dp
            ds = (w - p * jnp.sum(w, axis=1, keepdims=True)).astype(jnp.bfloat16)
            dq.append(dot(ds, k))
            dk.append(dot(ds, q, TN))
            dv.append(dot(p.astype(jnp.bfloat16), g, TN))
        dq_ref[first:end, :] = (jnp.where(low, dq[0], dq[1]) * scale).astype(jnp.bfloat16)
        ka[start:end, :] += jnp.where(low, dk[0], dk[1])
        va[start:end, :] += jnp.where(low, dv[0], dv[1])
    dk_ref[...] = (ka[...] * scale).astype(jnp.bfloat16)
    dv_ref[...] = va[...].astype(jnp.bfloat16)


def columns(offset, slots):
    return pl.BlockSpec((slots, 128), lambda pair: (0, pair + offset))


def whole(shape):
    return pl.BlockSpec(shape, lambda pair: (0, 0))


def attention(projected, segment):
    slots = projected.shape[0]
    pairs = HEADS // 2
    return pl.pallas_call(
        forward_kernel,
        grid=(pairs,),
        in_specs=[whole((slots, 1)), whole((1, slots))] + [columns(pairs * n, slots) for n in range(3)],
        out_specs=[columns(0, slots), pl.BlockSpec((1, slots, 2), lambda pair: (pair, 0, 0))],
        out_shape=[
            jax.ShapeDtypeStruct((slots, pairs * 128), jnp.bfloat16),
            jax.ShapeDtypeStruct((pairs, slots, 2), jnp.float32),
        ],
        compiler_params=pltpu.CompilerParams(vmem_limit_bytes=48 * 1024 * 1024),
        name="attention",
    )(segment[:, None], segment[None, :], projected, projected, projected)


def attention_back(projected, grad_mixed, logs, segment):
    slots = projected.shape[0]
    pairs = HEADS // 2
    out = jax.ShapeDtypeStruct((slots, pairs * 128), jnp.bfloat16)
    return pl.pallas_call(
        backward_kernel,
        grid=(pairs,),
        in_specs=[whole((slots, 1)), whole((1, slots))]
        + [columns(pairs * n, slots) for n in range(3)]
        + [columns(0, slots), pl.BlockSpec((1, slots, 2), lambda pair: (pair, 0, 0))],
        out_specs=[columns(0, slots)] * 3,
        out_shape=[out] * 3,
        scratch_shapes=[pltpu.VMEM((slots, 128), jnp.float32)] * 2,
        compiler_params=pltpu.CompilerParams(vmem_limit_bytes=48 * 1024 * 1024),
        name="attention_back",
    )(segment[:, None], segment[None, :], projected, projected, projected, grad_mixed, logs)


def adam(master, mean, square, grad, rate, decay):
    mean_new = BETA_ONE * mean + (1.0 - BETA_ONE) * grad
    square_new = BETA_TWO * square + (1.0 - BETA_TWO) * grad * grad
    mean_hat = mean_new / (1.0 - BETA_ONE**STEP)
    square_hat = square_new / (1.0 - BETA_TWO**STEP)
    master_new = master - rate * (mean_hat / (jnp.sqrt(square_hat) + ADAM_EPS) + decay * master)
    return (mean_new, square_new, master_new)


class Ring:
    def __init__(self):
        self.group = lax.axis_size("shard")
        self.data = lax.axis_size("dp")
        self.plane = self.data // 2
        self.side = math.isqrt(self.plane)
        self.square = self.data == 2 * self.side * self.side
        self.z = lax.axis_index("shard")
        device = lax.axis_index("dp")
        self.core = device % 2
        chip = device // 2
        high, low = chip // self.side, chip % self.side
        straight = low * self.side + high
        crossed = high * self.side + low
        self.block = jnp.where(self.core == 0, straight, crossed)
        self.block_other = jnp.where(self.core == 0, crossed, straight)

    def fits(self, rows, columns):
        return self.square and rows % (16 * self.plane) == 0 and columns % 256 == 0

    def send_core(self, value):
        return lax.ppermute(value, "dp", [(i, i ^ 1) for i in range(self.data)])

    def send_plane(self, value, step):
        side = self.side
        first, second = step // side, step % side
        pairs = []
        for device in range(self.data):
            core, chip = device % 2, device // 2
            high, low = chip // side, chip % side
            if core == 0:
                low, high = (low + first) % side, (high + second) % side
            else:
                high, low = (high + first) % side, (low + second) % side
            pairs.append((device, (high * side + low) * 2 + core))
        return lax.ppermute(value, "dp", pairs)

    def shifted(self, block, step):
        side = self.side
        first, second = step // side, step % side
        return (block // side + first) % side * side + (block % side + second) % side

    def back(self, block, step):
        side = self.side
        first, second = step // side, step % side
        return (block // side - first) % side * side + (block % side - second) % side

    def send_shard(self, value, step):
        group = self.group
        return lax.ppermute(value, "shard", [(i, (i + step) % group) for i in range(group)])


def place_pieces(own, mine, other, ring):
    group, plane = ring.group, ring.plane
    rows, columns = own.shape
    piece, half = rows // plane, columns // 2
    scalars = [ring.z, ring.core]
    scalars += [ring.back(ring.block, step) for step in range(plane)]
    scalars += [ring.back(ring.block_other, step) for step in range(plane)]
    where = jnp.stack([jnp.asarray(v, jnp.int32) for v in scalars])
    count = 1 + 2 * plane * (group - 1)

    def kernel(where_ref, own_ref, *refs):
        pieces, out_ref, sems = refs[: 2 * plane], refs[-2], refs[-1]
        z, core = where_ref[0], where_ref[1]
        copies = []

        def begin(source, first_row, height, first_column, width):
            target = out_ref.at[pl.ds(first_row, height), pl.ds(first_column, width)]
            copy = pltpu.make_async_copy(source, target, sems.at[len(copies)])
            copy.start()
            copies.append(copy)

        begin(own_ref, pl.multiple_of(z * rows, 16), rows, 0, columns)
        for number, ref in enumerate(pieces):
            block = where_ref[2 + number]
            column = pl.multiple_of((core if number < plane else 1 - core) * half, 128)
            for step in range(1, group):
                source = lax.rem(z - step + group, group)
                row = pl.multiple_of(source * rows + block * piece, 16)
                begin(ref.at[step - 1], row, piece, column, half)
        for copy in copies:
            copy.wait()

    return pl.pallas_call(
        kernel,
        out_shape=jax.ShapeDtypeStruct((rows * group, columns), own.dtype),
        in_specs=[pl.BlockSpec(memory_space=pltpu.SMEM)]
        + [pl.BlockSpec(memory_space=pl.ANY)] * (1 + 2 * plane),
        out_specs=pl.BlockSpec(memory_space=pltpu.VMEM),
        scratch_shapes=[pltpu.SemaphoreType.DMA((count,))],
        compiler_params=pltpu.CompilerParams(vmem_limit_bytes=16 * 1024 * 1024),
        name="place_pieces",
    )(where, own, *mine, *other)


def gather_weight(master, ring):
    rows, columns = master.shape
    own = master.astype(jnp.bfloat16)
    if not ring.fits(rows, columns):
        return lax.all_gather(own, "shard", axis=0, tiled=True)
    piece, half = rows // ring.plane, columns // 2
    chunk = lax.dynamic_slice(
        master, (ring.block * piece, ring.core * half), (piece, half)
    ).astype(jnp.bfloat16)
    foreign = jnp.stack([ring.send_shard(chunk, step) for step in range(1, ring.group)])
    mine = [foreign] + [ring.send_plane(foreign, step) for step in range(1, ring.plane)]
    other = [ring.send_core(value) for value in mine]
    return place_pieces(own, mine, other, ring)


def sum_gradient(grad, ring):
    total, columns = grad.shape
    group, plane = ring.group, ring.plane
    rows = total // group
    if not ring.fits(rows, columns):
        whole = lax.psum_scatter(
            grad.astype(jnp.float32), "shard", scatter_dimension=0, tiled=True
        )
        return lax.psum(whole, "dp")
    piece, half = rows // plane, columns // 2
    kept = lax.dynamic_slice(grad, (0, ring.core * half), (total, half))
    sent = lax.dynamic_slice(grad, (0, (1 - ring.core) * half), (total, half))
    got = ring.send_core(sent)
    chip = (kept.astype(jnp.float32) + got.astype(jnp.float32)).astype(jnp.bfloat16)
    chip = chip.reshape(group, plane, piece, half)

    def block_of(step):
        block = ring.shifted(ring.block, step)
        return lax.dynamic_index_in_dim(chip, block, 1, keepdims=False)

    arrived = [ring.send_plane(block_of(step), step) for step in range(1, plane)]
    level = block_of(0).astype(jnp.float32)
    for value in arrived:
        level = level + value.astype(jnp.float32)
    level = level.astype(jnp.bfloat16)

    def shard_of(step):
        return lax.dynamic_index_in_dim(level, (ring.z + step) % group, 0, keepdims=False)

    arrived = [ring.send_shard(shard_of(step), step) for step in range(1, group)]
    done = shard_of(0).astype(jnp.float32)
    for value in arrived:
        done = done + value.astype(jnp.float32)
    done = done.astype(jnp.bfloat16)
    blocks = [done] + [ring.send_plane(done, step) for step in range(1, plane)]
    column = in_order(blocks, ring, ring.block)
    other = ring.send_core(column)
    low = jnp.where(ring.core == 0, column, other)
    high = jnp.where(ring.core == 0, other, column)
    return jnp.concatenate([low, high], axis=1).astype(jnp.float32)


def in_order(blocks, ring, block):
    side, plane = ring.side, ring.plane
    parts = []
    for target in range(plane):
        value = blocks[0]
        for step in range(1, plane):
            value = jnp.where(ring.back(block, step) == target, blocks[step], value)
        parts.append(value)
    return jnp.concatenate(parts, axis=0)


def gather_vector(master, ring):
    own = master.astype(jnp.bfloat16)
    group = ring.group
    parts = [own] + [ring.send_shard(own, step) for step in range(1, group)]
    stacked = jnp.stack(parts)
    order = (ring.z - jnp.arange(group)) % group
    return jnp.take(stacked, order, axis=0).reshape(group * own.shape[0], own.shape[1])


def sum_vector(grad, ring):
    group = ring.group
    if not ring.square or ring.side != 2:
        whole = lax.psum_scatter(grad, "shard", scatter_dimension=0, tiled=True)
        return lax.psum(whole, "dp")
    flat = grad.reshape(group, -1, 128)
    flat = flat + ring.send_core(flat)
    for bit in (2, 4):
        flat = flat + lax.ppermute(flat, "dp", [(i, i ^ bit) for i in range(ring.data)])

    def shard_of(step):
        return lax.dynamic_index_in_dim(flat, (ring.z + step) % group, 0, keepdims=False)

    done = shard_of(0)
    for step in range(1, group):
        done = done + ring.send_shard(shard_of(step), step)
    return done.reshape(grad.shape[0] // group, grad.shape[1])


def on_device(
    tokens,
    cotangent,
    seq_lengths,
    seq_owner,
    attend_master,
    expand_master,
    project_master,
    vector_master,
    attend_mean,
    expand_mean,
    project_mean,
    vector_mean,
    attend_square,
    expand_square,
    project_square,
    vector_square,
):
    ring = Ring()
    width = tokens.shape[1]
    vector = gather_vector(vector_master, ring)
    inner = gather_weight(attend_master[:, : 3 * width], ring)
    outer = gather_weight(attend_master[:, 3 * width :], ring)
    expand = gather_weight(expand_master, ring)
    project = gather_weight(project_master, ring)
    slots, width = tokens.shape
    device = lax.axis_index("dp") * ring.group + ring.z
    segment = slot_segments(seq_lengths, seq_owner, device, slots)
    live = (segment >= 0).astype(jnp.float32)[:, None]
    params = vector.astype(jnp.float32)
    rows = tokens.astype(jnp.float32)
    normed_one, pull_one = jax.vjp(layer_norm, rows, params[:, 0], params[:, 1])
    normed_one_low = normed_one.astype(jnp.bfloat16)
    bias_inner = jnp.concatenate([params[:, 4], jnp.zeros((width,), jnp.float32), params[:, 5]])
    projected = (
        jnp.dot(normed_one_low, inner, preferred_element_type=jnp.float32) + bias_inner
    ).astype(jnp.bfloat16)
    mixed_flat, logs = attention(projected, segment)
    resid = rows + (jnp.dot(mixed_flat, outer, preferred_element_type=jnp.float32) + params[:, 6])
    normed_two, pull_two = jax.vjp(layer_norm, resid, params[:, 2], params[:, 3])
    normed_two_low = normed_two.astype(jnp.bfloat16)
    pre = jnp.dot(normed_two_low, expand, preferred_element_type=jnp.float32) + params[
        :, 8:
    ].reshape(-1)
    act, pull_gelu = jax.vjp(exact_gelu, pre)
    act_low = act.astype(jnp.bfloat16)
    layer_output = (
        (resid + jnp.dot(act_low, project, preferred_element_type=jnp.float32) + params[:, 7])
        * live
    ).astype(jnp.bfloat16)
    back = cotangent.astype(jnp.float32) * live
    back_low = back.astype(jnp.bfloat16)
    project_grad = jnp.einsum("tf,td->fd", act_low, back_low, preferred_element_type=jnp.float32)
    grad_act = jnp.einsum("td,fd->tf", back_low, project, preferred_element_type=jnp.float32)
    grad_pre = pull_gelu(grad_act)[0]
    grad_pre_low = grad_pre.astype(jnp.bfloat16)
    expand_grad = jnp.einsum(
        "td,tf->df", normed_two_low, grad_pre_low, preferred_element_type=jnp.float32
    )
    grad_two = jnp.einsum("tf,df->td", grad_pre_low, expand, preferred_element_type=jnp.float32)
    grad_resid_norm, gain_two, shift_two = pull_two(grad_two)
    grad_resid = back + grad_resid_norm
    grad_attn_low = grad_resid.astype(jnp.bfloat16)
    outer_grad = jnp.einsum(
        "td,te->de", mixed_flat, grad_attn_low, preferred_element_type=jnp.float32
    )
    grad_mixed = jnp.einsum("te,de->td", grad_attn_low, outer, preferred_element_type=jnp.float32)
    grad_mixed_low = grad_mixed.astype(jnp.bfloat16)
    grad_inner_low = jnp.concatenate(
        attention_back(projected, grad_mixed_low, logs, segment), axis=1
    )
    inner_grad = jnp.einsum(
        "td,te->de", normed_one_low, grad_inner_low, preferred_element_type=jnp.float32
    )
    grad_one = jnp.einsum("te,de->td", grad_inner_low, inner, preferred_element_type=jnp.float32)
    grad_rows_norm, gain_one, shift_one = pull_one(grad_one)
    input_grad = grad_resid + grad_rows_norm
    inner_sums = jnp.sum(grad_inner_low, axis=0, dtype=jnp.float32)
    columns = jnp.stack(
        [
            gain_one,
            shift_one,
            gain_two,
            shift_two,
            inner_sums[:width],
            inner_sums[2 * width :],
            jnp.sum(grad_attn_low, axis=0, dtype=jnp.float32),
            jnp.sum(back, axis=0),
        ],
        axis=1,
    )
    vector_grad = jnp.concatenate(
        [columns, jnp.sum(grad_pre_low, axis=0, dtype=jnp.float32).reshape(width, 4)], axis=1
    )
    attend_sum = jnp.concatenate(
        [
            sum_gradient(inner_grad.astype(jnp.bfloat16), ring),
            sum_gradient(outer_grad.astype(jnp.bfloat16), ring),
        ],
        axis=1,
    )
    expand_sum = sum_gradient(expand_grad.astype(jnp.bfloat16), ring)
    project_sum = sum_gradient(project_grad.astype(jnp.bfloat16), ring)
    vector_sum = sum_vector(vector_grad, ring)
    attend_state = adam(
        attend_master, attend_mean, attend_square, attend_sum, RATE_MATRIX, DECAY_MATRIX
    )
    expand_state = adam(
        expand_master, expand_mean, expand_square, expand_sum, RATE_MATRIX, DECAY_MATRIX
    )
    project_state = adam(
        project_master, project_mean, project_square, project_sum, RATE_MATRIX, DECAY_MATRIX
    )
    vector_state = adam(vector_master, vector_mean, vector_square, vector_sum, RATE_VECTOR, 0.0)
    return (
        layer_output,
        input_grad,
        attend_state[0],
        expand_state[0],
        project_state[0],
        vector_state[0],
        attend_state[1],
        expand_state[1],
        project_state[1],
        vector_state[1],
        attend_state[2],
        expand_state[2],
        project_state[2],
        vector_state[2],
    )


def solution(mesh):
    return jax.shard_map(
        on_device,
        mesh=mesh,
        in_specs=(
            P(("dp", "shard"), None),
            P(("dp", "shard"), None),
            P(),
            P(),
            P("shard", None),
            P("shard", None),
            P("shard", None),
            P("shard", None),
            P("shard", None),
            P("shard", None),
            P("shard", None),
            P("shard", None),
            P("shard", None),
            P("shard", None),
            P("shard", None),
            P("shard", None),
        ),
        out_specs=(
            P(("dp", "shard"), None),
            P(("dp", "shard"), None),
            P("shard", None),
            P("shard", None),
            P("shard", None),
            P("shard", None),
            P("shard", None),
            P("shard", None),
            P("shard", None),
            P("shard", None),
            P("shard", None),
            P("shard", None),
            P("shard", None),
            P("shard", None),
        ),
        check_vma=False,
    )
```

```python
import functools
import math

import jax
import jax.numpy as jnp
from jax import lax
from jax.experimental import pallas as pl
from jax.experimental.pallas import tpu as pltpu
from jax.sharding import PartitionSpec as P

HEADS = 12
HEAD_DIM = 64
STEP = 10


NORM_EPS = 1e-05
MASK_FILL = -1e30
BETA_ONE = 0.9
BETA_TWO = 0.999
ADAM_EPS = 1e-08
RATE_MATRIX = 0.05
RATE_VECTOR = 0.3
DECAY_MATRIX = 0.01
BLOCK = 256
NT = (((1,), (1,)), ((), ()))
TN = (((0,), (0,)), ((), ()))


def slot_segments(seq_lengths, seq_owner, device, slots):
    mine = seq_owner == device
    owned = jnp.where(mine, seq_lengths, 0)
    starts = jnp.cumsum(owned) - owned
    place = jnp.arange(slots, dtype=jnp.int32)[:, None]
    inside = mine[None, :] & (place >= starts[None, :]) & (place < (starts + owned)[None, :])
    labels = jnp.arange(seq_lengths.shape[0], dtype=jnp.int32)[None, :] + 1
    return jnp.sum(jnp.where(inside, labels, 0), axis=1) - 1


def dot(a, b, dims=(((1,), (0,)), ((), ()))):
    return lax.dot_general(a, b, dims, preferred_element_type=jnp.float32)


def mask_of(column, row, first, end, start):
    later = lax.broadcasted_iota(jnp.int32, (end - first, end - start), 0) + first
    earlier = lax.broadcasted_iota(jnp.int32, (end - first, end - start), 1) + start
    return (column == row) & (earlier <= later)


def forward_kernel(column_ref, row_ref, q_ref, k_ref, v_ref, mixed_ref, log_ref):
    slots = q_ref.shape[0]
    scale = HEAD_DIM**-0.5
    low = lax.broadcasted_iota(jnp.int32, (1, 128), 1) < HEAD_DIM
    for index in range(slots // BLOCK):
        first, end = index * BLOCK, (index + 1) * BLOCK
        start = max(0, first - 512)
        ok = mask_of(column_ref[first:end, :], row_ref[:, start:end], first, end, start)
        q = q_ref[first:end, :]
        k = k_ref[start:end, :]
        v = v_ref[start:end, :]
        mixed, logs = [], []
        for head in range(2):
            mine = low if head == 0 else ~low
            s = dot(jnp.where(mine, q, jnp.zeros_like(q)), k, NT) * scale
            s = jnp.where(ok, s, MASK_FILL)
            top = jnp.max(s, axis=1, keepdims=True)
            e = jnp.exp(s - top)
            total = jnp.sum(e, axis=1, keepdims=True)
            p = (e * (1.0 / total)).astype(jnp.bfloat16)
            mixed.append(dot(p, v))
            logs.append(top + jnp.log(total))
        mixed_ref[first:end, :] = jnp.where(low, mixed[0], mixed[1]).astype(jnp.bfloat16)
        log_ref[0, first:end, :] = jnp.concatenate(logs, axis=1)


def backward_kernel(column_ref, row_ref, q_ref, k_ref, v_ref, g_ref, log_ref, out_ref, ka, va):
    slots = q_ref.shape[0]
    scale = HEAD_DIM**-0.5
    low = lax.broadcasted_iota(jnp.int32, (1, 128), 1) < HEAD_DIM
    ka[...] = jnp.zeros_like(ka)
    va[...] = jnp.zeros_like(va)
    for index in range(slots // BLOCK):
        first, end = index * BLOCK, (index + 1) * BLOCK
        start = max(0, first - 512)
        ok = mask_of(column_ref[first:end, :], row_ref[:, start:end], first, end, start)
        q = q_ref[first:end, :]
        g = g_ref[first:end, :]
        k = k_ref[start:end, :]
        v = v_ref[start:end, :]
        dq, dk, dv = [], [], []
        for head in range(2):
            mine = low if head == 0 else ~low
            s = dot(jnp.where(mine, q, jnp.zeros_like(q)), k, NT) * scale
            p = jnp.exp(jnp.where(ok, s - log_ref[0, first:end, head : head + 1], MASK_FILL))
            dp = dot(jnp.where(mine, g, jnp.zeros_like(g)), v, NT)
            w = p * dp
            ds = (w - p * jnp.sum(w, axis=1, keepdims=True)).astype(jnp.bfloat16)
            dq.append(dot(ds, k))
            dk.append(dot(ds, q, TN))
            dv.append(dot(p.astype(jnp.bfloat16), g, TN))
        out_ref[0, first:end, :] = (jnp.where(low, dq[0], dq[1]) * scale).astype(jnp.bfloat16)
        ka[start:end, :] += jnp.where(low, dk[0], dk[1])
        va[start:end, :] += jnp.where(low, dv[0], dv[1])
    out_ref[1] = (ka[...] * scale).astype(jnp.bfloat16)
    out_ref[2] = va[...].astype(jnp.bfloat16)


def columns(offset, slots):
    return pl.BlockSpec((slots, 128), lambda pair: (0, pair + offset))


def whole(shape):
    return pl.BlockSpec(shape, lambda pair: (0, 0))


def attention(projected, segment):
    slots = projected.shape[0]
    pairs = HEADS // 2
    return pl.pallas_call(
        forward_kernel,
        grid=(pairs,),
        in_specs=[whole((slots, 1)), whole((1, slots))] + [columns(pairs * n, slots) for n in range(3)],
        out_specs=[columns(0, slots), pl.BlockSpec((1, slots, 2), lambda pair: (pair, 0, 0))],
        out_shape=[
            jax.ShapeDtypeStruct((slots, pairs * 128), jnp.bfloat16),
            jax.ShapeDtypeStruct((pairs, slots, 2), jnp.float32),
        ],
        compiler_params=pltpu.CompilerParams(vmem_limit_bytes=48 * 1024 * 1024),
        cost_estimate=cost(2 * slots * slots * pairs * 256, 8 * slots * pairs * 128),
        name="attention",
    )(segment[:, None], segment[None, :], projected, projected, projected)


def attention_back(projected, grad_mixed, logs, segment):
    slots = projected.shape[0]
    pairs = HEADS // 2
    return pl.pallas_call(
        backward_kernel,
        grid=(pairs,),
        in_specs=[whole((slots, 1)), whole((1, slots))]
        + [columns(pairs * n, slots) for n in range(3)]
        + [columns(0, slots), pl.BlockSpec((1, slots, 2), lambda pair: (pair, 0, 0))],
        out_specs=pl.BlockSpec((3, slots, 128), lambda pair: (0, 0, pair)),
        out_shape=jax.ShapeDtypeStruct((3, slots, pairs * 128), jnp.bfloat16),
        scratch_shapes=[pltpu.VMEM((slots, 128), jnp.float32)] * 2,
        compiler_params=pltpu.CompilerParams(vmem_limit_bytes=48 * 1024 * 1024),
        cost_estimate=cost(5 * slots * slots * pairs * 256, 16 * slots * pairs * 128),
        name="attention_back",
    )(segment[:, None], segment[None, :], projected, projected, projected, grad_mixed, logs)


def adam(master, mean, square, grad, rate, decay):
    mean_new = BETA_ONE * mean + (1.0 - BETA_ONE) * grad
    square_new = BETA_TWO * square + (1.0 - BETA_TWO) * grad * grad
    mean_hat = mean_new / (1.0 - BETA_ONE**STEP)
    square_hat = square_new / (1.0 - BETA_TWO**STEP)
    master_new = master - rate * (mean_hat / (jnp.sqrt(square_hat) + ADAM_EPS) + decay * master)
    return (mean_new, square_new, master_new)


class Ring:
    def __init__(self):
        self.group = lax.axis_size("shard")
        self.data = lax.axis_size("dp")
        self.plane = self.data // 2
        self.side = math.isqrt(self.plane)
        self.square = self.data == 2 * self.side * self.side
        self.z = lax.axis_index("shard")
        device = lax.axis_index("dp")
        self.core = device % 2
        chip = device // 2
        high, low = chip // self.side, chip % self.side
        straight = low * self.side + high
        crossed = high * self.side + low
        self.block = jnp.where(self.core == 0, straight, crossed)
        self.block_other = jnp.where(self.core == 0, crossed, straight)

    def send_core(self, value):
        return lax.ppermute(value, "dp", [(i, i ^ 1) for i in range(self.data)])

    def send_plane(self, value, step):
        side = self.side
        first, second = step // side, step % side
        pairs = []
        for device in range(self.data):
            core, chip = device % 2, device // 2
            high, low = chip // side, chip % side
            if core == 0:
                low, high = (low + first) % side, (high + second) % side
            else:
                high, low = (high + first) % side, (low + second) % side
            pairs.append((device, (high * side + low) * 2 + core))
        return lax.ppermute(value, "dp", pairs)

    def shifted(self, block, step):
        side = self.side
        first, second = step // side, step % side
        return (block // side + first) % side * side + (block % side + second) % side

    def back(self, block, step):
        side = self.side
        first, second = step // side, step % side
        return (block // side - first) % side * side + (block % side - second) % side

    def send_shard(self, value, step):
        group = self.group
        return lax.ppermute(value, "shard", [(i, (i + step) % group) for i in range(group)])


TILE = 384
ROW_BLOCKS = 16
CHUNK = 256


def compiler(megabytes):
    return pltpu.CompilerParams(vmem_limit_bytes=megabytes * 1024 * 1024)


def cost(flops, bytes_accessed):
    return pl.CostEstimate(flops=flops, bytes_accessed=bytes_accessed, transcendentals=0)


def fold(matrix, high):
    rows, columns = matrix.shape
    tiles = columns // (2 * TILE)
    parts = matrix.reshape(rows // high, high, 2, tiles, TILE).transpose(2, 0, 3, 1, 4)
    return parts.reshape(2, rows // high, tiles * high, TILE)


def unfold(packed, high):
    blocks, tiles = packed.shape[1], packed.shape[2] // high
    parts = packed.reshape(2, blocks, tiles, high, TILE).transpose(1, 3, 0, 2, 4)
    return parts.reshape(blocks * high, 2 * tiles * TILE)


def gather_packed(own, ring):
    blocks = own.shape[1]
    if not ring.square or blocks != ring.plane:
        whole = lax.all_gather(own, "shard", axis=1, tiled=True)
        return [whole], [(None, 0)]
    chunk = lax.dynamic_index_in_dim(
        lax.dynamic_index_in_dim(own, ring.core, 0, keepdims=False), ring.block, 0, keepdims=False
    )
    foreign = jnp.stack([ring.send_shard(chunk, step) for step in range(1, ring.group)])
    mine = [foreign] + [ring.send_plane(foreign, step) for step in range(1, ring.plane)]
    other = [ring.send_core(value) for value in mine]
    places = [(ring.core, ring.back(ring.block, step)) for step in range(ring.plane)]
    places += [(1 - ring.core, ring.back(ring.block_other, step)) for step in range(ring.plane)]
    return [own] + mine + other, [(None, ring.z * blocks)] + places


def where_array(places, ring):
    scalars = [ring.z]
    for half, block in places:
        scalars += [0 if half is None else half, block]
    return jnp.stack([jnp.asarray(v, jnp.int32) for v in scalars])


def copy_count(sources, group):
    return 1 if len(sources) == 1 else 2 + (len(sources) - 1) * (group - 1)


def start_pieces(where_ref, refs, group, out_ref, sems):
    copies = []

    def begin(source, target):
        copy = pltpu.make_async_copy(source, target, sems.at[len(copies)])
        copy.start()
        copies.append(copy)

    if len(refs) == 1:
        begin(refs[0], out_ref)
        return copies
    blocks = refs[0].shape[1]
    first = where_ref[2]
    for half in range(2):
        begin(refs[0].at[half], out_ref.at[half, pl.ds(first, blocks)])
    for number, ref in enumerate(refs[1:], 1):
        half, block = where_ref[1 + 2 * number], where_ref[2 + 2 * number]
        for step in range(1, group):
            source = lax.rem(where_ref[0] - step + group, group)
            begin(ref.at[step - 1], out_ref.at[half, source * blocks + block])
    return copies


def sum_packed(grad, ring):
    group, plane = ring.group, ring.plane
    rows = grad.shape[2]
    blocks = ROW_BLOCKS // group
    if not ring.square or blocks != plane:
        whole = lax.psum_scatter(
            grad.astype(jnp.float32), "shard", scatter_dimension=1, tiled=True
        )
        return lax.psum(whole, "dp")
    kept = lax.dynamic_index_in_dim(grad, ring.core, 0, keepdims=False)
    sent = lax.dynamic_index_in_dim(grad, 1 - ring.core, 0, keepdims=False)
    got = ring.send_core(sent)
    chip = (kept.astype(jnp.float32) + got.astype(jnp.float32)).astype(jnp.bfloat16)
    chip = chip.reshape(group, plane, rows, TILE)

    def block_of(step):
        return lax.dynamic_index_in_dim(chip, ring.shifted(ring.block, step), 1, keepdims=False)

    arrived = [ring.send_plane(block_of(step), step) for step in range(1, plane)]
    level = block_of(0).astype(jnp.float32)
    for value in arrived:
        level = level + value.astype(jnp.float32)
    level = level.astype(jnp.bfloat16)

    def shard_of(step):
        return lax.dynamic_index_in_dim(level, (ring.z + step) % group, 0, keepdims=False)

    arrived = [ring.send_shard(shard_of(step), step) for step in range(1, group)]
    done = shard_of(0).astype(jnp.float32)
    for value in arrived:
        done = done + value.astype(jnp.float32)
    done = done.astype(jnp.bfloat16)
    pieces = [done] + [ring.send_plane(done, step) for step in range(1, plane)]
    column = in_order(pieces, ring, ring.block)
    other = ring.send_core(column)
    low = jnp.where(ring.core == 0, column, other)
    high = jnp.where(ring.core == 0, other, column)
    return jnp.stack([low, high])


def in_order(blocks, ring, block):
    parts = []
    for target in range(ring.plane):
        value = blocks[0]
        for step in range(1, ring.plane):
            value = jnp.where(ring.back(block, step) == target, blocks[step], value)
        parts.append(value)
    return jnp.stack(parts, axis=0)


def tile_of(packed_ref, half, row, high):
    part = packed_ref[half, :, pl.ds(row, high), :]
    return part.reshape(ROW_BLOCKS * high, TILE)


def normal_of(rows):
    centre = jnp.mean(rows, axis=1, keepdims=True)
    centred = rows - centre
    spread = jnp.mean(centred * centred, axis=1, keepdims=True)
    ratio = lax.rsqrt(spread + NORM_EPS)
    return centred * ratio, ratio


def normal_back(normal, ratio, scaled):
    along = jnp.mean(scaled * normal, axis=1, keepdims=True)
    return ratio * (scaled - jnp.mean(scaled, axis=1, keepdims=True) - normal * along)


def project_kernel(group, where_ref, tokens_ref, params_ref, *refs):
    pieces, (out_ref, turned_ref, packed_ref, sems) = refs[:-4], refs[-4:]
    slots, width = tokens_ref.shape
    high = width // ROW_BLOCKS
    copies = start_pieces(where_ref, pieces, group, packed_ref, sems)
    lows = []
    for first in range(0, slots, CHUNK):
        normal, _ = normal_of(tokens_ref[first : first + CHUNK, :].astype(jnp.float32))
        low = (normal * params_ref[0:1, :] + params_ref[1:2, :]).astype(jnp.bfloat16)
        turned_ref[:, first : first + CHUNK] = low.T
        lows.append(low)
    for copy in copies:
        copy.wait()
    for part in range(3):
        weight = jnp.concatenate(
            [tile_of(packed_ref, t // 3, t % 3 * high, high) for t in (2 * part, 2 * part + 1)], axis=1
        )
        for number, low in enumerate(lows):
            value = dot(low, weight)
            if part != 1:
                row = 4 if part == 0 else 5
                value = value + params_ref[row : row + 1, :]
            out_ref[number * CHUNK : (number + 1) * CHUNK, part * width : (part + 1) * width] = (
                value.astype(jnp.bfloat16)
            )


def project_rows(tokens, params, sources, where, group):
    slots, width = tokens.shape
    high = width // ROW_BLOCKS
    vmem = pl.BlockSpec(memory_space=pltpu.VMEM)
    return pl.pallas_call(
        functools.partial(project_kernel, group),
        in_specs=[pl.BlockSpec(memory_space=pltpu.SMEM), vmem, vmem]
        + [pl.BlockSpec(memory_space=pl.ANY)] * len(sources),
        out_specs=[vmem] * 3,
        out_shape=[
            jax.ShapeDtypeStruct((slots, 3 * width), jnp.bfloat16),
            jax.ShapeDtypeStruct((width, slots), jnp.bfloat16),
            jax.ShapeDtypeStruct((2, ROW_BLOCKS, 3 * high, TILE), jnp.bfloat16),
        ],
        scratch_shapes=[pltpu.SemaphoreType.DMA((copy_count(sources, group),))],
        compiler_params=compiler(40),
        cost_estimate=cost(6 * slots * width * width, 16 * slots * width),
        name="project_rows",
    )(where, tokens, params, *sources)


def tail_of(values):
    size = jnp.abs(values) * (0.5**0.5)
    bell = jnp.exp(-0.5 * values * values)
    t = 1.0 / (1.0 + 0.5 * size)
    series = jnp.full_like(t, 0.17087277)
    for c in (
        -0.82215223, 1.48851587, -1.13520398, 0.27886807, -0.18628806, 0.09678418, 0.37409196, 1.00002368, -1.26551223,
    ):
        series = series * t + c
    tail = 0.5 * t * bell * jnp.exp(series)
    return bell, jnp.where(values > 0, 1.0 - tail, tail)


def middle_kernel(group, where_ref, tokens_ref, cotangent_ref, mixed_ref, live_ref, params_ref, *refs):
    pieces = refs[:-16]
    (out_ref, resid_ref, low_ref, grad_ref, sums_ref) = refs[-16:-11]
    (packed_ref, turned_ref, back_ref, total_ref, two_ref, act_ref, pre_ref, bias_ref, mean_ref, ratio_ref, sems) = refs[-11:]
    slots, width = tokens_ref.shape
    high = width // ROW_BLOCKS
    deep = 4 * high
    copies = start_pieces(where_ref, pieces, group, packed_ref, sems)
    sums_ref[...] = jnp.zeros_like(sums_ref)
    for first in range(0, slots, CHUNK):
        here = slice(first, first + CHUNK)
        back_ref[here, :] = (cotangent_ref[here, :].astype(jnp.float32) * live_ref[here, :]).astype(jnp.bfloat16)
    for copy in copies:
        copy.wait()

    def outer():
        return jnp.concatenate([tile_of(packed_ref, half, 2 * deep, high) for half in range(2)], axis=1)

    weight = outer()
    for first in range(0, slots, CHUNK):
        here = slice(first, first + CHUNK)
        resid = tokens_ref[here, :].astype(jnp.float32) + (dot(mixed_ref[here, :], weight) + params_ref[6:7, :])
        normal, ratio = normal_of(resid)
        low = (normal * params_ref[2:3, :] + params_ref[3:4, :]).astype(jnp.bfloat16)
        low_ref[here, :] = low
        turned_ref[:, here] = low.T
        resid_ref[here, :] = normal
        ratio_ref[here, :] = ratio
        total_ref[here, :] = resid + params_ref[7:8, :]
        two_ref[here, :] = jnp.zeros((CHUNK, width), jnp.float32)

    def step(number, carry):
        half = number // 2
        row = pl.multiple_of(number % 2 * (2 * high), 16)
        wide = jnp.concatenate(
            [tile_of(packed_ref, half, row, high), tile_of(packed_ref, half, row + high, high)], axis=1
        )
        blocks = pl.ds(number * 4, 4)
        deep_weight = jnp.concatenate(
            [packed_ref[side, blocks, deep : 2 * deep, :].reshape(4 * deep, TILE) for side in range(2)], axis=1
        )
        bias = params_ref[pl.ds(8 + number, 1), :]
        bias_sum = jnp.zeros((1, width), jnp.float32)
        for first in range(0, slots, CHUNK):
            here = slice(first, first + CHUNK)
            pre = dot(low_ref[here, :], wide) + bias
            bell, below = tail_of(pre)
            act = (pre * below).astype(jnp.bfloat16)
            act_ref[here, :] = act
            slope = below + pre * bell * 0.3989422804014327
            grad = (dot(back_ref[here, :], deep_weight, NT) * slope).astype(jnp.bfloat16)
            pre_ref[here, :] = grad
            bias_sum = bias_sum + jnp.sum(grad.astype(jnp.float32), axis=0, keepdims=True)
            total_ref[here, :] += dot(act, deep_weight)
            two_ref[here, :] += dot(grad, wide, NT)
        bias_ref[pl.ds(number, 1), :] = bias_sum
        expand_grad = dot(turned_ref[...], pre_ref[...]).astype(jnp.bfloat16)
        for side in range(2):
            grad_ref[half, :, pl.ds(pl.multiple_of(row + side * high, 16), high), :] = expand_grad[
                :, side * TILE : (side + 1) * TILE
            ].reshape(ROW_BLOCKS, high, TILE)
        project_grad = dot(act_ref[...], back_ref[...], TN).astype(jnp.bfloat16)
        for side in range(2):
            grad_ref[side, blocks, deep : 2 * deep, :] = project_grad[
                :, side * TILE : (side + 1) * TILE
            ].reshape(4, deep, TILE)
        return carry

    lax.fori_loop(0, 4, step, 0)
    sums_ref[8:12, :] = bias_ref[0:4, :]
    weight = outer()
    for first in range(0, slots, CHUNK):
        here = slice(first, first + CHUNK)
        normal = resid_ref[here, :]
        two = two_ref[here, :]
        back = back_ref[here, :].astype(jnp.float32)
        grad = back + normal_back(normal, ratio_ref[here, :], two * params_ref[2:3, :])
        low = grad.astype(jnp.bfloat16)
        sums_ref[2:3, :] += jnp.sum(two * normal, axis=0, keepdims=True)
        sums_ref[3:4, :] += jnp.sum(two, axis=0, keepdims=True)
        sums_ref[6:7, :] += jnp.sum(low.astype(jnp.float32), axis=0, keepdims=True)
        sums_ref[7:8, :] += jnp.sum(back, axis=0, keepdims=True)
        resid_ref[here, :] = grad
        act_ref[here, :] = low
        low_ref[here, :] = dot(low, weight, NT).astype(jnp.bfloat16)
        out_ref[here, :] = (total_ref[here, :] * live_ref[here, :]).astype(jnp.bfloat16)
    outer_grad = dot(mixed_ref[...], act_ref[...], TN).astype(jnp.bfloat16)
    for side in range(2):
        grad_ref[side, :, 2 * deep : 2 * deep + high, :] = outer_grad[:, side * TILE : (side + 1) * TILE].reshape(
            ROW_BLOCKS, high, TILE
        )


def middle(tokens, cotangent, mixed, live, params, sources, where, group):
    slots, width = tokens.shape
    high = width // ROW_BLOCKS
    packed = (2, ROW_BLOCKS, 9 * high, TILE)
    vmem = pl.BlockSpec(memory_space=pltpu.VMEM)
    low = jax.ShapeDtypeStruct((slots, width), jnp.bfloat16)
    return pl.pallas_call(
        functools.partial(middle_kernel, group),
        in_specs=[pl.BlockSpec(memory_space=pltpu.SMEM)] + [vmem] * 5
        + [pl.BlockSpec(memory_space=pl.ANY)] * len(sources),
        out_specs=[vmem] * 5,
        out_shape=[
            low,
            jax.ShapeDtypeStruct((slots, width), jnp.float32),
            low,
            jax.ShapeDtypeStruct(packed, jnp.bfloat16),
            jax.ShapeDtypeStruct((16, width), jnp.float32),
        ],
        scratch_shapes=[
            pltpu.VMEM(packed, jnp.bfloat16),
            pltpu.VMEM((width, slots), jnp.bfloat16),
            pltpu.VMEM((slots, width), jnp.bfloat16),
            pltpu.VMEM((slots, width), jnp.float32),
            pltpu.VMEM((slots, width), jnp.float32),
            pltpu.VMEM((slots, width), jnp.bfloat16),
            pltpu.VMEM((slots, width), jnp.bfloat16),
            pltpu.VMEM((8, width), jnp.float32),
            pltpu.VMEM((8, width), jnp.float32),
            pltpu.VMEM((slots, 1), jnp.float32),
            pltpu.SemaphoreType.DMA((copy_count(sources, group),)),
        ],
        compiler_params=compiler(60),
        cost_estimate=cost(54 * slots * width * width, 40 * slots * width),
        name="middle",
    )(where, tokens, cotangent, mixed, live, params, *sources)


def inner_kernel(turned_ref, grads_ref, grad_ref, sums_ref):
    width = turned_ref.shape[0]
    high = width // ROW_BLOCKS
    turned = turned_ref[...]
    sums_ref[...] = jnp.zeros_like(sums_ref)
    for part in range(3):
        values = grads_ref[part]
        grad = dot(turned, values).astype(jnp.bfloat16)
        for side in range(2):
            t = 2 * part + side
            grad_ref[t // 3, :, t % 3 * high : (t % 3 + 1) * high, :] = grad[
                :, side * TILE : (side + 1) * TILE
            ].reshape(ROW_BLOCKS, high, TILE)
        if part != 1:
            row = 4 if part == 0 else 5
            sums_ref[row : row + 1, :] = jnp.sum(values.astype(jnp.float32), axis=0, keepdims=True)


def inner_gradient(turned, grads):
    width, slots = turned.shape
    vmem = pl.BlockSpec(memory_space=pltpu.VMEM)
    return pl.pallas_call(
        inner_kernel,
        in_specs=[vmem] * 2,
        out_specs=[vmem] * 2,
        out_shape=[
            jax.ShapeDtypeStruct((2, ROW_BLOCKS, 3 * (width // ROW_BLOCKS), TILE), jnp.bfloat16),
            jax.ShapeDtypeStruct((16, width), jnp.float32),
        ],
        compiler_params=compiler(40),
        cost_estimate=cost(6 * slots * width * width, 8 * slots * width),
        name="inner_gradient",
    )(turned, grads)


def input_kernel(tokens_ref, params_ref, packed_ref, grads_ref, resid_ref, out_ref, sums_ref):
    slots, width = tokens_ref.shape
    high = width // ROW_BLOCKS
    sums_ref[...] = jnp.zeros_like(sums_ref)
    weights = [
        jnp.concatenate(
            [tile_of(packed_ref, t // 3, t % 3 * high, high) for t in (2 * part, 2 * part + 1)], axis=1
        )
        for part in range(3)
    ]
    for first in range(0, slots, CHUNK):
        here = slice(first, first + CHUNK)
        grad = dot(grads_ref[0, here, :], weights[0], NT)
        for part in (1, 2):
            grad = grad + dot(grads_ref[part, here, :], weights[part], NT)
        normal, ratio = normal_of(tokens_ref[here, :].astype(jnp.float32))
        sums_ref[0:1, :] += jnp.sum(grad * normal, axis=0, keepdims=True)
        sums_ref[1:2, :] += jnp.sum(grad, axis=0, keepdims=True)
        out_ref[here, :] = resid_ref[here, :] + normal_back(normal, ratio, grad * params_ref[0:1, :])


def input_gradient(tokens, params, packed, grads, resid):
    slots, width = tokens.shape
    vmem = pl.BlockSpec(memory_space=pltpu.VMEM)
    return pl.pallas_call(
        input_kernel,
        in_specs=[vmem] * 5,
        out_specs=[vmem] * 2,
        out_shape=[
            jax.ShapeDtypeStruct((slots, width), jnp.float32),
            jax.ShapeDtypeStruct((16, width), jnp.float32),
        ],
        compiler_params=compiler(48),
        cost_estimate=cost(6 * slots * width * width, 16 * slots * width),
        name="input_gradient",
    )(tokens, params, packed, grads, resid)


def gather_vector(master, ring):
    own = master.astype(jnp.bfloat16)
    group = ring.group
    parts = [own] + [ring.send_shard(own, step) for step in range(1, group)]
    stacked = jnp.stack(parts)
    order = (ring.z - jnp.arange(group)) % group
    return jnp.take(stacked, order, axis=0).reshape(group * own.shape[0], own.shape[1])


def sum_vector(grad, ring):
    group = ring.group
    if not ring.square or ring.side != 2:
        whole = lax.psum_scatter(grad, "shard", scatter_dimension=0, tiled=True)
        return lax.psum(whole, "dp")
    flat = grad.reshape(group, -1, 128)
    flat = flat + ring.send_core(flat)
    for bit in (2, 4):
        flat = flat + lax.ppermute(flat, "dp", [(i, i ^ bit) for i in range(ring.data)])

    def shard_of(step):
        return lax.dynamic_index_in_dim(flat, (ring.z + step) % group, 0, keepdims=False)

    done = shard_of(0)
    for step in range(1, group):
        done = done + ring.send_shard(shard_of(step), step)
    return done.reshape(grad.shape[0] // group, grad.shape[1])


def on_device(
    tokens,
    cotangent,
    seq_lengths,
    seq_owner,
    attend_master,
    expand_master,
    project_master,
    vector_master,
    attend_mean,
    expand_mean,
    project_mean,
    vector_mean,
    attend_square,
    expand_square,
    project_square,
    vector_square,
):
    ring = Ring()
    slots, width = tokens.shape
    high = width // ROW_BLOCKS
    low = jnp.bfloat16
    own_inner = fold(attend_master[:, : 3 * width].astype(low), high)
    own_rest = jnp.concatenate(
        [
            fold(expand_master.astype(low), high),
            fold(project_master.astype(low), 4 * high),
            fold(attend_master[:, 3 * width :].astype(low), high),
        ],
        axis=2,
    )
    vector = gather_vector(vector_master, ring).astype(jnp.float32)
    inner_sources, inner_places = gather_packed(own_inner, ring)
    rest_sources, rest_places = gather_packed(own_rest, ring)
    device = lax.axis_index("dp") * ring.group + ring.z
    segment = slot_segments(seq_lengths, seq_owner, device, slots)
    live = (segment >= 0).astype(jnp.float32)[:, None]
    params = jnp.concatenate(
        [vector[:, :8].T, vector[:, 8:].reshape(4, width), jnp.zeros((4, width), jnp.float32)]
    )
    projected, turned, inner = project_rows(
        tokens, params, inner_sources, where_array(inner_places, ring), ring.group
    )
    mixed, logs = attention(projected, segment)
    layer_output, grad_resid, grad_mixed, rest_grad, rest_sums = middle(
        tokens, cotangent, mixed, live, params, rest_sources, where_array(rest_places, ring), ring.group
    )
    grads = attention_back(projected, grad_mixed, logs, segment)
    inner_grad, inner_sums = inner_gradient(turned, grads)
    input_grad, input_sums = input_gradient(tokens, params, inner, grads, grad_resid)
    sums = rest_sums + inner_sums + input_sums
    vector_grad = jnp.concatenate([sums[:8].T, sums[8:12].reshape(width, 4)], axis=1)
    rest_sum = sum_packed(rest_grad, ring).astype(jnp.float32)
    inner_sum = sum_packed(inner_grad, ring).astype(jnp.float32)
    expand_sum = unfold(rest_sum[:, :, : 4 * high], high)
    project_sum = unfold(rest_sum[:, :, 4 * high : 8 * high], 4 * high)
    attend_sum = jnp.concatenate(
        [unfold(inner_sum, high), unfold(rest_sum[:, :, 8 * high :], high)], axis=1
    )
    vector_sum = sum_vector(vector_grad, ring)
    attend_state = adam(
        attend_master, attend_mean, attend_square, attend_sum, RATE_MATRIX, DECAY_MATRIX
    )
    expand_state = adam(
        expand_master, expand_mean, expand_square, expand_sum, RATE_MATRIX, DECAY_MATRIX
    )
    project_state = adam(
        project_master, project_mean, project_square, project_sum, RATE_MATRIX, DECAY_MATRIX
    )
    vector_state = adam(vector_master, vector_mean, vector_square, vector_sum, RATE_VECTOR, 0.0)
    return (
        layer_output,
        input_grad,
        attend_state[0],
        expand_state[0],
        project_state[0],
        vector_state[0],
        attend_state[1],
        expand_state[1],
        project_state[1],
        vector_state[1],
        attend_state[2],
        expand_state[2],
        project_state[2],
        vector_state[2],
    )


def solution(mesh):
    return jax.shard_map(
        on_device,
        mesh=mesh,
        in_specs=(
            P(("dp", "shard"), None),
            P(("dp", "shard"), None),
            P(),
            P(),
            P("shard", None),
            P("shard", None),
            P("shard", None),
            P("shard", None),
            P("shard", None),
            P("shard", None),
            P("shard", None),
            P("shard", None),
            P("shard", None),
            P("shard", None),
            P("shard", None),
            P("shard", None),
        ),
        out_specs=(
            P(("dp", "shard"), None),
            P(("dp", "shard"), None),
            P("shard", None),
            P("shard", None),
            P("shard", None),
            P("shard", None),
            P("shard", None),
            P("shard", None),
            P("shard", None),
            P("shard", None),
            P("shard", None),
            P("shard", None),
            P("shard", None),
            P("shard", None),
        ),
        check_vma=False,
    )
```

```python
import functools
import math

import jax
import jax.numpy as jnp
from jax import lax
from jax.experimental import pallas as pl
from jax.experimental.pallas import tpu as pltpu
from jax.sharding import PartitionSpec as P

HEADS = 12
HEAD_DIM = 64
STEP = 10


NORM_EPS = 1e-05
MASK_FILL = -1e30
BETA_ONE = 0.9
BETA_TWO = 0.999
ADAM_EPS = 1e-08
RATE_MATRIX = 0.05
RATE_VECTOR = 0.3
DECAY_MATRIX = 0.01
BLOCK = 256
NT = (((1,), (1,)), ((), ()))
TN = (((0,), (0,)), ((), ()))


def slot_segments(seq_lengths, seq_owner, device, slots):
    mine = seq_owner == device
    owned = jnp.where(mine, seq_lengths, 0)
    starts = jnp.cumsum(owned) - owned
    place = jnp.arange(slots, dtype=jnp.int32)[:, None]
    inside = mine[None, :] & (place >= starts[None, :]) & (place < (starts + owned)[None, :])
    labels = jnp.arange(seq_lengths.shape[0], dtype=jnp.int32)[None, :] + 1
    return jnp.sum(jnp.where(inside, labels, 0), axis=1) - 1


def dot(a, b, dims=(((1,), (0,)), ((), ()))):
    return lax.dot_general(a, b, dims, preferred_element_type=jnp.float32)


def mask_of(column, row, first, end, start):
    later = lax.broadcasted_iota(jnp.int32, (end - first, end - start), 0) + first
    earlier = lax.broadcasted_iota(jnp.int32, (end - first, end - start), 1) + start
    return (column == row) & (earlier <= later)


def forward_kernel(column_ref, row_ref, q_ref, k_ref, v_ref, mixed_ref, log_ref):
    slots = q_ref.shape[0]
    scale = HEAD_DIM**-0.5
    low = lax.broadcasted_iota(jnp.int32, (1, 128), 1) < HEAD_DIM
    for index in range(slots // BLOCK):
        first, end = index * BLOCK, (index + 1) * BLOCK
        start = max(0, first - 512)
        ok = mask_of(column_ref[first:end, :], row_ref[:, start:end], first, end, start)
        q = q_ref[first:end, :]
        k = k_ref[start:end, :]
        v = v_ref[start:end, :]
        mixed, logs = [], []
        for head in range(2):
            mine = low if head == 0 else ~low
            s = dot(jnp.where(mine, q, jnp.zeros_like(q)), k, NT) * scale
            s = jnp.where(ok, s, MASK_FILL)
            top = jnp.max(s, axis=1, keepdims=True)
            e = jnp.exp(s - top)
            total = jnp.sum(e, axis=1, keepdims=True)
            p = (e * (1.0 / total)).astype(jnp.bfloat16)
            mixed.append(dot(p, v))
            logs.append(top + jnp.log(total))
        mixed_ref[first:end, :] = jnp.where(low, mixed[0], mixed[1]).astype(jnp.bfloat16)
        log_ref[0, first:end, :] = jnp.concatenate(logs, axis=1)


def backward_kernel(column_ref, row_ref, q_ref, k_ref, v_ref, g_ref, log_ref, out_ref, ka, va):
    slots = q_ref.shape[0]
    scale = HEAD_DIM**-0.5
    low = lax.broadcasted_iota(jnp.int32, (1, 128), 1) < HEAD_DIM
    ka[...] = jnp.zeros_like(ka)
    va[...] = jnp.zeros_like(va)
    for index in range(slots // BLOCK):
        first, end = index * BLOCK, (index + 1) * BLOCK
        start = max(0, first - 512)
        ok = mask_of(column_ref[first:end, :], row_ref[:, start:end], first, end, start)
        q = q_ref[first:end, :]
        g = g_ref[first:end, :]
        k = k_ref[start:end, :]
        v = v_ref[start:end, :]
        dq, dk, dv = [], [], []
        for head in range(2):
            mine = low if head == 0 else ~low
            s = dot(jnp.where(mine, q, jnp.zeros_like(q)), k, NT) * scale
            p = jnp.exp(jnp.where(ok, s - log_ref[0, first:end, head : head + 1], MASK_FILL))
            dp = dot(jnp.where(mine, g, jnp.zeros_like(g)), v, NT)
            w = p * dp
            ds = (w - p * jnp.sum(w, axis=1, keepdims=True)).astype(jnp.bfloat16)
            dq.append(dot(ds, k))
            dk.append(dot(ds, q, TN))
            dv.append(dot(p.astype(jnp.bfloat16), g, TN))
        out_ref[0, first:end, :] = (jnp.where(low, dq[0], dq[1]) * scale).astype(jnp.bfloat16)
        ka[start:end, :] += jnp.where(low, dk[0], dk[1])
        va[start:end, :] += jnp.where(low, dv[0], dv[1])
    out_ref[1] = (ka[...] * scale).astype(jnp.bfloat16)
    out_ref[2] = va[...].astype(jnp.bfloat16)


def columns(offset, slots):
    return pl.BlockSpec((slots, 128), lambda pair: (0, pair + offset))


def whole(shape):
    return pl.BlockSpec(shape, lambda pair: (0, 0))


def attention(projected, segment):
    slots = projected.shape[0]
    pairs = HEADS // 2
    return pl.pallas_call(
        forward_kernel,
        grid=(pairs,),
        in_specs=[whole((slots, 1)), whole((1, slots))] + [columns(pairs * n, slots) for n in range(3)],
        out_specs=[columns(0, slots), pl.BlockSpec((1, slots, 2), lambda pair: (pair, 0, 0))],
        out_shape=[
            jax.ShapeDtypeStruct((slots, pairs * 128), jnp.bfloat16),
            jax.ShapeDtypeStruct((pairs, slots, 2), jnp.float32),
        ],
        compiler_params=pltpu.CompilerParams(vmem_limit_bytes=48 * 1024 * 1024),
        cost_estimate=cost(2 * slots * slots * pairs * 256, 8 * slots * pairs * 128),
        name="attention",
    )(segment[:, None], segment[None, :], projected, projected, projected)


def attention_back(projected, grad_mixed, logs, segment, first, count):
    slots = projected.shape[0]
    pairs = HEADS // 2
    return pl.pallas_call(
        backward_kernel,
        grid=(count,),
        in_specs=[whole((slots, 1)), whole((1, slots))]
        + [columns(pairs * n + first, slots) for n in range(3)]
        + [columns(first, slots), pl.BlockSpec((1, slots, 2), lambda pair: (pair + first, 0, 0))],
        out_specs=pl.BlockSpec((3, slots, 128), lambda pair: (0, 0, pair)),
        out_shape=jax.ShapeDtypeStruct((3, slots, count * 128), jnp.bfloat16),
        scratch_shapes=[pltpu.VMEM((slots, 128), jnp.float32)] * 2,
        compiler_params=pltpu.CompilerParams(vmem_limit_bytes=48 * 1024 * 1024),
        cost_estimate=cost(5 * slots * slots * count * 256, 16 * slots * count * 128),
        name="attention_back",
    )(segment[:, None], segment[None, :], projected, projected, projected, grad_mixed, logs)


def adam(master, mean, square, grad, rate, decay):
    mean_new = BETA_ONE * mean + (1.0 - BETA_ONE) * grad
    square_new = BETA_TWO * square + (1.0 - BETA_TWO) * grad * grad
    mean_hat = mean_new / (1.0 - BETA_ONE**STEP)
    square_hat = square_new / (1.0 - BETA_TWO**STEP)
    master_new = master - rate * (mean_hat / (jnp.sqrt(square_hat) + ADAM_EPS) + decay * master)
    return (mean_new, square_new, master_new)


class Ring:
    def __init__(self):
        self.group = lax.axis_size("shard")
        self.data = lax.axis_size("dp")
        self.plane = self.data // 2
        self.side = math.isqrt(self.plane)
        self.square = self.data == 2 * self.side * self.side
        self.z = lax.axis_index("shard")
        device = lax.axis_index("dp")
        self.core = device % 2
        chip = device // 2
        high, low = chip // self.side, chip % self.side
        straight = low * self.side + high
        crossed = high * self.side + low
        self.block = jnp.where(self.core == 0, straight, crossed)
        self.block_other = jnp.where(self.core == 0, crossed, straight)

    def send_core(self, value):
        return lax.ppermute(value, "dp", [(i, i ^ 1) for i in range(self.data)])

    def send_plane(self, value, step):
        side = self.side
        first, second = step // side, step % side
        pairs = []
        for device in range(self.data):
            core, chip = device % 2, device // 2
            high, low = chip // side, chip % side
            if core == 0:
                low, high = (low + first) % side, (high + second) % side
            else:
                high, low = (high + first) % side, (low + second) % side
            pairs.append((device, (high * side + low) * 2 + core))
        return lax.ppermute(value, "dp", pairs)

    def spread(self, value, direct):
        if direct or self.side != 2:
            return [self.send_plane(value, step) for step in range(1, self.plane)]
        second, first = self.send_plane(value, 1), self.send_plane(value, 2)
        return [second, first, self.send_plane(first, 1)]

    def shifted(self, block, step):
        side = self.side
        first, second = step // side, step % side
        return (block // side + first) % side * side + (block % side + second) % side

    def back(self, block, step):
        side = self.side
        first, second = step // side, step % side
        return (block // side - first) % side * side + (block % side - second) % side

    def send_shard(self, value, step):
        group = self.group
        return lax.ppermute(value, "shard", [(i, (i + step) % group) for i in range(group)])


TILE = 384
ROW_BLOCKS = 16
CHUNK = 256


def compiler(megabytes):
    return pltpu.CompilerParams(vmem_limit_bytes=megabytes * 1024 * 1024)


def cost(flops, bytes_accessed):
    return pl.CostEstimate(flops=flops, bytes_accessed=bytes_accessed, transcendentals=0)


def pack_kernel(kinds, *refs):
    out_ref = refs[-1]
    row = 0
    for (first, columns, high), ref in zip(kinds, refs[:-1], strict=True):
        tiles = columns // (2 * TILE)
        for half in range(2):
            for tile in range(tiles):
                column = first + (half * tiles + tile) * TILE
                part = ref[:, column : column + TILE].astype(jnp.bfloat16)
                out_ref[half, :, row + tile * high : row + (tile + 1) * high, :] = part.reshape(-1, high, TILE)
        row += tiles * high


def pack(parts):
    blocks = parts[0][0].shape[0] // parts[0][3]
    rows = sum(columns // (2 * TILE) * high for _, _, columns, high in parts)
    vmem = pl.BlockSpec(memory_space=pltpu.VMEM)
    return pl.pallas_call(
        functools.partial(pack_kernel, [part[1:] for part in parts]),
        in_specs=[vmem] * len(parts),
        out_specs=vmem,
        out_shape=jax.ShapeDtypeStruct((2, blocks, rows, TILE), jnp.bfloat16),
        compiler_params=compiler(40),
        cost_estimate=cost(0, 12 * blocks * rows * TILE),
        name="pack",
    )(*[part[0] for part in parts])


def gather_packed(own, ring, direct):
    blocks = own.shape[1]
    if not ring.square or blocks != ring.plane:
        whole = lax.all_gather(own, "shard", axis=1, tiled=True)
        return [whole], [(None, 0)]
    chunk = lax.dynamic_index_in_dim(
        lax.dynamic_index_in_dim(own, ring.core, 0, keepdims=False), ring.block, 0, keepdims=False
    )
    foreign = jnp.stack([ring.send_shard(chunk, step) for step in range(1, ring.group)])
    mine = [foreign] + ring.spread(foreign, direct)
    other = [ring.send_core(value) for value in mine]
    places = [(ring.core, ring.back(ring.block, step)) for step in range(ring.plane)]
    places += [(1 - ring.core, ring.back(ring.block_other, step)) for step in range(ring.plane)]
    return [own] + mine + other, [(None, ring.z * blocks)] + places


def where_array(places, ring):
    scalars = [ring.z]
    for half, block in places:
        scalars += [0 if half is None else half, block]
    return jnp.stack([jnp.asarray(v, jnp.int32) for v in scalars])


def copy_count(sources, group):
    return 1 if len(sources) == 1 else 2 + (len(sources) - 1) * (group - 1)


def start_pieces(where_ref, refs, group, out_ref, sems):
    copies = []

    def begin(source, target):
        copy = pltpu.make_async_copy(source, target, sems.at[len(copies)])
        copy.start()
        copies.append(copy)

    if len(refs) == 1:
        begin(refs[0], out_ref)
        return copies
    blocks = refs[0].shape[1]
    first = where_ref[2]
    for half in range(2):
        begin(refs[0].at[half], out_ref.at[half, pl.ds(first, blocks)])
    for number, ref in enumerate(refs[1:], 1):
        half, block = where_ref[1 + 2 * number], where_ref[2 + 2 * number]
        for step in range(1, group):
            source = lax.rem(where_ref[0] - step + group, group)
            begin(ref.at[step - 1], out_ref.at[half, source * blocks + block])
    return copies


class Sum:
    def __init__(self, grad, ring):
        self.ring, self.rows = ring, grad.shape[2]
        self.blocks = ROW_BLOCKS // ring.group
        self.staged = ring.square and self.blocks == ring.plane
        self.grad = grad
        if self.staged:
            sent = lax.dynamic_index_in_dim(grad, 1 - ring.core, 0, keepdims=False)
            self.got = ring.send_core(sent)

    def chip(self, after):
        if not self.staged:
            return after
        ring = self.ring
        grad, after = lax.optimization_barrier((self.grad, after))
        kept = lax.dynamic_index_in_dim(grad, ring.core, 0, keepdims=False)
        chip = (kept.astype(jnp.float32) + self.got.astype(jnp.float32)).astype(jnp.bfloat16)
        chip, after = lax.optimization_barrier((chip, after))
        chip = chip.reshape(ring.group, ring.plane, self.rows, TILE)

        def block_of(step):
            return lax.dynamic_index_in_dim(
                chip, ring.shifted(ring.block, step), 1, keepdims=False
            )

        self.arrived = [ring.send_plane(block_of(step), step) for step in range(1, ring.plane)]
        self.level = block_of(0)
        return after

    def plane(self, after):
        if not self.staged:
            return after
        ring = self.ring
        level, after = lax.optimization_barrier((self.level, after))
        level = level.astype(jnp.float32)
        for value in self.arrived:
            level = level + value.astype(jnp.float32)
        level, after = lax.optimization_barrier((level.astype(jnp.bfloat16), after))

        def shard_of(step):
            return lax.dynamic_index_in_dim(
                level, (ring.z + step) % ring.group, 0, keepdims=False
            )

        self.arrived = [ring.send_shard(shard_of(step), step) for step in range(1, ring.group)]
        self.level = shard_of(0)
        return after

    def finish(self):
        ring = self.ring
        if not self.staged:
            whole = lax.psum_scatter(
                self.grad.astype(jnp.float32), "shard", scatter_dimension=1, tiled=True
            )
            return [lax.psum(whole, "dp").astype(jnp.bfloat16)], [(None, 0)]
        done = self.level.astype(jnp.float32)
        for value in self.arrived:
            done = done + value.astype(jnp.float32)
        mine = [done.astype(jnp.bfloat16)]
        mine += ring.spread(mine[0], True)
        other = [ring.send_core(value) for value in mine]
        places = [(ring.core, ring.back(ring.block, step)) for step in range(ring.plane)]
        places += [(1 - ring.core, ring.back(ring.block_other, step)) for step in range(ring.plane)]
        return mine + other, places


def adam_kernel(kinds, counts, where_ref, *refs):
    number = sum(counts)
    sources, (master_ref, mean_ref, square_ref) = refs[:number], refs[number : number + 3]
    mean_out, square_out, master_out = refs[number + 3 : number + 6]
    packed, sems = refs[number + 6 : -1], refs[-1]
    copies, scalar, position = [], 0, 0
    for target, count in zip(packed, counts, strict=True):
        for ref in sources[position : position + count]:
            if count == 1:
                place = target
            else:
                place = target.at[where_ref[scalar], where_ref[scalar + 1]]
            copy = pltpu.make_async_copy(ref, place, sems.at[len(copies)])
            copy.start()
            copies.append(copy)
            scalar += 2
        position += count
    for copy in copies:
        copy.wait()
    for gradient, row, first, columns, high in kinds:
        tiles = columns // (2 * TILE)
        target = packed[gradient]
        for half in range(2):
            for tile in range(tiles):
                column = first + (half * tiles + tile) * TILE
                here = slice(column, column + TILE)
                for block in range(target.shape[1]):
                    rows = slice(block * high, (block + 1) * high)
                    grad = target[half, block, row + tile * high : row + (tile + 1) * high, :].astype(jnp.float32)
                    state = adam(
                        master_ref[rows, here], mean_ref[rows, here], square_ref[rows, here], grad, RATE_MATRIX, DECAY_MATRIX
                    )
                    mean_out[rows, here], square_out[rows, here], master_out[rows, here] = state


def adam_packed(master, mean, square, gradients, kinds):
    sources = [source for group, _ in gradients for source in group]
    counts = [len(group) for group, _ in gradients]
    scalars = [v for _, places in gradients for half, block in places for v in (0 if half is None else half, block)]
    where = jnp.stack([jnp.asarray(v, jnp.int32) for v in scalars])
    shapes = []
    for group, places in gradients:
        if len(group) == 1:
            shapes.append(group[0].shape)
        else:
            shapes.append((2, len(group) // 2) + group[0].shape)
    vmem = pl.BlockSpec(memory_space=pltpu.VMEM)
    return pl.pallas_call(
        functools.partial(adam_kernel, kinds, counts),
        in_specs=[pl.BlockSpec(memory_space=pltpu.SMEM)]
        + [pl.BlockSpec(memory_space=pl.ANY)] * len(sources)
        + [vmem] * 3,
        out_specs=[vmem] * 3,
        out_shape=[jax.ShapeDtypeStruct(master.shape, jnp.float32)] * 3,
        scratch_shapes=[pltpu.VMEM(shape, jnp.bfloat16) for shape in shapes]
        + [pltpu.SemaphoreType.DMA((len(sources),))],
        compiler_params=compiler(32),
        cost_estimate=cost(20 * master.size, 26 * master.size),
        name="adam_packed",
    )(where, *sources, master, mean, square)


def tile_of(packed_ref, half, row, high):
    part = packed_ref[half, :, pl.ds(row, high), :]
    return part.reshape(ROW_BLOCKS * high, TILE)


def normal_of(rows):
    centre = jnp.mean(rows, axis=1, keepdims=True)
    centred = rows - centre
    spread = jnp.mean(centred * centred, axis=1, keepdims=True)
    ratio = lax.rsqrt(spread + NORM_EPS)
    return centred * ratio, ratio


def normal_back(normal, ratio, scaled):
    along = jnp.mean(scaled * normal, axis=1, keepdims=True)
    return ratio * (scaled - jnp.mean(scaled, axis=1, keepdims=True) - normal * along)


def project_kernel(group, where_ref, tokens_ref, params_ref, *refs):
    pieces, (out_ref, turned_ref, packed_ref, sems) = refs[:-4], refs[-4:]
    slots, width = tokens_ref.shape
    high = width // ROW_BLOCKS
    copies = start_pieces(where_ref, pieces, group, packed_ref, sems)
    lows = []
    for first in range(0, slots, CHUNK):
        normal, _ = normal_of(tokens_ref[first : first + CHUNK, :].astype(jnp.float32))
        low = (normal * params_ref[0:1, :] + params_ref[1:2, :]).astype(jnp.bfloat16)
        turned_ref[:, first : first + CHUNK] = low.T
        lows.append(low)
    for copy in copies:
        copy.wait()
    for part in range(3):
        weight = jnp.concatenate(
            [tile_of(packed_ref, t // 3, t % 3 * high, high) for t in (2 * part, 2 * part + 1)], axis=1
        )
        for number, low in enumerate(lows):
            value = dot(low, weight)
            if part != 1:
                row = 4 if part == 0 else 5
                value = value + params_ref[row : row + 1, :]
            out_ref[number * CHUNK : (number + 1) * CHUNK, part * width : (part + 1) * width] = (
                value.astype(jnp.bfloat16)
            )


def project_rows(tokens, params, sources, where, group):
    slots, width = tokens.shape
    high = width // ROW_BLOCKS
    vmem = pl.BlockSpec(memory_space=pltpu.VMEM)
    return pl.pallas_call(
        functools.partial(project_kernel, group),
        in_specs=[pl.BlockSpec(memory_space=pltpu.SMEM), vmem, vmem]
        + [pl.BlockSpec(memory_space=pl.ANY)] * len(sources),
        out_specs=[vmem] * 3,
        out_shape=[
            jax.ShapeDtypeStruct((slots, 3 * width), jnp.bfloat16),
            jax.ShapeDtypeStruct((width, slots), jnp.bfloat16),
            jax.ShapeDtypeStruct((2, ROW_BLOCKS, 3 * high, TILE), jnp.bfloat16),
        ],
        scratch_shapes=[pltpu.SemaphoreType.DMA((copy_count(sources, group),))],
        compiler_params=compiler(40),
        cost_estimate=cost(6 * slots * width * width, 16 * slots * width),
        name="project_rows",
    )(where, tokens, params, *sources)


def tail_of(values):
    size = jnp.abs(values) * (0.5**0.5)
    bell = jnp.exp(-0.5 * values * values)
    t = 1.0 / (1.0 + 0.5 * size)
    series = jnp.full_like(t, 0.17087277)
    for c in (
        -0.82215223, 1.48851587, -1.13520398, 0.27886807, -0.18628806, 0.09678418, 0.37409196, 1.00002368, -1.26551223,
    ):
        series = series * t + c
    tail = 0.5 * t * bell * jnp.exp(series)
    return bell, jnp.where(values > 0, 1.0 - tail, tail)


def middle_kernel(group, where_ref, tokens_ref, cotangent_ref, mixed_ref, live_ref, params_ref, *refs):
    pieces = refs[:-16]
    (out_ref, resid_ref, low_ref, wide_ref, deep_ref, sums_ref) = refs[-16:-10]
    (packed_ref, turned_ref, back_ref, total_ref, two_ref, act_ref, pre_ref, bias_ref, ratio_ref, sems) = refs[-10:]
    slots, width = tokens_ref.shape
    high = width // ROW_BLOCKS
    deep = 4 * high
    copies = start_pieces(where_ref, pieces, group, packed_ref, sems)
    sums_ref[...] = jnp.zeros_like(sums_ref)
    for first in range(0, slots, CHUNK):
        here = slice(first, first + CHUNK)
        back_ref[here, :] = (cotangent_ref[here, :].astype(jnp.float32) * live_ref[here, :]).astype(jnp.bfloat16)
    for copy in copies:
        copy.wait()

    def outer():
        return jnp.concatenate([tile_of(packed_ref, half, 2 * deep, high) for half in range(2)], axis=1)

    weight = outer()
    for first in range(0, slots, CHUNK):
        here = slice(first, first + CHUNK)
        resid = tokens_ref[here, :].astype(jnp.float32) + (dot(mixed_ref[here, :], weight) + params_ref[6:7, :])
        normal, ratio = normal_of(resid)
        low = (normal * params_ref[2:3, :] + params_ref[3:4, :]).astype(jnp.bfloat16)
        low_ref[here, :] = low
        turned_ref[:, here] = low.T
        resid_ref[here, :] = normal
        ratio_ref[here, :] = ratio
        total_ref[here, :] = resid + params_ref[7:8, :]
        two_ref[here, :] = jnp.zeros((CHUNK, width), jnp.float32)

    def step(number, carry):
        half = number // 2
        row = pl.multiple_of(number % 2 * (2 * high), 16)
        wide = jnp.concatenate(
            [tile_of(packed_ref, half, row, high), tile_of(packed_ref, half, row + high, high)], axis=1
        )
        blocks = pl.ds(number * 4, 4)
        deep_weight = jnp.concatenate(
            [packed_ref[side, blocks, deep : 2 * deep, :].reshape(4 * deep, TILE) for side in range(2)], axis=1
        )
        bias = params_ref[pl.ds(8 + number, 1), :]
        bias_sum = jnp.zeros((1, width), jnp.float32)
        for first in range(0, slots, CHUNK):
            here = slice(first, first + CHUNK)
            pre = dot(low_ref[here, :], wide) + bias
            bell, below = tail_of(pre)
            act = (pre * below).astype(jnp.bfloat16)
            act_ref[here, :] = act
            slope = below + pre * bell * 0.3989422804014327
            grad = (dot(back_ref[here, :], deep_weight, NT) * slope).astype(jnp.bfloat16)
            pre_ref[here, :] = grad
            bias_sum = bias_sum + jnp.sum(grad.astype(jnp.float32), axis=0, keepdims=True)
            total_ref[here, :] += dot(act, deep_weight)
            two_ref[here, :] += dot(grad, wide, NT)
        bias_ref[pl.ds(number, 1), :] = bias_sum
        expand_grad = dot(turned_ref[...], pre_ref[...]).astype(jnp.bfloat16)
        for side in range(2):
            wide_ref[half, :, pl.ds(pl.multiple_of(row + side * high, 16), high), :] = expand_grad[
                :, side * TILE : (side + 1) * TILE
            ].reshape(ROW_BLOCKS, high, TILE)
        project_grad = dot(act_ref[...], back_ref[...], TN).astype(jnp.bfloat16)
        for side in range(2):
            deep_ref[side, blocks, 0:deep, :] = project_grad[
                :, side * TILE : (side + 1) * TILE
            ].reshape(4, deep, TILE)
        return carry

    lax.fori_loop(0, 4, step, 0)
    sums_ref[8:12, :] = bias_ref[0:4, :]
    weight = outer()
    for first in range(0, slots, CHUNK):
        here = slice(first, first + CHUNK)
        normal = resid_ref[here, :]
        two = two_ref[here, :]
        back = back_ref[here, :].astype(jnp.float32)
        grad = back + normal_back(normal, ratio_ref[here, :], two * params_ref[2:3, :])
        low = grad.astype(jnp.bfloat16)
        sums_ref[2:3, :] += jnp.sum(two * normal, axis=0, keepdims=True)
        sums_ref[3:4, :] += jnp.sum(two, axis=0, keepdims=True)
        sums_ref[6:7, :] += jnp.sum(low.astype(jnp.float32), axis=0, keepdims=True)
        sums_ref[7:8, :] += jnp.sum(back, axis=0, keepdims=True)
        resid_ref[here, :] = grad
        act_ref[here, :] = low
        low_ref[here, :] = dot(low, weight, NT).astype(jnp.bfloat16)
        out_ref[here, :] = (total_ref[here, :] * live_ref[here, :]).astype(jnp.bfloat16)
    outer_grad = dot(mixed_ref[...], act_ref[...], TN).astype(jnp.bfloat16)
    for side in range(2):
        deep_ref[side, :, deep : deep + high, :] = outer_grad[:, side * TILE : (side + 1) * TILE].reshape(
            ROW_BLOCKS, high, TILE
        )


def middle(tokens, cotangent, mixed, live, params, sources, where, group):
    slots, width = tokens.shape
    high = width // ROW_BLOCKS
    packed = (2, ROW_BLOCKS, 9 * high, TILE)
    vmem = pl.BlockSpec(memory_space=pltpu.VMEM)
    low = jax.ShapeDtypeStruct((slots, width), jnp.bfloat16)
    return pl.pallas_call(
        functools.partial(middle_kernel, group),
        in_specs=[pl.BlockSpec(memory_space=pltpu.SMEM)] + [vmem] * 5
        + [pl.BlockSpec(memory_space=pl.ANY)] * len(sources),
        out_specs=[vmem] * 6,
        out_shape=[
            low,
            jax.ShapeDtypeStruct((slots, width), jnp.float32),
            low,
            jax.ShapeDtypeStruct((2, ROW_BLOCKS, 4 * high, TILE), jnp.bfloat16),
            jax.ShapeDtypeStruct((2, ROW_BLOCKS, 5 * high, TILE), jnp.bfloat16),
            jax.ShapeDtypeStruct((16, width), jnp.float32),
        ],
        scratch_shapes=[
            pltpu.VMEM(packed, jnp.bfloat16),
            pltpu.VMEM((width, slots), jnp.bfloat16),
            pltpu.VMEM((slots, width), jnp.bfloat16),
            pltpu.VMEM((slots, width), jnp.float32),
            pltpu.VMEM((slots, width), jnp.float32),
            pltpu.VMEM((slots, width), jnp.bfloat16),
            pltpu.VMEM((slots, width), jnp.bfloat16),
            pltpu.VMEM((8, width), jnp.float32),
            pltpu.VMEM((slots, 1), jnp.float32),
            pltpu.SemaphoreType.DMA((copy_count(sources, group),)),
        ],
        compiler_params=compiler(60),
        cost_estimate=cost(54 * slots * width * width, 40 * slots * width),
        name="middle",
    )(where, tokens, cotangent, mixed, live, params, *sources)


def inner_kernel(turned_ref, *refs):
    grads, (grad_ref, sums_ref) = refs[:-2], refs[-2:]
    width = turned_ref.shape[0]
    high = width // ROW_BLOCKS
    turned = turned_ref[...]
    sums_ref[...] = jnp.zeros_like(sums_ref)
    for part in range(3):
        values = jnp.concatenate([ref[part] for ref in grads], axis=1)
        grad = dot(turned, values).astype(jnp.bfloat16)
        for side in range(2):
            t = 2 * part + side
            grad_ref[t // 3, :, t % 3 * high : (t % 3 + 1) * high, :] = grad[
                :, side * TILE : (side + 1) * TILE
            ].reshape(ROW_BLOCKS, high, TILE)
        if part != 1:
            row = 4 if part == 0 else 5
            sums_ref[row : row + 1, :] = jnp.sum(values.astype(jnp.float32), axis=0, keepdims=True)


def inner_gradient(turned, grads):
    width, slots = turned.shape
    vmem = pl.BlockSpec(memory_space=pltpu.VMEM)
    return pl.pallas_call(
        inner_kernel,
        in_specs=[vmem] * (1 + len(grads)),
        out_specs=[vmem] * 2,
        out_shape=[
            jax.ShapeDtypeStruct((2, ROW_BLOCKS, 3 * (width // ROW_BLOCKS), TILE), jnp.bfloat16),
            jax.ShapeDtypeStruct((16, width), jnp.float32),
        ],
        compiler_params=compiler(40),
        cost_estimate=cost(6 * slots * width * width, 8 * slots * width),
        name="inner_gradient",
    )(turned, *grads)


def input_kernel(tokens_ref, params_ref, packed_ref, resid_ref, *refs):
    grads, (out_ref, sums_ref) = refs[:-2], refs[-2:]
    slots, width = tokens_ref.shape
    high = width // ROW_BLOCKS
    sums_ref[...] = jnp.zeros_like(sums_ref)
    weights = [
        jnp.concatenate(
            [tile_of(packed_ref, t // 3, t % 3 * high, high) for t in (2 * part, 2 * part + 1)], axis=1
        )
        for part in range(3)
    ]
    for first in range(0, slots, CHUNK):
        here = slice(first, first + CHUNK)
        grad = jnp.zeros((CHUNK, width), jnp.float32)
        for part in range(3):
            values = jnp.concatenate([ref[part, here, :] for ref in grads], axis=1)
            grad = grad + dot(values, weights[part], NT)
        normal, ratio = normal_of(tokens_ref[here, :].astype(jnp.float32))
        sums_ref[0:1, :] += jnp.sum(grad * normal, axis=0, keepdims=True)
        sums_ref[1:2, :] += jnp.sum(grad, axis=0, keepdims=True)
        out_ref[here, :] = resid_ref[here, :] + normal_back(normal, ratio, grad * params_ref[0:1, :])


def input_gradient(tokens, params, packed, grads, resid):
    slots, width = tokens.shape
    vmem = pl.BlockSpec(memory_space=pltpu.VMEM)
    return pl.pallas_call(
        input_kernel,
        in_specs=[vmem] * (4 + len(grads)),
        out_specs=[vmem] * 2,
        out_shape=[
            jax.ShapeDtypeStruct((slots, width), jnp.float32),
            jax.ShapeDtypeStruct((16, width), jnp.float32),
        ],
        compiler_params=compiler(48),
        cost_estimate=cost(6 * slots * width * width, 16 * slots * width),
        name="input_gradient",
    )(tokens, params, packed, resid, *grads)


def gather_vector(master, ring):
    own = master.astype(jnp.bfloat16)
    group = ring.group
    parts = [own] + [ring.send_shard(own, step) for step in range(1, group)]
    stacked = jnp.stack(parts)
    order = (ring.z - jnp.arange(group)) % group
    return jnp.take(stacked, order, axis=0).reshape(group * own.shape[0], own.shape[1])


def sum_vector(grad, ring):
    group = ring.group
    if not ring.square or ring.side != 2:
        whole = lax.psum_scatter(grad, "shard", scatter_dimension=0, tiled=True)
        return lax.psum(whole, "dp")
    flat = grad.reshape(group, -1, 128)
    flat = flat + ring.send_core(flat)
    for bit in (2, 4):
        flat = flat + lax.ppermute(flat, "dp", [(i, i ^ bit) for i in range(ring.data)])

    def shard_of(step):
        return lax.dynamic_index_in_dim(flat, (ring.z + step) % group, 0, keepdims=False)

    done = shard_of(0)
    for step in range(1, group):
        done = done + ring.send_shard(shard_of(step), step)
    return done.reshape(grad.shape[0] // group, grad.shape[1])


def on_device(
    tokens,
    cotangent,
    seq_lengths,
    seq_owner,
    attend_master,
    expand_master,
    project_master,
    vector_master,
    attend_mean,
    expand_mean,
    project_mean,
    vector_mean,
    attend_square,
    expand_square,
    project_square,
    vector_square,
):
    ring = Ring()
    slots, width = tokens.shape
    high = width // ROW_BLOCKS
    own_inner = pack([(attend_master, 0, 3 * width, high)])
    inner_sources, inner_places = gather_packed(own_inner, ring, True)
    vector = gather_vector(vector_master, ring).astype(jnp.float32)
    rest_masters = lax.optimization_barrier(
        ((attend_master, expand_master, project_master), inner_sources[min(1, len(inner_sources) - 1)])
    )[0]
    own_rest = pack(
        [
            (rest_masters[1], 0, 4 * width, high),
            (rest_masters[2], 0, width, 4 * high),
            (rest_masters[0], 3 * width, width, high),
        ]
    )
    rest_sources, rest_places = gather_packed(own_rest, ring, False)
    device = lax.axis_index("dp") * ring.group + ring.z
    segment = slot_segments(seq_lengths, seq_owner, device, slots)
    live = (segment >= 0).astype(jnp.float32)[:, None]
    params = jnp.concatenate(
        [vector[:, :8].T, vector[:, 8:].reshape(4, width), jnp.zeros((4, width), jnp.float32)]
    )
    projected, turned, inner = project_rows(
        tokens, params, inner_sources, where_array(inner_places, ring), ring.group
    )
    mixed, logs = attention(projected, segment)
    layer_output, grad_resid, grad_mixed, wide_grad, deep_grad, rest_sums = middle(
        tokens, cotangent, mixed, live, params, rest_sources, where_array(rest_places, ring), ring.group
    )
    wide, deep = Sum(wide_grad, ring), Sum(deep_grad, ring)
    part = HEADS // 6
    grads = [attention_back(projected, grad_mixed, logs, segment, 0, part)]
    grads[0] = deep.chip(wide.chip(grads[0]))
    grad_mixed, grads[0] = lax.optimization_barrier((grad_mixed, grads[0]))
    grads.append(attention_back(projected, grad_mixed, logs, segment, part, part))
    grads.append(attention_back(projected, grad_mixed, logs, segment, 2 * part, part))
    grads[2] = wide.plane(grads[2])
    inner_grad, inner_sums = inner_gradient(turned, grads)
    inner_part = Sum(inner_grad, ring)
    input_grad, input_sums = input_gradient(tokens, params, inner, grads, grad_resid)
    input_sums = inner_part.chip(input_sums)
    sums = rest_sums + inner_sums + input_sums
    vector_grad = jnp.concatenate([sums[:8].T, sums[8:12].reshape(width, 4)], axis=1)
    vector_sum = sum_vector(vector_grad, ring)
    vector_sum = inner_part.plane(deep.plane(vector_sum))
    wide_sum, deep_sum, inner_sum = wide.finish(), deep.finish(), inner_part.finish()
    expand_state = adam_packed(
        expand_master, expand_mean, expand_square, [wide_sum], [(0, 0, 0, 4 * width, high)]
    )
    project_state = adam_packed(
        project_master, project_mean, project_square, [deep_sum], [(0, 0, 0, width, 4 * high)]
    )
    attend_state = adam_packed(
        attend_master,
        attend_mean,
        attend_square,
        [inner_sum, deep_sum],
        [(0, 0, 0, 3 * width, high), (1, 4 * high, 3 * width, width, high)],
    )
    vector_state = adam(vector_master, vector_mean, vector_square, vector_sum, RATE_VECTOR, 0.0)
    return (
        layer_output,
        input_grad,
        attend_state[0],
        expand_state[0],
        project_state[0],
        vector_state[0],
        attend_state[1],
        expand_state[1],
        project_state[1],
        vector_state[1],
        attend_state[2],
        expand_state[2],
        project_state[2],
        vector_state[2],
    )


def solution(mesh):
    return jax.shard_map(
        on_device,
        mesh=mesh,
        in_specs=(
            P(("dp", "shard"), None),
            P(("dp", "shard"), None),
            P(),
            P(),
            P("shard", None),
            P("shard", None),
            P("shard", None),
            P("shard", None),
            P("shard", None),
            P("shard", None),
            P("shard", None),
            P("shard", None),
            P("shard", None),
            P("shard", None),
            P("shard", None),
            P("shard", None),
        ),
        out_specs=(
            P(("dp", "shard"), None),
            P(("dp", "shard"), None),
            P("shard", None),
            P("shard", None),
            P("shard", None),
            P("shard", None),
            P("shard", None),
            P("shard", None),
            P("shard", None),
            P("shard", None),
            P("shard", None),
            P("shard", None),
            P("shard", None),
            P("shard", None),
        ),
        check_vma=False,
    )
```

```python
import functools
import math

import jax
import jax.numpy as jnp
from jax import lax
from jax.experimental import pallas as pl
from jax.experimental.pallas import tpu as pltpu
from jax.sharding import PartitionSpec as P

HEADS = 12
HEAD_DIM = 64
STEP = 10


NORM_EPS = 1e-05
MASK_FILL = -1e30
BETA_ONE = 0.9
BETA_TWO = 0.999
ADAM_EPS = 1e-08
RATE_MATRIX = 0.05
RATE_VECTOR = 0.3
DECAY_MATRIX = 0.01
BLOCK = 256
NT = (((1,), (1,)), ((), ()))
TN = (((0,), (0,)), ((), ()))


def slot_segments(seq_lengths, seq_owner, device, slots):
    mine = seq_owner == device
    owned = jnp.where(mine, seq_lengths, 0)
    starts = jnp.cumsum(owned) - owned
    place = jnp.arange(slots, dtype=jnp.int32)[:, None]
    inside = mine[None, :] & (place >= starts[None, :]) & (place < (starts + owned)[None, :])
    labels = jnp.arange(seq_lengths.shape[0], dtype=jnp.int32)[None, :] + 1
    return jnp.sum(jnp.where(inside, labels, 0), axis=1) - 1


def dot(a, b, dims=(((1,), (0,)), ((), ()))):
    return lax.dot_general(a, b, dims, preferred_element_type=jnp.float32)


def mask_of(column, row, first, end, start):
    later = lax.broadcasted_iota(jnp.int32, (end - first, end - start), 0) + first
    earlier = lax.broadcasted_iota(jnp.int32, (end - first, end - start), 1) + start
    return (column == row) & (earlier <= later)


def forward_kernel(column_ref, row_ref, q_ref, k_ref, v_ref, mixed_ref, log_ref):
    slots = q_ref.shape[0]
    scale = HEAD_DIM**-0.5
    low = lax.broadcasted_iota(jnp.int32, (1, 128), 1) < HEAD_DIM
    for index in range(slots // BLOCK):
        first, end = index * BLOCK, (index + 1) * BLOCK
        start = max(0, first - 512)
        ok = mask_of(column_ref[first:end, :], row_ref[:, start:end], first, end, start)
        q = q_ref[first:end, :]
        k = k_ref[start:end, :]
        v = v_ref[start:end, :]
        mixed, logs = [], []
        for head in range(2):
            mine = low if head == 0 else ~low
            s = dot(jnp.where(mine, q, jnp.zeros_like(q)), k, NT) * scale
            s = jnp.where(ok, s, MASK_FILL)
            top = jnp.max(s, axis=1, keepdims=True)
            e = jnp.exp(s - top)
            total = jnp.sum(e, axis=1, keepdims=True)
            p = (e * (1.0 / total)).astype(jnp.bfloat16)
            mixed.append(dot(p, v))
            logs.append(top + jnp.log(total))
        mixed_ref[first:end, :] = jnp.where(low, mixed[0], mixed[1]).astype(jnp.bfloat16)
        log_ref[0, first:end, :] = jnp.concatenate(logs, axis=1)


def backward_kernel(column_ref, row_ref, q_ref, k_ref, v_ref, g_ref, log_ref, out_ref, ka, va):
    slots = q_ref.shape[0]
    scale = HEAD_DIM**-0.5
    low = lax.broadcasted_iota(jnp.int32, (1, 128), 1) < HEAD_DIM
    ka[...] = jnp.zeros_like(ka)
    va[...] = jnp.zeros_like(va)
    for index in range(slots // BLOCK):
        first, end = index * BLOCK, (index + 1) * BLOCK
        start = max(0, first - 512)
        ok = mask_of(column_ref[first:end, :], row_ref[:, start:end], first, end, start)
        q = q_ref[first:end, :]
        g = g_ref[first:end, :]
        k = k_ref[start:end, :]
        v = v_ref[start:end, :]
        dq, dk, dv = [], [], []
        for head in range(2):
            mine = low if head == 0 else ~low
            s = dot(jnp.where(mine, q, jnp.zeros_like(q)), k, NT) * scale
            p = jnp.exp(jnp.where(ok, s - log_ref[0, first:end, head : head + 1], MASK_FILL))
            dp = dot(jnp.where(mine, g, jnp.zeros_like(g)), v, NT)
            w = p * dp
            ds = (w - p * jnp.sum(w, axis=1, keepdims=True)).astype(jnp.bfloat16)
            dq.append(dot(ds, k))
            dk.append(dot(ds, q, TN))
            dv.append(dot(p.astype(jnp.bfloat16), g, TN))
        out_ref[0, first:end, :] = (jnp.where(low, dq[0], dq[1]) * scale).astype(jnp.bfloat16)
        ka[start:end, :] += jnp.where(low, dk[0], dk[1])
        va[start:end, :] += jnp.where(low, dv[0], dv[1])
    out_ref[1] = (ka[...] * scale).astype(jnp.bfloat16)
    out_ref[2] = va[...].astype(jnp.bfloat16)


def columns(offset, slots):
    return pl.BlockSpec((slots, 128), lambda pair: (0, pair + offset))


def whole(shape):
    return pl.BlockSpec(shape, lambda pair: (0, 0))


def attention(projected, segment, first, count):
    slots = projected.shape[0]
    pairs = HEADS // 2
    return pl.pallas_call(
        forward_kernel,
        grid=(count,),
        in_specs=[whole((slots, 1)), whole((1, slots))] + [columns(pairs * n + first, slots) for n in range(3)],
        out_specs=[columns(0, slots), pl.BlockSpec((1, slots, 2), lambda pair: (pair, 0, 0))],
        out_shape=[
            jax.ShapeDtypeStruct((slots, count * 128), jnp.bfloat16),
            jax.ShapeDtypeStruct((count, slots, 2), jnp.float32),
        ],
        compiler_params=pltpu.CompilerParams(vmem_limit_bytes=48 * 1024 * 1024),
        cost_estimate=cost(2 * slots * slots * count * 256, 8 * slots * count * 128),
        name="attention",
    )(segment[:, None], segment[None, :], projected, projected, projected)


def attention_back(projected, grad_mixed, logs, log_first, segment, first, count):
    slots = projected.shape[0]
    pairs = HEADS // 2
    return pl.pallas_call(
        backward_kernel,
        grid=(count,),
        in_specs=[whole((slots, 1)), whole((1, slots))]
        + [columns(pairs * n + first, slots) for n in range(3)]
        + [columns(first, slots), pl.BlockSpec((1, slots, 2), lambda pair: (pair + log_first, 0, 0))],
        out_specs=pl.BlockSpec((3, slots, 128), lambda pair: (0, 0, pair)),
        out_shape=jax.ShapeDtypeStruct((3, slots, count * 128), jnp.bfloat16),
        scratch_shapes=[pltpu.VMEM((slots, 128), jnp.float32)] * 2,
        compiler_params=pltpu.CompilerParams(vmem_limit_bytes=48 * 1024 * 1024),
        cost_estimate=cost(5 * slots * slots * count * 256, 16 * slots * count * 128),
        name="attention_back",
    )(segment[:, None], segment[None, :], projected, projected, projected, grad_mixed, logs)


def adam(master, mean, square, grad, rate, decay):
    mean_new = BETA_ONE * mean + (1.0 - BETA_ONE) * grad
    square_new = BETA_TWO * square + (1.0 - BETA_TWO) * grad * grad
    mean_hat = mean_new / (1.0 - BETA_ONE**STEP)
    square_hat = square_new / (1.0 - BETA_TWO**STEP)
    master_new = master - rate * (mean_hat / (jnp.sqrt(square_hat) + ADAM_EPS) + decay * master)
    return (mean_new, square_new, master_new)


class Ring:
    def __init__(self):
        self.group = lax.axis_size("shard")
        self.data = lax.axis_size("dp")
        self.plane = self.data // 2
        self.side = math.isqrt(self.plane)
        self.square = self.data == 2 * self.side * self.side
        self.z = lax.axis_index("shard")
        device = lax.axis_index("dp")
        self.core = device % 2
        chip = device // 2
        high, low = chip // self.side, chip % self.side
        straight = low * self.side + high
        crossed = high * self.side + low
        self.block = jnp.where(self.core == 0, straight, crossed)
        self.block_other = jnp.where(self.core == 0, crossed, straight)

    def staged(self):
        return self.side == 2 and self.square and self.group * self.plane == ROW_BLOCKS

    def send_core(self, value):
        return lax.ppermute(value, "dp", [(i, i ^ 1) for i in range(self.data)])

    def send_plane(self, value, step):
        side = self.side
        first, second = step // side, step % side
        pairs = []
        for device in range(self.data):
            core, chip = device % 2, device // 2
            high, low = chip // side, chip % side
            if core == 0:
                low, high = (low + first) % side, (high + second) % side
            else:
                high, low = (high + first) % side, (low + second) % side
            pairs.append((device, (high * side + low) * 2 + core))
        return lax.ppermute(value, "dp", pairs)

    def spread(self, value, direct):
        if direct:
            return [self.send_plane(value, step) for step in range(1, self.plane)]
        second, first = self.send_plane(value, 1), self.send_plane(value, 2)
        return [second, first, self.send_plane(first, 1)]

    def shifted(self, block, step):
        side = self.side
        first, second = step // side, step % side
        return (block // side + first) % side * side + (block % side + second) % side

    def back(self, block, step):
        side = self.side
        first, second = step // side, step % side
        return (block // side - first) % side * side + (block % side - second) % side

    def send_shard(self, value, step):
        group = self.group
        return lax.ppermute(value, "shard", [(i, (i + step) % group) for i in range(group)])


TILE = 384
ROW_BLOCKS = 16
CHUNK = 256


def compiler(megabytes):
    return pltpu.CompilerParams(vmem_limit_bytes=megabytes * 1024 * 1024)


def cost(flops, bytes_accessed):
    return pl.CostEstimate(flops=flops, bytes_accessed=bytes_accessed, transcendentals=0)


def halves_of(first, tiles):
    return [[first + (half * tiles + tile) * TILE for tile in range(tiles)] for half in range(2)]


def hidden_of(parity):
    return [[(4 * half + 2 * tile + parity) * TILE for tile in range(2)] for half in range(2)]


def starts_of(rows, parity):
    return [first + parity * TILE for first in range(0, rows, 2 * TILE)]


def pack_kernel(specs, *refs):
    out_ref = refs[-1]
    row = 0
    for (columns, high, starts, count), ref in zip(specs, refs[:-1], strict=True):
        for number, start in enumerate(starts):
            blocks = slice(number * (count // high), (number + 1) * (count // high))
            for half in range(2):
                for tile, column in enumerate(columns[half]):
                    part = ref[start : start + count, column : column + TILE].astype(jnp.bfloat16)
                    out_ref[half, blocks, row + tile * high : row + (tile + 1) * high, :] = part.reshape(
                        count // high, high, TILE
                    )
        row += len(columns[0]) * high


def pack(parts):
    blocks = len(parts[0][3]) * parts[0][4] // parts[0][2]
    rows = sum(len(part[1][0]) * part[2] for part in parts)
    vmem = pl.BlockSpec(memory_space=pltpu.VMEM)
    return pl.pallas_call(
        functools.partial(pack_kernel, [part[1:] for part in parts]),
        in_specs=[vmem] * len(parts),
        out_specs=vmem,
        out_shape=jax.ShapeDtypeStruct((2, blocks, rows, TILE), jnp.bfloat16),
        compiler_params=compiler(40),
        cost_estimate=cost(0, 12 * blocks * rows * TILE),
        name="pack",
    )(*[part[0] for part in parts])


def after(value, *others):
    return lax.optimization_barrier((value, *others))[0]


class Gather:
    def __init__(self, own, ring):
        self.own, self.ring = own, ring
        chunk = lax.dynamic_index_in_dim(
            lax.dynamic_index_in_dim(own, ring.core, 0, keepdims=False),
            ring.block,
            0,
            keepdims=False,
        )
        self.arrived = [ring.send_shard(chunk, step) for step in range(1, ring.group)]

    def foreign(self, *others):
        self.far = after(jnp.stack(self.arrived), *others)
        return self.far

    def plane(self, direct):
        self.mine = [self.far] + self.ring.spread(self.far, direct)

    def cores(self, *others):
        ring = self.ring
        self.mine = list(lax.optimization_barrier((*self.mine, *others))[: ring.plane])
        self.other = [ring.send_core(value) for value in self.mine]

    def sources(self):
        return [self.own] + self.mine + self.other

    def places(self):
        ring = self.ring
        steps = range(ring.plane)
        places = [(None, ring.z * self.own.shape[1])]
        places += [(ring.core, ring.back(ring.block, step)) for step in steps]
        return places + [(1 - ring.core, ring.back(ring.block_other, step)) for step in steps]


def where_array(places, ring):
    scalars = [ring.z]
    for half, block in places:
        scalars += [0 if half is None else half, block]
    scalars.append(ring.core)
    return jnp.stack([jnp.asarray(v, jnp.int32) for v in scalars])


def copy_count(sources, group):
    return 1 if len(sources) == 1 else 2 + (len(sources) - 1) * (group - 1)


def start_pieces(where_ref, refs, group, out_ref, sems):
    copies = []

    def begin(source, target):
        copy = pltpu.make_async_copy(source, target, sems.at[len(copies)])
        copy.start()
        copies.append(copy)

    if len(refs) == 1:
        begin(refs[0], out_ref)
        return copies
    blocks = refs[0].shape[1]
    first = where_ref[2]
    for half in range(2):
        begin(refs[0].at[half], out_ref.at[half, pl.ds(first, blocks)])
    for number, ref in enumerate(refs[1:], 1):
        half, block = where_ref[1 + 2 * number], where_ref[2 + 2 * number]
        for step in range(1, group):
            source = lax.rem(where_ref[0] - step + group, group)
            begin(ref.at[step - 1], out_ref.at[half, source * blocks + block])
    return copies


class Sum:
    def __init__(self, kept, sent, ring):
        self.ring, self.kept = ring, kept
        self.got = ring.send_core(sent)

    def chip(self, direct, *others):
        ring = self.ring
        kept = after(self.kept, *others)
        chip = (kept.astype(jnp.float32) + self.got.astype(jnp.float32)).astype(jnp.bfloat16)
        rows = chip.shape[1]
        self.direct = direct
        if direct:
            chip = lax.optimization_barrier(chip.reshape(ring.group, ring.plane, rows, TILE))

            def block_of(step):
                return lax.dynamic_index_in_dim(
                    chip, ring.shifted(ring.block, step), 1, keepdims=False
                )

            self.arrived = [ring.send_plane(block_of(step), step) for step in range(1, ring.plane)]
            self.level = block_of(0)
            return self.level
        chip = lax.optimization_barrier(chip.reshape(ring.group, 2, 2 * rows, TILE))
        mine = ring.block // 2
        away = lax.dynamic_index_in_dim(chip, 1 - mine, 1, keepdims=False)
        self.arrived = [ring.send_plane(away, 2)]
        self.level = lax.dynamic_index_in_dim(chip, mine, 1, keepdims=False)
        return self.level

    def halfway(self, *others):
        ring = self.ring
        level = after(self.level, *others).astype(jnp.float32) + self.arrived[0].astype(jnp.float32)
        rows = level.shape[1] // 2
        level = lax.optimization_barrier(
            level.astype(jnp.bfloat16).reshape(ring.group, 2, rows, TILE)
        )
        mine = ring.block % 2
        away = lax.dynamic_index_in_dim(level, 1 - mine, 1, keepdims=False)
        self.arrived = [ring.send_plane(away, 1)]
        self.level = lax.dynamic_index_in_dim(level, mine, 1, keepdims=False)
        return self.level

    def plane(self, *others):
        ring = self.ring
        level = after(self.level, *others).astype(jnp.float32)
        for value in self.arrived:
            level = level + value.astype(jnp.float32)
        level = lax.optimization_barrier(level.astype(jnp.bfloat16))

        def shard_of(step):
            return lax.dynamic_index_in_dim(
                level, (ring.z + step) % ring.group, 0, keepdims=False
            )

        self.arrived = [ring.send_shard(shard_of(step), step) for step in range(1, ring.group)]
        self.level = shard_of(0)
        return self.level

    def finish(self, *others):
        ring = self.ring
        done = after(self.level, *others).astype(jnp.float32)
        for value in self.arrived:
            done = done + value.astype(jnp.float32)
        mine = [lax.optimization_barrier(done.astype(jnp.bfloat16))]
        mine += ring.spread(mine[0], True)
        other = [ring.send_core(value) for value in mine]
        places = [(ring.core, ring.back(ring.block, step)) for step in range(ring.plane)]
        places += [(1 - ring.core, ring.back(ring.block_other, step)) for step in range(ring.plane)]
        return mine + other, places


def plain_gradients(even, odd, inner, core, high):
    def both(halves):
        kept, sent = (value.astype(jnp.float32) for value in halves)
        return jnp.stack([jnp.where(core == 0, kept, sent), jnp.where(core == 0, sent, kept)])

    def columns(packed, first, tiles):
        part = packed[:, :, first : first + tiles * high].reshape(2, ROW_BLOCKS, tiles, high, TILE)
        return part.transpose(1, 3, 0, 2, 4)

    even, odd, inner = both(even), both(odd), both(inner)
    width = ROW_BLOCKS * high
    expand = jnp.stack([columns(even, 0, 2), columns(odd, 0, 2)], axis=4).reshape(width, -1)
    deep = [
        packed[:, :, 2 * high : 4 * high].transpose(1, 2, 0, 3).reshape(4, TILE, width)
        for packed in (even, odd)
    ]
    project = jnp.stack(deep, axis=1).reshape(-1, width)
    attend = jnp.concatenate(
        [columns(inner, 0, 3).reshape(width, -1), columns(odd, 4 * high, 1).reshape(width, -1)], axis=1
    )
    return attend, expand, project


def adam_kernel(kinds, counts, where_ref, *refs):
    number = sum(counts)
    sources, (master_ref, mean_ref, square_ref) = refs[:number], refs[number : number + 3]
    mean_out, square_out, master_out = refs[number + 3 : number + 6]
    packed, sems = refs[number + 6 : -1], refs[-1]
    copies, scalar, position = [], 0, 0
    for target, count in zip(packed, counts, strict=True):
        for ref in sources[position : position + count]:
            if count == 1:
                place = target
            else:
                place = target.at[where_ref[scalar], where_ref[scalar + 1]]
            copy = pltpu.make_async_copy(ref, place, sems.at[len(copies)])
            copy.start()
            copies.append(copy)
            scalar += 2
        position += count
    for copy in copies:
        copy.wait()
    for gradient, row, columns, high, first in kinds:
        target = packed[gradient]
        for half in range(2):
            for tile, column in enumerate(columns[half]):
                here = slice(column, column + TILE)
                for block in range(target.shape[1]):
                    rows = slice(first + block * high, first + (block + 1) * high)
                    grad = target[half, block, row + tile * high : row + (tile + 1) * high, :].astype(jnp.float32)
                    state = adam(
                        master_ref[rows, here], mean_ref[rows, here], square_ref[rows, here], grad, RATE_MATRIX, DECAY_MATRIX
                    )
                    mean_out[rows, here], square_out[rows, here], master_out[rows, here] = state


def adam_packed(master, mean, square, gradients, kinds):
    sources = [source for group, _ in gradients for source in group]
    counts = [len(group) for group, _ in gradients]
    scalars = [v for _, places in gradients for half, block in places for v in (0 if half is None else half, block)]
    where = jnp.stack([jnp.asarray(v, jnp.int32) for v in scalars])
    shapes = []
    for group, places in gradients:
        if len(group) == 1:
            shapes.append(group[0].shape)
        else:
            shapes.append((2, len(group) // 2) + group[0].shape)
    vmem = pl.BlockSpec(memory_space=pltpu.VMEM)
    return pl.pallas_call(
        functools.partial(adam_kernel, kinds, counts),
        in_specs=[pl.BlockSpec(memory_space=pltpu.SMEM)]
        + [pl.BlockSpec(memory_space=pl.ANY)] * len(sources)
        + [vmem] * 3,
        out_specs=[vmem] * 3,
        out_shape=[jax.ShapeDtypeStruct(master.shape, jnp.float32)] * 3,
        scratch_shapes=[pltpu.VMEM(shape, jnp.bfloat16) for shape in shapes]
        + [pltpu.SemaphoreType.DMA((len(sources),))],
        compiler_params=compiler(32),
        cost_estimate=cost(20 * master.size, 26 * master.size),
        name="adam_packed",
    )(where, *sources, master, mean, square)


def tile_of(packed_ref, half, row, high):
    part = packed_ref[half, :, pl.ds(row, high), :]
    return part.reshape(ROW_BLOCKS * high, TILE)


def normal_of(rows):
    centre = jnp.mean(rows, axis=1, keepdims=True)
    centred = rows - centre
    spread = jnp.mean(centred * centred, axis=1, keepdims=True)
    ratio = lax.rsqrt(spread + NORM_EPS)
    return centred * ratio, ratio


def normal_back(normal, ratio, scaled):
    along = jnp.mean(scaled * normal, axis=1, keepdims=True)
    return ratio * (scaled - jnp.mean(scaled, axis=1, keepdims=True) - normal * along)


def project_kernel(group, where_ref, tokens_ref, params_ref, *refs):
    pieces, (out_ref, turned_ref, packed_ref, sems) = refs[:-4], refs[-4:]
    slots, width = tokens_ref.shape
    high = width // ROW_BLOCKS
    copies = start_pieces(where_ref, pieces, group, packed_ref, sems)
    lows = []
    for first in range(0, slots, CHUNK):
        normal, _ = normal_of(tokens_ref[first : first + CHUNK, :].astype(jnp.float32))
        low = (normal * params_ref[0:1, :] + params_ref[1:2, :]).astype(jnp.bfloat16)
        turned_ref[:, first : first + CHUNK] = low.T
        lows.append(low)
    for copy in copies:
        copy.wait()
    for part in range(3):
        weight = jnp.concatenate(
            [tile_of(packed_ref, t // 3, t % 3 * high, high) for t in (2 * part, 2 * part + 1)], axis=1
        )
        for number, low in enumerate(lows):
            value = dot(low, weight)
            if part != 1:
                row = 4 if part == 0 else 5
                value = value + params_ref[row : row + 1, :]
            out_ref[number * CHUNK : (number + 1) * CHUNK, part * width : (part + 1) * width] = (
                value.astype(jnp.bfloat16)
            )


def project_rows(tokens, params, sources, where, group):
    slots, width = tokens.shape
    high = width // ROW_BLOCKS
    vmem = pl.BlockSpec(memory_space=pltpu.VMEM)
    return pl.pallas_call(
        functools.partial(project_kernel, group),
        in_specs=[pl.BlockSpec(memory_space=pltpu.SMEM), vmem, vmem]
        + [pl.BlockSpec(memory_space=pl.ANY)] * len(sources),
        out_specs=[vmem] * 3,
        out_shape=[
            jax.ShapeDtypeStruct((slots, 3 * width), jnp.bfloat16),
            jax.ShapeDtypeStruct((width, slots), jnp.bfloat16),
            jax.ShapeDtypeStruct((2, ROW_BLOCKS, 3 * high, TILE), jnp.bfloat16),
        ],
        scratch_shapes=[pltpu.SemaphoreType.DMA((copy_count(sources, group),))],
        compiler_params=compiler(40),
        cost_estimate=cost(6 * slots * width * width, 16 * slots * width),
        name="project_rows",
    )(where, tokens, params, *sources)


def tail_of(values):
    size = jnp.abs(values) * (0.5**0.5)
    bell = jnp.exp(-0.5 * values * values)
    t = 1.0 / (1.0 + 0.5 * size)
    series = jnp.full_like(t, 0.17087277)
    for c in (
        -0.82215223, 1.48851587, -1.13520398, 0.27886807, -0.18628806, 0.09678418, 0.37409196, 1.00002368, -1.26551223,
    ):
        series = series * t + c
    tail = 0.5 * t * bell * jnp.exp(series)
    return bell, jnp.where(values > 0, 1.0 - tail, tail)


def halves_out(scratch_ref, core, kept_ref, sent_ref, sems):
    copies = [
        pltpu.make_async_copy(scratch_ref.at[core], kept_ref, sems.at[0]),
        pltpu.make_async_copy(scratch_ref.at[1 - core], sent_ref, sems.at[1]),
    ]
    for copy in copies:
        copy.start()
    return copies


def feed(parity, packed_ref, params_ref, low_ref, turned_ref, back_ref, total_ref, two_ref, act_ref, pre_ref, bias_ref, grad_ref):
    slots, width = low_ref.shape
    high = width // ROW_BLOCKS
    deep = slice(2 * high, 4 * high)

    def step(number, carry):
        wide = jnp.concatenate(
            [tile_of(packed_ref, number, tile * high, high) for tile in range(2)], axis=1
        )
        blocks = pl.ds(number * (ROW_BLOCKS // 2), ROW_BLOCKS // 2)
        deep_weight = jnp.concatenate(
            [packed_ref[side, blocks, deep, :].reshape(width, TILE) for side in range(2)], axis=1
        )
        bias = params_ref[pl.ds(8 + 2 * parity + number, 1), :]
        bias_sum = jnp.zeros((1, width), jnp.float32)
        for first in range(0, slots, CHUNK):
            here = slice(first, first + CHUNK)
            pre = dot(low_ref[here, :], wide) + bias
            bell, below = tail_of(pre)
            act = (pre * below).astype(jnp.bfloat16)
            act_ref[here, :] = act
            slope = below + pre * bell * 0.3989422804014327
            grad = (dot(back_ref[here, :], deep_weight, NT) * slope).astype(jnp.bfloat16)
            pre_ref[here, :] = grad
            bias_sum = bias_sum + jnp.sum(grad.astype(jnp.float32), axis=0, keepdims=True)
            total_ref[here, :] += dot(act, deep_weight)
            two_ref[here, :] += dot(grad, wide, NT)
        bias_ref[pl.ds(number, 1), :] = bias_sum
        expand_grad = dot(turned_ref[...], pre_ref[...]).astype(jnp.bfloat16)
        project_grad = dot(act_ref[...], back_ref[...], TN).astype(jnp.bfloat16)
        for side in range(2):
            here = slice(side * TILE, (side + 1) * TILE)
            grad_ref[number, :, side * high : (side + 1) * high, :] = expand_grad[:, here].reshape(
                ROW_BLOCKS, high, TILE
            )
            grad_ref[side, blocks, deep, :] = project_grad[:, here].reshape(
                ROW_BLOCKS // 2, 2 * high, TILE
            )
        return carry

    lax.fori_loop(0, 2, step, 0)


def first_kernel(group, count, where_ref, tokens_ref, cotangent_ref, live_ref, params_ref, *refs):
    mixed_parts, pieces = refs[:count], refs[count:-17]
    (resid_ref, total_ref, two_ref, back_ref, outer_ref, kept_ref, sent_ref, sums_ref) = refs[-17:-9]
    (packed_ref, grad_ref, low_ref, turned_ref, act_ref, pre_ref, bias_ref, sems, out_sems) = refs[-9:]
    slots, width = tokens_ref.shape
    high = width // ROW_BLOCKS
    copies = start_pieces(where_ref, pieces, group, packed_ref, sems)
    sums_ref[...] = jnp.zeros_like(sums_ref)
    for first in range(0, slots, CHUNK):
        here = slice(first, first + CHUNK)
        back_ref[here, :] = (cotangent_ref[here, :].astype(jnp.float32) * live_ref[here, :]).astype(
            jnp.bfloat16
        )
    for copy in copies:
        copy.wait()
    weight = jnp.concatenate([tile_of(packed_ref, half, 4 * high, high) for half in range(2)], axis=1)
    outer_ref[...] = weight
    for first in range(0, slots, CHUNK):
        here = slice(first, first + CHUNK)
        mixed = jnp.concatenate([ref[here, :] for ref in mixed_parts], axis=1)
        resid = tokens_ref[here, :].astype(jnp.float32) + (dot(mixed, weight) + params_ref[6:7, :])
        normal, _ = normal_of(resid)
        low = (normal * params_ref[2:3, :] + params_ref[3:4, :]).astype(jnp.bfloat16)
        low_ref[here, :] = low
        turned_ref[:, here] = low.T
        resid_ref[here, :] = resid
        total_ref[here, :] = resid + params_ref[7:8, :]
        two_ref[here, :] = jnp.zeros((CHUNK, width), jnp.float32)
    feed(0, packed_ref, params_ref, low_ref, turned_ref, back_ref, total_ref, two_ref, act_ref, pre_ref, bias_ref, grad_ref)
    sums_ref[8:10, :] = bias_ref[0:2, :]
    for copy in halves_out(grad_ref, where_ref[where_ref.shape[0] - 1], kept_ref, sent_ref, out_sems):
        copy.wait()


def second_kernel(group, count, where_ref, live_ref, params_ref, resid_in, total_in, two_in, back_ref, outer_ref, *refs):
    mixed_parts, pieces = refs[:count], refs[count:-18]
    (out_ref, resid_ref, mixed_grad_ref, kept_ref, sent_ref, sums_ref) = refs[-18:-12]
    (packed_ref, grad_ref, low_ref, turned_ref, total_ref, two_ref, act_ref, pre_ref, bias_ref, ratio_ref, sems, out_sems) = refs[-12:]
    slots, width = resid_in.shape
    high = width // ROW_BLOCKS
    copies = start_pieces(where_ref, pieces, group, packed_ref, sems)
    sums_ref[...] = jnp.zeros_like(sums_ref)
    for first in range(0, slots, CHUNK):
        here = slice(first, first + CHUNK)
        normal, ratio = normal_of(resid_in[here, :])
        low = (normal * params_ref[2:3, :] + params_ref[3:4, :]).astype(jnp.bfloat16)
        low_ref[here, :] = low
        turned_ref[:, here] = low.T
        resid_ref[here, :] = normal
        ratio_ref[here, :] = ratio
        total_ref[here, :] = total_in[here, :]
        two_ref[here, :] = two_in[here, :]
    for copy in copies:
        copy.wait()
    feed(1, packed_ref, params_ref, low_ref, turned_ref, back_ref, total_ref, two_ref, act_ref, pre_ref, bias_ref, grad_ref)
    sums_ref[10:12, :] = bias_ref[0:2, :]
    weight = outer_ref[...]
    for first in range(0, slots, CHUNK):
        here = slice(first, first + CHUNK)
        normal = resid_ref[here, :]
        two = two_ref[here, :]
        back = back_ref[here, :].astype(jnp.float32)
        grad = back + normal_back(normal, ratio_ref[here, :], two * params_ref[2:3, :])
        low = grad.astype(jnp.bfloat16)
        sums_ref[2:3, :] += jnp.sum(two * normal, axis=0, keepdims=True)
        sums_ref[3:4, :] += jnp.sum(two, axis=0, keepdims=True)
        sums_ref[6:7, :] += jnp.sum(low.astype(jnp.float32), axis=0, keepdims=True)
        sums_ref[7:8, :] += jnp.sum(back, axis=0, keepdims=True)
        resid_ref[here, :] = grad
        act_ref[here, :] = low
        mixed_grad_ref[here, :] = dot(low, weight, NT).astype(jnp.bfloat16)
        out_ref[here, :] = (total_ref[here, :] * live_ref[here, :]).astype(jnp.bfloat16)
    mixed = jnp.concatenate([ref[...] for ref in mixed_parts], axis=1)
    outer_grad = dot(mixed, act_ref[...], TN).astype(jnp.bfloat16)
    for side in range(2):
        grad_ref[side, :, 4 * high : 5 * high, :] = outer_grad[
            :, side * TILE : (side + 1) * TILE
        ].reshape(ROW_BLOCKS, high, TILE)
    for copy in halves_out(grad_ref, where_ref[where_ref.shape[0] - 1], kept_ref, sent_ref, out_sems):
        copy.wait()


def middle(kernel, name, in_vmem, mixed, sources, where, outs, rows, weight_rows, extra, group):
    slots, width = mixed[0].shape[0], in_vmem[1].shape[1]
    vmem, anywhere = pl.BlockSpec(memory_space=pltpu.VMEM), pl.BlockSpec(memory_space=pl.ANY)
    half = jax.ShapeDtypeStruct((ROW_BLOCKS, rows, TILE), jnp.bfloat16)
    low = pltpu.VMEM((slots, width), jnp.bfloat16)
    return pl.pallas_call(
        functools.partial(kernel, group, len(mixed)),
        in_specs=[pl.BlockSpec(memory_space=pltpu.SMEM)]
        + [vmem] * (len(in_vmem) + len(mixed))
        + [anywhere] * len(sources),
        out_specs=[vmem] * len(outs) + [anywhere] * 2 + [vmem],
        out_shape=outs + [half, half, jax.ShapeDtypeStruct((16, width), jnp.float32)],
        scratch_shapes=[
            pltpu.VMEM((2, ROW_BLOCKS, weight_rows, TILE), jnp.bfloat16),
            pltpu.VMEM((2, ROW_BLOCKS, rows, TILE), jnp.bfloat16),
            low,
            pltpu.VMEM((width, slots), jnp.bfloat16),
        ]
        + [pltpu.VMEM((slots, width), jnp.float32)] * extra
        + [low, low, pltpu.VMEM((8, width), jnp.float32)]
        + [pltpu.VMEM((slots, 1), jnp.float32)] * (extra // 2)
        + [
            pltpu.SemaphoreType.DMA((copy_count(sources, group),)),
            pltpu.SemaphoreType.DMA((2,)),
        ],
        compiler_params=compiler(60),
        cost_estimate=cost(27 * slots * width * width, 40 * slots * width),
        name=name,
    )(where, *in_vmem, *mixed, *sources)


def inner_kernel(where_ref, turned_ref, *refs):
    grads, (kept_ref, sent_ref, sums_ref, grad_ref, sems) = refs[:-5], refs[-5:]
    width = turned_ref.shape[0]
    high = width // ROW_BLOCKS
    turned = turned_ref[...]
    sums_ref[...] = jnp.zeros_like(sums_ref)
    for part in range(3):
        values = jnp.concatenate([ref[part] for ref in grads], axis=1)
        grad = dot(turned, values).astype(jnp.bfloat16)
        for side in range(2):
            t = 2 * part + side
            grad_ref[t // 3, :, t % 3 * high : (t % 3 + 1) * high, :] = grad[
                :, side * TILE : (side + 1) * TILE
            ].reshape(ROW_BLOCKS, high, TILE)
        if part != 1:
            row = 4 if part == 0 else 5
            sums_ref[row : row + 1, :] = jnp.sum(values.astype(jnp.float32), axis=0, keepdims=True)
    for copy in halves_out(grad_ref, where_ref[where_ref.shape[0] - 1], kept_ref, sent_ref, sems):
        copy.wait()


def inner_gradient(where, turned, grads):
    width, slots = turned.shape
    rows = 3 * (width // ROW_BLOCKS)
    vmem, anywhere = pl.BlockSpec(memory_space=pltpu.VMEM), pl.BlockSpec(memory_space=pl.ANY)
    half = jax.ShapeDtypeStruct((ROW_BLOCKS, rows, TILE), jnp.bfloat16)
    return pl.pallas_call(
        inner_kernel,
        in_specs=[pl.BlockSpec(memory_space=pltpu.SMEM)] + [vmem] * (1 + len(grads)),
        out_specs=[anywhere, anywhere, vmem],
        out_shape=[half, half, jax.ShapeDtypeStruct((16, width), jnp.float32)],
        scratch_shapes=[
            pltpu.VMEM((2, ROW_BLOCKS, rows, TILE), jnp.bfloat16),
            pltpu.SemaphoreType.DMA((2,)),
        ],
        compiler_params=compiler(40),
        cost_estimate=cost(6 * slots * width * width, 8 * slots * width),
        name="inner_gradient",
    )(where, turned, *grads)


def input_kernel(tokens_ref, params_ref, packed_ref, resid_ref, *refs):
    grads, (out_ref, sums_ref) = refs[:-2], refs[-2:]
    slots, width = tokens_ref.shape
    high = width // ROW_BLOCKS
    sums_ref[...] = jnp.zeros_like(sums_ref)
    weights = [
        jnp.concatenate(
            [tile_of(packed_ref, t // 3, t % 3 * high, high) for t in (2 * part, 2 * part + 1)], axis=1
        )
        for part in range(3)
    ]
    for first in range(0, slots, CHUNK):
        here = slice(first, first + CHUNK)
        grad = jnp.zeros((CHUNK, width), jnp.float32)
        for part in range(3):
            values = jnp.concatenate([ref[part, here, :] for ref in grads], axis=1)
            grad = grad + dot(values, weights[part], NT)
        normal, ratio = normal_of(tokens_ref[here, :].astype(jnp.float32))
        sums_ref[0:1, :] += jnp.sum(grad * normal, axis=0, keepdims=True)
        sums_ref[1:2, :] += jnp.sum(grad, axis=0, keepdims=True)
        out_ref[here, :] = resid_ref[here, :] + normal_back(normal, ratio, grad * params_ref[0:1, :])


def input_gradient(tokens, params, packed, grads, resid):
    slots, width = tokens.shape
    vmem = pl.BlockSpec(memory_space=pltpu.VMEM)
    return pl.pallas_call(
        input_kernel,
        in_specs=[vmem] * (4 + len(grads)),
        out_specs=[vmem] * 2,
        out_shape=[
            jax.ShapeDtypeStruct((slots, width), jnp.float32),
            jax.ShapeDtypeStruct((16, width), jnp.float32),
        ],
        compiler_params=compiler(48),
        cost_estimate=cost(6 * slots * width * width, 16 * slots * width),
        name="input_gradient",
    )(tokens, params, packed, resid, *grads)


def gather_vector(master, ring):
    own = master.astype(jnp.bfloat16)
    group = ring.group
    parts = [own] + [ring.send_shard(own, step) for step in range(1, group)]
    stacked = jnp.stack(parts)
    order = (ring.z - jnp.arange(group)) % group
    return jnp.take(stacked, order, axis=0).reshape(group * own.shape[0], own.shape[1])


def sum_vector(grad, ring):
    group = ring.group
    if not ring.square or ring.side != 2:
        whole = lax.psum_scatter(grad, "shard", scatter_dimension=0, tiled=True)
        return lax.psum(whole, "dp")
    flat = grad.reshape(group, -1, 128)
    flat = flat + ring.send_core(flat)
    for bit in (2, 4):
        flat = flat + lax.ppermute(flat, "dp", [(i, i ^ bit) for i in range(ring.data)])

    def shard_of(step):
        return lax.dynamic_index_in_dim(flat, (ring.z + step) % group, 0, keepdims=False)

    done = shard_of(0)
    for step in range(1, group):
        done = done + ring.send_shard(shard_of(step), step)
    return done.reshape(grad.shape[0] // group, grad.shape[1])


def on_device(
    tokens,
    cotangent,
    seq_lengths,
    seq_owner,
    attend_master,
    expand_master,
    project_master,
    vector_master,
    attend_mean,
    expand_mean,
    project_mean,
    vector_mean,
    attend_square,
    expand_square,
    project_square,
    vector_square,
):
    ring = Ring()
    slots, width = tokens.shape
    high = width // ROW_BLOCKS
    staged = ring.staged()
    masters = (attend_master, expand_master, project_master)
    if not staged:
        masters = tuple(
            lax.all_gather(m.astype(jnp.bfloat16), "shard", axis=0, tiled=True) for m in masters
        )
    tall = masters[0].shape[0]

    def pack_group(parity, tie):
        attend, expand, project = lax.optimization_barrier((*masters, tie))[:3] if staged else masters
        parts = [
            (expand, hidden_of(parity), high, [0], tall),
            (project, halves_of(0, 1), 2 * high, starts_of(project.shape[0], parity), TILE),
        ]
        if parity == 0:
            parts.append((attend, halves_of(3 * width, 1), high, [0], tall))
        return pack(parts)

    own_inner = pack([(masters[0], halves_of(0, 3), high, [0], tall)])
    vector = gather_vector(vector_master, ring).astype(jnp.float32)
    device = lax.axis_index("dp") * ring.group + ring.z
    segment = slot_segments(seq_lengths, seq_owner, device, slots)
    live = (segment >= 0).astype(jnp.float32)[:, None]
    hidden_bias = vector[:, 8:].reshape(2, 2, 2, TILE).transpose(2, 0, 1, 3).reshape(4, width)
    params = jnp.concatenate(
        [vector[:, :8].T, hidden_bias, jnp.zeros((4, width), jnp.float32)]
    )
    rows = tokens
    if staged:
        inner_part = Gather(own_inner, ring)
        far = inner_part.foreign()
        inner_part.plane(True)
        even_part = Gather(pack_group(0, far), ring)
        inner_part.cores()
        far = even_part.foreign(*inner_part.other)
        even_part.plane(False)
        odd_part = Gather(pack_group(1, far), ring)
        rows = after(tokens, far)
        inner_sources = inner_part.sources()
        inner_where = where_array(inner_part.places(), ring)
    else:
        inner_sources, inner_where = [own_inner], where_array([(None, 0)], ring)
    projected, turned, inner = project_rows(rows, params, inner_sources, inner_where, ring.group)
    if staged:
        projected = after(projected, even_part.mine[2])
    half = HEADS // 4
    mixed, logs = [None, None], [None, None]
    mixed[0], logs[0] = attention(projected, segment, 0, half)
    later = projected
    if staged:
        even_part.cores(mixed[0])
        far = odd_part.foreign(mixed[0])
        odd_part.plane(False)
        later = after(projected, *even_part.mine, far)
    mixed[1], logs[1] = attention(later, segment, half, half)
    if staged:
        odd_part.cores(mixed[1])
        even_sources, even_where = even_part.sources(), where_array(even_part.places(), ring)
        odd_sources, odd_where = odd_part.sources(), where_array(odd_part.places(), ring)
        mixed[0] = after(mixed[0], *odd_part.mine)
    else:
        even_sources, even_where = [pack_group(0, None)], inner_where
        odd_sources, odd_where = [pack_group(1, None)], inner_where
    low = jax.ShapeDtypeStruct((slots, width), jnp.bfloat16)
    wide = jax.ShapeDtypeStruct((slots, width), jnp.float32)
    square = jax.ShapeDtypeStruct((width, width), jnp.bfloat16)
    resid, total, two, back, outer, *even_halves, even_sums = middle(
        first_kernel,
        "first_half",
        [tokens, cotangent, live, params],
        mixed,
        even_sources,
        even_where,
        [wide, wide, wide, low, square],
        4 * high,
        5 * high,
        0,
        ring.group,
    )
    if staged:
        even = Sum(*even_halves, ring)
    layer_output, grad_resid, grad_mixed, *odd_halves, odd_sums = middle(
        second_kernel,
        "second_half",
        [live, params, resid, total, two, back, outer],
        mixed,
        odd_sources,
        odd_where,
        [low, wide, low],
        5 * high,
        4 * high,
        2,
        ring.group,
    )
    if staged:
        odd = Sum(*odd_halves, ring)
        level = even.chip(False, grad_mixed)
        grad_mixed = after(grad_mixed, level)
    part = HEADS // 6
    grads = [attention_back(projected, grad_mixed, logs[0], 0, segment, 0, part)]
    back_logs = jnp.concatenate([logs[0][part:], logs[1][: 2 * part - half]])
    if staged:
        level = even.halfway(grads[0])
        grad_mixed = after(grad_mixed, level, odd.chip(False, grads[0]))
    grads.append(attention_back(projected, grad_mixed, back_logs, 0, segment, part, part))
    if staged:
        level = even.plane(grads[1])
        grad_mixed = after(grad_mixed, level, odd.halfway(grads[1]))
    grads.append(attention_back(projected, grad_mixed, logs[1], 2 * part - half, segment, 2 * part, part))
    *inner_halves, inner_sums = inner_gradient(inner_where, turned, grads)
    last = grads
    if staged:
        tail = Sum(*inner_halves, ring)
        level = odd.plane(inner_sums)
        even_sum = even.finish(inner_sums)
        level = tail.chip(True, level, even_sum[0][0])
        last = grads[:2] + [after(grads[2], level)]
    input_grad, input_sums = input_gradient(tokens, params, inner, last, grad_resid)
    sums = even_sums + odd_sums + inner_sums + input_sums
    hidden_sum = sums[8:12].reshape(2, 2, 2, TILE).transpose(1, 2, 0, 3).reshape(width, 4)
    vector_grad = jnp.concatenate([sums[:8].T, hidden_sum], axis=1)
    vector_sum = sum_vector(vector_grad, ring)
    if staged:
        odd_sum = odd.finish(input_sums)
        tail.plane(odd_sum[0][0])
        tail_sum = tail.finish()
        expand_state = adam_packed(
            expand_master,
            expand_mean,
            expand_square,
            [even_sum, odd_sum],
            [(parity, 0, hidden_of(parity), high, 0) for parity in range(2)],
        )
        project_state = adam_packed(
            project_master,
            project_mean,
            project_square,
            [even_sum, odd_sum],
            [(parity, 2 * high, halves_of(0, 1), 2 * high, parity * TILE) for parity in range(2)],
        )
        attend_state = adam_packed(
            attend_master,
            attend_mean,
            attend_square,
            [tail_sum, odd_sum],
            [
                (0, 0, halves_of(0, 3), high, 0),
                (1, 4 * high, halves_of(3 * width, 1), high, 0),
            ],
        )
    else:
        plain = plain_gradients(even_halves, odd_halves, inner_halves, ring.core, high)
        attend_sum, expand_sum, project_sum = (
            lax.psum(lax.psum_scatter(g, "shard", scatter_dimension=0, tiled=True), "dp")
            for g in plain
        )
        attend_state = adam(
            attend_master, attend_mean, attend_square, attend_sum, RATE_MATRIX, DECAY_MATRIX
        )
        expand_state = adam(
            expand_master, expand_mean, expand_square, expand_sum, RATE_MATRIX, DECAY_MATRIX
        )
        project_state = adam(
            project_master, project_mean, project_square, project_sum, RATE_MATRIX, DECAY_MATRIX
        )
    vector_state = adam(vector_master, vector_mean, vector_square, vector_sum, RATE_VECTOR, 0.0)
    return (
        layer_output,
        input_grad,
        attend_state[0],
        expand_state[0],
        project_state[0],
        vector_state[0],
        attend_state[1],
        expand_state[1],
        project_state[1],
        vector_state[1],
        attend_state[2],
        expand_state[2],
        project_state[2],
        vector_state[2],
    )


def solution(mesh):
    return jax.shard_map(
        on_device,
        mesh=mesh,
        in_specs=(
            P(("dp", "shard"), None),
            P(("dp", "shard"), None),
            P(),
            P(),
            P("shard", None),
            P("shard", None),
            P("shard", None),
            P("shard", None),
            P("shard", None),
            P("shard", None),
            P("shard", None),
            P("shard", None),
            P("shard", None),
            P("shard", None),
            P("shard", None),
            P("shard", None),
        ),
        out_specs=(
            P(("dp", "shard"), None),
            P(("dp", "shard"), None),
            P("shard", None),
            P("shard", None),
            P("shard", None),
            P("shard", None),
            P("shard", None),
            P("shard", None),
            P("shard", None),
            P("shard", None),
            P("shard", None),
            P("shard", None),
            P("shard", None),
            P("shard", None),
        ),
        check_vma=False,
    )
```

```python
import functools
import math

import jax
import jax.numpy as jnp
from jax import lax
from jax.experimental import pallas as pl
from jax.experimental.pallas import tpu as pltpu
from jax.sharding import PartitionSpec as P

HEADS = 12
HEAD_DIM = 64
STEP = 10


NORM_EPS = 1e-05
MASK_FILL = -1e30
BETA_ONE = 0.9
BETA_TWO = 0.999
ADAM_EPS = 1e-08
RATE_MATRIX = 0.05
RATE_VECTOR = 0.3
DECAY_MATRIX = 0.01
BLOCK = 256
NT = (((1,), (1,)), ((), ()))
TN = (((0,), (0,)), ((), ()))


def slot_segments(seq_lengths, seq_owner, device, slots):
    mine = seq_owner == device
    owned = jnp.where(mine, seq_lengths, 0)
    starts = jnp.cumsum(owned) - owned
    place = jnp.arange(slots, dtype=jnp.int32)[:, None]
    inside = mine[None, :] & (place >= starts[None, :]) & (place < (starts + owned)[None, :])
    labels = jnp.arange(seq_lengths.shape[0], dtype=jnp.int32)[None, :] + 1
    return jnp.sum(jnp.where(inside, labels, 0), axis=1) - 1


def dot(a, b, dims=(((1,), (0,)), ((), ()))):
    return lax.dot_general(a, b, dims, preferred_element_type=jnp.float32)


def mask_of(column, row, first, end, start):
    later = lax.broadcasted_iota(jnp.int32, (end - first, end - start), 0) + first
    earlier = lax.broadcasted_iota(jnp.int32, (end - first, end - start), 1) + start
    return (column == row) & (earlier <= later)


def forward_kernel(column_ref, row_ref, q_ref, k_ref, v_ref, mixed_ref, log_ref):
    slots = q_ref.shape[0]
    scale = HEAD_DIM**-0.5
    low = lax.broadcasted_iota(jnp.int32, (1, 128), 1) < HEAD_DIM
    for index in range(slots // BLOCK):
        first, end = index * BLOCK, (index + 1) * BLOCK
        start = max(0, first - 512)
        ok = mask_of(column_ref[first:end, :], row_ref[:, start:end], first, end, start)
        q = q_ref[first:end, :]
        k = k_ref[start:end, :]
        v = v_ref[start:end, :]
        mixed, logs = [], []
        for head in range(2):
            mine = low if head == 0 else ~low
            s = dot(jnp.where(mine, q, jnp.zeros_like(q)), k, NT) * scale
            s = jnp.where(ok, s, MASK_FILL)
            top = jnp.max(s, axis=1, keepdims=True)
            e = jnp.exp(s - top)
            total = jnp.sum(e, axis=1, keepdims=True)
            p = (e * (1.0 / total)).astype(jnp.bfloat16)
            mixed.append(dot(p, v))
            logs.append(top + jnp.log(total))
        mixed_ref[first:end, :] = jnp.where(low, mixed[0], mixed[1]).astype(jnp.bfloat16)
        log_ref[0, first:end, :] = jnp.concatenate(logs, axis=1)


def backward_kernel(column_ref, row_ref, q_ref, k_ref, v_ref, g_ref, log_ref, out_ref, ka, va):
    slots = q_ref.shape[0]
    scale = HEAD_DIM**-0.5
    low = lax.broadcasted_iota(jnp.int32, (1, 128), 1) < HEAD_DIM
    ka[...] = jnp.zeros_like(ka)
    va[...] = jnp.zeros_like(va)
    for index in range(slots // BLOCK):
        first, end = index * BLOCK, (index + 1) * BLOCK
        start = max(0, first - 512)
        ok = mask_of(column_ref[first:end, :], row_ref[:, start:end], first, end, start)
        q = q_ref[first:end, :]
        g = g_ref[first:end, :]
        k = k_ref[start:end, :]
        v = v_ref[start:end, :]
        dq, dk, dv = [], [], []
        for head in range(2):
            mine = low if head == 0 else ~low
            s = dot(jnp.where(mine, q, jnp.zeros_like(q)), k, NT) * scale
            p = jnp.exp(jnp.where(ok, s - log_ref[0, first:end, head : head + 1], MASK_FILL))
            dp = dot(jnp.where(mine, g, jnp.zeros_like(g)), v, NT)
            w = p * dp
            ds = (w - p * jnp.sum(w, axis=1, keepdims=True)).astype(jnp.bfloat16)
            dq.append(dot(ds, k))
            dk.append(dot(ds, q, TN))
            dv.append(dot(p.astype(jnp.bfloat16), g, TN))
        out_ref[0, first:end, :] = (jnp.where(low, dq[0], dq[1]) * scale).astype(jnp.bfloat16)
        ka[start:end, :] += jnp.where(low, dk[0], dk[1])
        va[start:end, :] += jnp.where(low, dv[0], dv[1])
    out_ref[1] = (ka[...] * scale).astype(jnp.bfloat16)
    out_ref[2] = va[...].astype(jnp.bfloat16)


def columns(offset, slots):
    return pl.BlockSpec((slots, 128), lambda pair: (0, pair + offset))


def whole(shape):
    return pl.BlockSpec(shape, lambda pair: (0, 0))


def attention(projected, segment, first, count):
    slots = projected.shape[0]
    pairs = HEADS // 2
    return pl.pallas_call(
        forward_kernel,
        grid=(count,),
        in_specs=[whole((slots, 1)), whole((1, slots))] + [columns(pairs * n + first, slots) for n in range(3)],
        out_specs=[columns(0, slots), pl.BlockSpec((1, slots, 2), lambda pair: (pair, 0, 0))],
        out_shape=[
            jax.ShapeDtypeStruct((slots, count * 128), jnp.bfloat16),
            jax.ShapeDtypeStruct((count, slots, 2), jnp.float32),
        ],
        compiler_params=pltpu.CompilerParams(vmem_limit_bytes=48 * 1024 * 1024),
        cost_estimate=cost(2 * slots * slots * count * 256, 8 * slots * count * 128),
        name="attention",
    )(segment[:, None], segment[None, :], projected, projected, projected)


def attention_back(projected, grad_mixed, logs, log_first, segment, first, count):
    slots = projected.shape[0]
    pairs = HEADS // 2
    return pl.pallas_call(
        backward_kernel,
        grid=(count,),
        in_specs=[whole((slots, 1)), whole((1, slots))]
        + [columns(pairs * n + first, slots) for n in range(3)]
        + [columns(first, slots), pl.BlockSpec((1, slots, 2), lambda pair: (pair + log_first, 0, 0))],
        out_specs=pl.BlockSpec((3, slots, 128), lambda pair: (0, 0, pair)),
        out_shape=jax.ShapeDtypeStruct((3, slots, count * 128), jnp.bfloat16),
        scratch_shapes=[pltpu.VMEM((slots, 128), jnp.float32)] * 2,
        compiler_params=pltpu.CompilerParams(vmem_limit_bytes=48 * 1024 * 1024),
        cost_estimate=cost(5 * slots * slots * count * 256, 16 * slots * count * 128),
        name="attention_back",
    )(segment[:, None], segment[None, :], projected, projected, projected, grad_mixed, logs)


def adam(master, mean, square, grad, rate, decay):
    mean_new = BETA_ONE * mean + (1.0 - BETA_ONE) * grad
    square_new = BETA_TWO * square + (1.0 - BETA_TWO) * grad * grad
    mean_hat = mean_new / (1.0 - BETA_ONE**STEP)
    square_hat = square_new / (1.0 - BETA_TWO**STEP)
    master_new = master - rate * (mean_hat / (jnp.sqrt(square_hat) + ADAM_EPS) + decay * master)
    return (mean_new, square_new, master_new)


class Ring:
    def __init__(self):
        self.group = lax.axis_size("shard")
        self.data = lax.axis_size("dp")
        self.plane = self.data // 2
        self.side = math.isqrt(self.plane)
        self.square = self.data == 2 * self.side * self.side
        self.z = lax.axis_index("shard")
        device = lax.axis_index("dp")
        self.core = device % 2
        chip = device // 2
        high, low = chip // self.side, chip % self.side
        straight = low * self.side + high
        crossed = high * self.side + low
        self.block = jnp.where(self.core == 0, straight, crossed)
        self.block_other = jnp.where(self.core == 0, crossed, straight)

    def staged(self):
        return self.side == 2 and self.square and self.group * self.plane == ROW_BLOCKS

    def send_core(self, value):
        return lax.ppermute(value, "dp", [(i, i ^ 1) for i in range(self.data)])

    def send_plane(self, value, step):
        side = self.side
        first, second = step // side, step % side
        pairs = []
        for device in range(self.data):
            core, chip = device % 2, device // 2
            high, low = chip // side, chip % side
            if core == 0:
                low, high = (low + first) % side, (high + second) % side
            else:
                high, low = (high + first) % side, (low + second) % side
            pairs.append((device, (high * side + low) * 2 + core))
        return lax.ppermute(value, "dp", pairs)

    def spread(self, value, direct):
        if direct:
            return [self.send_plane(value, step) for step in range(1, self.plane)]
        second, first = self.send_plane(value, 1), self.send_plane(value, 2)
        return [second, first, self.send_plane(first, 1)]

    def shifted(self, block, step):
        side = self.side
        first, second = step // side, step % side
        return (block // side + first) % side * side + (block % side + second) % side

    def back(self, block, step):
        side = self.side
        first, second = step // side, step % side
        return (block // side - first) % side * side + (block % side - second) % side

    def send_shard(self, value, step):
        group = self.group
        return lax.ppermute(value, "shard", [(i, (i + step) % group) for i in range(group)])


TILE = 384
ROW_BLOCKS = 16
CHUNK = 256


def compiler(megabytes):
    return pltpu.CompilerParams(vmem_limit_bytes=megabytes * 1024 * 1024)


def cost(flops, bytes_accessed):
    return pl.CostEstimate(flops=flops, bytes_accessed=bytes_accessed, transcendentals=0)


def halves_of(first, tiles):
    return [[first + (half * tiles + tile) * TILE for tile in range(tiles)] for half in range(2)]


def hidden_of(parity):
    return [[(4 * half + 2 * tile + parity) * TILE for tile in range(2)] for half in range(2)]


def starts_of(rows, parity):
    return [first + parity * TILE for first in range(0, rows, 2 * TILE)]


def pack_kernel(specs, *refs):
    out_ref = refs[-1]
    row = 0
    for (columns, high, starts, count), ref in zip(specs, refs[:-1], strict=True):
        for number, start in enumerate(starts):
            blocks = slice(number * (count // high), (number + 1) * (count // high))
            for half in range(2):
                for tile, column in enumerate(columns[half]):
                    part = ref[start : start + count, column : column + TILE].astype(jnp.bfloat16)
                    out_ref[half, blocks, row + tile * high : row + (tile + 1) * high, :] = part.reshape(
                        count // high, high, TILE
                    )
        row += len(columns[0]) * high


def pack(parts):
    blocks = len(parts[0][3]) * parts[0][4] // parts[0][2]
    rows = sum(len(part[1][0]) * part[2] for part in parts)
    vmem = pl.BlockSpec(memory_space=pltpu.VMEM)
    return pl.pallas_call(
        functools.partial(pack_kernel, [part[1:] for part in parts]),
        in_specs=[vmem] * len(parts),
        out_specs=vmem,
        out_shape=jax.ShapeDtypeStruct((2, blocks, rows, TILE), jnp.bfloat16),
        compiler_params=compiler(40),
        cost_estimate=cost(0, 12 * blocks * rows * TILE),
        name="pack",
    )(*[part[0] for part in parts])


def after(value, *others):
    return lax.optimization_barrier((value, *others))[0]


class Gather:
    def __init__(self, own, ring):
        self.own, self.ring = own, ring
        chunk = lax.dynamic_index_in_dim(
            lax.dynamic_index_in_dim(own, ring.core, 0, keepdims=False),
            ring.block,
            0,
            keepdims=False,
        )
        self.arrived = [ring.send_shard(chunk, step) for step in range(1, ring.group)]

    def foreign(self, *others):
        self.far = after(jnp.stack(self.arrived), *others)
        return self.far

    def plane(self, direct):
        self.mine = [self.far] + self.ring.spread(self.far, direct)

    def cores(self, *others):
        ring = self.ring
        self.mine = list(lax.optimization_barrier((*self.mine, *others))[: ring.plane])
        self.other = [ring.send_core(value) for value in self.mine]

    def sources(self):
        return [self.own] + self.mine + self.other

    def places(self):
        ring = self.ring
        steps = range(ring.plane)
        places = [(None, ring.z * self.own.shape[1])]
        places += [(ring.core, ring.back(ring.block, step)) for step in steps]
        return places + [(1 - ring.core, ring.back(ring.block_other, step)) for step in steps]


def where_array(places, ring):
    scalars = [ring.z]
    for half, block in places:
        scalars += [0 if half is None else half, block]
    scalars.append(ring.core)
    return jnp.stack([jnp.asarray(v, jnp.int32) for v in scalars])


def copy_count(sources, group):
    return 1 if len(sources) == 1 else 2 + (len(sources) - 1) * (group - 1)


def start_pieces(where_ref, refs, group, out_ref, sems):
    copies = []

    def begin(source, target):
        copy = pltpu.make_async_copy(source, target, sems.at[len(copies)])
        copy.start()
        copies.append(copy)

    if len(refs) == 1:
        begin(refs[0], out_ref)
        return copies
    blocks = refs[0].shape[1]
    first = where_ref[2]
    for half in range(2):
        begin(refs[0].at[half], out_ref.at[half, pl.ds(first, blocks)])
    for number, ref in enumerate(refs[1:], 1):
        half, block = where_ref[1 + 2 * number], where_ref[2 + 2 * number]
        for step in range(1, group):
            source = lax.rem(where_ref[0] - step + group, group)
            begin(ref.at[step - 1], out_ref.at[half, source * blocks + block])
    return copies


class Sum:
    def __init__(self, kept, sent, ring):
        self.ring, self.kept = ring, kept
        self.got = ring.send_core(sent)

    def chip(self, direct, *others):
        ring = self.ring
        kept = after(self.kept, *others)
        chip = (kept.astype(jnp.float32) + self.got.astype(jnp.float32)).astype(jnp.bfloat16)
        rows = chip.shape[1]
        self.direct = direct
        if direct:
            chip = lax.optimization_barrier(chip.reshape(ring.group, ring.plane, rows, TILE))

            def block_of(step):
                return lax.dynamic_index_in_dim(
                    chip, ring.shifted(ring.block, step), 1, keepdims=False
                )

            self.arrived = [ring.send_plane(block_of(step), step) for step in range(1, ring.plane)]
            self.level = block_of(0)
            return self.level
        chip = lax.optimization_barrier(chip.reshape(ring.group, 2, 2 * rows, TILE))
        mine = ring.block // 2
        away = lax.dynamic_index_in_dim(chip, 1 - mine, 1, keepdims=False)
        self.arrived = [ring.send_plane(away, 2)]
        self.level = lax.dynamic_index_in_dim(chip, mine, 1, keepdims=False)
        return self.level

    def halfway(self, *others):
        ring = self.ring
        level = after(self.level, *others).astype(jnp.float32) + self.arrived[0].astype(jnp.float32)
        rows = level.shape[1] // 2
        level = lax.optimization_barrier(
            level.astype(jnp.bfloat16).reshape(ring.group, 2, rows, TILE)
        )
        mine = ring.block % 2
        away = lax.dynamic_index_in_dim(level, 1 - mine, 1, keepdims=False)
        self.arrived = [ring.send_plane(away, 1)]
        self.level = lax.dynamic_index_in_dim(level, mine, 1, keepdims=False)
        return self.level

    def plane(self, *others):
        ring = self.ring
        level = after(self.level, *others).astype(jnp.float32)
        for value in self.arrived:
            level = level + value.astype(jnp.float32)
        level = lax.optimization_barrier(level.astype(jnp.bfloat16))

        def shard_of(step):
            return lax.dynamic_index_in_dim(
                level, (ring.z + step) % ring.group, 0, keepdims=False
            )

        self.arrived = [ring.send_shard(shard_of(step), step) for step in range(1, ring.group)]
        self.level = shard_of(0)
        return self.level

    def finish(self, *others):
        ring = self.ring
        done = after(self.level, *others).astype(jnp.float32)
        for value in self.arrived:
            done = done + value.astype(jnp.float32)
        self.mine = [lax.optimization_barrier(done.astype(jnp.bfloat16))]
        self.mine += ring.spread(self.mine[0], True)
        return self.mine[0]

    def cores(self, *others):
        ring = self.ring
        mine = list(lax.optimization_barrier((*self.mine, *others))[: ring.plane])
        other = [ring.send_core(value) for value in mine]
        places = [(ring.core, ring.back(ring.block, step)) for step in range(ring.plane)]
        places += [(1 - ring.core, ring.back(ring.block_other, step)) for step in range(ring.plane)]
        return mine + other, places


def plain_gradients(even, odd, inner, core, high):
    def both(halves):
        kept, sent = (value.astype(jnp.float32) for value in halves)
        return jnp.stack([jnp.where(core == 0, kept, sent), jnp.where(core == 0, sent, kept)])

    def columns(packed, first, tiles):
        part = packed[:, :, first : first + tiles * high].reshape(2, ROW_BLOCKS, tiles, high, TILE)
        return part.transpose(1, 3, 0, 2, 4)

    even, odd, inner = both(even), both(odd), both(inner)
    width = ROW_BLOCKS * high
    expand = jnp.stack([columns(even, 0, 2), columns(odd, 0, 2)], axis=4).reshape(width, -1)
    deep = [
        packed[:, :, 2 * high : 4 * high].transpose(1, 2, 0, 3).reshape(4, TILE, width)
        for packed in (even, odd)
    ]
    project = jnp.stack(deep, axis=1).reshape(-1, width)
    attend = jnp.concatenate(
        [columns(inner, 0, 3).reshape(width, -1), columns(odd, 4 * high, 1).reshape(width, -1)], axis=1
    )
    return attend, expand, project


def adam_kernel(kinds, counts, where_ref, *refs):
    number = sum(counts)
    sources, (master_ref, mean_ref, square_ref) = refs[:number], refs[number : number + 3]
    mean_out, square_out, master_out = refs[number + 3 : number + 6]
    packed, sems = refs[number + 6 : -1], refs[-1]
    copies, scalar, position = [], 0, 0
    for target, count in zip(packed, counts, strict=True):
        for ref in sources[position : position + count]:
            if count == 1:
                place = target
            else:
                place = target.at[where_ref[scalar], where_ref[scalar + 1]]
            copy = pltpu.make_async_copy(ref, place, sems.at[len(copies)])
            copy.start()
            copies.append(copy)
            scalar += 2
        position += count
    for copy in copies:
        copy.wait()
    for gradient, row, columns, high, first in kinds:
        target = packed[gradient]
        for half in range(2):
            for tile, column in enumerate(columns[half]):
                here = slice(column, column + TILE)
                for block in range(target.shape[1]):
                    rows = slice(first + block * high, first + (block + 1) * high)
                    grad = target[half, block, row + tile * high : row + (tile + 1) * high, :].astype(jnp.float32)
                    master = master_ref[rows, here]
                    mean = BETA_ONE * mean_ref[rows, here] + (1.0 - BETA_ONE) * grad
                    square = BETA_TWO * square_ref[rows, here] + (1.0 - BETA_TWO) * grad * grad
                    root = jnp.sqrt(square * (1.0 / (1.0 - BETA_TWO**STEP))) + ADAM_EPS
                    move = mean * (RATE_MATRIX / (1.0 - BETA_ONE**STEP)) / root
                    mean_out[rows, here] = mean
                    square_out[rows, here] = square
                    master_out[rows, here] = master * (1.0 - RATE_MATRIX * DECAY_MATRIX) - move


def adam_packed(master, mean, square, gradients, kinds):
    sources = [source for group, _ in gradients for source in group]
    counts = [len(group) for group, _ in gradients]
    scalars = [v for _, places in gradients for half, block in places for v in (0 if half is None else half, block)]
    where = jnp.stack([jnp.asarray(v, jnp.int32) for v in scalars])
    shapes = []
    for group, places in gradients:
        if len(group) == 1:
            shapes.append(group[0].shape)
        else:
            shapes.append((2, len(group) // 2) + group[0].shape)
    vmem = pl.BlockSpec(memory_space=pltpu.VMEM)
    return pl.pallas_call(
        functools.partial(adam_kernel, kinds, counts),
        in_specs=[pl.BlockSpec(memory_space=pltpu.SMEM)]
        + [pl.BlockSpec(memory_space=pl.ANY)] * len(sources)
        + [vmem] * 3,
        out_specs=[vmem] * 3,
        out_shape=[jax.ShapeDtypeStruct(master.shape, jnp.float32)] * 3,
        scratch_shapes=[pltpu.VMEM(shape, jnp.bfloat16) for shape in shapes]
        + [pltpu.SemaphoreType.DMA((len(sources),))],
        compiler_params=compiler(32),
        cost_estimate=cost(20 * master.size, 26 * master.size),
        name="adam_packed",
    )(where, *sources, master, mean, square)


def tile_of(packed_ref, half, row, high):
    part = packed_ref[half, :, pl.ds(row, high), :]
    return part.reshape(ROW_BLOCKS * high, TILE)


def normal_of(rows):
    centre = jnp.mean(rows, axis=1, keepdims=True)
    centred = rows - centre
    spread = jnp.mean(centred * centred, axis=1, keepdims=True)
    ratio = lax.rsqrt(spread + NORM_EPS)
    return centred * ratio, ratio


def normal_back(normal, ratio, scaled):
    along = jnp.mean(scaled * normal, axis=1, keepdims=True)
    return ratio * (scaled - jnp.mean(scaled, axis=1, keepdims=True) - normal * along)


def project_kernel(group, where_ref, tokens_ref, params_ref, *refs):
    pieces, (out_ref, turned_ref, packed_ref, sems) = refs[:-4], refs[-4:]
    slots, width = tokens_ref.shape
    high = width // ROW_BLOCKS
    copies = start_pieces(where_ref, pieces, group, packed_ref, sems)
    lows = []
    for first in range(0, slots, CHUNK):
        normal, _ = normal_of(tokens_ref[first : first + CHUNK, :].astype(jnp.float32))
        low = (normal * params_ref[0:1, :] + params_ref[1:2, :]).astype(jnp.bfloat16)
        turned_ref[:, first : first + CHUNK] = low.T
        lows.append(low)
    for copy in copies:
        copy.wait()
    for part in range(3):
        weight = jnp.concatenate(
            [tile_of(packed_ref, t // 3, t % 3 * high, high) for t in (2 * part, 2 * part + 1)], axis=1
        )
        for number, low in enumerate(lows):
            value = dot(low, weight)
            if part != 1:
                row = 4 if part == 0 else 5
                value = value + params_ref[row : row + 1, :]
            out_ref[number * CHUNK : (number + 1) * CHUNK, part * width : (part + 1) * width] = (
                value.astype(jnp.bfloat16)
            )


def project_rows(tokens, params, sources, where, group):
    slots, width = tokens.shape
    high = width // ROW_BLOCKS
    vmem = pl.BlockSpec(memory_space=pltpu.VMEM)
    return pl.pallas_call(
        functools.partial(project_kernel, group),
        in_specs=[pl.BlockSpec(memory_space=pltpu.SMEM), vmem, vmem]
        + [pl.BlockSpec(memory_space=pl.ANY)] * len(sources),
        out_specs=[vmem] * 3,
        out_shape=[
            jax.ShapeDtypeStruct((slots, 3 * width), jnp.bfloat16),
            jax.ShapeDtypeStruct((width, slots), jnp.bfloat16),
            jax.ShapeDtypeStruct((2, ROW_BLOCKS, 3 * high, TILE), jnp.bfloat16),
        ],
        scratch_shapes=[pltpu.SemaphoreType.DMA((copy_count(sources, group),))],
        compiler_params=compiler(40),
        cost_estimate=cost(6 * slots * width * width, 16 * slots * width),
        name="project_rows",
    )(where, tokens, params, *sources)


def tail_of(values):
    size = jnp.abs(values) * (0.5**0.5)
    bell = jnp.exp(-0.5 * values * values)
    t = 1.0 / (1.0 + 0.5 * size)
    series = jnp.full_like(t, 0.17087277)
    for c in (
        -0.82215223, 1.48851587, -1.13520398, 0.27886807, -0.18628806, 0.09678418, 0.37409196, 1.00002368, -1.26551223,
    ):
        series = series * t + c
    tail = 0.5 * t * bell * jnp.exp(series)
    return bell, jnp.where(values > 0, 1.0 - tail, tail)


def halves_out(scratch_ref, core, kept_ref, sent_ref, sems):
    copies = [
        pltpu.make_async_copy(scratch_ref.at[core], kept_ref, sems.at[0]),
        pltpu.make_async_copy(scratch_ref.at[1 - core], sent_ref, sems.at[1]),
    ]
    for copy in copies:
        copy.start()
    return copies


def feed(parity, packed_ref, params_ref, low_ref, turned_ref, back_ref, total_ref, two_ref, act_ref, pre_ref, bias_ref, grad_ref):
    slots, width = low_ref.shape
    high = width // ROW_BLOCKS
    deep = slice(2 * high, 4 * high)

    def step(number, carry):
        wide = jnp.concatenate(
            [tile_of(packed_ref, number, tile * high, high) for tile in range(2)], axis=1
        )
        blocks = pl.ds(number * (ROW_BLOCKS // 2), ROW_BLOCKS // 2)
        deep_weight = jnp.concatenate(
            [packed_ref[side, blocks, deep, :].reshape(width, TILE) for side in range(2)], axis=1
        )
        bias = params_ref[pl.ds(8 + 2 * parity + number, 1), :]
        bias_sum = jnp.zeros((1, width), jnp.float32)
        for first in range(0, slots, CHUNK):
            here = slice(first, first + CHUNK)
            pre = dot(low_ref[here, :], wide) + bias
            bell, below = tail_of(pre)
            act = (pre * below).astype(jnp.bfloat16)
            act_ref[here, :] = act
            slope = below + pre * bell * 0.3989422804014327
            grad = (dot(back_ref[here, :], deep_weight, NT) * slope).astype(jnp.bfloat16)
            pre_ref[here, :] = grad
            bias_sum = bias_sum + jnp.sum(grad.astype(jnp.float32), axis=0, keepdims=True)
            total_ref[here, :] += dot(act, deep_weight)
            two_ref[here, :] += dot(grad, wide, NT)
        bias_ref[pl.ds(number, 1), :] = bias_sum
        expand_grad = dot(turned_ref[...], pre_ref[...]).astype(jnp.bfloat16)
        project_grad = dot(act_ref[...], back_ref[...], TN).astype(jnp.bfloat16)
        for side in range(2):
            here = slice(side * TILE, (side + 1) * TILE)
            grad_ref[number, :, side * high : (side + 1) * high, :] = expand_grad[:, here].reshape(
                ROW_BLOCKS, high, TILE
            )
            grad_ref[side, blocks, deep, :] = project_grad[:, here].reshape(
                ROW_BLOCKS // 2, 2 * high, TILE
            )
        return carry

    lax.fori_loop(0, 2, step, 0)


def first_kernel(group, count, where_ref, tokens_ref, cotangent_ref, live_ref, params_ref, *refs):
    mixed_parts, pieces = refs[:count], refs[count:-17]
    (resid_ref, total_ref, two_ref, back_ref, outer_ref, kept_ref, sent_ref, sums_ref) = refs[-17:-9]
    (packed_ref, grad_ref, low_ref, turned_ref, act_ref, pre_ref, bias_ref, sems, out_sems) = refs[-9:]
    slots, width = tokens_ref.shape
    high = width // ROW_BLOCKS
    copies = start_pieces(where_ref, pieces, group, packed_ref, sems)
    sums_ref[...] = jnp.zeros_like(sums_ref)
    for first in range(0, slots, CHUNK):
        here = slice(first, first + CHUNK)
        back_ref[here, :] = (cotangent_ref[here, :].astype(jnp.float32) * live_ref[here, :]).astype(
            jnp.bfloat16
        )
    for copy in copies:
        copy.wait()
    weight = jnp.concatenate([tile_of(packed_ref, half, 4 * high, high) for half in range(2)], axis=1)
    outer_ref[...] = weight
    for first in range(0, slots, CHUNK):
        here = slice(first, first + CHUNK)
        mixed = jnp.concatenate([ref[here, :] for ref in mixed_parts], axis=1)
        resid = tokens_ref[here, :].astype(jnp.float32) + (dot(mixed, weight) + params_ref[6:7, :])
        normal, _ = normal_of(resid)
        low = (normal * params_ref[2:3, :] + params_ref[3:4, :]).astype(jnp.bfloat16)
        low_ref[here, :] = low
        turned_ref[:, here] = low.T
        resid_ref[here, :] = resid
        total_ref[here, :] = resid + params_ref[7:8, :]
        two_ref[here, :] = jnp.zeros((CHUNK, width), jnp.float32)
    feed(0, packed_ref, params_ref, low_ref, turned_ref, back_ref, total_ref, two_ref, act_ref, pre_ref, bias_ref, grad_ref)
    sums_ref[8:10, :] = bias_ref[0:2, :]
    for copy in halves_out(grad_ref, where_ref[where_ref.shape[0] - 1], kept_ref, sent_ref, out_sems):
        copy.wait()


def second_kernel(group, count, where_ref, live_ref, params_ref, resid_in, total_in, two_in, back_ref, outer_ref, *refs):
    mixed_parts, pieces = refs[:count], refs[count:-18]
    (out_ref, resid_ref, mixed_grad_ref, kept_ref, sent_ref, sums_ref) = refs[-18:-12]
    (packed_ref, grad_ref, low_ref, turned_ref, total_ref, two_ref, act_ref, pre_ref, bias_ref, ratio_ref, sems, out_sems) = refs[-12:]
    slots, width = resid_in.shape
    high = width // ROW_BLOCKS
    copies = start_pieces(where_ref, pieces, group, packed_ref, sems)
    sums_ref[...] = jnp.zeros_like(sums_ref)
    for first in range(0, slots, CHUNK):
        here = slice(first, first + CHUNK)
        normal, ratio = normal_of(resid_in[here, :])
        low = (normal * params_ref[2:3, :] + params_ref[3:4, :]).astype(jnp.bfloat16)
        low_ref[here, :] = low
        turned_ref[:, here] = low.T
        resid_ref[here, :] = normal
        ratio_ref[here, :] = ratio
        total_ref[here, :] = total_in[here, :]
        two_ref[here, :] = two_in[here, :]
    for copy in copies:
        copy.wait()
    feed(1, packed_ref, params_ref, low_ref, turned_ref, back_ref, total_ref, two_ref, act_ref, pre_ref, bias_ref, grad_ref)
    sums_ref[10:12, :] = bias_ref[0:2, :]
    weight = outer_ref[...]
    for first in range(0, slots, CHUNK):
        here = slice(first, first + CHUNK)
        normal = resid_ref[here, :]
        two = two_ref[here, :]
        back = back_ref[here, :].astype(jnp.float32)
        grad = back + normal_back(normal, ratio_ref[here, :], two * params_ref[2:3, :])
        low = grad.astype(jnp.bfloat16)
        sums_ref[2:3, :] += jnp.sum(two * normal, axis=0, keepdims=True)
        sums_ref[3:4, :] += jnp.sum(two, axis=0, keepdims=True)
        sums_ref[6:7, :] += jnp.sum(low.astype(jnp.float32), axis=0, keepdims=True)
        sums_ref[7:8, :] += jnp.sum(back, axis=0, keepdims=True)
        resid_ref[here, :] = grad
        act_ref[here, :] = low
        mixed_grad_ref[here, :] = dot(low, weight, NT).astype(jnp.bfloat16)
        out_ref[here, :] = (total_ref[here, :] * live_ref[here, :]).astype(jnp.bfloat16)
    mixed = jnp.concatenate([ref[...] for ref in mixed_parts], axis=1)
    outer_grad = dot(mixed, act_ref[...], TN).astype(jnp.bfloat16)
    for side in range(2):
        grad_ref[side, :, 4 * high : 5 * high, :] = outer_grad[
            :, side * TILE : (side + 1) * TILE
        ].reshape(ROW_BLOCKS, high, TILE)
    for copy in halves_out(grad_ref, where_ref[where_ref.shape[0] - 1], kept_ref, sent_ref, out_sems):
        copy.wait()


def middle(kernel, name, in_vmem, mixed, sources, where, outs, rows, weight_rows, extra, group):
    slots, width = mixed[0].shape[0], in_vmem[1].shape[1]
    vmem, anywhere = pl.BlockSpec(memory_space=pltpu.VMEM), pl.BlockSpec(memory_space=pl.ANY)
    half = jax.ShapeDtypeStruct((ROW_BLOCKS, rows, TILE), jnp.bfloat16)
    low = pltpu.VMEM((slots, width), jnp.bfloat16)
    return pl.pallas_call(
        functools.partial(kernel, group, len(mixed)),
        in_specs=[pl.BlockSpec(memory_space=pltpu.SMEM)]
        + [vmem] * (len(in_vmem) + len(mixed))
        + [anywhere] * len(sources),
        out_specs=[vmem] * len(outs) + [anywhere] * 2 + [vmem],
        out_shape=outs + [half, half, jax.ShapeDtypeStruct((16, width), jnp.float32)],
        scratch_shapes=[
            pltpu.VMEM((2, ROW_BLOCKS, weight_rows, TILE), jnp.bfloat16),
            pltpu.VMEM((2, ROW_BLOCKS, rows, TILE), jnp.bfloat16),
            low,
            pltpu.VMEM((width, slots), jnp.bfloat16),
        ]
        + [pltpu.VMEM((slots, width), jnp.float32)] * extra
        + [low, low, pltpu.VMEM((8, width), jnp.float32)]
        + [pltpu.VMEM((slots, 1), jnp.float32)] * (extra // 2)
        + [
            pltpu.SemaphoreType.DMA((copy_count(sources, group),)),
            pltpu.SemaphoreType.DMA((2,)),
        ],
        compiler_params=compiler(60),
        cost_estimate=cost(27 * slots * width * width, 40 * slots * width),
        name=name,
    )(where, *in_vmem, *mixed, *sources)


def inner_kernel(where_ref, turned_ref, *refs):
    grads, (kept_ref, sent_ref, sums_ref, grad_ref, sems) = refs[:-5], refs[-5:]
    width = turned_ref.shape[0]
    high = width // ROW_BLOCKS
    turned = turned_ref[...]
    sums_ref[...] = jnp.zeros_like(sums_ref)
    for part in range(3):
        values = jnp.concatenate([ref[part] for ref in grads], axis=1)
        grad = dot(turned, values).astype(jnp.bfloat16)
        for side in range(2):
            t = 2 * part + side
            grad_ref[t // 3, :, t % 3 * high : (t % 3 + 1) * high, :] = grad[
                :, side * TILE : (side + 1) * TILE
            ].reshape(ROW_BLOCKS, high, TILE)
        if part != 1:
            row = 4 if part == 0 else 5
            sums_ref[row : row + 1, :] = jnp.sum(values.astype(jnp.float32), axis=0, keepdims=True)
    for copy in halves_out(grad_ref, where_ref[where_ref.shape[0] - 1], kept_ref, sent_ref, sems):
        copy.wait()


def inner_gradient(where, turned, grads):
    width, slots = turned.shape
    rows = 3 * (width // ROW_BLOCKS)
    vmem, anywhere = pl.BlockSpec(memory_space=pltpu.VMEM), pl.BlockSpec(memory_space=pl.ANY)
    half = jax.ShapeDtypeStruct((ROW_BLOCKS, rows, TILE), jnp.bfloat16)
    return pl.pallas_call(
        inner_kernel,
        in_specs=[pl.BlockSpec(memory_space=pltpu.SMEM)] + [vmem] * (1 + len(grads)),
        out_specs=[anywhere, anywhere, vmem],
        out_shape=[half, half, jax.ShapeDtypeStruct((16, width), jnp.float32)],
        scratch_shapes=[
            pltpu.VMEM((2, ROW_BLOCKS, rows, TILE), jnp.bfloat16),
            pltpu.SemaphoreType.DMA((2,)),
        ],
        compiler_params=compiler(40),
        cost_estimate=cost(6 * slots * width * width, 8 * slots * width),
        name="inner_gradient",
    )(where, turned, *grads)


def input_kernel(tokens_ref, params_ref, packed_ref, resid_ref, *refs):
    grads, (out_ref, sums_ref) = refs[:-2], refs[-2:]
    slots, width = tokens_ref.shape
    high = width // ROW_BLOCKS
    sums_ref[...] = jnp.zeros_like(sums_ref)
    weights = [
        jnp.concatenate(
            [tile_of(packed_ref, t // 3, t % 3 * high, high) for t in (2 * part, 2 * part + 1)], axis=1
        )
        for part in range(3)
    ]
    for first in range(0, slots, CHUNK):
        here = slice(first, first + CHUNK)
        grad = jnp.zeros((CHUNK, width), jnp.float32)
        for part in range(3):
            values = jnp.concatenate([ref[part, here, :] for ref in grads], axis=1)
            grad = grad + dot(values, weights[part], NT)
        normal, ratio = normal_of(tokens_ref[here, :].astype(jnp.float32))
        sums_ref[0:1, :] += jnp.sum(grad * normal, axis=0, keepdims=True)
        sums_ref[1:2, :] += jnp.sum(grad, axis=0, keepdims=True)
        out_ref[here, :] = resid_ref[here, :] + normal_back(normal, ratio, grad * params_ref[0:1, :])


def input_gradient(tokens, params, packed, grads, resid):
    slots, width = tokens.shape
    vmem = pl.BlockSpec(memory_space=pltpu.VMEM)
    return pl.pallas_call(
        input_kernel,
        in_specs=[vmem] * (4 + len(grads)),
        out_specs=[vmem] * 2,
        out_shape=[
            jax.ShapeDtypeStruct((slots, width), jnp.float32),
            jax.ShapeDtypeStruct((16, width), jnp.float32),
        ],
        compiler_params=compiler(48),
        cost_estimate=cost(6 * slots * width * width, 16 * slots * width),
        name="input_gradient",
    )(tokens, params, packed, resid, *grads)


def gather_vector(master, ring):
    own = master.astype(jnp.bfloat16)
    group = ring.group
    parts = [own] + [ring.send_shard(own, step) for step in range(1, group)]
    stacked = jnp.stack(parts)
    order = (ring.z - jnp.arange(group)) % group
    return jnp.take(stacked, order, axis=0).reshape(group * own.shape[0], own.shape[1])


class VectorSum:
    def __init__(self, grad, ring):
        self.grad, self.ring = grad, ring
        if ring.staged():
            self.flat = grad.reshape(ring.group, -1, 128)
            self.arrived = [
                lax.ppermute(self.flat, "dp", [(i, i ^ bits) for i in range(ring.data)])
                for bits in range(1, ring.data)
            ]

    def plane(self, *others):
        ring = self.ring
        if not ring.staged():
            return
        terms = [after(self.flat, *others)] + self.arrived
        while len(terms) > 1:
            terms = [terms[i] + terms[i + 1] for i in range(0, len(terms), 2)]

        def shard_of(step):
            return lax.dynamic_index_in_dim(
                terms[0], (ring.z + step) % ring.group, 0, keepdims=False
            )

        self.arrived = [ring.send_shard(shard_of(step), step) for step in range(1, ring.group)]
        self.flat = shard_of(0)

    def finish(self):
        if not self.ring.staged():
            whole = lax.psum_scatter(self.grad, "shard", scatter_dimension=0, tiled=True)
            return lax.psum(whole, "dp")
        done = self.flat
        for value in self.arrived:
            done = done + value
        return done.reshape(self.grad.shape[0] // self.ring.group, self.grad.shape[1])


def on_device(
    tokens,
    cotangent,
    seq_lengths,
    seq_owner,
    attend_master,
    expand_master,
    project_master,
    vector_master,
    attend_mean,
    expand_mean,
    project_mean,
    vector_mean,
    attend_square,
    expand_square,
    project_square,
    vector_square,
):
    ring = Ring()
    slots, width = tokens.shape
    high = width // ROW_BLOCKS
    staged = ring.staged()
    masters = (attend_master, expand_master, project_master)
    if not staged:
        masters = tuple(
            lax.all_gather(m.astype(jnp.bfloat16), "shard", axis=0, tiled=True) for m in masters
        )
    tall = masters[0].shape[0]

    def pack_group(parity, tie):
        attend, expand, project = lax.optimization_barrier((*masters, tie))[:3] if staged else masters
        parts = [
            (expand, hidden_of(parity), high, [0], tall),
            (project, halves_of(0, 1), 2 * high, starts_of(project.shape[0], parity), TILE),
        ]
        if parity == 0:
            parts.append((attend, halves_of(3 * width, 1), high, [0], tall))
        return pack(parts)

    own_inner = pack([(masters[0], halves_of(0, 3), high, [0], tall)])
    vector = gather_vector(vector_master, ring).astype(jnp.float32)
    device = lax.axis_index("dp") * ring.group + ring.z
    segment = slot_segments(seq_lengths, seq_owner, device, slots)
    live = (segment >= 0).astype(jnp.float32)[:, None]
    hidden_bias = vector[:, 8:].reshape(2, 2, 2, TILE).transpose(2, 0, 1, 3).reshape(4, width)
    params = jnp.concatenate(
        [vector[:, :8].T, hidden_bias, jnp.zeros((4, width), jnp.float32)]
    )
    rows = tokens
    if staged:
        inner_part = Gather(own_inner, ring)
        far = inner_part.foreign()
        inner_part.plane(True)
        even_part = Gather(pack_group(0, far), ring)
        inner_part.cores()
        far = even_part.foreign(*inner_part.other)
        even_part.plane(False)
        odd_part = Gather(pack_group(1, far), ring)
        rows = after(tokens, far)
        inner_sources = inner_part.sources()
        inner_where = where_array(inner_part.places(), ring)
    else:
        inner_sources, inner_where = [own_inner], where_array([(None, 0)], ring)
    projected, turned, inner = project_rows(rows, params, inner_sources, inner_where, ring.group)
    if staged:
        projected = after(projected, even_part.mine[2])
    half = HEADS // 4
    mixed, logs = [None, None], [None, None]
    mixed[0], logs[0] = attention(projected, segment, 0, half)
    later = projected
    if staged:
        even_part.cores(mixed[0])
        far = odd_part.foreign(mixed[0])
        odd_part.plane(False)
        later = after(projected, *even_part.mine, far)
    mixed[1], logs[1] = attention(later, segment, half, half)
    if staged:
        odd_part.cores(mixed[1])
        even_sources, even_where = even_part.sources(), where_array(even_part.places(), ring)
        odd_sources, odd_where = odd_part.sources(), where_array(odd_part.places(), ring)
        mixed[0] = after(mixed[0], *odd_part.mine)
    else:
        even_sources, even_where = [pack_group(0, None)], inner_where
        odd_sources, odd_where = [pack_group(1, None)], inner_where
    low = jax.ShapeDtypeStruct((slots, width), jnp.bfloat16)
    wide = jax.ShapeDtypeStruct((slots, width), jnp.float32)
    square = jax.ShapeDtypeStruct((width, width), jnp.bfloat16)
    resid, total, two, back, outer, *even_halves, even_sums = middle(
        first_kernel,
        "first_half",
        [tokens, cotangent, live, params],
        mixed,
        even_sources,
        even_where,
        [wide, wide, wide, low, square],
        4 * high,
        5 * high,
        0,
        ring.group,
    )
    if staged:
        even = Sum(*even_halves, ring)
    layer_output, grad_resid, grad_mixed, *odd_halves, odd_sums = middle(
        second_kernel,
        "second_half",
        [live, params, resid, total, two, back, outer],
        mixed,
        odd_sources,
        odd_where,
        [low, wide, low],
        5 * high,
        4 * high,
        2,
        ring.group,
    )
    if staged:
        odd = Sum(*odd_halves, ring)
        level = even.chip(False, grad_mixed)
        grad_mixed = after(grad_mixed, level)
    part = HEADS // 6
    grads = [attention_back(projected, grad_mixed, logs[0], 0, segment, 0, part)]
    back_logs = jnp.concatenate([logs[0][part:], logs[1][: 2 * part - half]])
    if staged:
        level = even.halfway(grads[0])
        grad_mixed = after(grad_mixed, level, odd.chip(False, grads[0]))
    grads.append(attention_back(projected, grad_mixed, back_logs, 0, segment, part, part))
    if staged:
        level = even.plane(grads[1])
        grad_mixed = after(grad_mixed, level, odd.halfway(grads[1]))
    grads.append(attention_back(projected, grad_mixed, logs[1], 2 * part - half, segment, 2 * part, part))
    *inner_halves, inner_sums = inner_gradient(inner_where, turned, grads)
    last = grads
    if staged:
        tail = Sum(*inner_halves, ring)
        level = odd.plane(even.finish(inner_sums))
        level = tail.chip(True, level)
        last = grads[:2] + [after(grads[2], level)]
    input_grad, input_sums = input_gradient(tokens, params, inner, last, grad_resid)
    sums = even_sums + odd_sums + inner_sums + input_sums
    hidden_sum = sums[8:12].reshape(2, 2, 2, TILE).transpose(1, 2, 0, 3).reshape(width, 4)
    vector_grad = jnp.concatenate([sums[:8].T, hidden_sum], axis=1)
    vector_part = VectorSum(vector_grad, ring)
    if staged:
        even_sum = even.cores(input_sums)
        level = odd.finish(*even_sum[0][: ring.plane])
        level = tail.plane(level)
        vector_part.plane(level)
        odd_sum = odd.cores(level)
        expand_state = adam_packed(
            expand_master,
            expand_mean,
            expand_square,
            [even_sum, odd_sum],
            [(parity, 0, hidden_of(parity), high, 0) for parity in range(2)],
        )
        level = tail.finish(expand_state[0])
        project_state = adam_packed(
            after(project_master, level),
            project_mean,
            project_square,
            [even_sum, odd_sum],
            [(parity, 2 * high, halves_of(0, 1), 2 * high, parity * TILE) for parity in range(2)],
        )
        tail_sum = tail.cores(project_state[0])
        attend_state = adam_packed(
            attend_master,
            attend_mean,
            attend_square,
            [tail_sum, odd_sum],
            [
                (0, 0, halves_of(0, 3), high, 0),
                (1, 4 * high, halves_of(3 * width, 1), high, 0),
            ],
        )
    else:
        plain = plain_gradients(even_halves, odd_halves, inner_halves, ring.core, high)
        attend_sum, expand_sum, project_sum = (
            lax.psum(lax.psum_scatter(g, "shard", scatter_dimension=0, tiled=True), "dp")
            for g in plain
        )
        attend_state = adam(
            attend_master, attend_mean, attend_square, attend_sum, RATE_MATRIX, DECAY_MATRIX
        )
        expand_state = adam(
            expand_master, expand_mean, expand_square, expand_sum, RATE_MATRIX, DECAY_MATRIX
        )
        project_state = adam(
            project_master, project_mean, project_square, project_sum, RATE_MATRIX, DECAY_MATRIX
        )
    vector_sum = vector_part.finish()
    vector_state = adam(vector_master, vector_mean, vector_square, vector_sum, RATE_VECTOR, 0.0)
    return (
        layer_output,
        input_grad,
        attend_state[0],
        expand_state[0],
        project_state[0],
        vector_state[0],
        attend_state[1],
        expand_state[1],
        project_state[1],
        vector_state[1],
        attend_state[2],
        expand_state[2],
        project_state[2],
        vector_state[2],
    )


def solution(mesh):
    return jax.shard_map(
        on_device,
        mesh=mesh,
        in_specs=(
            P(("dp", "shard"), None),
            P(("dp", "shard"), None),
            P(),
            P(),
            P("shard", None),
            P("shard", None),
            P("shard", None),
            P("shard", None),
            P("shard", None),
            P("shard", None),
            P("shard", None),
            P("shard", None),
            P("shard", None),
            P("shard", None),
            P("shard", None),
            P("shard", None),
        ),
        out_specs=(
            P(("dp", "shard"), None),
            P(("dp", "shard"), None),
            P("shard", None),
            P("shard", None),
            P("shard", None),
            P("shard", None),
            P("shard", None),
            P("shard", None),
            P("shard", None),
            P("shard", None),
            P("shard", None),
            P("shard", None),
            P("shard", None),
            P("shard", None),
        ),
        check_vma=False,
    )
```

```python
import functools
import math

import jax
import jax.numpy as jnp
from jax import lax
from jax.experimental import pallas as pl
from jax.experimental.pallas import tpu as pltpu
from jax.sharding import PartitionSpec as P

HEADS = 12
HEAD_DIM = 64
STEP = 10


NORM_EPS = 1e-05
MASK_FILL = -1e30
BETA_ONE = 0.9
BETA_TWO = 0.999
ADAM_EPS = 1e-08
RATE_MATRIX = 0.05
RATE_VECTOR = 0.3
DECAY_MATRIX = 0.01
BLOCK = 256
NT = (((1,), (1,)), ((), ()))
TN = (((0,), (0,)), ((), ()))


def slot_segments(seq_lengths, seq_owner, device, slots):
    mine = seq_owner == device
    owned = jnp.where(mine, seq_lengths, 0)
    starts = jnp.cumsum(owned) - owned
    place = jnp.arange(slots, dtype=jnp.int32)[:, None]
    inside = mine[None, :] & (place >= starts[None, :]) & (place < (starts + owned)[None, :])
    labels = jnp.arange(seq_lengths.shape[0], dtype=jnp.int32)[None, :] + 1
    return jnp.sum(jnp.where(inside, labels, 0), axis=1) - 1


def dot(a, b, dims=(((1,), (0,)), ((), ()))):
    return lax.dot_general(a, b, dims, preferred_element_type=jnp.float32)


def mask_of(column, row, first, end, start):
    later = lax.broadcasted_iota(jnp.int32, (end - first, end - start), 0) + first
    earlier = lax.broadcasted_iota(jnp.int32, (end - first, end - start), 1) + start
    return (column == row) & (earlier <= later)


def forward_kernel(column_ref, row_ref, q_ref, k_ref, v_ref, mixed_ref, log_ref):
    slots = q_ref.shape[0]
    scale = HEAD_DIM**-0.5
    low = lax.broadcasted_iota(jnp.int32, (1, 128), 1) < HEAD_DIM
    for index in range(slots // BLOCK):
        first, end = index * BLOCK, (index + 1) * BLOCK
        start = max(0, first - 512)
        ok = mask_of(column_ref[first:end, :], row_ref[:, start:end], first, end, start)
        q = q_ref[first:end, :]
        k = k_ref[start:end, :]
        v = v_ref[start:end, :]
        mixed, logs = [], []
        for head in range(2):
            mine = low if head == 0 else ~low
            s = dot(jnp.where(mine, q, jnp.zeros_like(q)), k, NT) * scale
            s = jnp.where(ok, s, MASK_FILL)
            top = jnp.max(s, axis=1, keepdims=True)
            e = jnp.exp(s - top)
            total = jnp.sum(e, axis=1, keepdims=True)
            p = (e * (1.0 / total)).astype(jnp.bfloat16)
            mixed.append(dot(p, v))
            logs.append(top + jnp.log(total))
        mixed_ref[first:end, :] = jnp.where(low, mixed[0], mixed[1]).astype(jnp.bfloat16)
        log_ref[0, first:end, :] = jnp.concatenate(logs, axis=1)


def backward_kernel(column_ref, row_ref, q_ref, k_ref, v_ref, g_ref, log_ref, out_ref, ka, va):
    slots = q_ref.shape[0]
    scale = HEAD_DIM**-0.5
    low = lax.broadcasted_iota(jnp.int32, (1, 128), 1) < HEAD_DIM
    ka[...] = jnp.zeros_like(ka)
    va[...] = jnp.zeros_like(va)
    for index in range(slots // BLOCK):
        first, end = index * BLOCK, (index + 1) * BLOCK
        start = max(0, first - 512)
        ok = mask_of(column_ref[first:end, :], row_ref[:, start:end], first, end, start)
        q = q_ref[first:end, :]
        g = g_ref[first:end, :]
        k = k_ref[start:end, :]
        v = v_ref[start:end, :]
        dq, dk, dv = [], [], []
        for head in range(2):
            mine = low if head == 0 else ~low
            s = dot(jnp.where(mine, q, jnp.zeros_like(q)), k, NT) * scale
            p = jnp.exp(jnp.where(ok, s - log_ref[0, first:end, head : head + 1], MASK_FILL))
            dp = dot(jnp.where(mine, g, jnp.zeros_like(g)), v, NT)
            w = p * dp
            ds = (w - p * jnp.sum(w, axis=1, keepdims=True)).astype(jnp.bfloat16)
            dq.append(dot(ds, k))
            dk.append(dot(ds, q, TN))
            dv.append(dot(p.astype(jnp.bfloat16), g, TN))
        out_ref[0, first:end, :] = (jnp.where(low, dq[0], dq[1]) * scale).astype(jnp.bfloat16)
        ka[start:end, :] += jnp.where(low, dk[0], dk[1])
        va[start:end, :] += jnp.where(low, dv[0], dv[1])
    out_ref[1] = (ka[...] * scale).astype(jnp.bfloat16)
    out_ref[2] = va[...].astype(jnp.bfloat16)


def columns(offset, slots):
    return pl.BlockSpec((slots, 128), lambda pair: (0, pair + offset))


def whole(shape):
    return pl.BlockSpec(shape, lambda pair: (0, 0))


def attention(projected, segment, first, count):
    slots = projected.shape[0]
    pairs = HEADS // 2
    return pl.pallas_call(
        forward_kernel,
        grid=(count,),
        in_specs=[whole((slots, 1)), whole((1, slots))] + [columns(pairs * n + first, slots) for n in range(3)],
        out_specs=[columns(0, slots), pl.BlockSpec((1, slots, 2), lambda pair: (pair, 0, 0))],
        out_shape=[
            jax.ShapeDtypeStruct((slots, count * 128), jnp.bfloat16),
            jax.ShapeDtypeStruct((count, slots, 2), jnp.float32),
        ],
        compiler_params=pltpu.CompilerParams(vmem_limit_bytes=48 * 1024 * 1024),
        cost_estimate=cost(1, 1),
        name="attention",
    )(segment[:, None], segment[None, :], projected, projected, projected)


def attention_back(projected, grad_mixed, logs, log_first, segment, first, count):
    slots = projected.shape[0]
    pairs = HEADS // 2
    return pl.pallas_call(
        backward_kernel,
        grid=(count,),
        in_specs=[whole((slots, 1)), whole((1, slots))]
        + [columns(pairs * n + first, slots) for n in range(3)]
        + [columns(first, slots), pl.BlockSpec((1, slots, 2), lambda pair: (pair + log_first, 0, 0))],
        out_specs=pl.BlockSpec((3, slots, 128), lambda pair: (0, 0, pair)),
        out_shape=jax.ShapeDtypeStruct((3, slots, count * 128), jnp.bfloat16),
        scratch_shapes=[pltpu.VMEM((slots, 128), jnp.float32)] * 2,
        compiler_params=pltpu.CompilerParams(vmem_limit_bytes=48 * 1024 * 1024),
        cost_estimate=cost(1, 1),
        name="attention_back",
    )(segment[:, None], segment[None, :], projected, projected, projected, grad_mixed, logs)


def adam(master, mean, square, grad, rate, decay):
    mean_new = BETA_ONE * mean + (1.0 - BETA_ONE) * grad
    square_new = BETA_TWO * square + (1.0 - BETA_TWO) * grad * grad
    mean_hat = mean_new / (1.0 - BETA_ONE**STEP)
    square_hat = square_new / (1.0 - BETA_TWO**STEP)
    master_new = master - rate * (mean_hat / (jnp.sqrt(square_hat) + ADAM_EPS) + decay * master)
    return (mean_new, square_new, master_new)


class Ring:
    def __init__(self):
        self.group = lax.axis_size("shard")
        self.data = lax.axis_size("dp")
        self.plane = self.data // 2
        self.side = math.isqrt(self.plane)
        self.square = self.data == 2 * self.side * self.side
        self.z = lax.axis_index("shard")
        device = lax.axis_index("dp")
        self.core = device % 2
        chip = device // 2
        high, low = chip // self.side, chip % self.side
        straight = low * self.side + high
        crossed = high * self.side + low
        self.block = jnp.where(self.core == 0, straight, crossed)
        self.block_other = jnp.where(self.core == 0, crossed, straight)

    def staged(self):
        return self.side == 2 and self.square and self.group * self.plane == ROW_BLOCKS

    def send_core(self, value):
        return lax.ppermute(value, "dp", [(i, i ^ 1) for i in range(self.data)])

    def send_plane(self, value, step):
        side = self.side
        first, second = step // side, step % side
        pairs = []
        for device in range(self.data):
            core, chip = device % 2, device // 2
            high, low = chip // side, chip % side
            if core == 0:
                low, high = (low + first) % side, (high + second) % side
            else:
                high, low = (high + first) % side, (low + second) % side
            pairs.append((device, (high * side + low) * 2 + core))
        return lax.ppermute(value, "dp", pairs)

    def spread(self, value, direct):
        if direct:
            return [self.send_plane(value, step) for step in range(1, self.plane)]
        second, first = self.send_plane(value, 1), self.send_plane(value, 2)
        return [second, first, self.send_plane(first, 1)]

    def shifted(self, block, step):
        side = self.side
        first, second = step // side, step % side
        return (block // side + first) % side * side + (block % side + second) % side

    def back(self, block, step):
        side = self.side
        first, second = step // side, step % side
        return (block // side - first) % side * side + (block % side - second) % side

    def send_shard(self, value, step):
        group = self.group
        return lax.ppermute(value, "shard", [(i, (i + step) % group) for i in range(group)])


TILE = 384
ROW_BLOCKS = 16
CHUNK = 256


def compiler(megabytes):
    return pltpu.CompilerParams(vmem_limit_bytes=megabytes * 1024 * 1024)


def cost(flops, bytes_accessed):
    return pl.CostEstimate(flops=flops, bytes_accessed=bytes_accessed, transcendentals=0)


def halves_of(first, tiles):
    return [[first + (half * tiles + tile) * TILE for tile in range(tiles)] for half in range(2)]


def hidden_of(parity):
    return [[(4 * half + 2 * tile + parity) * TILE for tile in range(2)] for half in range(2)]


def starts_of(rows, parity):
    return [first + parity * TILE for first in range(0, rows, 2 * TILE)]


def pack_kernel(specs, *refs):
    out_ref = refs[-1]
    row = 0
    for (columns, high, starts, count), ref in zip(specs, refs[:-1], strict=True):
        for number, start in enumerate(starts):
            blocks = slice(number * (count // high), (number + 1) * (count // high))
            for half in range(2):
                for tile, column in enumerate(columns[half]):
                    part = ref[start : start + count, column : column + TILE].astype(jnp.bfloat16)
                    out_ref[half, blocks, row + tile * high : row + (tile + 1) * high, :] = part.reshape(
                        count // high, high, TILE
                    )
        row += len(columns[0]) * high


def pack(parts):
    blocks = len(parts[0][3]) * parts[0][4] // parts[0][2]
    rows = sum(len(part[1][0]) * part[2] for part in parts)
    vmem = pl.BlockSpec(memory_space=pltpu.VMEM)
    return pl.pallas_call(
        functools.partial(pack_kernel, [part[1:] for part in parts]),
        in_specs=[vmem] * len(parts),
        out_specs=vmem,
        out_shape=jax.ShapeDtypeStruct((2, blocks, rows, TILE), jnp.bfloat16),
        compiler_params=compiler(40),
        cost_estimate=cost(1, 1),
        name="pack",
    )(*[part[0] for part in parts])


def after(value, *others):
    return lax.optimization_barrier((value, *others))[0]


class Gather:
    def __init__(self, own, ring):
        self.own, self.ring = own, ring
        chunk = lax.dynamic_index_in_dim(
            lax.dynamic_index_in_dim(own, ring.core, 0, keepdims=False),
            ring.block,
            0,
            keepdims=False,
        )
        self.arrived = [ring.send_shard(chunk, step) for step in range(1, ring.group)]

    def foreign(self, *others):
        self.far = after(jnp.stack(self.arrived), *others)
        return self.far

    def plane(self, direct):
        self.mine = [self.far] + self.ring.spread(self.far, direct)

    def cores(self, *others):
        ring = self.ring
        self.mine = list(lax.optimization_barrier((*self.mine, *others))[: ring.plane])
        self.other = [ring.send_core(value) for value in self.mine]

    def sources(self):
        return [self.own] + self.mine + self.other

    def places(self):
        ring = self.ring
        steps = range(ring.plane)
        places = [(None, ring.z * self.own.shape[1])]
        places += [(ring.core, ring.back(ring.block, step)) for step in steps]
        return places + [(1 - ring.core, ring.back(ring.block_other, step)) for step in steps]


def where_array(places, ring):
    scalars = [ring.z]
    for half, block in places:
        scalars += [0 if half is None else half, block]
    scalars.append(ring.core)
    return jnp.stack([jnp.asarray(v, jnp.int32) for v in scalars])


def copy_count(sources, group):
    return 1 if len(sources) == 1 else 2 + (len(sources) - 1) * (group - 1)


def start_pieces(where_ref, refs, group, out_ref, sems):
    copies = []

    def begin(source, target):
        copy = pltpu.make_async_copy(source, target, sems.at[len(copies)])
        copy.start()
        copies.append(copy)

    if len(refs) == 1:
        begin(refs[0], out_ref)
        return copies
    blocks = refs[0].shape[1]
    first = where_ref[2]
    for half in range(2):
        begin(refs[0].at[half], out_ref.at[half, pl.ds(first, blocks)])
    for number, ref in enumerate(refs[1:], 1):
        half, block = where_ref[1 + 2 * number], where_ref[2 + 2 * number]
        for step in range(1, group):
            source = lax.rem(where_ref[0] - step + group, group)
            begin(ref.at[step - 1], out_ref.at[half, source * blocks + block])
    return copies


class Sum:
    def __init__(self, kept, sent, ring):
        self.ring, self.kept = ring, kept
        self.got = ring.send_core(sent)

    def chip(self, direct, *others):
        ring = self.ring
        kept = after(self.kept, *others)
        chip = (kept.astype(jnp.float32) + self.got.astype(jnp.float32)).astype(jnp.bfloat16)
        rows = chip.shape[1]
        self.direct = direct
        if direct:
            chip = lax.optimization_barrier(chip.reshape(ring.group, ring.plane, rows, TILE))

            def block_of(step):
                return lax.dynamic_index_in_dim(
                    chip, ring.shifted(ring.block, step), 1, keepdims=False
                )

            self.arrived = [ring.send_plane(block_of(step), step) for step in range(1, ring.plane)]
            self.level = block_of(0)
            return self.level
        chip = lax.optimization_barrier(chip.reshape(ring.group, 2, 2 * rows, TILE))
        mine = ring.block // 2
        away = lax.dynamic_index_in_dim(chip, 1 - mine, 1, keepdims=False)
        self.arrived = [ring.send_plane(away, 2)]
        self.level = lax.dynamic_index_in_dim(chip, mine, 1, keepdims=False)
        return self.level

    def halfway(self, *others):
        ring = self.ring
        level = after(self.level, *others).astype(jnp.float32) + self.arrived[0].astype(jnp.float32)
        rows = level.shape[1] // 2
        level = lax.optimization_barrier(
            level.astype(jnp.bfloat16).reshape(ring.group, 2, rows, TILE)
        )
        mine = ring.block % 2
        away = lax.dynamic_index_in_dim(level, 1 - mine, 1, keepdims=False)
        self.arrived = [ring.send_plane(away, 1)]
        self.level = lax.dynamic_index_in_dim(level, mine, 1, keepdims=False)
        return self.level

    def plane(self, *others):
        ring = self.ring
        level = after(self.level, *others).astype(jnp.float32)
        for value in self.arrived:
            level = level + value.astype(jnp.float32)
        level = lax.optimization_barrier(level.astype(jnp.bfloat16))

        def shard_of(step):
            return lax.dynamic_index_in_dim(
                level, (ring.z + step) % ring.group, 0, keepdims=False
            )

        self.arrived = [ring.send_shard(shard_of(step), step) for step in range(1, ring.group)]
        self.level = shard_of(0)
        return self.level

    def finish(self, *others):
        done = after(self.level, *others).astype(jnp.float32)
        for value in self.arrived:
            done = done + value.astype(jnp.float32)
        return done.astype(jnp.bfloat16)


class Spread:
    def __init__(self, piece, ring, direct):
        self.ring = ring
        piece = lax.optimization_barrier(piece)
        self.mine = [piece] + ring.spread(piece, direct)

    def cores(self, *others):
        ring = self.ring
        mine = after(jnp.stack(self.mine), *others)
        places = [(ring.core, ring.back(ring.block, step)) for step in range(ring.plane)]
        places += [(1 - ring.core, ring.back(ring.block_other, step)) for step in range(ring.plane)]
        return [mine, ring.send_core(mine)], places


def plain_gradients(even, odd, inner, core, high):
    def both(halves):
        kept, sent = (value.astype(jnp.float32) for value in halves)
        return jnp.stack([jnp.where(core == 0, kept, sent), jnp.where(core == 0, sent, kept)])

    def columns(packed, first, tiles):
        part = packed[:, :, first : first + tiles * high].reshape(2, ROW_BLOCKS, tiles, high, TILE)
        return part.transpose(1, 3, 0, 2, 4)

    even, odd, inner = both(even), both(odd), both(inner)
    width = ROW_BLOCKS * high
    expand = jnp.stack([columns(even, 0, 2), columns(odd, 0, 2)], axis=4).reshape(width, -1)
    deep = [
        packed[:, :, 2 * high : 4 * high].transpose(1, 2, 0, 3).reshape(4, TILE, width)
        for packed in (even, odd)
    ]
    project = jnp.stack(deep, axis=1).reshape(-1, width)
    attend = jnp.concatenate(
        [columns(inner, 0, 3).reshape(width, -1), columns(odd, 4 * high, 1).reshape(width, -1)], axis=1
    )
    return attend, expand, project


def adam_kernel(kinds, count, where_ref, *refs):
    sources, (master_ref, mean_ref, square_ref) = refs[: 2 * count], refs[2 * count : 2 * count + 3]
    mean_out, square_out, master_out = refs[2 * count + 3 : 2 * count + 6]
    packed, sems = refs[2 * count + 6 : -1], refs[-1]
    step = pl.program_id(0)
    plane = sources[0].shape[0]

    @pl.when(step == 0)
    def _():
        copies = []
        for number, ref in enumerate(sources):
            for block in range(plane):
                scalar = 2 * len(copies)
                place = packed[number // 2].at[where_ref[scalar], where_ref[scalar + 1]]
                copy = pltpu.make_async_copy(ref.at[block], place, sems.at[len(copies)])
                copy.start()
                copies.append(copy)
        for copy in copies:
            copy.wait()

    for gradient, row, columns, high, part in kinds:
        for half in range(2):
            for tile, column in enumerate(columns[half]):
                here = slice(column, column + TILE)
                rows = slice(row + tile * high, row + (tile + 1) * high)
                grad = packed[gradient][half, step, rows, :].astype(jnp.float32)
                master = master_ref[part, :, here]
                mean = BETA_ONE * mean_ref[part, :, here] + (1.0 - BETA_ONE) * grad
                square = BETA_TWO * square_ref[part, :, here] + (1.0 - BETA_TWO) * grad * grad
                root = jnp.sqrt(square * (1.0 / (1.0 - BETA_TWO**STEP))) + ADAM_EPS
                move = mean * (RATE_MATRIX / (1.0 - BETA_ONE**STEP)) / root
                mean_out[part, :, here] = mean
                square_out[part, :, here] = square
                master_out[part, :, here] = master * (1.0 - RATE_MATRIX * DECAY_MATRIX) - move


def adam_packed(master, mean, square, gradients, kinds, parts):
    sources = [source for group, _ in gradients for source in group]
    plane = sources[0].shape[0]
    scalars = [v for _, places in gradients for place in places for v in place]
    where = jnp.stack([jnp.asarray(v, jnp.int32) for v in scalars])
    rows, columns = master.shape
    shape = (parts, rows // parts, columns)
    spec = pl.BlockSpec((parts, rows // parts // plane, columns), lambda step: (0, step, 0))
    out = pl.pallas_call(
        functools.partial(adam_kernel, kinds, len(gradients)),
        grid=(plane,),
        in_specs=[pl.BlockSpec(memory_space=pltpu.SMEM)]
        + [pl.BlockSpec(memory_space=pl.ANY)] * len(sources)
        + [spec] * 3,
        out_specs=[spec] * 3,
        out_shape=[jax.ShapeDtypeStruct(shape, jnp.float32)] * 3,
        scratch_shapes=[
            pltpu.VMEM((2, plane) + group[0].shape[1:], jnp.bfloat16) for group, _ in gradients
        ]
        + [pltpu.SemaphoreType.DMA((len(sources) * plane,))],
        compiler_params=compiler(60),
        cost_estimate=cost(1, 1),
        name="adam_packed",
    )(where, *sources, *(value.reshape(shape) for value in (master, mean, square)))
    return tuple(value.reshape(rows, columns) for value in out)


def tile_of(packed_ref, half, row, high):
    part = packed_ref[half, :, pl.ds(row, high), :]
    return part.reshape(ROW_BLOCKS * high, TILE)


def normal_of(rows):
    centre = jnp.mean(rows, axis=1, keepdims=True)
    centred = rows - centre
    spread = jnp.mean(centred * centred, axis=1, keepdims=True)
    ratio = lax.rsqrt(spread + NORM_EPS)
    return centred * ratio, ratio


def normal_back(normal, ratio, scaled):
    along = jnp.mean(scaled * normal, axis=1, keepdims=True)
    return ratio * (scaled - jnp.mean(scaled, axis=1, keepdims=True) - normal * along)


def project_kernel(group, where_ref, tokens_ref, params_ref, *refs):
    pieces, (out_ref, turned_ref, packed_ref, sems) = refs[:-4], refs[-4:]
    slots, width = tokens_ref.shape
    high = width // ROW_BLOCKS
    copies = start_pieces(where_ref, pieces, group, packed_ref, sems)
    lows = []
    for first in range(0, slots, CHUNK):
        normal, _ = normal_of(tokens_ref[first : first + CHUNK, :].astype(jnp.float32))
        low = (normal * params_ref[0:1, :] + params_ref[1:2, :]).astype(jnp.bfloat16)
        turned_ref[:, first : first + CHUNK] = low.T
        lows.append(low)
    for copy in copies:
        copy.wait()
    for part in range(3):
        weight = jnp.concatenate(
            [tile_of(packed_ref, t // 3, t % 3 * high, high) for t in (2 * part, 2 * part + 1)], axis=1
        )
        for number, low in enumerate(lows):
            value = dot(low, weight)
            if part != 1:
                row = 4 if part == 0 else 5
                value = value + params_ref[row : row + 1, :]
            out_ref[number * CHUNK : (number + 1) * CHUNK, part * width : (part + 1) * width] = (
                value.astype(jnp.bfloat16)
            )


def project_rows(tokens, params, sources, where, group):
    slots, width = tokens.shape
    high = width // ROW_BLOCKS
    vmem = pl.BlockSpec(memory_space=pltpu.VMEM)
    return pl.pallas_call(
        functools.partial(project_kernel, group),
        in_specs=[pl.BlockSpec(memory_space=pltpu.SMEM), vmem, vmem]
        + [pl.BlockSpec(memory_space=pl.ANY)] * len(sources),
        out_specs=[vmem] * 3,
        out_shape=[
            jax.ShapeDtypeStruct((slots, 3 * width), jnp.bfloat16),
            jax.ShapeDtypeStruct((width, slots), jnp.bfloat16),
            jax.ShapeDtypeStruct((2, ROW_BLOCKS, 3 * high, TILE), jnp.bfloat16),
        ],
        scratch_shapes=[pltpu.SemaphoreType.DMA((copy_count(sources, group),))],
        compiler_params=compiler(40),
        cost_estimate=cost(1, 1),
        name="project_rows",
    )(where, tokens, params, *sources)


def tail_of(values):
    size = jnp.abs(values) * (0.5**0.5)
    bell = jnp.exp(-0.5 * values * values)
    t = 1.0 / (1.0 + 0.5 * size)
    series = jnp.full_like(t, 0.17087277)
    for c in (
        -0.82215223, 1.48851587, -1.13520398, 0.27886807, -0.18628806, 0.09678418, 0.37409196, 1.00002368, -1.26551223,
    ):
        series = series * t + c
    tail = 0.5 * t * bell * jnp.exp(series)
    return bell, jnp.where(values > 0, 1.0 - tail, tail)


def halves_out(scratch_ref, core, kept_ref, sent_ref, sems):
    copies = [
        pltpu.make_async_copy(scratch_ref.at[core], kept_ref, sems.at[0]),
        pltpu.make_async_copy(scratch_ref.at[1 - core], sent_ref, sems.at[1]),
    ]
    for copy in copies:
        copy.start()
    return copies


def feed(parity, packed_ref, params_ref, low_ref, turned_ref, back_ref, total_ref, two_ref, act_ref, pre_ref, bias_ref, grad_ref):
    slots, width = low_ref.shape
    high = width // ROW_BLOCKS
    deep = slice(2 * high, 4 * high)

    def step(number, carry):
        wide = jnp.concatenate(
            [tile_of(packed_ref, number, tile * high, high) for tile in range(2)], axis=1
        )
        blocks = pl.ds(number * (ROW_BLOCKS // 2), ROW_BLOCKS // 2)
        deep_weight = jnp.concatenate(
            [packed_ref[side, blocks, deep, :].reshape(width, TILE) for side in range(2)], axis=1
        )
        bias = params_ref[pl.ds(8 + 2 * parity + number, 1), :]
        bias_sum = jnp.zeros((1, width), jnp.float32)
        for first in range(0, slots, CHUNK):
            here = slice(first, first + CHUNK)
            pre = dot(low_ref[here, :], wide) + bias
            bell, below = tail_of(pre)
            act = (pre * below).astype(jnp.bfloat16)
            act_ref[here, :] = act
            slope = below + pre * bell * 0.3989422804014327
            grad = (dot(back_ref[here, :], deep_weight, NT) * slope).astype(jnp.bfloat16)
            pre_ref[here, :] = grad
            bias_sum = bias_sum + jnp.sum(grad.astype(jnp.float32), axis=0, keepdims=True)
            total_ref[here, :] += dot(act, deep_weight)
            two_ref[here, :] += dot(grad, wide, NT)
        bias_ref[pl.ds(number, 1), :] = bias_sum
        expand_grad = dot(turned_ref[...], pre_ref[...]).astype(jnp.bfloat16)
        project_grad = dot(act_ref[...], back_ref[...], TN).astype(jnp.bfloat16)
        for side in range(2):
            here = slice(side * TILE, (side + 1) * TILE)
            grad_ref[number, :, side * high : (side + 1) * high, :] = expand_grad[:, here].reshape(
                ROW_BLOCKS, high, TILE
            )
            grad_ref[side, blocks, deep, :] = project_grad[:, here].reshape(
                ROW_BLOCKS // 2, 2 * high, TILE
            )
        return carry

    lax.fori_loop(0, 2, step, 0)


def first_kernel(group, count, where_ref, tokens_ref, cotangent_ref, live_ref, params_ref, *refs):
    mixed_parts, pieces = refs[:count], refs[count:-17]
    (resid_ref, total_ref, two_ref, back_ref, outer_ref, kept_ref, sent_ref, sums_ref) = refs[-17:-9]
    (packed_ref, grad_ref, low_ref, turned_ref, act_ref, pre_ref, bias_ref, sems, out_sems) = refs[-9:]
    slots, width = tokens_ref.shape
    high = width // ROW_BLOCKS
    copies = start_pieces(where_ref, pieces, group, packed_ref, sems)
    sums_ref[...] = jnp.zeros_like(sums_ref)
    for first in range(0, slots, CHUNK):
        here = slice(first, first + CHUNK)
        back_ref[here, :] = (cotangent_ref[here, :].astype(jnp.float32) * live_ref[here, :]).astype(
            jnp.bfloat16
        )
    for copy in copies:
        copy.wait()
    weight = jnp.concatenate([tile_of(packed_ref, half, 4 * high, high) for half in range(2)], axis=1)
    outer_ref[...] = weight
    for first in range(0, slots, CHUNK):
        here = slice(first, first + CHUNK)
        mixed = jnp.concatenate([ref[here, :] for ref in mixed_parts], axis=1)
        resid = tokens_ref[here, :].astype(jnp.float32) + (dot(mixed, weight) + params_ref[6:7, :])
        normal, _ = normal_of(resid)
        low = (normal * params_ref[2:3, :] + params_ref[3:4, :]).astype(jnp.bfloat16)
        low_ref[here, :] = low
        turned_ref[:, here] = low.T
        resid_ref[here, :] = resid
        total_ref[here, :] = resid + params_ref[7:8, :]
        two_ref[here, :] = jnp.zeros((CHUNK, width), jnp.float32)
    feed(0, packed_ref, params_ref, low_ref, turned_ref, back_ref, total_ref, two_ref, act_ref, pre_ref, bias_ref, grad_ref)
    sums_ref[8:10, :] = bias_ref[0:2, :]
    for copy in halves_out(grad_ref, where_ref[where_ref.shape[0] - 1], kept_ref, sent_ref, out_sems):
        copy.wait()


def second_kernel(group, count, where_ref, live_ref, params_ref, resid_in, total_in, two_in, back_ref, outer_ref, *refs):
    mixed_parts, pieces = refs[:count], refs[count:-18]
    (out_ref, resid_ref, mixed_grad_ref, kept_ref, sent_ref, sums_ref) = refs[-18:-12]
    (packed_ref, grad_ref, low_ref, turned_ref, total_ref, two_ref, act_ref, pre_ref, bias_ref, ratio_ref, sems, out_sems) = refs[-12:]
    slots, width = resid_in.shape
    high = width // ROW_BLOCKS
    copies = start_pieces(where_ref, pieces, group, packed_ref, sems)
    sums_ref[...] = jnp.zeros_like(sums_ref)
    for first in range(0, slots, CHUNK):
        here = slice(first, first + CHUNK)
        normal, ratio = normal_of(resid_in[here, :])
        low = (normal * params_ref[2:3, :] + params_ref[3:4, :]).astype(jnp.bfloat16)
        low_ref[here, :] = low
        turned_ref[:, here] = low.T
        resid_ref[here, :] = normal
        ratio_ref[here, :] = ratio
        total_ref[here, :] = total_in[here, :]
        two_ref[here, :] = two_in[here, :]
    for copy in copies:
        copy.wait()
    feed(1, packed_ref, params_ref, low_ref, turned_ref, back_ref, total_ref, two_ref, act_ref, pre_ref, bias_ref, grad_ref)
    sums_ref[10:12, :] = bias_ref[0:2, :]
    weight = outer_ref[...]
    for first in range(0, slots, CHUNK):
        here = slice(first, first + CHUNK)
        normal = resid_ref[here, :]
        two = two_ref[here, :]
        back = back_ref[here, :].astype(jnp.float32)
        grad = back + normal_back(normal, ratio_ref[here, :], two * params_ref[2:3, :])
        low = grad.astype(jnp.bfloat16)
        sums_ref[2:3, :] += jnp.sum(two * normal, axis=0, keepdims=True)
        sums_ref[3:4, :] += jnp.sum(two, axis=0, keepdims=True)
        sums_ref[6:7, :] += jnp.sum(low.astype(jnp.float32), axis=0, keepdims=True)
        sums_ref[7:8, :] += jnp.sum(back, axis=0, keepdims=True)
        resid_ref[here, :] = grad
        act_ref[here, :] = low
        mixed_grad_ref[here, :] = dot(low, weight, NT).astype(jnp.bfloat16)
        out_ref[here, :] = (total_ref[here, :] * live_ref[here, :]).astype(jnp.bfloat16)
    mixed = jnp.concatenate([ref[...] for ref in mixed_parts], axis=1)
    outer_grad = dot(mixed, act_ref[...], TN).astype(jnp.bfloat16)
    for side in range(2):
        grad_ref[side, :, 4 * high : 5 * high, :] = outer_grad[
            :, side * TILE : (side + 1) * TILE
        ].reshape(ROW_BLOCKS, high, TILE)
    for copy in halves_out(grad_ref, where_ref[where_ref.shape[0] - 1], kept_ref, sent_ref, out_sems):
        copy.wait()


def middle(kernel, name, in_vmem, mixed, sources, where, outs, rows, weight_rows, extra, group):
    slots, width = mixed[0].shape[0], in_vmem[1].shape[1]
    vmem, anywhere = pl.BlockSpec(memory_space=pltpu.VMEM), pl.BlockSpec(memory_space=pl.ANY)
    half = jax.ShapeDtypeStruct((ROW_BLOCKS, rows, TILE), jnp.bfloat16)
    low = pltpu.VMEM((slots, width), jnp.bfloat16)
    return pl.pallas_call(
        functools.partial(kernel, group, len(mixed)),
        in_specs=[pl.BlockSpec(memory_space=pltpu.SMEM)]
        + [vmem] * (len(in_vmem) + len(mixed))
        + [anywhere] * len(sources),
        out_specs=[vmem] * len(outs) + [anywhere] * 2 + [vmem],
        out_shape=outs + [half, half, jax.ShapeDtypeStruct((16, width), jnp.float32)],
        scratch_shapes=[
            pltpu.VMEM((2, ROW_BLOCKS, weight_rows, TILE), jnp.bfloat16),
            pltpu.VMEM((2, ROW_BLOCKS, rows, TILE), jnp.bfloat16),
            low,
            pltpu.VMEM((width, slots), jnp.bfloat16),
        ]
        + [pltpu.VMEM((slots, width), jnp.float32)] * extra
        + [low, low, pltpu.VMEM((8, width), jnp.float32)]
        + [pltpu.VMEM((slots, 1), jnp.float32)] * (extra // 2)
        + [
            pltpu.SemaphoreType.DMA((copy_count(sources, group),)),
            pltpu.SemaphoreType.DMA((2,)),
        ],
        compiler_params=compiler(60),
        cost_estimate=cost(1, 1),
        name=name,
    )(where, *in_vmem, *mixed, *sources)


def inner_kernel(where_ref, turned_ref, *refs):
    grads, (kept_ref, sent_ref, sums_ref, grad_ref, sems) = refs[:-5], refs[-5:]
    width = turned_ref.shape[0]
    high = width // ROW_BLOCKS
    turned = turned_ref[...]
    sums_ref[...] = jnp.zeros_like(sums_ref)
    for part in range(3):
        values = jnp.concatenate([ref[part] for ref in grads], axis=1)
        grad = dot(turned, values).astype(jnp.bfloat16)
        for side in range(2):
            t = 2 * part + side
            grad_ref[t // 3, :, t % 3 * high : (t % 3 + 1) * high, :] = grad[
                :, side * TILE : (side + 1) * TILE
            ].reshape(ROW_BLOCKS, high, TILE)
        if part != 1:
            row = 4 if part == 0 else 5
            sums_ref[row : row + 1, :] = jnp.sum(values.astype(jnp.float32), axis=0, keepdims=True)
    for copy in halves_out(grad_ref, where_ref[where_ref.shape[0] - 1], kept_ref, sent_ref, sems):
        copy.wait()


def inner_gradient(where, turned, grads):
    width, slots = turned.shape
    rows = 3 * (width // ROW_BLOCKS)
    vmem, anywhere = pl.BlockSpec(memory_space=pltpu.VMEM), pl.BlockSpec(memory_space=pl.ANY)
    half = jax.ShapeDtypeStruct((ROW_BLOCKS, rows, TILE), jnp.bfloat16)
    return pl.pallas_call(
        inner_kernel,
        in_specs=[pl.BlockSpec(memory_space=pltpu.SMEM)] + [vmem] * (1 + len(grads)),
        out_specs=[anywhere, anywhere, vmem],
        out_shape=[half, half, jax.ShapeDtypeStruct((16, width), jnp.float32)],
        scratch_shapes=[
            pltpu.VMEM((2, ROW_BLOCKS, rows, TILE), jnp.bfloat16),
            pltpu.SemaphoreType.DMA((2,)),
        ],
        compiler_params=compiler(40),
        cost_estimate=cost(1, 1),
        name="inner_gradient",
    )(where, turned, *grads)


def input_kernel(tokens_ref, params_ref, packed_ref, resid_ref, *refs):
    grads, (out_ref, sums_ref) = refs[:-2], refs[-2:]
    slots, width = tokens_ref.shape
    high = width // ROW_BLOCKS
    sums_ref[...] = jnp.zeros_like(sums_ref)
    weights = [
        jnp.concatenate(
            [tile_of(packed_ref, t // 3, t % 3 * high, high) for t in (2 * part, 2 * part + 1)], axis=1
        )
        for part in range(3)
    ]
    for first in range(0, slots, CHUNK):
        here = slice(first, first + CHUNK)
        grad = jnp.zeros((CHUNK, width), jnp.float32)
        for part in range(3):
            values = jnp.concatenate([ref[part, here, :] for ref in grads], axis=1)
            grad = grad + dot(values, weights[part], NT)
        normal, ratio = normal_of(tokens_ref[here, :].astype(jnp.float32))
        sums_ref[0:1, :] += jnp.sum(grad * normal, axis=0, keepdims=True)
        sums_ref[1:2, :] += jnp.sum(grad, axis=0, keepdims=True)
        out_ref[here, :] = resid_ref[here, :] + normal_back(normal, ratio, grad * params_ref[0:1, :])


def input_gradient(tokens, params, packed, grads, resid):
    slots, width = tokens.shape
    vmem = pl.BlockSpec(memory_space=pltpu.VMEM)
    return pl.pallas_call(
        input_kernel,
        in_specs=[vmem] * (4 + len(grads)),
        out_specs=[vmem] * 2,
        out_shape=[
            jax.ShapeDtypeStruct((slots, width), jnp.float32),
            jax.ShapeDtypeStruct((16, width), jnp.float32),
        ],
        compiler_params=compiler(48),
        cost_estimate=cost(1, 1),
        name="input_gradient",
    )(tokens, params, packed, resid, *grads)


def gather_vector(master, ring):
    own = master.astype(jnp.bfloat16)
    group = ring.group
    parts = [own] + [ring.send_shard(own, step) for step in range(1, group)]
    stacked = jnp.stack(parts)
    order = (ring.z - jnp.arange(group)) % group
    return jnp.take(stacked, order, axis=0).reshape(group * own.shape[0], own.shape[1])


class VectorSum:
    def __init__(self, grad, ring):
        self.grad, self.ring = grad, ring
        self.flat = grad.reshape(ring.group, -1, 128) if ring.staged() else None

    def hop(self, bit):
        pairs = [(i, i ^ bit) for i in range(self.ring.data)]
        self.got = lax.ppermute(self.flat, "dp", pairs)

    def add(self, *others):
        self.flat = after(self.flat + after(self.got, *others))
        return self.flat

    def shards(self):
        ring = self.ring

        def shard_of(step):
            return lax.dynamic_index_in_dim(
                self.flat, (ring.z + step) % ring.group, 0, keepdims=False
            )

        self.arrived = [ring.send_shard(shard_of(step), step) for step in range(1, ring.group)]
        self.flat = shard_of(0)

    def finish(self, *others):
        if not self.ring.staged():
            whole = lax.psum_scatter(self.grad, "shard", scatter_dimension=0, tiled=True)
            return lax.psum(whole, "dp")
        arrived = lax.optimization_barrier((*self.arrived, *others))[: len(self.arrived)]
        done = self.flat
        for value in arrived:
            done = done + value
        return done.reshape(self.grad.shape[0] // self.ring.group, self.grad.shape[1])


def on_device(
    tokens,
    cotangent,
    seq_lengths,
    seq_owner,
    attend_master,
    expand_master,
    project_master,
    vector_master,
    attend_mean,
    expand_mean,
    project_mean,
    vector_mean,
    attend_square,
    expand_square,
    project_square,
    vector_square,
):
    ring = Ring()
    slots, width = tokens.shape
    high = width // ROW_BLOCKS
    staged = ring.staged()
    masters = (attend_master, expand_master, project_master)
    if not staged:
        masters = tuple(
            lax.all_gather(m.astype(jnp.bfloat16), "shard", axis=0, tiled=True) for m in masters
        )
    tall = masters[0].shape[0]

    def pack_group(parity, tie):
        attend, expand, project = lax.optimization_barrier((*masters, tie))[:3] if staged else masters
        parts = [
            (expand, hidden_of(parity), high, [0], tall),
            (project, halves_of(0, 1), 2 * high, starts_of(project.shape[0], parity), TILE),
        ]
        if parity == 0:
            parts.append((attend, halves_of(3 * width, 1), high, [0], tall))
        return pack(parts)

    own_inner = pack([(masters[0], halves_of(0, 3), high, [0], tall)])
    vector = gather_vector(vector_master, ring).astype(jnp.float32)
    device = lax.axis_index("dp") * ring.group + ring.z
    segment = slot_segments(seq_lengths, seq_owner, device, slots)
    live = (segment >= 0).astype(jnp.float32)[:, None]
    hidden_bias = vector[:, 8:].reshape(2, 2, 2, TILE).transpose(2, 0, 1, 3).reshape(4, width)
    params = jnp.concatenate(
        [vector[:, :8].T, hidden_bias, jnp.zeros((4, width), jnp.float32)]
    )
    rows = tokens
    if staged:
        inner_part = Gather(own_inner, ring)
        far = inner_part.foreign()
        inner_part.plane(True)
        even_part = Gather(pack_group(0, far), ring)
        inner_part.cores()
        far = even_part.foreign(*inner_part.other)
        even_part.plane(False)
        odd_part = Gather(pack_group(1, far), ring)
        rows = after(tokens, far)
        inner_sources = inner_part.sources()
        inner_where = where_array(inner_part.places(), ring)
    else:
        inner_sources, inner_where = [own_inner], where_array([(None, 0)], ring)
    projected, turned, inner = project_rows(rows, params, inner_sources, inner_where, ring.group)
    if staged:
        projected = after(projected, even_part.mine[2])
    half = HEADS // 4
    mixed, logs = [None, None], [None, None]
    mixed[0], logs[0] = attention(projected, segment, 0, half)
    later = projected
    if staged:
        even_part.cores(mixed[0])
        far = odd_part.foreign(mixed[0])
        odd_part.plane(False)
        later = after(projected, *even_part.mine, far)
    mixed[1], logs[1] = attention(later, segment, half, half)
    if staged:
        odd_part.cores(mixed[1])
        even_sources, even_where = even_part.sources(), where_array(even_part.places(), ring)
        odd_sources, odd_where = odd_part.sources(), where_array(odd_part.places(), ring)
        mixed[0] = after(mixed[0], *odd_part.mine)
    else:
        even_sources, even_where = [pack_group(0, None)], inner_where
        odd_sources, odd_where = [pack_group(1, None)], inner_where
    low = jax.ShapeDtypeStruct((slots, width), jnp.bfloat16)
    wide = jax.ShapeDtypeStruct((slots, width), jnp.float32)
    square = jax.ShapeDtypeStruct((width, width), jnp.bfloat16)
    resid, total, two, back, outer, *even_halves, even_sums = middle(
        first_kernel,
        "first_half",
        [tokens, cotangent, live, params],
        mixed,
        even_sources,
        even_where,
        [wide, wide, wide, low, square],
        4 * high,
        5 * high,
        0,
        ring.group,
    )
    if staged:
        even = Sum(*even_halves, ring)
    layer_output, grad_resid, grad_mixed, *odd_halves, odd_sums = middle(
        second_kernel,
        "second_half",
        [live, params, resid, total, two, back, outer],
        mixed,
        odd_sources,
        odd_where,
        [low, wide, low],
        5 * high,
        4 * high,
        2,
        ring.group,
    )
    if staged:
        odd = Sum(*odd_halves, ring)
        level = even.chip(False, grad_mixed)
        grad_mixed = after(grad_mixed, level)
    part = HEADS // 6
    grads = [attention_back(projected, grad_mixed, logs[0], 0, segment, 0, part)]
    back_logs = jnp.concatenate([logs[0][part:], logs[1][: 2 * part - half]])
    if staged:
        level = even.halfway(grads[0])
        grad_mixed = after(grad_mixed, level, odd.chip(False, grads[0]))
    grads.append(attention_back(projected, grad_mixed, back_logs, 0, segment, part, part))
    if staged:
        level = even.plane(grads[1])
        grad_mixed = after(grad_mixed, level, odd.halfway(grads[1]))
    grads.append(attention_back(projected, grad_mixed, logs[1], 2 * part - half, segment, 2 * part, part))
    if staged:
        even_done = even.finish(grads[2])
        turned = after(turned, even_done, odd.plane(grads[2]))
    *inner_halves, inner_sums = inner_gradient(inner_where, turned, grads)
    last = grads
    if staged:
        tail = Sum(*inner_halves, ring)
        last = grads[:2] + [after(grads[2], inner_sums)]
    input_grad, input_sums = input_gradient(tokens, params, inner, last, grad_resid)
    sums = even_sums + odd_sums + inner_sums + input_sums
    hidden_sum = sums[8:12].reshape(2, 2, 2, TILE).transpose(1, 2, 0, 3).reshape(width, 4)
    vector_grad = jnp.concatenate([sums[:8].T, hidden_sum], axis=1)
    vector_part = VectorSum(vector_grad, ring)
    vector_tie = ()
    if staged:
        vector_part.hop(1)
        odd_done = odd.finish(input_sums)
        level = tail.chip(True, input_sums, odd_done)
        level = vector_part.add(level)
        vector_part.hop(2)
        level = tail.plane(level)
        rest_part = Spread(after(jnp.concatenate([even_done, odd_done]), level), ring, False)
        tail_done = tail.finish(vector_part.add(rest_part.mine[0]))
        vector_part.hop(4)
        tail_part = Spread(tail_done, ring, True)
        rest_sum = rest_part.cores(tail_part.mine[0])
        level = vector_part.add(tail_part.mine[0])
        vector_part.shards()
        expand_state = adam_packed(
            after(expand_master, level),
            expand_mean,
            expand_square,
            [rest_sum],
            [(0, 4 * high * parity, hidden_of(parity), high, 0) for parity in range(2)],
            1,
        )
        tail_sum = tail_part.cores(expand_state[0])
        project_state = adam_packed(
            after(project_master, tail_sum[0]),
            project_mean,
            project_square,
            [rest_sum],
            [
                (0, 4 * high * parity + 2 * high, halves_of(0, 1), 2 * high, parity)
                for parity in range(2)
            ],
            2,
        )
        vector_tie = (project_state[0],)
        attend_state = adam_packed(
            attend_master,
            attend_mean,
            attend_square,
            [tail_sum, rest_sum],
            [
                (0, 0, halves_of(0, 3), high, 0),
                (1, 8 * high, halves_of(3 * width, 1), high, 0),
            ],
            1,
        )
    else:
        plain = plain_gradients(even_halves, odd_halves, inner_halves, ring.core, high)
        attend_sum, expand_sum, project_sum = (
            lax.psum(lax.psum_scatter(g, "shard", scatter_dimension=0, tiled=True), "dp")
            for g in plain
        )
        attend_state = adam(
            attend_master, attend_mean, attend_square, attend_sum, RATE_MATRIX, DECAY_MATRIX
        )
        expand_state = adam(
            expand_master, expand_mean, expand_square, expand_sum, RATE_MATRIX, DECAY_MATRIX
        )
        project_state = adam(
            project_master, project_mean, project_square, project_sum, RATE_MATRIX, DECAY_MATRIX
        )
    vector_sum = vector_part.finish(*vector_tie)
    vector_state = adam(vector_master, vector_mean, vector_square, vector_sum, RATE_VECTOR, 0.0)
    return (
        layer_output,
        input_grad,
        attend_state[0],
        expand_state[0],
        project_state[0],
        vector_state[0],
        attend_state[1],
        expand_state[1],
        project_state[1],
        vector_state[1],
        attend_state[2],
        expand_state[2],
        project_state[2],
        vector_state[2],
    )


def solution(mesh):
    return jax.shard_map(
        on_device,
        mesh=mesh,
        in_specs=(
            P(("dp", "shard"), None),
            P(("dp", "shard"), None),
            P(),
            P(),
            P("shard", None),
            P("shard", None),
            P("shard", None),
            P("shard", None),
            P("shard", None),
            P("shard", None),
            P("shard", None),
            P("shard", None),
            P("shard", None),
            P("shard", None),
            P("shard", None),
            P("shard", None),
        ),
        out_specs=(
            P(("dp", "shard"), None),
            P(("dp", "shard"), None),
            P("shard", None),
            P("shard", None),
            P("shard", None),
            P("shard", None),
            P("shard", None),
            P("shard", None),
            P("shard", None),
            P("shard", None),
            P("shard", None),
            P("shard", None),
            P("shard", None),
            P("shard", None),
        ),
        check_vma=False,
    )
```

```python
import functools
import math

import jax
import jax.numpy as jnp
from jax import lax
from jax.experimental import pallas as pl
from jax.experimental.pallas import tpu as pltpu
from jax.sharding import PartitionSpec as P

HEADS = 12
HEAD_DIM = 64
STEP = 10


NORM_EPS = 1e-05
MASK_FILL = -1e30
BETA_ONE = 0.9
BETA_TWO = 0.999
ADAM_EPS = 1e-08
RATE_MATRIX = 0.05
RATE_VECTOR = 0.3
DECAY_MATRIX = 0.01
BLOCK = 256
NT = (((1,), (1,)), ((), ()))
TN = (((0,), (0,)), ((), ()))


def slot_segments(seq_lengths, seq_owner, device, slots):
    mine = seq_owner == device
    owned = jnp.where(mine, seq_lengths, 0)
    starts = jnp.cumsum(owned) - owned
    place = jnp.arange(slots, dtype=jnp.int32)[:, None]
    inside = mine[None, :] & (place >= starts[None, :]) & (place < (starts + owned)[None, :])
    labels = jnp.arange(seq_lengths.shape[0], dtype=jnp.int32)[None, :] + 1
    return jnp.sum(jnp.where(inside, labels, 0), axis=1) - 1


def dot(a, b, dims=(((1,), (0,)), ((), ()))):
    return lax.dot_general(a, b, dims, preferred_element_type=jnp.float32)


def mask_of(column, row, first, end, start):
    later = lax.broadcasted_iota(jnp.int32, (end - first, end - start), 0) + first
    earlier = lax.broadcasted_iota(jnp.int32, (end - first, end - start), 1) + start
    return (column == row) & (earlier <= later)


def forward_kernel(column_ref, row_ref, q_ref, k_ref, v_ref, mixed_ref, log_ref):
    slots = q_ref.shape[0]
    scale = HEAD_DIM**-0.5
    low = lax.broadcasted_iota(jnp.int32, (1, 128), 1) < HEAD_DIM
    for index in range(slots // BLOCK):
        first, end = index * BLOCK, (index + 1) * BLOCK
        start = max(0, first - 512)
        ok = mask_of(column_ref[first:end, :], row_ref[:, start:end], first, end, start)
        q = q_ref[first:end, :]
        k = k_ref[start:end, :]
        v = v_ref[start:end, :]
        mixed, logs = [], []
        for head in range(2):
            mine = low if head == 0 else ~low
            s = dot(jnp.where(mine, q, jnp.zeros_like(q)), k, NT) * scale
            s = jnp.where(ok, s, MASK_FILL)
            top = jnp.max(s, axis=1, keepdims=True)
            e = jnp.exp(s - top)
            total = jnp.sum(e, axis=1, keepdims=True)
            p = (e * (1.0 / total)).astype(jnp.bfloat16)
            mixed.append(dot(p, v))
            logs.append(top + jnp.log(total))
        mixed_ref[first:end, :] = jnp.where(low, mixed[0], mixed[1]).astype(jnp.bfloat16)
        log_ref[0, first:end, :] = jnp.concatenate(logs, axis=1)


def backward_kernel(column_ref, row_ref, q_ref, k_ref, v_ref, g_ref, log_ref, out_ref, ka, va):
    slots = q_ref.shape[0]
    scale = HEAD_DIM**-0.5
    low = lax.broadcasted_iota(jnp.int32, (1, 128), 1) < HEAD_DIM
    ka[...] = jnp.zeros_like(ka)
    va[...] = jnp.zeros_like(va)
    for index in range(slots // BLOCK):
        first, end = index * BLOCK, (index + 1) * BLOCK
        start = max(0, first - 512)
        ok = mask_of(column_ref[first:end, :], row_ref[:, start:end], first, end, start)
        q = q_ref[first:end, :]
        g = g_ref[first:end, :]
        k = k_ref[start:end, :]
        v = v_ref[start:end, :]
        dq, dk, dv = [], [], []
        for head in range(2):
            mine = low if head == 0 else ~low
            s = dot(jnp.where(mine, q, jnp.zeros_like(q)), k, NT) * scale
            p = jnp.exp(jnp.where(ok, s - log_ref[0, first:end, head : head + 1], MASK_FILL))
            dp = dot(jnp.where(mine, g, jnp.zeros_like(g)), v, NT)
            w = p * dp
            ds = (w - p * jnp.sum(w, axis=1, keepdims=True)).astype(jnp.bfloat16)
            dq.append(dot(ds, k))
            dk.append(dot(ds, q, TN))
            dv.append(dot(p.astype(jnp.bfloat16), g, TN))
        out_ref[0, first:end, :] = (jnp.where(low, dq[0], dq[1]) * scale).astype(jnp.bfloat16)
        ka[start:end, :] += jnp.where(low, dk[0], dk[1])
        va[start:end, :] += jnp.where(low, dv[0], dv[1])
    out_ref[1] = (ka[...] * scale).astype(jnp.bfloat16)
    out_ref[2] = va[...].astype(jnp.bfloat16)


def columns(offset, slots):
    return pl.BlockSpec((slots, 128), lambda pair: (0, pair + offset))


def whole(shape):
    return pl.BlockSpec(shape, lambda pair: (0, 0))


def attention(projected, segment, first, count):
    slots = projected.shape[0]
    pairs = HEADS // 2
    return pl.pallas_call(
        forward_kernel,
        grid=(count,),
        in_specs=[whole((slots, 1)), whole((1, slots))] + [columns(pairs * n + first, slots) for n in range(3)],
        out_specs=[columns(0, slots), pl.BlockSpec((1, slots, 2), lambda pair: (pair, 0, 0))],
        out_shape=[
            jax.ShapeDtypeStruct((slots, count * 128), jnp.bfloat16),
            jax.ShapeDtypeStruct((count, slots, 2), jnp.float32),
        ],
        compiler_params=pltpu.CompilerParams(vmem_limit_bytes=48 * 1024 * 1024),
        cost_estimate=cost(2 * slots * slots * count * 256, 8 * slots * count * 128),
        name="attention",
    )(segment[:, None], segment[None, :], projected, projected, projected)


def attention_back(projected, grad_mixed, logs, log_first, segment, first, count):
    slots = projected.shape[0]
    pairs = HEADS // 2
    return pl.pallas_call(
        backward_kernel,
        grid=(count,),
        in_specs=[whole((slots, 1)), whole((1, slots))]
        + [columns(pairs * n + first, slots) for n in range(3)]
        + [columns(first, slots), pl.BlockSpec((1, slots, 2), lambda pair: (pair + log_first, 0, 0))],
        out_specs=pl.BlockSpec((3, slots, 128), lambda pair: (0, 0, pair)),
        out_shape=jax.ShapeDtypeStruct((3, slots, count * 128), jnp.bfloat16),
        scratch_shapes=[pltpu.VMEM((slots, 128), jnp.float32)] * 2,
        compiler_params=pltpu.CompilerParams(vmem_limit_bytes=48 * 1024 * 1024),
        cost_estimate=cost(5 * slots * slots * count * 256, 16 * slots * count * 128),
        name="attention_back",
    )(segment[:, None], segment[None, :], projected, projected, projected, grad_mixed, logs)


def adam(master, mean, square, grad, rate, decay):
    mean_new = BETA_ONE * mean + (1.0 - BETA_ONE) * grad
    square_new = BETA_TWO * square + (1.0 - BETA_TWO) * grad * grad
    mean_hat = mean_new / (1.0 - BETA_ONE**STEP)
    square_hat = square_new / (1.0 - BETA_TWO**STEP)
    master_new = master - rate * (mean_hat / (jnp.sqrt(square_hat) + ADAM_EPS) + decay * master)
    return (mean_new, square_new, master_new)


class Ring:
    def __init__(self):
        self.group = lax.axis_size("shard")
        self.data = lax.axis_size("dp")
        self.plane = self.data // 2
        self.side = math.isqrt(self.plane)
        self.square = self.data == 2 * self.side * self.side
        self.z = lax.axis_index("shard")
        device = lax.axis_index("dp")
        self.core = device % 2
        chip = device // 2
        high, low = chip // self.side, chip % self.side
        straight = low * self.side + high
        crossed = high * self.side + low
        self.block = jnp.where(self.core == 0, straight, crossed)
        self.block_other = jnp.where(self.core == 0, crossed, straight)

    def staged(self):
        return self.side == 2 and self.square and self.group * self.plane == ROW_BLOCKS

    def send_core(self, value):
        return lax.ppermute(value, "dp", [(i, i ^ 1) for i in range(self.data)])

    def send_plane(self, value, step):
        side = self.side
        first, second = step // side, step % side
        pairs = []
        for device in range(self.data):
            core, chip = device % 2, device // 2
            high, low = chip // side, chip % side
            if core == 0:
                low, high = (low + first) % side, (high + second) % side
            else:
                high, low = (high + first) % side, (low + second) % side
            pairs.append((device, (high * side + low) * 2 + core))
        return lax.ppermute(value, "dp", pairs)

    def spread(self, value, direct):
        if direct:
            return [self.send_plane(value, step) for step in range(1, self.plane)]
        second, first = self.send_plane(value, 1), self.send_plane(value, 2)
        return [second, first, self.send_plane(first, 1)]

    def shifted(self, block, step):
        side = self.side
        first, second = step // side, step % side
        return (block // side + first) % side * side + (block % side + second) % side

    def back(self, block, step):
        side = self.side
        first, second = step // side, step % side
        return (block // side - first) % side * side + (block % side - second) % side

    def send_shard(self, value, step):
        group = self.group
        return lax.ppermute(value, "shard", [(i, (i + step) % group) for i in range(group)])


TILE = 384
ROW_BLOCKS = 16
CHUNK = 256


def compiler(megabytes):
    return pltpu.CompilerParams(vmem_limit_bytes=megabytes * 1024 * 1024)


def cost(flops, bytes_accessed):
    return pl.CostEstimate(flops=flops, bytes_accessed=bytes_accessed, transcendentals=0)


def halves_of(first, tiles):
    return [[first + (half * tiles + tile) * TILE for tile in range(tiles)] for half in range(2)]


def hidden_of(parity):
    return [[(4 * half + 2 * tile + parity) * TILE for tile in range(2)] for half in range(2)]


def starts_of(rows, parity):
    return [first + parity * TILE for first in range(0, rows, 2 * TILE)]


def pack_kernel(specs, *refs):
    out_ref = refs[-1]
    row = 0
    for (columns, high, starts, count), ref in zip(specs, refs[:-1], strict=True):
        for number, start in enumerate(starts):
            blocks = slice(number * (count // high), (number + 1) * (count // high))
            for half in range(2):
                for tile, column in enumerate(columns[half]):
                    part = ref[start : start + count, column : column + TILE].astype(jnp.bfloat16)
                    out_ref[half, blocks, row + tile * high : row + (tile + 1) * high, :] = part.reshape(
                        count // high, high, TILE
                    )
        row += len(columns[0]) * high


def pack(parts):
    blocks = len(parts[0][3]) * parts[0][4] // parts[0][2]
    rows = sum(len(part[1][0]) * part[2] for part in parts)
    vmem = pl.BlockSpec(memory_space=pltpu.VMEM)
    return pl.pallas_call(
        functools.partial(pack_kernel, [part[1:] for part in parts]),
        in_specs=[vmem] * len(parts),
        out_specs=vmem,
        out_shape=jax.ShapeDtypeStruct((2, blocks, rows, TILE), jnp.bfloat16),
        compiler_params=compiler(40),
        cost_estimate=cost(0, 12 * blocks * rows * TILE),
        name="pack",
    )(*[part[0] for part in parts])


def after(value, *others):
    return lax.optimization_barrier((value, *others))[0]


class Gather:
    def __init__(self, own, ring):
        self.own, self.ring = own, ring
        chunk = lax.dynamic_index_in_dim(
            lax.dynamic_index_in_dim(own, ring.core, 0, keepdims=False),
            ring.block,
            0,
            keepdims=False,
        )
        self.arrived = [ring.send_shard(chunk, step) for step in range(1, ring.group)]

    def foreign(self, *others):
        self.far = after(jnp.stack(self.arrived), *others)
        return self.far

    def plane(self, direct):
        self.mine = [self.far] + self.ring.spread(self.far, direct)

    def cores(self, *others):
        ring = self.ring
        self.mine = list(lax.optimization_barrier((*self.mine, *others))[: ring.plane])
        self.other = [ring.send_core(value) for value in self.mine]

    def sources(self):
        return [self.own] + self.mine + self.other

    def places(self):
        ring = self.ring
        steps = range(ring.plane)
        places = [(None, ring.z * self.own.shape[1])]
        places += [(ring.core, ring.back(ring.block, step)) for step in steps]
        return places + [(1 - ring.core, ring.back(ring.block_other, step)) for step in steps]


def where_array(places, ring):
    scalars = [ring.z]
    for half, block in places:
        scalars += [0 if half is None else half, block]
    scalars.append(ring.core)
    return jnp.stack([jnp.asarray(v, jnp.int32) for v in scalars])


def copy_count(sources, group):
    return 1 if len(sources) == 1 else 2 + (len(sources) - 1) * (group - 1)


def start_pieces(where_ref, refs, group, out_ref, sems):
    copies = []

    def begin(source, target):
        copy = pltpu.make_async_copy(source, target, sems.at[len(copies)])
        copy.start()
        copies.append(copy)

    if len(refs) == 1:
        begin(refs[0], out_ref)
        return copies
    blocks = refs[0].shape[1]
    first = where_ref[2]
    for half in range(2):
        begin(refs[0].at[half], out_ref.at[half, pl.ds(first, blocks)])
    for number, ref in enumerate(refs[1:], 1):
        half, block = where_ref[1 + 2 * number], where_ref[2 + 2 * number]
        for step in range(1, group):
            source = lax.rem(where_ref[0] - step + group, group)
            begin(ref.at[step - 1], out_ref.at[half, source * blocks + block])
    return copies


class Sum:
    def __init__(self, kept, sent, ring):
        self.ring, self.kept = ring, kept
        self.got = ring.send_core(sent)

    def chip(self, direct, *others):
        ring = self.ring
        kept = after(self.kept, *others)
        chip = (kept.astype(jnp.float32) + self.got.astype(jnp.float32)).astype(jnp.bfloat16)
        rows = chip.shape[1]
        self.direct = direct
        if direct:
            chip = lax.optimization_barrier(chip.reshape(ring.group, ring.plane, rows, TILE))

            def block_of(step):
                return lax.dynamic_index_in_dim(
                    chip, ring.shifted(ring.block, step), 1, keepdims=False
                )

            self.arrived = [ring.send_plane(block_of(step), step) for step in range(1, ring.plane)]
            self.level = block_of(0)
            return self.level
        chip = lax.optimization_barrier(chip.reshape(ring.group, 2, 2 * rows, TILE))
        mine = ring.block // 2
        away = lax.dynamic_index_in_dim(chip, 1 - mine, 1, keepdims=False)
        self.arrived = [ring.send_plane(away, 2)]
        self.level = lax.dynamic_index_in_dim(chip, mine, 1, keepdims=False)
        return self.level

    def halfway(self, *others):
        ring = self.ring
        level = after(self.level, *others).astype(jnp.float32) + self.arrived[0].astype(jnp.float32)
        rows = level.shape[1] // 2
        level = lax.optimization_barrier(
            level.astype(jnp.bfloat16).reshape(ring.group, 2, rows, TILE)
        )
        mine = ring.block % 2
        away = lax.dynamic_index_in_dim(level, 1 - mine, 1, keepdims=False)
        self.arrived = [ring.send_plane(away, 1)]
        self.level = lax.dynamic_index_in_dim(level, mine, 1, keepdims=False)
        return self.level

    def plane(self, *others):
        ring = self.ring
        level = after(self.level, *others).astype(jnp.float32)
        for value in self.arrived:
            level = level + value.astype(jnp.float32)
        level = lax.optimization_barrier(level.astype(jnp.bfloat16))

        def shard_of(step):
            return lax.dynamic_index_in_dim(
                level, (ring.z + step) % ring.group, 0, keepdims=False
            )

        self.arrived = [ring.send_shard(shard_of(step), step) for step in range(1, ring.group)]
        self.level = shard_of(0)
        return self.level

    def finish(self, *others):
        done = after(self.level, *others).astype(jnp.float32)
        for value in self.arrived:
            done = done + value.astype(jnp.float32)
        return done.astype(jnp.bfloat16)


class Spread:
    def __init__(self, piece, ring, direct):
        self.ring = ring
        piece = lax.optimization_barrier(piece)
        self.mine = [piece] + ring.spread(piece, direct)

    def cores(self, *others):
        ring = self.ring
        mine = after(jnp.stack(self.mine), *others)
        places = [(ring.core, ring.back(ring.block, step)) for step in range(ring.plane)]
        places += [(1 - ring.core, ring.back(ring.block_other, step)) for step in range(ring.plane)]
        return [mine, ring.send_core(mine)], places


def plain_gradients(even, odd, inner, core, high):
    def both(halves):
        kept, sent = (value.astype(jnp.float32) for value in halves)
        return jnp.stack([jnp.where(core == 0, kept, sent), jnp.where(core == 0, sent, kept)])

    def columns(packed, first, tiles):
        part = packed[:, :, first : first + tiles * high].reshape(2, ROW_BLOCKS, tiles, high, TILE)
        return part.transpose(1, 3, 0, 2, 4)

    even, odd, inner = both(even), both(odd), both(inner)
    width = ROW_BLOCKS * high
    expand = jnp.stack([columns(even, 0, 2), columns(odd, 0, 2)], axis=4).reshape(width, -1)
    deep = [
        packed[:, :, 2 * high : 4 * high].transpose(1, 2, 0, 3).reshape(4, TILE, width)
        for packed in (even, odd)
    ]
    project = jnp.stack(deep, axis=1).reshape(-1, width)
    attend = jnp.concatenate(
        [columns(inner, 0, 3).reshape(width, -1), columns(odd, 4 * high, 1).reshape(width, -1)], axis=1
    )
    return attend, expand, project


def place_kernel(matrices, count, where_ref, *refs):
    sources, outs = refs[: 2 * count], refs[2 * count : 2 * count + len(matrices)]
    packed, sems = refs[2 * count + len(matrices) : -1], refs[-1]
    plane = sources[0].shape[0]
    copies = []
    for number, ref in enumerate(sources):
        for block in range(plane):
            scalar = 2 * len(copies)
            place = packed[number // 2].at[where_ref[scalar], where_ref[scalar + 1]]
            copy = pltpu.make_async_copy(ref.at[block], place, sems.at[len(copies)])
            copy.start()
            copies.append(copy)
    for copy in copies:
        copy.wait()
    for kinds, out_ref in zip(matrices, outs, strict=True):
        for gradient, row, columns, high, first in kinds:
            for half in range(2):
                for tile, column in enumerate(columns[half]):
                    rows = slice(row + tile * high, row + (tile + 1) * high)
                    value = packed[gradient][half, :, rows, :].reshape(plane * high, TILE)
                    out_ref[first : first + plane * high, column : column + TILE] = value


def place_sums(gradients, shapes, matrices):
    sources = [source for group, _ in gradients for source in group]
    plane = sources[0].shape[0]
    scalars = [v for _, places in gradients for place in places for v in place]
    where = jnp.stack([jnp.asarray(v, jnp.int32) for v in scalars])
    return pl.pallas_call(
        functools.partial(place_kernel, matrices, len(gradients)),
        in_specs=[pl.BlockSpec(memory_space=pltpu.SMEM)]
        + [pl.BlockSpec(memory_space=pl.ANY)] * len(sources),
        out_specs=[pl.BlockSpec(memory_space=pltpu.VMEM)] * len(shapes),
        out_shape=[jax.ShapeDtypeStruct(shape, jnp.bfloat16) for shape in shapes],
        scratch_shapes=[
            pltpu.VMEM((2, plane) + group[0].shape[1:], jnp.bfloat16) for group, _ in gradients
        ]
        + [pltpu.SemaphoreType.DMA((len(sources) * plane,))],
        compiler_params=compiler(32),
        cost_estimate=cost(0, 4 * sum(rows * columns for rows, columns in shapes)),
        name="place_sums",
    )(where, *sources)


def tile_of(packed_ref, half, row, high):
    part = packed_ref[half, :, pl.ds(row, high), :]
    return part.reshape(ROW_BLOCKS * high, TILE)


def normal_of(rows):
    centre = jnp.mean(rows, axis=1, keepdims=True)
    centred = rows - centre
    spread = jnp.mean(centred * centred, axis=1, keepdims=True)
    ratio = lax.rsqrt(spread + NORM_EPS)
    return centred * ratio, ratio


def normal_back(normal, ratio, scaled):
    along = jnp.mean(scaled * normal, axis=1, keepdims=True)
    return ratio * (scaled - jnp.mean(scaled, axis=1, keepdims=True) - normal * along)


def project_kernel(group, where_ref, tokens_ref, params_ref, *refs):
    pieces, (out_ref, turned_ref, packed_ref, sems) = refs[:-4], refs[-4:]
    slots, width = tokens_ref.shape
    high = width // ROW_BLOCKS
    copies = start_pieces(where_ref, pieces, group, packed_ref, sems)
    lows = []
    for first in range(0, slots, CHUNK):
        normal, _ = normal_of(tokens_ref[first : first + CHUNK, :].astype(jnp.float32))
        low = (normal * params_ref[0:1, :] + params_ref[1:2, :]).astype(jnp.bfloat16)
        turned_ref[:, first : first + CHUNK] = low.T
        lows.append(low)
    for copy in copies:
        copy.wait()
    for part in range(3):
        weight = jnp.concatenate(
            [tile_of(packed_ref, t // 3, t % 3 * high, high) for t in (2 * part, 2 * part + 1)], axis=1
        )
        for number, low in enumerate(lows):
            value = dot(low, weight)
            if part != 1:
                row = 4 if part == 0 else 5
                value = value + params_ref[row : row + 1, :]
            out_ref[number * CHUNK : (number + 1) * CHUNK, part * width : (part + 1) * width] = (
                value.astype(jnp.bfloat16)
            )


def project_rows(tokens, params, sources, where, group):
    slots, width = tokens.shape
    high = width // ROW_BLOCKS
    vmem = pl.BlockSpec(memory_space=pltpu.VMEM)
    return pl.pallas_call(
        functools.partial(project_kernel, group),
        in_specs=[pl.BlockSpec(memory_space=pltpu.SMEM), vmem, vmem]
        + [pl.BlockSpec(memory_space=pl.ANY)] * len(sources),
        out_specs=[vmem] * 3,
        out_shape=[
            jax.ShapeDtypeStruct((slots, 3 * width), jnp.bfloat16),
            jax.ShapeDtypeStruct((width, slots), jnp.bfloat16),
            jax.ShapeDtypeStruct((2, ROW_BLOCKS, 3 * high, TILE), jnp.bfloat16),
        ],
        scratch_shapes=[pltpu.SemaphoreType.DMA((copy_count(sources, group),))],
        compiler_params=compiler(40),
        cost_estimate=cost(6 * slots * width * width, 16 * slots * width),
        name="project_rows",
    )(where, tokens, params, *sources)


def tail_of(values):
    size = jnp.abs(values) * (0.5**0.5)
    bell = jnp.exp(-0.5 * values * values)
    t = 1.0 / (1.0 + 0.5 * size)
    series = jnp.full_like(t, 0.17087277)
    for c in (
        -0.82215223, 1.48851587, -1.13520398, 0.27886807, -0.18628806, 0.09678418, 0.37409196, 1.00002368, -1.26551223,
    ):
        series = series * t + c
    tail = 0.5 * t * bell * jnp.exp(series)
    return bell, jnp.where(values > 0, 1.0 - tail, tail)


def halves_out(scratch_ref, core, kept_ref, sent_ref, sems):
    copies = [
        pltpu.make_async_copy(scratch_ref.at[core], kept_ref, sems.at[0]),
        pltpu.make_async_copy(scratch_ref.at[1 - core], sent_ref, sems.at[1]),
    ]
    for copy in copies:
        copy.start()
    return copies


def feed(parity, packed_ref, params_ref, low_ref, turned_ref, back_ref, total_ref, two_ref, act_ref, pre_ref, bias_ref, grad_ref):
    slots, width = low_ref.shape
    high = width // ROW_BLOCKS
    deep = slice(2 * high, 4 * high)

    def step(number, carry):
        wide = jnp.concatenate(
            [tile_of(packed_ref, number, tile * high, high) for tile in range(2)], axis=1
        )
        blocks = pl.ds(number * (ROW_BLOCKS // 2), ROW_BLOCKS // 2)
        deep_weight = jnp.concatenate(
            [packed_ref[side, blocks, deep, :].reshape(width, TILE) for side in range(2)], axis=1
        )
        bias = params_ref[pl.ds(8 + 2 * parity + number, 1), :]
        bias_sum = jnp.zeros((1, width), jnp.float32)
        for first in range(0, slots, CHUNK):
            here = slice(first, first + CHUNK)
            pre = dot(low_ref[here, :], wide) + bias
            bell, below = tail_of(pre)
            act = (pre * below).astype(jnp.bfloat16)
            act_ref[here, :] = act
            slope = below + pre * bell * 0.3989422804014327
            grad = (dot(back_ref[here, :], deep_weight, NT) * slope).astype(jnp.bfloat16)
            pre_ref[here, :] = grad
            bias_sum = bias_sum + jnp.sum(grad.astype(jnp.float32), axis=0, keepdims=True)
            total_ref[here, :] += dot(act, deep_weight)
            two_ref[here, :] += dot(grad, wide, NT)
        bias_ref[pl.ds(number, 1), :] = bias_sum
        expand_grad = dot(turned_ref[...], pre_ref[...]).astype(jnp.bfloat16)
        project_grad = dot(act_ref[...], back_ref[...], TN).astype(jnp.bfloat16)
        for side in range(2):
            here = slice(side * TILE, (side + 1) * TILE)
            grad_ref[number, :, side * high : (side + 1) * high, :] = expand_grad[:, here].reshape(
                ROW_BLOCKS, high, TILE
            )
            grad_ref[side, blocks, deep, :] = project_grad[:, here].reshape(
                ROW_BLOCKS // 2, 2 * high, TILE
            )
        return carry

    lax.fori_loop(0, 2, step, 0)


def first_kernel(group, count, where_ref, tokens_ref, cotangent_ref, live_ref, params_ref, *refs):
    mixed_parts, pieces = refs[:count], refs[count:-17]
    (resid_ref, total_ref, two_ref, back_ref, outer_ref, kept_ref, sent_ref, sums_ref) = refs[-17:-9]
    (packed_ref, grad_ref, low_ref, turned_ref, act_ref, pre_ref, bias_ref, sems, out_sems) = refs[-9:]
    slots, width = tokens_ref.shape
    high = width // ROW_BLOCKS
    copies = start_pieces(where_ref, pieces, group, packed_ref, sems)
    sums_ref[...] = jnp.zeros_like(sums_ref)
    for first in range(0, slots, CHUNK):
        here = slice(first, first + CHUNK)
        back_ref[here, :] = (cotangent_ref[here, :].astype(jnp.float32) * live_ref[here, :]).astype(
            jnp.bfloat16
        )
    for copy in copies:
        copy.wait()
    weight = jnp.concatenate([tile_of(packed_ref, half, 4 * high, high) for half in range(2)], axis=1)
    outer_ref[...] = weight
    for first in range(0, slots, CHUNK):
        here = slice(first, first + CHUNK)
        mixed = jnp.concatenate([ref[here, :] for ref in mixed_parts], axis=1)
        resid = tokens_ref[here, :].astype(jnp.float32) + (dot(mixed, weight) + params_ref[6:7, :])
        normal, _ = normal_of(resid)
        low = (normal * params_ref[2:3, :] + params_ref[3:4, :]).astype(jnp.bfloat16)
        low_ref[here, :] = low
        turned_ref[:, here] = low.T
        resid_ref[here, :] = resid
        total_ref[here, :] = resid + params_ref[7:8, :]
        two_ref[here, :] = jnp.zeros((CHUNK, width), jnp.float32)
    feed(0, packed_ref, params_ref, low_ref, turned_ref, back_ref, total_ref, two_ref, act_ref, pre_ref, bias_ref, grad_ref)
    sums_ref[8:10, :] = bias_ref[0:2, :]
    for copy in halves_out(grad_ref, where_ref[where_ref.shape[0] - 1], kept_ref, sent_ref, out_sems):
        copy.wait()


def second_kernel(group, count, where_ref, live_ref, params_ref, resid_in, total_in, two_in, back_ref, outer_ref, *refs):
    mixed_parts, pieces = refs[:count], refs[count:-18]
    (out_ref, resid_ref, mixed_grad_ref, kept_ref, sent_ref, sums_ref) = refs[-18:-12]
    (packed_ref, grad_ref, low_ref, turned_ref, total_ref, two_ref, act_ref, pre_ref, bias_ref, ratio_ref, sems, out_sems) = refs[-12:]
    slots, width = resid_in.shape
    high = width // ROW_BLOCKS
    copies = start_pieces(where_ref, pieces, group, packed_ref, sems)
    sums_ref[...] = jnp.zeros_like(sums_ref)
    for first in range(0, slots, CHUNK):
        here = slice(first, first + CHUNK)
        normal, ratio = normal_of(resid_in[here, :])
        low = (normal * params_ref[2:3, :] + params_ref[3:4, :]).astype(jnp.bfloat16)
        low_ref[here, :] = low
        turned_ref[:, here] = low.T
        resid_ref[here, :] = normal
        ratio_ref[here, :] = ratio
        total_ref[here, :] = total_in[here, :]
        two_ref[here, :] = two_in[here, :]
    for copy in copies:
        copy.wait()
    feed(1, packed_ref, params_ref, low_ref, turned_ref, back_ref, total_ref, two_ref, act_ref, pre_ref, bias_ref, grad_ref)
    sums_ref[10:12, :] = bias_ref[0:2, :]
    weight = outer_ref[...]
    for first in range(0, slots, CHUNK):
        here = slice(first, first + CHUNK)
        normal = resid_ref[here, :]
        two = two_ref[here, :]
        back = back_ref[here, :].astype(jnp.float32)
        grad = back + normal_back(normal, ratio_ref[here, :], two * params_ref[2:3, :])
        low = grad.astype(jnp.bfloat16)
        sums_ref[2:3, :] += jnp.sum(two * normal, axis=0, keepdims=True)
        sums_ref[3:4, :] += jnp.sum(two, axis=0, keepdims=True)
        sums_ref[6:7, :] += jnp.sum(low.astype(jnp.float32), axis=0, keepdims=True)
        sums_ref[7:8, :] += jnp.sum(back, axis=0, keepdims=True)
        resid_ref[here, :] = grad
        act_ref[here, :] = low
        mixed_grad_ref[here, :] = dot(low, weight, NT).astype(jnp.bfloat16)
        out_ref[here, :] = (total_ref[here, :] * live_ref[here, :]).astype(jnp.bfloat16)
    mixed = jnp.concatenate([ref[...] for ref in mixed_parts], axis=1)
    outer_grad = dot(mixed, act_ref[...], TN).astype(jnp.bfloat16)
    for side in range(2):
        grad_ref[side, :, 4 * high : 5 * high, :] = outer_grad[
            :, side * TILE : (side + 1) * TILE
        ].reshape(ROW_BLOCKS, high, TILE)
    for copy in halves_out(grad_ref, where_ref[where_ref.shape[0] - 1], kept_ref, sent_ref, out_sems):
        copy.wait()


def middle(kernel, name, in_vmem, mixed, sources, where, outs, rows, weight_rows, extra, group):
    slots, width = mixed[0].shape[0], in_vmem[1].shape[1]
    vmem, anywhere = pl.BlockSpec(memory_space=pltpu.VMEM), pl.BlockSpec(memory_space=pl.ANY)
    half = jax.ShapeDtypeStruct((ROW_BLOCKS, rows, TILE), jnp.bfloat16)
    low = pltpu.VMEM((slots, width), jnp.bfloat16)
    return pl.pallas_call(
        functools.partial(kernel, group, len(mixed)),
        in_specs=[pl.BlockSpec(memory_space=pltpu.SMEM)]
        + [vmem] * (len(in_vmem) + len(mixed))
        + [anywhere] * len(sources),
        out_specs=[vmem] * len(outs) + [anywhere] * 2 + [vmem],
        out_shape=outs + [half, half, jax.ShapeDtypeStruct((16, width), jnp.float32)],
        scratch_shapes=[
            pltpu.VMEM((2, ROW_BLOCKS, weight_rows, TILE), jnp.bfloat16),
            pltpu.VMEM((2, ROW_BLOCKS, rows, TILE), jnp.bfloat16),
            low,
            pltpu.VMEM((width, slots), jnp.bfloat16),
        ]
        + [pltpu.VMEM((slots, width), jnp.float32)] * extra
        + [low, low, pltpu.VMEM((8, width), jnp.float32)]
        + [pltpu.VMEM((slots, 1), jnp.float32)] * (extra // 2)
        + [
            pltpu.SemaphoreType.DMA((copy_count(sources, group),)),
            pltpu.SemaphoreType.DMA((2,)),
        ],
        compiler_params=compiler(60),
        cost_estimate=cost(27 * slots * width * width, 40 * slots * width),
        name=name,
    )(where, *in_vmem, *mixed, *sources)


def inner_kernel(where_ref, turned_ref, *refs):
    grads, (kept_ref, sent_ref, sums_ref, grad_ref, sems) = refs[:-5], refs[-5:]
    width = turned_ref.shape[0]
    high = width // ROW_BLOCKS
    turned = turned_ref[...]
    sums_ref[...] = jnp.zeros_like(sums_ref)
    for part in range(3):
        values = jnp.concatenate([ref[part] for ref in grads], axis=1)
        grad = dot(turned, values).astype(jnp.bfloat16)
        for side in range(2):
            t = 2 * part + side
            grad_ref[t // 3, :, t % 3 * high : (t % 3 + 1) * high, :] = grad[
                :, side * TILE : (side + 1) * TILE
            ].reshape(ROW_BLOCKS, high, TILE)
        if part != 1:
            row = 4 if part == 0 else 5
            sums_ref[row : row + 1, :] = jnp.sum(values.astype(jnp.float32), axis=0, keepdims=True)
    for copy in halves_out(grad_ref, where_ref[where_ref.shape[0] - 1], kept_ref, sent_ref, sems):
        copy.wait()


def inner_gradient(where, turned, grads):
    width, slots = turned.shape
    rows = 3 * (width // ROW_BLOCKS)
    vmem, anywhere = pl.BlockSpec(memory_space=pltpu.VMEM), pl.BlockSpec(memory_space=pl.ANY)
    half = jax.ShapeDtypeStruct((ROW_BLOCKS, rows, TILE), jnp.bfloat16)
    return pl.pallas_call(
        inner_kernel,
        in_specs=[pl.BlockSpec(memory_space=pltpu.SMEM)] + [vmem] * (1 + len(grads)),
        out_specs=[anywhere, anywhere, vmem],
        out_shape=[half, half, jax.ShapeDtypeStruct((16, width), jnp.float32)],
        scratch_shapes=[
            pltpu.VMEM((2, ROW_BLOCKS, rows, TILE), jnp.bfloat16),
            pltpu.SemaphoreType.DMA((2,)),
        ],
        compiler_params=compiler(40),
        cost_estimate=cost(6 * slots * width * width, 8 * slots * width),
        name="inner_gradient",
    )(where, turned, *grads)


def input_kernel(tokens_ref, params_ref, packed_ref, resid_ref, *refs):
    grads, (out_ref, sums_ref) = refs[:-2], refs[-2:]
    slots, width = tokens_ref.shape
    high = width // ROW_BLOCKS
    sums_ref[...] = jnp.zeros_like(sums_ref)
    weights = [
        jnp.concatenate(
            [tile_of(packed_ref, t // 3, t % 3 * high, high) for t in (2 * part, 2 * part + 1)], axis=1
        )
        for part in range(3)
    ]
    for first in range(0, slots, CHUNK):
        here = slice(first, first + CHUNK)
        grad = jnp.zeros((CHUNK, width), jnp.float32)
        for part in range(3):
            values = jnp.concatenate([ref[part, here, :] for ref in grads], axis=1)
            grad = grad + dot(values, weights[part], NT)
        normal, ratio = normal_of(tokens_ref[here, :].astype(jnp.float32))
        sums_ref[0:1, :] += jnp.sum(grad * normal, axis=0, keepdims=True)
        sums_ref[1:2, :] += jnp.sum(grad, axis=0, keepdims=True)
        out_ref[here, :] = resid_ref[here, :] + normal_back(normal, ratio, grad * params_ref[0:1, :])


def input_gradient(tokens, params, packed, grads, resid):
    slots, width = tokens.shape
    vmem = pl.BlockSpec(memory_space=pltpu.VMEM)
    return pl.pallas_call(
        input_kernel,
        in_specs=[vmem] * (4 + len(grads)),
        out_specs=[vmem] * 2,
        out_shape=[
            jax.ShapeDtypeStruct((slots, width), jnp.float32),
            jax.ShapeDtypeStruct((16, width), jnp.float32),
        ],
        compiler_params=compiler(48),
        cost_estimate=cost(6 * slots * width * width, 16 * slots * width),
        name="input_gradient",
    )(tokens, params, packed, resid, *grads)


def gather_vector(master, ring):
    own = master.astype(jnp.bfloat16)
    group = ring.group
    parts = [own] + [ring.send_shard(own, step) for step in range(1, group)]
    stacked = jnp.stack(parts)
    order = (ring.z - jnp.arange(group)) % group
    return jnp.take(stacked, order, axis=0).reshape(group * own.shape[0], own.shape[1])


class VectorSum:
    def __init__(self, grad, ring):
        self.grad, self.ring = grad, ring
        self.flat = grad.reshape(ring.group, -1, 128) if ring.staged() else None

    def hop(self, bit):
        pairs = [(i, i ^ bit) for i in range(self.ring.data)]
        self.got = lax.ppermute(self.flat, "dp", pairs)

    def add(self, *others):
        self.flat = after(self.flat + after(self.got, *others))
        return self.flat

    def shards(self):
        ring = self.ring

        def shard_of(step):
            return lax.dynamic_index_in_dim(
                self.flat, (ring.z + step) % ring.group, 0, keepdims=False
            )

        self.arrived = [ring.send_shard(shard_of(step), step) for step in range(1, ring.group)]
        self.flat = shard_of(0)

    def finish(self, *others):
        if not self.ring.staged():
            whole = lax.psum_scatter(self.grad, "shard", scatter_dimension=0, tiled=True)
            return lax.psum(whole, "dp")
        arrived = lax.optimization_barrier((*self.arrived, *others))[: len(self.arrived)]
        done = self.flat
        for value in arrived:
            done = done + value
        return done.reshape(self.grad.shape[0] // self.ring.group, self.grad.shape[1])


def on_device(
    tokens,
    cotangent,
    seq_lengths,
    seq_owner,
    attend_master,
    expand_master,
    project_master,
    vector_master,
    attend_mean,
    expand_mean,
    project_mean,
    vector_mean,
    attend_square,
    expand_square,
    project_square,
    vector_square,
):
    ring = Ring()
    slots, width = tokens.shape
    high = width // ROW_BLOCKS
    staged = ring.staged()
    masters = (attend_master, expand_master, project_master)
    if not staged:
        masters = tuple(
            lax.all_gather(m.astype(jnp.bfloat16), "shard", axis=0, tiled=True) for m in masters
        )
    tall = masters[0].shape[0]

    def pack_group(parity, tie):
        attend, expand, project = lax.optimization_barrier((*masters, tie))[:3] if staged else masters
        parts = [
            (expand, hidden_of(parity), high, [0], tall),
            (project, halves_of(0, 1), 2 * high, starts_of(project.shape[0], parity), TILE),
        ]
        if parity == 0:
            parts.append((attend, halves_of(3 * width, 1), high, [0], tall))
        return pack(parts)

    own_inner = pack([(masters[0], halves_of(0, 3), high, [0], tall)])
    vector = gather_vector(vector_master, ring).astype(jnp.float32)
    device = lax.axis_index("dp") * ring.group + ring.z
    segment = slot_segments(seq_lengths, seq_owner, device, slots)
    live = (segment >= 0).astype(jnp.float32)[:, None]
    hidden_bias = vector[:, 8:].reshape(2, 2, 2, TILE).transpose(2, 0, 1, 3).reshape(4, width)
    params = jnp.concatenate(
        [vector[:, :8].T, hidden_bias, jnp.zeros((4, width), jnp.float32)]
    )
    rows = tokens
    if staged:
        inner_part = Gather(own_inner, ring)
        far = inner_part.foreign()
        inner_part.plane(True)
        even_part = Gather(pack_group(0, far), ring)
        inner_part.cores()
        far = even_part.foreign(*inner_part.other)
        even_part.plane(False)
        odd_part = Gather(pack_group(1, far), ring)
        rows = after(tokens, far)
        inner_sources = inner_part.sources()
        inner_where = where_array(inner_part.places(), ring)
    else:
        inner_sources, inner_where = [own_inner], where_array([(None, 0)], ring)
    projected, turned, inner = project_rows(rows, params, inner_sources, inner_where, ring.group)
    if staged:
        projected = after(projected, even_part.mine[2])
    half = HEADS // 4
    mixed, logs = [None, None], [None, None]
    mixed[0], logs[0] = attention(projected, segment, 0, half)
    later = projected
    if staged:
        even_part.cores(mixed[0])
        far = odd_part.foreign(mixed[0])
        odd_part.plane(False)
        later = after(projected, *even_part.mine, far)
    mixed[1], logs[1] = attention(later, segment, half, half)
    if staged:
        odd_part.cores(mixed[1])
        even_sources, even_where = even_part.sources(), where_array(even_part.places(), ring)
        odd_sources, odd_where = odd_part.sources(), where_array(odd_part.places(), ring)
        mixed[0] = after(mixed[0], *odd_part.mine)
    else:
        even_sources, even_where = [pack_group(0, None)], inner_where
        odd_sources, odd_where = [pack_group(1, None)], inner_where
    low = jax.ShapeDtypeStruct((slots, width), jnp.bfloat16)
    wide = jax.ShapeDtypeStruct((slots, width), jnp.float32)
    square = jax.ShapeDtypeStruct((width, width), jnp.bfloat16)
    resid, total, two, back, outer, *even_halves, even_sums = middle(
        first_kernel,
        "first_half",
        [tokens, cotangent, live, params],
        mixed,
        even_sources,
        even_where,
        [wide, wide, wide, low, square],
        4 * high,
        5 * high,
        0,
        ring.group,
    )
    if staged:
        even = Sum(*even_halves, ring)
    layer_output, grad_resid, grad_mixed, *odd_halves, odd_sums = middle(
        second_kernel,
        "second_half",
        [live, params, resid, total, two, back, outer],
        mixed,
        odd_sources,
        odd_where,
        [low, wide, low],
        5 * high,
        4 * high,
        2,
        ring.group,
    )
    if staged:
        odd = Sum(*odd_halves, ring)
        level = even.chip(False, grad_mixed)
        grad_mixed = after(grad_mixed, level)
    part = HEADS // 6
    grads = [attention_back(projected, grad_mixed, logs[0], 0, segment, 0, part)]
    back_logs = jnp.concatenate([logs[0][part:], logs[1][: 2 * part - half]])
    if staged:
        level = even.halfway(grads[0])
        grad_mixed = after(grad_mixed, level, odd.chip(False, grads[0]))
    grads.append(attention_back(projected, grad_mixed, back_logs, 0, segment, part, part))
    if staged:
        level = even.plane(grads[1])
        grad_mixed = after(grad_mixed, level, odd.halfway(grads[1]))
    grads.append(attention_back(projected, grad_mixed, logs[1], 2 * part - half, segment, 2 * part, part))
    if staged:
        even_done = even.finish(grads[2])
        turned = after(turned, even_done, odd.plane(grads[2]))
    *inner_halves, inner_sums = inner_gradient(inner_where, turned, grads)
    last = grads
    if staged:
        tail = Sum(*inner_halves, ring)
        last = grads[:2] + [after(grads[2], inner_sums)]
    input_grad, input_sums = input_gradient(tokens, params, inner, last, grad_resid)
    sums = even_sums + odd_sums + inner_sums + input_sums
    hidden_sum = sums[8:12].reshape(2, 2, 2, TILE).transpose(1, 2, 0, 3).reshape(width, 4)
    vector_grad = jnp.concatenate([sums[:8].T, hidden_sum], axis=1)
    vector_part = VectorSum(vector_grad, ring)
    if staged:
        vector_part.hop(1)
        level = tail.chip(True, input_sums)
        odd_done = odd.finish(level)
        level = vector_part.add(odd_done)
        vector_part.hop(2)
        level = tail.plane(level)
        rest_part = Spread(after(jnp.concatenate([even_done, odd_done]), level), ring, False)
        tail_done = tail.finish(vector_part.add(rest_part.mine[0]))
        vector_part.hop(4)
        tail_part = Spread(tail_done, ring, True)
        rest_sum = rest_part.cores(tail_part.mine[0])
        level = vector_part.add(tail_part.mine[0])
        vector_part.shards()
        expand_sum, project_sum = place_sums(
            [rest_sum],
            [expand_master.shape, project_master.shape],
            [
                [(0, 4 * high * parity, hidden_of(parity), high, 0) for parity in range(2)],
                [
                    (0, 4 * high * parity + 2 * high, halves_of(0, 1), 2 * high, parity * TILE)
                    for parity in range(2)
                ],
            ],
        )
        expand_state = adam(
            expand_master,
            expand_mean,
            expand_square,
            expand_sum.astype(jnp.float32),
            RATE_MATRIX,
            DECAY_MATRIX,
        )
        tail_sum = tail_part.cores(level, expand_state[0])
        (attend_sum,) = place_sums(
            [tail_sum, rest_sum],
            [attend_master.shape],
            [
                [
                    (0, 0, halves_of(0, 3), high, 0),
                    (1, 8 * high, halves_of(3 * width, 1), high, 0),
                ]
            ],
        )
    else:
        plain = plain_gradients(even_halves, odd_halves, inner_halves, ring.core, high)
        attend_sum, expand_sum, project_sum = (
            lax.psum(lax.psum_scatter(g, "shard", scatter_dimension=0, tiled=True), "dp")
            for g in plain
        )
        expand_state = adam(
            expand_master, expand_mean, expand_square, expand_sum, RATE_MATRIX, DECAY_MATRIX
        )
    attend_sum, project_sum = attend_sum.astype(jnp.float32), project_sum.astype(jnp.float32)
    attend_state = adam(
        attend_master, attend_mean, attend_square, attend_sum, RATE_MATRIX, DECAY_MATRIX
    )
    project_state = adam(
        project_master, project_mean, project_square, project_sum, RATE_MATRIX, DECAY_MATRIX
    )
    vector_sum = vector_part.finish()
    vector_state = adam(vector_master, vector_mean, vector_square, vector_sum, RATE_VECTOR, 0.0)
    return (
        layer_output,
        input_grad,
        attend_state[0],
        expand_state[0],
        project_state[0],
        vector_state[0],
        attend_state[1],
        expand_state[1],
        project_state[1],
        vector_state[1],
        attend_state[2],
        expand_state[2],
        project_state[2],
        vector_state[2],
    )


def solution(mesh):
    return jax.shard_map(
        on_device,
        mesh=mesh,
        in_specs=(
            P(("dp", "shard"), None),
            P(("dp", "shard"), None),
            P(),
            P(),
            P("shard", None),
            P("shard", None),
            P("shard", None),
            P("shard", None),
            P("shard", None),
            P("shard", None),
            P("shard", None),
            P("shard", None),
            P("shard", None),
            P("shard", None),
            P("shard", None),
            P("shard", None),
        ),
        out_specs=(
            P(("dp", "shard"), None),
            P(("dp", "shard"), None),
            P("shard", None),
            P("shard", None),
            P("shard", None),
            P("shard", None),
            P("shard", None),
            P("shard", None),
            P("shard", None),
            P("shard", None),
            P("shard", None),
            P("shard", None),
            P("shard", None),
            P("shard", None),
        ),
        check_vma=False,
    )
```

```python
import functools
import math

import jax
import jax.numpy as jnp
from jax import lax
from jax.experimental import pallas as pl
from jax.experimental.pallas import tpu as pltpu
from jax.sharding import PartitionSpec as P

HEADS = 12
HEAD_DIM = 64
STEP = 10


NORM_EPS = 1e-05
MASK_FILL = -1e30
BETA_ONE = 0.9
BETA_TWO = 0.999
ADAM_EPS = 1e-08
RATE_MATRIX = 0.05
RATE_VECTOR = 0.3
DECAY_MATRIX = 0.01
BLOCK = 256
NT = (((1,), (1,)), ((), ()))
TN = (((0,), (0,)), ((), ()))


def slot_segments(seq_lengths, seq_owner, device, slots):
    mine = seq_owner == device
    owned = jnp.where(mine, seq_lengths, 0)
    starts = jnp.cumsum(owned) - owned
    place = jnp.arange(slots, dtype=jnp.int32)[:, None]
    inside = mine[None, :] & (place >= starts[None, :]) & (place < (starts + owned)[None, :])
    labels = jnp.arange(seq_lengths.shape[0], dtype=jnp.int32)[None, :] + 1
    return jnp.sum(jnp.where(inside, labels, 0), axis=1) - 1


def dot(a, b, dims=(((1,), (0,)), ((), ()))):
    return lax.dot_general(a, b, dims, preferred_element_type=jnp.float32)


def mask_of(column, row, first, end, start):
    later = lax.broadcasted_iota(jnp.int32, (end - first, end - start), 0) + first
    earlier = lax.broadcasted_iota(jnp.int32, (end - first, end - start), 1) + start
    return (column == row) & (earlier <= later)


def forward_kernel(column_ref, row_ref, q_ref, k_ref, v_ref, mixed_ref, log_ref):
    slots = q_ref.shape[0]
    scale = HEAD_DIM**-0.5
    low = lax.broadcasted_iota(jnp.int32, (1, 128), 1) < HEAD_DIM
    for index in range(slots // BLOCK):
        first, end = index * BLOCK, (index + 1) * BLOCK
        start = max(0, first - 512)
        ok = mask_of(column_ref[first:end, :], row_ref[:, start:end], first, end, start)
        q = q_ref[first:end, :]
        k = k_ref[start:end, :]
        v = v_ref[start:end, :]
        mixed, logs = [], []
        for head in range(2):
            mine = low if head == 0 else ~low
            s = dot(jnp.where(mine, q, jnp.zeros_like(q)), k, NT) * scale
            s = jnp.where(ok, s, MASK_FILL)
            top = jnp.max(s, axis=1, keepdims=True)
            e = jnp.exp(s - top)
            total = jnp.sum(e, axis=1, keepdims=True)
            p = (e * (1.0 / total)).astype(jnp.bfloat16)
            mixed.append(dot(p, v))
            logs.append(top + jnp.log(total))
        mixed_ref[first:end, :] = jnp.where(low, mixed[0], mixed[1]).astype(jnp.bfloat16)
        log_ref[0, first:end, :] = jnp.concatenate(logs, axis=1)


def backward_kernel(column_ref, row_ref, q_ref, k_ref, v_ref, g_ref, log_ref, out_ref, ka, va):
    slots = q_ref.shape[0]
    scale = HEAD_DIM**-0.5
    low = lax.broadcasted_iota(jnp.int32, (1, 128), 1) < HEAD_DIM
    ka[...] = jnp.zeros_like(ka)
    va[...] = jnp.zeros_like(va)
    for index in range(slots // BLOCK):
        first, end = index * BLOCK, (index + 1) * BLOCK
        start = max(0, first - 512)
        ok = mask_of(column_ref[first:end, :], row_ref[:, start:end], first, end, start)
        q = q_ref[first:end, :]
        g = g_ref[first:end, :]
        k = k_ref[start:end, :]
        v = v_ref[start:end, :]
        dq, dk, dv = [], [], []
        for head in range(2):
            mine = low if head == 0 else ~low
            s = dot(jnp.where(mine, q, jnp.zeros_like(q)), k, NT) * scale
            p = jnp.exp(jnp.where(ok, s - log_ref[0, first:end, head : head + 1], MASK_FILL))
            dp = dot(jnp.where(mine, g, jnp.zeros_like(g)), v, NT)
            w = p * dp
            ds = (w - p * jnp.sum(w, axis=1, keepdims=True)).astype(jnp.bfloat16)
            dq.append(dot(ds, k))
            dk.append(dot(ds, q, TN))
            dv.append(dot(p.astype(jnp.bfloat16), g, TN))
        out_ref[0, first:end, :] = (jnp.where(low, dq[0], dq[1]) * scale).astype(jnp.bfloat16)
        ka[start:end, :] += jnp.where(low, dk[0], dk[1])
        va[start:end, :] += jnp.where(low, dv[0], dv[1])
    out_ref[1] = (ka[...] * scale).astype(jnp.bfloat16)
    out_ref[2] = va[...].astype(jnp.bfloat16)


def columns(offset, slots):
    return pl.BlockSpec((slots, 128), lambda pair: (0, pair + offset))


def whole(shape):
    return pl.BlockSpec(shape, lambda pair: (0, 0))


def attention(projected, segment, first, count):
    slots = projected.shape[0]
    pairs = HEADS // 2
    return pl.pallas_call(
        forward_kernel,
        grid=(count,),
        in_specs=[whole((slots, 1)), whole((1, slots))] + [columns(pairs * n + first, slots) for n in range(3)],
        out_specs=[columns(0, slots), pl.BlockSpec((1, slots, 2), lambda pair: (pair, 0, 0))],
        out_shape=[
            jax.ShapeDtypeStruct((slots, count * 128), jnp.bfloat16),
            jax.ShapeDtypeStruct((count, slots, 2), jnp.float32),
        ],
        compiler_params=pltpu.CompilerParams(vmem_limit_bytes=48 * 1024 * 1024),
        cost_estimate=cost(2 * slots * slots * count * 256, 8 * slots * count * 128),
        name="attention",
    )(segment[:, None], segment[None, :], projected, projected, projected)


def attention_back(projected, grad_mixed, logs, log_first, segment, first, count):
    slots = projected.shape[0]
    pairs = HEADS // 2
    return pl.pallas_call(
        backward_kernel,
        grid=(count,),
        in_specs=[whole((slots, 1)), whole((1, slots))]
        + [columns(pairs * n + first, slots) for n in range(3)]
        + [columns(first, slots), pl.BlockSpec((1, slots, 2), lambda pair: (pair + log_first, 0, 0))],
        out_specs=pl.BlockSpec((3, slots, 128), lambda pair: (0, 0, pair)),
        out_shape=jax.ShapeDtypeStruct((3, slots, count * 128), jnp.bfloat16),
        scratch_shapes=[pltpu.VMEM((slots, 128), jnp.float32)] * 2,
        compiler_params=pltpu.CompilerParams(vmem_limit_bytes=48 * 1024 * 1024),
        cost_estimate=cost(5 * slots * slots * count * 256, 16 * slots * count * 128),
        name="attention_back",
    )(segment[:, None], segment[None, :], projected, projected, projected, grad_mixed, logs)


def adam(master, mean, square, grad, rate, decay):
    mean_new = BETA_ONE * mean + (1.0 - BETA_ONE) * grad
    square_new = BETA_TWO * square + (1.0 - BETA_TWO) * grad * grad
    mean_hat = mean_new / (1.0 - BETA_ONE**STEP)
    square_hat = square_new / (1.0 - BETA_TWO**STEP)
    master_new = master - rate * (mean_hat / (jnp.sqrt(square_hat) + ADAM_EPS) + decay * master)
    return (mean_new, square_new, master_new)


class Ring:
    def __init__(self):
        self.group = lax.axis_size("shard")
        self.data = lax.axis_size("dp")
        self.plane = self.data // 2
        self.side = math.isqrt(self.plane)
        self.square = self.data == 2 * self.side * self.side
        self.z = lax.axis_index("shard")
        device = lax.axis_index("dp")
        self.core = device % 2
        chip = device // 2
        high, low = chip // self.side, chip % self.side
        straight = low * self.side + high
        crossed = high * self.side + low
        self.block = jnp.where(self.core == 0, straight, crossed)
        self.block_other = jnp.where(self.core == 0, crossed, straight)

    def staged(self):
        return self.side == 2 and self.square and self.group * self.plane == ROW_BLOCKS

    def send_core(self, value):
        return lax.ppermute(value, "dp", [(i, i ^ 1) for i in range(self.data)])

    def send_plane(self, value, step):
        side = self.side
        first, second = step // side, step % side
        pairs = []
        for device in range(self.data):
            core, chip = device % 2, device // 2
            high, low = chip // side, chip % side
            if core == 0:
                low, high = (low + first) % side, (high + second) % side
            else:
                high, low = (high + first) % side, (low + second) % side
            pairs.append((device, (high * side + low) * 2 + core))
        return lax.ppermute(value, "dp", pairs)

    def spread(self, value, direct):
        if direct:
            return [self.send_plane(value, step) for step in range(1, self.plane)]
        second, first = self.send_plane(value, 1), self.send_plane(value, 2)
        return [second, first, self.send_plane(first, 1)]

    def shifted(self, block, step):
        side = self.side
        first, second = step // side, step % side
        return (block // side + first) % side * side + (block % side + second) % side

    def back(self, block, step):
        side = self.side
        first, second = step // side, step % side
        return (block // side - first) % side * side + (block % side - second) % side

    def send_shard(self, value, step):
        group = self.group
        return lax.ppermute(value, "shard", [(i, (i + step) % group) for i in range(group)])


TILE = 384
ROW_BLOCKS = 16
CHUNK = 256


def compiler(megabytes):
    return pltpu.CompilerParams(vmem_limit_bytes=megabytes * 1024 * 1024)


def cost(flops, bytes_accessed):
    return pl.CostEstimate(flops=flops, bytes_accessed=bytes_accessed, transcendentals=0)


def halves_of(first, tiles):
    return [[first + (half * tiles + tile) * TILE for tile in range(tiles)] for half in range(2)]


def hidden_of(parity):
    return [[(4 * half + 2 * tile + parity) * TILE for tile in range(2)] for half in range(2)]


def starts_of(rows, parity):
    return [first + parity * TILE for first in range(0, rows, 2 * TILE)]


def pack_kernel(specs, *refs):
    out_ref = refs[-1]
    row = 0
    for (columns, high, starts, count), ref in zip(specs, refs[:-1], strict=True):
        for number, start in enumerate(starts):
            blocks = slice(number * (count // high), (number + 1) * (count // high))
            for half in range(2):
                for tile, column in enumerate(columns[half]):
                    part = ref[start : start + count, column : column + TILE].astype(jnp.bfloat16)
                    out_ref[half, blocks, row + tile * high : row + (tile + 1) * high, :] = part.reshape(
                        count // high, high, TILE
                    )
        row += len(columns[0]) * high


def pack(parts):
    blocks = len(parts[0][3]) * parts[0][4] // parts[0][2]
    rows = sum(len(part[1][0]) * part[2] for part in parts)
    vmem = pl.BlockSpec(memory_space=pltpu.VMEM)
    return pl.pallas_call(
        functools.partial(pack_kernel, [part[1:] for part in parts]),
        in_specs=[vmem] * len(parts),
        out_specs=vmem,
        out_shape=jax.ShapeDtypeStruct((2, blocks, rows, TILE), jnp.bfloat16),
        compiler_params=compiler(40),
        cost_estimate=cost(0, 12 * blocks * rows * TILE),
        name="pack",
    )(*[part[0] for part in parts])


def after(value, *others):
    return lax.optimization_barrier((value, *others))[0]


class Gather:
    def __init__(self, own, ring):
        self.own, self.ring = own, ring
        chunk = lax.dynamic_index_in_dim(
            lax.dynamic_index_in_dim(own, ring.core, 0, keepdims=False),
            ring.block,
            0,
            keepdims=False,
        )
        self.arrived = [ring.send_shard(chunk, step) for step in range(1, ring.group)]

    def foreign(self, *others):
        self.far = after(jnp.stack(self.arrived), *others)
        return self.far

    def plane(self, direct):
        self.mine = [self.far] + self.ring.spread(self.far, direct)

    def cores(self, *others):
        ring = self.ring
        self.mine = list(lax.optimization_barrier((*self.mine, *others))[: ring.plane])
        self.other = [ring.send_core(value) for value in self.mine]

    def sources(self):
        return [self.own] + self.mine + self.other

    def places(self):
        ring = self.ring
        steps = range(ring.plane)
        places = [(None, ring.z * self.own.shape[1])]
        places += [(ring.core, ring.back(ring.block, step)) for step in steps]
        return places + [(1 - ring.core, ring.back(ring.block_other, step)) for step in steps]


def where_array(places, ring):
    scalars = [ring.z]
    for half, block in places:
        scalars += [0 if half is None else half, block]
    scalars.append(ring.core)
    return jnp.stack([jnp.asarray(v, jnp.int32) for v in scalars])


def copy_count(sources, group):
    return 1 if len(sources) == 1 else 2 + (len(sources) - 1) * (group - 1)


def start_pieces(where_ref, refs, group, out_ref, sems):
    copies = []

    def begin(source, target):
        copy = pltpu.make_async_copy(source, target, sems.at[len(copies)])
        copy.start()
        copies.append(copy)

    if len(refs) == 1:
        begin(refs[0], out_ref)
        return copies
    blocks = refs[0].shape[1]
    first = where_ref[2]
    for half in range(2):
        begin(refs[0].at[half], out_ref.at[half, pl.ds(first, blocks)])
    for number, ref in enumerate(refs[1:], 1):
        half, block = where_ref[1 + 2 * number], where_ref[2 + 2 * number]
        for step in range(1, group):
            source = lax.rem(where_ref[0] - step + group, group)
            begin(ref.at[step - 1], out_ref.at[half, source * blocks + block])
    return copies


class Sum:
    def __init__(self, kept, sent, ring):
        self.ring, self.kept = ring, kept
        self.got = ring.send_core(sent)

    def chip(self, direct, *others):
        ring = self.ring
        kept = after(self.kept, *others)
        chip = (kept.astype(jnp.float32) + self.got.astype(jnp.float32)).astype(jnp.bfloat16)
        rows = chip.shape[1]
        self.direct = direct
        if direct:
            chip = lax.optimization_barrier(chip.reshape(ring.group, ring.plane, rows, TILE))

            def block_of(step):
                return lax.dynamic_index_in_dim(
                    chip, ring.shifted(ring.block, step), 1, keepdims=False
                )

            self.arrived = [ring.send_plane(block_of(step), step) for step in range(1, ring.plane)]
            self.level = block_of(0)
            return self.level
        chip = lax.optimization_barrier(chip.reshape(ring.group, 2, 2 * rows, TILE))
        mine = ring.block // 2
        away = lax.dynamic_index_in_dim(chip, 1 - mine, 1, keepdims=False)
        self.arrived = [ring.send_plane(away, 2)]
        self.level = lax.dynamic_index_in_dim(chip, mine, 1, keepdims=False)
        return self.level

    def halfway(self, *others):
        ring = self.ring
        level = after(self.level, *others).astype(jnp.float32) + self.arrived[0].astype(jnp.float32)
        rows = level.shape[1] // 2
        level = lax.optimization_barrier(
            level.astype(jnp.bfloat16).reshape(ring.group, 2, rows, TILE)
        )
        mine = ring.block % 2
        away = lax.dynamic_index_in_dim(level, 1 - mine, 1, keepdims=False)
        self.arrived = [ring.send_plane(away, 1)]
        self.level = lax.dynamic_index_in_dim(level, mine, 1, keepdims=False)
        return self.level

    def plane(self, *others):
        ring = self.ring
        level = after(self.level, *others).astype(jnp.float32)
        for value in self.arrived:
            level = level + value.astype(jnp.float32)
        level = lax.optimization_barrier(level.astype(jnp.bfloat16))

        def shard_of(step):
            return lax.dynamic_index_in_dim(
                level, (ring.z + step) % ring.group, 0, keepdims=False
            )

        self.arrived = [ring.send_shard(shard_of(step), step) for step in range(1, ring.group)]
        self.level = shard_of(0)
        return self.level

    def finish(self, *others):
        done = after(self.level, *others).astype(jnp.float32)
        for value in self.arrived:
            done = done + value.astype(jnp.float32)
        return done.astype(jnp.bfloat16)


class Spread:
    def __init__(self, piece, ring, direct):
        self.ring = ring
        piece = lax.optimization_barrier(piece)
        self.mine = [piece] + ring.spread(piece, direct)

    def cores(self, *others):
        ring = self.ring
        mine = after(jnp.stack(self.mine), *others)
        places = [(ring.core, ring.back(ring.block, step)) for step in range(ring.plane)]
        places += [(1 - ring.core, ring.back(ring.block_other, step)) for step in range(ring.plane)]
        return [mine, ring.send_core(mine)], places


def plain_gradients(even, odd, inner, core, high):
    def both(halves):
        kept, sent = (value.astype(jnp.float32) for value in halves)
        return jnp.stack([jnp.where(core == 0, kept, sent), jnp.where(core == 0, sent, kept)])

    def columns(packed, first, tiles):
        part = packed[:, :, first : first + tiles * high].reshape(2, ROW_BLOCKS, tiles, high, TILE)
        return part.transpose(1, 3, 0, 2, 4)

    even, odd, inner = both(even), both(odd), both(inner)
    width = ROW_BLOCKS * high
    expand = jnp.stack([columns(even, 0, 2), columns(odd, 0, 2)], axis=4).reshape(width, -1)
    deep = [
        packed[:, :, 2 * high : 4 * high].transpose(1, 2, 0, 3).reshape(4, TILE, width)
        for packed in (even, odd)
    ]
    project = jnp.stack(deep, axis=1).reshape(-1, width)
    attend = jnp.concatenate(
        [columns(inner, 0, 3).reshape(width, -1), columns(odd, 4 * high, 1).reshape(width, -1)], axis=1
    )
    return attend, expand, project


def place_kernel(matrices, count, where_ref, *refs):
    sources, outs = refs[: 2 * count], refs[2 * count : 2 * count + len(matrices)]
    packed, sems = refs[2 * count + len(matrices) : -1], refs[-1]
    plane = sources[0].shape[0]
    copies = []
    for number, ref in enumerate(sources):
        for block in range(plane):
            scalar = 2 * len(copies)
            place = packed[number // 2].at[where_ref[scalar], where_ref[scalar + 1]]
            copy = pltpu.make_async_copy(ref.at[block], place, sems.at[len(copies)])
            copy.start()
            copies.append(copy)
    for copy in copies:
        copy.wait()
    for kinds, out_ref in zip(matrices, outs, strict=True):
        for gradient, row, columns, high, first in kinds:
            for half in range(2):
                for tile, column in enumerate(columns[half]):
                    rows = slice(row + tile * high, row + (tile + 1) * high)
                    value = packed[gradient][half, :, rows, :].reshape(plane * high, TILE)
                    out_ref[first : first + plane * high, column : column + TILE] = value


def place_sums(gradients, shapes, matrices):
    sources = [source for group, _ in gradients for source in group]
    plane = sources[0].shape[0]
    scalars = [v for _, places in gradients for place in places for v in place]
    where = jnp.stack([jnp.asarray(v, jnp.int32) for v in scalars])
    return pl.pallas_call(
        functools.partial(place_kernel, matrices, len(gradients)),
        in_specs=[pl.BlockSpec(memory_space=pltpu.SMEM)]
        + [pl.BlockSpec(memory_space=pl.ANY)] * len(sources),
        out_specs=[pl.BlockSpec(memory_space=pltpu.VMEM)] * len(shapes),
        out_shape=[jax.ShapeDtypeStruct(shape, jnp.bfloat16) for shape in shapes],
        scratch_shapes=[
            pltpu.VMEM((2, plane) + group[0].shape[1:], jnp.bfloat16) for group, _ in gradients
        ]
        + [pltpu.SemaphoreType.DMA((len(sources) * plane,))],
        compiler_params=compiler(32),
        cost_estimate=cost(0, 4 * sum(rows * columns for rows, columns in shapes)),
        name="place_sums",
    )(where, *sources)


def tile_of(packed_ref, half, row, high):
    part = packed_ref[half, :, pl.ds(row, high), :]
    return part.reshape(ROW_BLOCKS * high, TILE)


def normal_of(rows):
    centre = jnp.mean(rows, axis=1, keepdims=True)
    centred = rows - centre
    spread = jnp.mean(centred * centred, axis=1, keepdims=True)
    ratio = lax.rsqrt(spread + NORM_EPS)
    return centred * ratio, ratio


def normal_back(normal, ratio, scaled):
    along = jnp.mean(scaled * normal, axis=1, keepdims=True)
    return ratio * (scaled - jnp.mean(scaled, axis=1, keepdims=True) - normal * along)


def project_kernel(group, where_ref, tokens_ref, params_ref, *refs):
    pieces, (out_ref, turned_ref, packed_ref, sems) = refs[:-4], refs[-4:]
    slots, width = tokens_ref.shape
    high = width // ROW_BLOCKS
    copies = start_pieces(where_ref, pieces, group, packed_ref, sems)
    lows = []
    for first in range(0, slots, CHUNK):
        normal, _ = normal_of(tokens_ref[first : first + CHUNK, :].astype(jnp.float32))
        low = (normal * params_ref[0:1, :] + params_ref[1:2, :]).astype(jnp.bfloat16)
        turned_ref[:, first : first + CHUNK] = low.T
        lows.append(low)
    for copy in copies:
        copy.wait()
    for part in range(3):
        weight = jnp.concatenate(
            [tile_of(packed_ref, t // 3, t % 3 * high, high) for t in (2 * part, 2 * part + 1)], axis=1
        )
        for number, low in enumerate(lows):
            value = dot(low, weight)
            if part != 1:
                row = 4 if part == 0 else 5
                value = value + params_ref[row : row + 1, :]
            out_ref[number * CHUNK : (number + 1) * CHUNK, part * width : (part + 1) * width] = (
                value.astype(jnp.bfloat16)
            )


def project_rows(tokens, params, sources, where, group):
    slots, width = tokens.shape
    high = width // ROW_BLOCKS
    vmem = pl.BlockSpec(memory_space=pltpu.VMEM)
    return pl.pallas_call(
        functools.partial(project_kernel, group),
        in_specs=[pl.BlockSpec(memory_space=pltpu.SMEM), vmem, vmem]
        + [pl.BlockSpec(memory_space=pl.ANY)] * len(sources),
        out_specs=[vmem] * 3,
        out_shape=[
            jax.ShapeDtypeStruct((slots, 3 * width), jnp.bfloat16),
            jax.ShapeDtypeStruct((width, slots), jnp.bfloat16),
            jax.ShapeDtypeStruct((2, ROW_BLOCKS, 3 * high, TILE), jnp.bfloat16),
        ],
        scratch_shapes=[pltpu.SemaphoreType.DMA((copy_count(sources, group),))],
        compiler_params=compiler(40),
        cost_estimate=cost(6 * slots * width * width, 16 * slots * width),
        name="project_rows",
    )(where, tokens, params, *sources)


def tail_of(values):
    size = jnp.abs(values) * (0.5**0.5)
    bell = jnp.exp(-0.5 * values * values)
    t = 1.0 / (1.0 + 0.5 * size)
    series = jnp.full_like(t, 0.17087277)
    for c in (
        -0.82215223, 1.48851587, -1.13520398, 0.27886807, -0.18628806, 0.09678418, 0.37409196, 1.00002368, -1.26551223,
    ):
        series = series * t + c
    tail = 0.5 * t * bell * jnp.exp(series)
    return bell, jnp.where(values > 0, 1.0 - tail, tail)


def halves_out(scratch_ref, core, kept_ref, sent_ref, sems):
    copies = [
        pltpu.make_async_copy(scratch_ref.at[core], kept_ref, sems.at[0]),
        pltpu.make_async_copy(scratch_ref.at[1 - core], sent_ref, sems.at[1]),
    ]
    for copy in copies:
        copy.start()
    return copies


def feed(parity, packed_ref, params_ref, low_ref, turned_ref, back_ref, total_ref, two_ref, act_ref, pre_ref, bias_ref, grad_ref):
    slots, width = low_ref.shape
    high = width // ROW_BLOCKS
    deep = slice(2 * high, 4 * high)

    def step(number, carry):
        wide = jnp.concatenate(
            [tile_of(packed_ref, number, tile * high, high) for tile in range(2)], axis=1
        )
        blocks = pl.ds(number * (ROW_BLOCKS // 2), ROW_BLOCKS // 2)
        deep_weight = jnp.concatenate(
            [packed_ref[side, blocks, deep, :].reshape(width, TILE) for side in range(2)], axis=1
        )
        bias = params_ref[pl.ds(8 + 2 * parity + number, 1), :]
        bias_sum = jnp.zeros((1, width), jnp.float32)
        for first in range(0, slots, CHUNK):
            here = slice(first, first + CHUNK)
            pre = dot(low_ref[here, :], wide) + bias
            bell, below = tail_of(pre)
            act = (pre * below).astype(jnp.bfloat16)
            act_ref[here, :] = act
            slope = below + pre * bell * 0.3989422804014327
            grad = (dot(back_ref[here, :], deep_weight, NT) * slope).astype(jnp.bfloat16)
            pre_ref[here, :] = grad
            bias_sum = bias_sum + jnp.sum(grad.astype(jnp.float32), axis=0, keepdims=True)
            total_ref[here, :] += dot(act, deep_weight)
            two_ref[here, :] += dot(grad, wide, NT)
        bias_ref[pl.ds(number, 1), :] = bias_sum
        expand_grad = dot(turned_ref[...], pre_ref[...]).astype(jnp.bfloat16)
        project_grad = dot(act_ref[...], back_ref[...], TN).astype(jnp.bfloat16)
        for side in range(2):
            here = slice(side * TILE, (side + 1) * TILE)
            grad_ref[number, :, side * high : (side + 1) * high, :] = expand_grad[:, here].reshape(
                ROW_BLOCKS, high, TILE
            )
            grad_ref[side, blocks, deep, :] = project_grad[:, here].reshape(
                ROW_BLOCKS // 2, 2 * high, TILE
            )
        return carry

    lax.fori_loop(0, 2, step, 0)


def first_kernel(group, count, where_ref, tokens_ref, cotangent_ref, live_ref, params_ref, *refs):
    mixed_parts, pieces = refs[:count], refs[count:-17]
    (resid_ref, total_ref, two_ref, back_ref, outer_ref, kept_ref, sent_ref, sums_ref) = refs[-17:-9]
    (packed_ref, grad_ref, low_ref, turned_ref, act_ref, pre_ref, bias_ref, sems, out_sems) = refs[-9:]
    slots, width = tokens_ref.shape
    high = width // ROW_BLOCKS
    copies = start_pieces(where_ref, pieces, group, packed_ref, sems)
    sums_ref[...] = jnp.zeros_like(sums_ref)
    for first in range(0, slots, CHUNK):
        here = slice(first, first + CHUNK)
        back_ref[here, :] = (cotangent_ref[here, :].astype(jnp.float32) * live_ref[here, :]).astype(
            jnp.bfloat16
        )
    for copy in copies:
        copy.wait()
    weight = jnp.concatenate([tile_of(packed_ref, half, 4 * high, high) for half in range(2)], axis=1)
    outer_ref[...] = weight
    for first in range(0, slots, CHUNK):
        here = slice(first, first + CHUNK)
        mixed = jnp.concatenate([ref[here, :] for ref in mixed_parts], axis=1)
        resid = tokens_ref[here, :].astype(jnp.float32) + (dot(mixed, weight) + params_ref[6:7, :])
        normal, _ = normal_of(resid)
        low = (normal * params_ref[2:3, :] + params_ref[3:4, :]).astype(jnp.bfloat16)
        low_ref[here, :] = low
        turned_ref[:, here] = low.T
        resid_ref[here, :] = resid
        total_ref[here, :] = resid + params_ref[7:8, :]
        two_ref[here, :] = jnp.zeros((CHUNK, width), jnp.float32)
    feed(0, packed_ref, params_ref, low_ref, turned_ref, back_ref, total_ref, two_ref, act_ref, pre_ref, bias_ref, grad_ref)
    sums_ref[8:10, :] = bias_ref[0:2, :]
    for copy in halves_out(grad_ref, where_ref[where_ref.shape[0] - 1], kept_ref, sent_ref, out_sems):
        copy.wait()


def second_kernel(group, count, where_ref, live_ref, params_ref, resid_in, total_in, two_in, back_ref, outer_ref, *refs):
    mixed_parts, pieces = refs[:count], refs[count:-18]
    (out_ref, resid_ref, mixed_grad_ref, kept_ref, sent_ref, sums_ref) = refs[-18:-12]
    (packed_ref, grad_ref, low_ref, turned_ref, total_ref, two_ref, act_ref, pre_ref, bias_ref, ratio_ref, sems, out_sems) = refs[-12:]
    slots, width = resid_in.shape
    high = width // ROW_BLOCKS
    copies = start_pieces(where_ref, pieces, group, packed_ref, sems)
    sums_ref[...] = jnp.zeros_like(sums_ref)
    for first in range(0, slots, CHUNK):
        here = slice(first, first + CHUNK)
        normal, ratio = normal_of(resid_in[here, :])
        low = (normal * params_ref[2:3, :] + params_ref[3:4, :]).astype(jnp.bfloat16)
        low_ref[here, :] = low
        turned_ref[:, here] = low.T
        resid_ref[here, :] = normal
        ratio_ref[here, :] = ratio
        total_ref[here, :] = total_in[here, :]
        two_ref[here, :] = two_in[here, :]
    for copy in copies:
        copy.wait()
    feed(1, packed_ref, params_ref, low_ref, turned_ref, back_ref, total_ref, two_ref, act_ref, pre_ref, bias_ref, grad_ref)
    sums_ref[10:12, :] = bias_ref[0:2, :]
    weight = outer_ref[...]
    for first in range(0, slots, CHUNK):
        here = slice(first, first + CHUNK)
        normal = resid_ref[here, :]
        two = two_ref[here, :]
        back = back_ref[here, :].astype(jnp.float32)
        grad = back + normal_back(normal, ratio_ref[here, :], two * params_ref[2:3, :])
        low = grad.astype(jnp.bfloat16)
        sums_ref[2:3, :] += jnp.sum(two * normal, axis=0, keepdims=True)
        sums_ref[3:4, :] += jnp.sum(two, axis=0, keepdims=True)
        sums_ref[6:7, :] += jnp.sum(low.astype(jnp.float32), axis=0, keepdims=True)
        sums_ref[7:8, :] += jnp.sum(back, axis=0, keepdims=True)
        resid_ref[here, :] = grad
        act_ref[here, :] = low
        mixed_grad_ref[here, :] = dot(low, weight, NT).astype(jnp.bfloat16)
        out_ref[here, :] = (total_ref[here, :] * live_ref[here, :]).astype(jnp.bfloat16)
    mixed = jnp.concatenate([ref[...] for ref in mixed_parts], axis=1)
    outer_grad = dot(mixed, act_ref[...], TN).astype(jnp.bfloat16)
    for side in range(2):
        grad_ref[side, :, 4 * high : 5 * high, :] = outer_grad[
            :, side * TILE : (side + 1) * TILE
        ].reshape(ROW_BLOCKS, high, TILE)
    for copy in halves_out(grad_ref, where_ref[where_ref.shape[0] - 1], kept_ref, sent_ref, out_sems):
        copy.wait()


def middle(kernel, name, in_vmem, mixed, sources, where, outs, rows, weight_rows, extra, group):
    slots, width = mixed[0].shape[0], in_vmem[1].shape[1]
    vmem, anywhere = pl.BlockSpec(memory_space=pltpu.VMEM), pl.BlockSpec(memory_space=pl.ANY)
    half = jax.ShapeDtypeStruct((ROW_BLOCKS, rows, TILE), jnp.bfloat16)
    low = pltpu.VMEM((slots, width), jnp.bfloat16)
    return pl.pallas_call(
        functools.partial(kernel, group, len(mixed)),
        in_specs=[pl.BlockSpec(memory_space=pltpu.SMEM)]
        + [vmem] * (len(in_vmem) + len(mixed))
        + [anywhere] * len(sources),
        out_specs=[vmem] * len(outs) + [anywhere] * 2 + [vmem],
        out_shape=outs + [half, half, jax.ShapeDtypeStruct((16, width), jnp.float32)],
        scratch_shapes=[
            pltpu.VMEM((2, ROW_BLOCKS, weight_rows, TILE), jnp.bfloat16),
            pltpu.VMEM((2, ROW_BLOCKS, rows, TILE), jnp.bfloat16),
            low,
            pltpu.VMEM((width, slots), jnp.bfloat16),
        ]
        + [pltpu.VMEM((slots, width), jnp.float32)] * extra
        + [low, low, pltpu.VMEM((8, width), jnp.float32)]
        + [pltpu.VMEM((slots, 1), jnp.float32)] * (extra // 2)
        + [
            pltpu.SemaphoreType.DMA((copy_count(sources, group),)),
            pltpu.SemaphoreType.DMA((2,)),
        ],
        compiler_params=compiler(60),
        cost_estimate=cost(27 * slots * width * width, 40 * slots * width),
        name=name,
    )(where, *in_vmem, *mixed, *sources)


def inner_kernel(where_ref, turned_ref, *refs):
    grads, (kept_ref, sent_ref, sums_ref, grad_ref, sems) = refs[:-5], refs[-5:]
    width = turned_ref.shape[0]
    high = width // ROW_BLOCKS
    turned = turned_ref[...]
    sums_ref[...] = jnp.zeros_like(sums_ref)
    for part in range(3):
        values = jnp.concatenate([ref[part] for ref in grads], axis=1)
        grad = dot(turned, values).astype(jnp.bfloat16)
        for side in range(2):
            t = 2 * part + side
            grad_ref[t // 3, :, t % 3 * high : (t % 3 + 1) * high, :] = grad[
                :, side * TILE : (side + 1) * TILE
            ].reshape(ROW_BLOCKS, high, TILE)
        if part != 1:
            row = 4 if part == 0 else 5
            sums_ref[row : row + 1, :] = jnp.sum(values.astype(jnp.float32), axis=0, keepdims=True)
    for copy in halves_out(grad_ref, where_ref[where_ref.shape[0] - 1], kept_ref, sent_ref, sems):
        copy.wait()


def inner_gradient(where, turned, grads):
    width, slots = turned.shape
    rows = 3 * (width // ROW_BLOCKS)
    vmem, anywhere = pl.BlockSpec(memory_space=pltpu.VMEM), pl.BlockSpec(memory_space=pl.ANY)
    half = jax.ShapeDtypeStruct((ROW_BLOCKS, rows, TILE), jnp.bfloat16)
    return pl.pallas_call(
        inner_kernel,
        in_specs=[pl.BlockSpec(memory_space=pltpu.SMEM)] + [vmem] * (1 + len(grads)),
        out_specs=[anywhere, anywhere, vmem],
        out_shape=[half, half, jax.ShapeDtypeStruct((16, width), jnp.float32)],
        scratch_shapes=[
            pltpu.VMEM((2, ROW_BLOCKS, rows, TILE), jnp.bfloat16),
            pltpu.SemaphoreType.DMA((2,)),
        ],
        compiler_params=compiler(40),
        cost_estimate=cost(6 * slots * width * width, 8 * slots * width),
        name="inner_gradient",
    )(where, turned, *grads)


def input_kernel(tokens_ref, params_ref, packed_ref, resid_ref, *refs):
    grads, (out_ref, sums_ref) = refs[:-2], refs[-2:]
    slots, width = tokens_ref.shape
    high = width // ROW_BLOCKS
    sums_ref[...] = jnp.zeros_like(sums_ref)
    weights = [
        jnp.concatenate(
            [tile_of(packed_ref, t // 3, t % 3 * high, high) for t in (2 * part, 2 * part + 1)], axis=1
        )
        for part in range(3)
    ]
    for first in range(0, slots, CHUNK):
        here = slice(first, first + CHUNK)
        grad = jnp.zeros((CHUNK, width), jnp.float32)
        for part in range(3):
            values = jnp.concatenate([ref[part, here, :] for ref in grads], axis=1)
            grad = grad + dot(values, weights[part], NT)
        normal, ratio = normal_of(tokens_ref[here, :].astype(jnp.float32))
        sums_ref[0:1, :] += jnp.sum(grad * normal, axis=0, keepdims=True)
        sums_ref[1:2, :] += jnp.sum(grad, axis=0, keepdims=True)
        out_ref[here, :] = resid_ref[here, :] + normal_back(normal, ratio, grad * params_ref[0:1, :])


def input_gradient(tokens, params, packed, grads, resid):
    slots, width = tokens.shape
    vmem = pl.BlockSpec(memory_space=pltpu.VMEM)
    return pl.pallas_call(
        input_kernel,
        in_specs=[vmem] * (4 + len(grads)),
        out_specs=[vmem] * 2,
        out_shape=[
            jax.ShapeDtypeStruct((slots, width), jnp.float32),
            jax.ShapeDtypeStruct((16, width), jnp.float32),
        ],
        compiler_params=compiler(48),
        cost_estimate=cost(6 * slots * width * width, 16 * slots * width),
        name="input_gradient",
    )(tokens, params, packed, resid, *grads)


def gather_vector(master, ring):
    own = master.astype(jnp.bfloat16)
    group = ring.group
    parts = [own] + [ring.send_shard(own, step) for step in range(1, group)]
    stacked = jnp.stack(parts)
    order = (ring.z - jnp.arange(group)) % group
    return jnp.take(stacked, order, axis=0).reshape(group * own.shape[0], own.shape[1])


class VectorSum:
    def __init__(self, grad, ring):
        self.grad, self.ring = grad, ring
        self.flat = grad.reshape(ring.group, -1, 128) if ring.staged() else None

    def hop(self, bit):
        pairs = [(i, i ^ bit) for i in range(self.ring.data)]
        self.got = lax.ppermute(self.flat, "dp", pairs)

    def add(self, *others):
        self.flat = after(self.flat + after(self.got, *others))
        return self.flat

    def shards(self):
        ring = self.ring

        def shard_of(step):
            return lax.dynamic_index_in_dim(
                self.flat, (ring.z + step) % ring.group, 0, keepdims=False
            )

        self.arrived = [ring.send_shard(shard_of(step), step) for step in range(1, ring.group)]
        self.flat = shard_of(0)

    def finish(self, *others):
        if not self.ring.staged():
            whole = lax.psum_scatter(self.grad, "shard", scatter_dimension=0, tiled=True)
            return lax.psum(whole, "dp")
        arrived = lax.optimization_barrier((*self.arrived, *others))[: len(self.arrived)]
        done = self.flat
        for value in arrived:
            done = done + value
        return done.reshape(self.grad.shape[0] // self.ring.group, self.grad.shape[1])


def on_device(
    tokens,
    cotangent,
    seq_lengths,
    seq_owner,
    attend_master,
    expand_master,
    project_master,
    vector_master,
    attend_mean,
    expand_mean,
    project_mean,
    vector_mean,
    attend_square,
    expand_square,
    project_square,
    vector_square,
):
    ring = Ring()
    slots, width = tokens.shape
    high = width // ROW_BLOCKS
    staged = ring.staged()
    masters = (attend_master, expand_master, project_master)
    if not staged:
        masters = tuple(
            lax.all_gather(m.astype(jnp.bfloat16), "shard", axis=0, tiled=True) for m in masters
        )
    tall = masters[0].shape[0]

    def pack_group(parity, tie):
        attend, expand, project = lax.optimization_barrier((*masters, tie))[:3] if staged else masters
        parts = [
            (expand, hidden_of(parity), high, [0], tall),
            (project, halves_of(0, 1), 2 * high, starts_of(project.shape[0], parity), TILE),
        ]
        if parity == 0:
            parts.append((attend, halves_of(3 * width, 1), high, [0], tall))
        return pack(parts)

    own_inner = pack([(masters[0], halves_of(0, 3), high, [0], tall)])
    vector = gather_vector(vector_master, ring).astype(jnp.float32)
    device = lax.axis_index("dp") * ring.group + ring.z
    segment = slot_segments(seq_lengths, seq_owner, device, slots)
    live = (segment >= 0).astype(jnp.float32)[:, None]
    hidden_bias = vector[:, 8:].reshape(2, 2, 2, TILE).transpose(2, 0, 1, 3).reshape(4, width)
    params = jnp.concatenate(
        [vector[:, :8].T, hidden_bias, jnp.zeros((4, width), jnp.float32)]
    )
    rows = tokens
    if staged:
        inner_part = Gather(own_inner, ring)
        far = inner_part.foreign()
        inner_part.plane(True)
        even_part = Gather(pack_group(0, far), ring)
        inner_part.cores()
        far = even_part.foreign(*inner_part.other)
        even_part.plane(False)
        odd_part = Gather(pack_group(1, far), ring)
        rows = after(tokens, far)
        inner_sources = inner_part.sources()
        inner_where = where_array(inner_part.places(), ring)
    else:
        inner_sources, inner_where = [own_inner], where_array([(None, 0)], ring)
    projected, turned, inner = project_rows(rows, params, inner_sources, inner_where, ring.group)
    if staged:
        projected = after(projected, even_part.mine[2])
    half = HEADS // 4
    mixed, logs = [None, None], [None, None]
    mixed[0], logs[0] = attention(projected, segment, 0, half)
    later = projected
    if staged:
        even_part.cores(mixed[0])
        far = odd_part.foreign(mixed[0])
        odd_part.plane(False)
        later = after(projected, *even_part.mine, far)
    mixed[1], logs[1] = attention(later, segment, half, half)
    if staged:
        odd_part.cores(mixed[1])
        even_sources, even_where = even_part.sources(), where_array(even_part.places(), ring)
        odd_sources, odd_where = odd_part.sources(), where_array(odd_part.places(), ring)
        mixed[0] = after(mixed[0], *odd_part.mine)
    else:
        even_sources, even_where = [pack_group(0, None)], inner_where
        odd_sources, odd_where = [pack_group(1, None)], inner_where
    low = jax.ShapeDtypeStruct((slots, width), jnp.bfloat16)
    wide = jax.ShapeDtypeStruct((slots, width), jnp.float32)
    square = jax.ShapeDtypeStruct((width, width), jnp.bfloat16)
    resid, total, two, back, outer, *even_halves, even_sums = middle(
        first_kernel,
        "first_half",
        [tokens, cotangent, live, params],
        mixed,
        even_sources,
        even_where,
        [wide, wide, wide, low, square],
        4 * high,
        5 * high,
        0,
        ring.group,
    )
    if staged:
        even = Sum(*even_halves, ring)
    layer_output, grad_resid, grad_mixed, *odd_halves, odd_sums = middle(
        second_kernel,
        "second_half",
        [live, params, resid, total, two, back, outer],
        mixed,
        odd_sources,
        odd_where,
        [low, wide, low],
        5 * high,
        4 * high,
        2,
        ring.group,
    )
    if staged:
        odd = Sum(*odd_halves, ring)
        level = even.chip(False, grad_mixed)
        grad_mixed = after(grad_mixed, level)
    part = HEADS // 6
    grads = [attention_back(projected, grad_mixed, logs[0], 0, segment, 0, part)]
    back_logs = jnp.concatenate([logs[0][part:], logs[1][: 2 * part - half]])
    if staged:
        level = even.halfway(grads[0])
        grad_mixed = after(grad_mixed, odd.chip(False, grads[0], level))
    grads.append(attention_back(projected, grad_mixed, back_logs, 0, segment, part, part))
    if staged:
        level = even.plane(grads[1])
        grad_mixed = after(grad_mixed, level, odd.halfway(grads[1]))
    grads.append(attention_back(projected, grad_mixed, logs[1], 2 * part - half, segment, 2 * part, part))
    if staged:
        even_done = even.finish(grads[2])
        turned = after(turned, even_done, odd.plane(grads[2]))
    *inner_halves, inner_sums = inner_gradient(inner_where, turned, grads)
    last = grads
    if staged:
        tail = Sum(*inner_halves, ring)
        last = grads[:2] + [after(grads[2], inner_sums)]
    input_grad, input_sums = input_gradient(tokens, params, inner, last, grad_resid)
    sums = even_sums + odd_sums + inner_sums + input_sums
    hidden_sum = sums[8:12].reshape(2, 2, 2, TILE).transpose(1, 2, 0, 3).reshape(width, 4)
    vector_grad = jnp.concatenate([sums[:8].T, hidden_sum], axis=1)
    vector_part = VectorSum(vector_grad, ring)
    if staged:
        vector_part.hop(1)
        level = tail.chip(True, input_sums)
        odd_done = odd.finish(level)
        level = vector_part.add(odd_done)
        vector_part.hop(2)
        level = tail.plane(level)
        rest_part = Spread(after(jnp.concatenate([even_done, odd_done]), level), ring, False)
        tail_done = tail.finish(vector_part.add(rest_part.mine[0]))
        vector_part.hop(4)
        tail_part = Spread(tail_done, ring, True)
        rest_sum = rest_part.cores(tail_part.mine[0])
        level = vector_part.add(rest_sum[1])
        vector_part.shards()
        expand_sum, project_sum = place_sums(
            [rest_sum],
            [expand_master.shape, project_master.shape],
            [
                [(0, 4 * high * parity, hidden_of(parity), high, 0) for parity in range(2)],
                [
                    (0, 4 * high * parity + 2 * high, halves_of(0, 1), 2 * high, parity * TILE)
                    for parity in range(2)
                ],
            ],
        )
        expand_state = adam(
            expand_master,
            expand_mean,
            expand_square,
            expand_sum.astype(jnp.float32),
            RATE_MATRIX,
            DECAY_MATRIX,
        )
        tail_sum = tail_part.cores(expand_state[0])
        (attend_sum,) = place_sums(
            [tail_sum, rest_sum],
            [attend_master.shape],
            [
                [
                    (0, 0, halves_of(0, 3), high, 0),
                    (1, 8 * high, halves_of(3 * width, 1), high, 0),
                ]
            ],
        )
    else:
        plain = plain_gradients(even_halves, odd_halves, inner_halves, ring.core, high)
        attend_sum, expand_sum, project_sum = (
            lax.psum(lax.psum_scatter(g, "shard", scatter_dimension=0, tiled=True), "dp")
            for g in plain
        )
        expand_state = adam(
            expand_master, expand_mean, expand_square, expand_sum, RATE_MATRIX, DECAY_MATRIX
        )
    attend_sum, project_sum = attend_sum.astype(jnp.float32), project_sum.astype(jnp.float32)
    attend_state = adam(
        attend_master, attend_mean, attend_square, attend_sum, RATE_MATRIX, DECAY_MATRIX
    )
    project_state = adam(
        project_master, project_mean, project_square, project_sum, RATE_MATRIX, DECAY_MATRIX
    )
    vector_sum = vector_part.finish(expand_state[0])
    vector_state = adam(vector_master, vector_mean, vector_square, vector_sum, RATE_VECTOR, 0.0)
    return (
        layer_output,
        input_grad,
        attend_state[0],
        expand_state[0],
        project_state[0],
        vector_state[0],
        attend_state[1],
        expand_state[1],
        project_state[1],
        vector_state[1],
        attend_state[2],
        expand_state[2],
        project_state[2],
        vector_state[2],
    )


def solution(mesh):
    return jax.shard_map(
        on_device,
        mesh=mesh,
        in_specs=(
            P(("dp", "shard"), None),
            P(("dp", "shard"), None),
            P(),
            P(),
            P("shard", None),
            P("shard", None),
            P("shard", None),
            P("shard", None),
            P("shard", None),
            P("shard", None),
            P("shard", None),
            P("shard", None),
            P("shard", None),
            P("shard", None),
            P("shard", None),
            P("shard", None),
        ),
        out_specs=(
            P(("dp", "shard"), None),
            P(("dp", "shard"), None),
            P("shard", None),
            P("shard", None),
            P("shard", None),
            P("shard", None),
            P("shard", None),
            P("shard", None),
            P("shard", None),
            P("shard", None),
            P("shard", None),
            P("shard", None),
            P("shard", None),
            P("shard", None),
        ),
        check_vma=False,
    )
```

```python
import functools
import math

import jax
import jax.numpy as jnp
from jax import lax
from jax.experimental import pallas as pl
from jax.experimental.pallas import tpu as pltpu
from jax.sharding import PartitionSpec as P

HEADS = 12
HEAD_DIM = 64
STEP = 10


NORM_EPS = 1e-05
MASK_FILL = -1e30
BETA_ONE = 0.9
BETA_TWO = 0.999
ADAM_EPS = 1e-08
RATE_MATRIX = 0.05
RATE_VECTOR = 0.3
DECAY_MATRIX = 0.01
BLOCK = 256
NT = (((1,), (1,)), ((), ()))
TN = (((0,), (0,)), ((), ()))


def slot_segments(seq_lengths, seq_owner, device, slots):
    mine = seq_owner == device
    owned = jnp.where(mine, seq_lengths, 0)
    starts = jnp.cumsum(owned) - owned
    place = jnp.arange(slots, dtype=jnp.int32)[:, None]
    inside = mine[None, :] & (place >= starts[None, :]) & (place < (starts + owned)[None, :])
    labels = jnp.arange(seq_lengths.shape[0], dtype=jnp.int32)[None, :] + 1
    return jnp.sum(jnp.where(inside, labels, 0), axis=1) - 1


def dot(a, b, dims=(((1,), (0,)), ((), ()))):
    return lax.dot_general(a, b, dims, preferred_element_type=jnp.float32)


def mask_of(column, row, first, end, start):
    later = lax.broadcasted_iota(jnp.int32, (end - first, end - start), 0) + first
    earlier = lax.broadcasted_iota(jnp.int32, (end - first, end - start), 1) + start
    return (column == row) & (earlier <= later)


def forward_kernel(column_ref, row_ref, q_ref, k_ref, v_ref, mixed_ref, log_ref):
    slots = q_ref.shape[0]
    scale = HEAD_DIM**-0.5
    low = lax.broadcasted_iota(jnp.int32, (1, 128), 1) < HEAD_DIM
    for index in range(slots // BLOCK):
        first, end = index * BLOCK, (index + 1) * BLOCK
        start = max(0, first - 512)
        ok = mask_of(column_ref[first:end, :], row_ref[:, start:end], first, end, start)
        q = q_ref[first:end, :]
        k = k_ref[start:end, :]
        v = v_ref[start:end, :]
        mixed, logs = [], []
        for head in range(2):
            mine = low if head == 0 else ~low
            s = dot(jnp.where(mine, q, jnp.zeros_like(q)), k, NT) * scale
            s = jnp.where(ok, s, MASK_FILL)
            top = jnp.max(s, axis=1, keepdims=True)
            e = jnp.exp(s - top)
            total = jnp.sum(e, axis=1, keepdims=True)
            p = (e * (1.0 / total)).astype(jnp.bfloat16)
            mixed.append(dot(p, v))
            logs.append(top + jnp.log(total))
        mixed_ref[first:end, :] = jnp.where(low, mixed[0], mixed[1]).astype(jnp.bfloat16)
        log_ref[0, first:end, :] = jnp.concatenate(logs, axis=1)


def backward_kernel(column_ref, row_ref, q_ref, k_ref, v_ref, g_ref, log_ref, out_ref, ka, va):
    slots = q_ref.shape[0]
    scale = HEAD_DIM**-0.5
    low = lax.broadcasted_iota(jnp.int32, (1, 128), 1) < HEAD_DIM
    ka[...] = jnp.zeros_like(ka)
    va[...] = jnp.zeros_like(va)
    for index in range(slots // BLOCK):
        first, end = index * BLOCK, (index + 1) * BLOCK
        start = max(0, first - 512)
        ok = mask_of(column_ref[first:end, :], row_ref[:, start:end], first, end, start)
        q = q_ref[first:end, :]
        g = g_ref[first:end, :]
        k = k_ref[start:end, :]
        v = v_ref[start:end, :]
        dq, dk, dv = [], [], []
        for head in range(2):
            mine = low if head == 0 else ~low
            s = dot(jnp.where(mine, q, jnp.zeros_like(q)), k, NT) * scale
            p = jnp.exp(jnp.where(ok, s - log_ref[0, first:end, head : head + 1], MASK_FILL))
            dp = dot(jnp.where(mine, g, jnp.zeros_like(g)), v, NT)
            w = p * dp
            ds = (w - p * jnp.sum(w, axis=1, keepdims=True)).astype(jnp.bfloat16)
            dq.append(dot(ds, k))
            dk.append(dot(ds, q, TN))
            dv.append(dot(p.astype(jnp.bfloat16), g, TN))
        out_ref[0, first:end, :] = (jnp.where(low, dq[0], dq[1]) * scale).astype(jnp.bfloat16)
        ka[start:end, :] += jnp.where(low, dk[0], dk[1])
        va[start:end, :] += jnp.where(low, dv[0], dv[1])
    out_ref[1] = (ka[...] * scale).astype(jnp.bfloat16)
    out_ref[2] = va[...].astype(jnp.bfloat16)


def columns(offset, slots):
    return pl.BlockSpec((slots, 128), lambda pair: (0, pair + offset))


def whole(shape):
    return pl.BlockSpec(shape, lambda pair: (0, 0))


def attention(projected, segment, first, count):
    slots = projected.shape[0]
    pairs = HEADS // 2
    return pl.pallas_call(
        forward_kernel,
        grid=(count,),
        in_specs=[whole((slots, 1)), whole((1, slots))] + [columns(pairs * n + first, slots) for n in range(3)],
        out_specs=[columns(0, slots), pl.BlockSpec((1, slots, 2), lambda pair: (pair, 0, 0))],
        out_shape=[
            jax.ShapeDtypeStruct((slots, count * 128), jnp.bfloat16),
            jax.ShapeDtypeStruct((count, slots, 2), jnp.float32),
        ],
        compiler_params=pltpu.CompilerParams(vmem_limit_bytes=48 * 1024 * 1024),
        cost_estimate=cost(2 * slots * slots * count * 256, 8 * slots * count * 128),
        name="attention",
    )(segment[:, None], segment[None, :], projected, projected, projected)


def attention_back(projected, grad_mixed, logs, log_first, segment, first, count):
    slots = projected.shape[0]
    pairs = HEADS // 2
    return pl.pallas_call(
        backward_kernel,
        grid=(count,),
        in_specs=[whole((slots, 1)), whole((1, slots))]
        + [columns(pairs * n + first, slots) for n in range(3)]
        + [columns(first, slots), pl.BlockSpec((1, slots, 2), lambda pair: (pair + log_first, 0, 0))],
        out_specs=pl.BlockSpec((3, slots, 128), lambda pair: (0, 0, pair)),
        out_shape=jax.ShapeDtypeStruct((3, slots, count * 128), jnp.bfloat16),
        scratch_shapes=[pltpu.VMEM((slots, 128), jnp.float32)] * 2,
        compiler_params=pltpu.CompilerParams(vmem_limit_bytes=48 * 1024 * 1024),
        cost_estimate=cost(5 * slots * slots * count * 256, 16 * slots * count * 128),
        name="attention_back",
    )(segment[:, None], segment[None, :], projected, projected, projected, grad_mixed, logs)


def adam(master, mean, square, grad, rate, decay):
    mean_new = BETA_ONE * mean + (1.0 - BETA_ONE) * grad
    square_new = BETA_TWO * square + (1.0 - BETA_TWO) * grad * grad
    mean_hat = mean_new / (1.0 - BETA_ONE**STEP)
    square_hat = square_new / (1.0 - BETA_TWO**STEP)
    master_new = master - rate * (mean_hat / (jnp.sqrt(square_hat) + ADAM_EPS) + decay * master)
    return (mean_new, square_new, master_new)


class Ring:
    def __init__(self):
        self.group = lax.axis_size("shard")
        self.data = lax.axis_size("dp")
        self.plane = self.data // 2
        self.side = math.isqrt(self.plane)
        self.square = self.data == 2 * self.side * self.side
        self.z = lax.axis_index("shard")
        device = lax.axis_index("dp")
        self.core = device % 2
        chip = device // 2
        high, low = chip // self.side, chip % self.side
        straight = low * self.side + high
        crossed = high * self.side + low
        self.block = jnp.where(self.core == 0, straight, crossed)
        self.block_other = jnp.where(self.core == 0, crossed, straight)

    def staged(self):
        return self.side == 2 and self.square and self.group * self.plane == ROW_BLOCKS

    def send_core(self, value):
        return lax.ppermute(value, "dp", [(i, i ^ 1) for i in range(self.data)])

    def send_plane(self, value, step):
        side = self.side
        first, second = step // side, step % side
        pairs = []
        for device in range(self.data):
            core, chip = device % 2, device // 2
            high, low = chip // side, chip % side
            if core == 0:
                low, high = (low + first) % side, (high + second) % side
            else:
                high, low = (high + first) % side, (low + second) % side
            pairs.append((device, (high * side + low) * 2 + core))
        return lax.ppermute(value, "dp", pairs)

    def spread(self, value, direct):
        if direct:
            return [self.send_plane(value, step) for step in range(1, self.plane)]
        second, first = self.send_plane(value, 1), self.send_plane(value, 2)
        return [second, first, self.send_plane(first, 1)]

    def shifted(self, block, step):
        side = self.side
        first, second = step // side, step % side
        return (block // side + first) % side * side + (block % side + second) % side

    def back(self, block, step):
        side = self.side
        first, second = step // side, step % side
        return (block // side - first) % side * side + (block % side - second) % side

    def send_shard(self, value, step):
        group = self.group
        return lax.ppermute(value, "shard", [(i, (i + step) % group) for i in range(group)])


TILE = 384
ROW_BLOCKS = 16
CHUNK = 256


def compiler(megabytes):
    return pltpu.CompilerParams(vmem_limit_bytes=megabytes * 1024 * 1024)


def cost(flops, bytes_accessed):
    return pl.CostEstimate(flops=flops, bytes_accessed=bytes_accessed, transcendentals=0)


def halves_of(first, tiles):
    return [[first + (half * tiles + tile) * TILE for tile in range(tiles)] for half in range(2)]


def hidden_of(parity):
    return [[(4 * half + 2 * tile + parity) * TILE for tile in range(2)] for half in range(2)]


def starts_of(rows, parity):
    return [first + parity * TILE for first in range(0, rows, 2 * TILE)]


def pack_kernel(specs, *refs):
    out_ref = refs[-1]
    row = 0
    for (columns, high, starts, count), ref in zip(specs, refs[:-1], strict=True):
        for number, start in enumerate(starts):
            blocks = slice(number * (count // high), (number + 1) * (count // high))
            for half in range(2):
                for tile, column in enumerate(columns[half]):
                    part = ref[start : start + count, column : column + TILE].astype(jnp.bfloat16)
                    out_ref[half, blocks, row + tile * high : row + (tile + 1) * high, :] = part.reshape(
                        count // high, high, TILE
                    )
        row += len(columns[0]) * high


def pack(parts):
    blocks = len(parts[0][3]) * parts[0][4] // parts[0][2]
    rows = sum(len(part[1][0]) * part[2] for part in parts)
    vmem = pl.BlockSpec(memory_space=pltpu.VMEM)
    return pl.pallas_call(
        functools.partial(pack_kernel, [part[1:] for part in parts]),
        in_specs=[vmem] * len(parts),
        out_specs=vmem,
        out_shape=jax.ShapeDtypeStruct((2, blocks, rows, TILE), jnp.bfloat16),
        compiler_params=compiler(40),
        cost_estimate=cost(0, 12 * blocks * rows * TILE),
        name="pack",
    )(*[part[0] for part in parts])


def after(value, *others):
    return lax.optimization_barrier((value, *others))[0]


class Gather:
    def __init__(self, own, ring):
        self.own, self.ring = own, ring
        chunk = lax.dynamic_index_in_dim(
            lax.dynamic_index_in_dim(own, ring.core, 0, keepdims=False),
            ring.block,
            0,
            keepdims=False,
        )
        self.arrived = [ring.send_shard(chunk, step) for step in range(1, ring.group)]

    def foreign(self, *others):
        self.far = after(jnp.stack(self.arrived), *others)
        return self.far

    def plane(self, direct):
        self.mine = [self.far] + self.ring.spread(self.far, direct)

    def cores(self, *others):
        ring = self.ring
        self.mine = list(lax.optimization_barrier((*self.mine, *others))[: ring.plane])
        self.other = [ring.send_core(value) for value in self.mine]

    def sources(self):
        return [self.own] + self.mine + self.other

    def places(self):
        ring = self.ring
        steps = range(ring.plane)
        places = [(None, ring.z * self.own.shape[1])]
        places += [(ring.core, ring.back(ring.block, step)) for step in steps]
        return places + [(1 - ring.core, ring.back(ring.block_other, step)) for step in steps]


def where_array(places, ring):
    scalars = [ring.z]
    for half, block in places:
        scalars += [0 if half is None else half, block]
    scalars.append(ring.core)
    return jnp.stack([jnp.asarray(v, jnp.int32) for v in scalars])


def copy_count(sources, group):
    return 1 if len(sources) == 1 else 2 + (len(sources) - 1) * (group - 1)


def start_pieces(where_ref, refs, group, out_ref, sems):
    copies = []

    def begin(source, target):
        copy = pltpu.make_async_copy(source, target, sems.at[len(copies)])
        copy.start()
        copies.append(copy)

    if len(refs) == 1:
        begin(refs[0], out_ref)
        return copies
    blocks = refs[0].shape[1]
    first = where_ref[2]
    for half in range(2):
        begin(refs[0].at[half], out_ref.at[half, pl.ds(first, blocks)])
    for number, ref in enumerate(refs[1:], 1):
        half, block = where_ref[1 + 2 * number], where_ref[2 + 2 * number]
        for step in range(1, group):
            source = lax.rem(where_ref[0] - step + group, group)
            begin(ref.at[step - 1], out_ref.at[half, source * blocks + block])
    return copies


class Sum:
    def __init__(self, kept, sent, ring):
        self.ring, self.kept = ring, kept
        self.got = ring.send_core(sent)

    def chip(self, direct, *others):
        ring = self.ring
        kept = after(self.kept, *others)
        chip = (kept.astype(jnp.float32) + self.got.astype(jnp.float32)).astype(jnp.bfloat16)
        rows = chip.shape[1]
        self.direct = direct
        if direct:
            chip = lax.optimization_barrier(chip.reshape(ring.group, ring.plane, rows, TILE))

            def block_of(step):
                return lax.dynamic_index_in_dim(
                    chip, ring.shifted(ring.block, step), 1, keepdims=False
                )

            self.arrived = [ring.send_plane(block_of(step), step) for step in range(1, ring.plane)]
            self.level = block_of(0)
            return self.level
        chip = lax.optimization_barrier(chip.reshape(ring.group, 2, 2 * rows, TILE))
        mine = ring.block // 2
        away = lax.dynamic_index_in_dim(chip, 1 - mine, 1, keepdims=False)
        self.arrived = [ring.send_plane(away, 2)]
        self.level = lax.dynamic_index_in_dim(chip, mine, 1, keepdims=False)
        return self.level

    def halfway(self, *others):
        ring = self.ring
        level = after(self.level, *others).astype(jnp.float32) + self.arrived[0].astype(jnp.float32)
        rows = level.shape[1] // 2
        level = lax.optimization_barrier(
            level.astype(jnp.bfloat16).reshape(ring.group, 2, rows, TILE)
        )
        mine = ring.block % 2
        away = lax.dynamic_index_in_dim(level, 1 - mine, 1, keepdims=False)
        self.arrived = [ring.send_plane(away, 1)]
        self.level = lax.dynamic_index_in_dim(level, mine, 1, keepdims=False)
        return self.level

    def plane(self, *others):
        ring = self.ring
        level = after(self.level, *others).astype(jnp.float32)
        for value in self.arrived:
            level = level + value.astype(jnp.float32)
        level = lax.optimization_barrier(level.astype(jnp.bfloat16))

        def shard_of(step):
            return lax.dynamic_index_in_dim(
                level, (ring.z + step) % ring.group, 0, keepdims=False
            )

        self.arrived = [ring.send_shard(shard_of(step), step) for step in range(1, ring.group)]
        self.level = shard_of(0)
        return self.level

    def finish(self, *others):
        done = after(self.level, *others).astype(jnp.float32)
        for value in self.arrived:
            done = done + value.astype(jnp.float32)
        return done.astype(jnp.bfloat16)


class Spread:
    def __init__(self, piece, ring, direct):
        self.ring = ring
        piece = lax.optimization_barrier(piece)
        self.mine = [piece] + ring.spread(piece, direct)

    def cores(self, *others):
        ring = self.ring
        mine = after(jnp.stack(self.mine), *others)
        places = [(ring.core, ring.back(ring.block, step)) for step in range(ring.plane)]
        places += [(1 - ring.core, ring.back(ring.block_other, step)) for step in range(ring.plane)]
        return [mine, ring.send_core(mine)], places


def plain_gradients(even, odd, inner, core, high):
    def both(halves):
        kept, sent = (value.astype(jnp.float32) for value in halves)
        return jnp.stack([jnp.where(core == 0, kept, sent), jnp.where(core == 0, sent, kept)])

    def columns(packed, first, tiles):
        part = packed[:, :, first : first + tiles * high].reshape(2, ROW_BLOCKS, tiles, high, TILE)
        return part.transpose(1, 3, 0, 2, 4)

    even, odd, inner = both(even), both(odd), both(inner)
    width = ROW_BLOCKS * high
    expand = jnp.stack([columns(even, 0, 2), columns(odd, 0, 2)], axis=4).reshape(width, -1)
    deep = [
        packed[:, :, 2 * high : 4 * high].transpose(1, 2, 0, 3).reshape(4, TILE, width)
        for packed in (even, odd)
    ]
    project = jnp.stack(deep, axis=1).reshape(-1, width)
    attend = jnp.concatenate(
        [columns(inner, 0, 3).reshape(width, -1), columns(odd, 4 * high, 1).reshape(width, -1)], axis=1
    )
    return attend, expand, project


def place_kernel(matrices, count, where_ref, *refs):
    sources, outs = refs[: 2 * count], refs[2 * count : 2 * count + len(matrices)]
    packed, sems = refs[2 * count + len(matrices) : -1], refs[-1]
    plane = sources[0].shape[0]
    copies = []
    for number, ref in enumerate(sources):
        for block in range(plane):
            scalar = 2 * len(copies)
            place = packed[number // 2].at[where_ref[scalar], where_ref[scalar + 1]]
            copy = pltpu.make_async_copy(ref.at[block], place, sems.at[len(copies)])
            copy.start()
            copies.append(copy)
    for copy in copies:
        copy.wait()
    for kinds, out_ref in zip(matrices, outs, strict=True):
        for gradient, row, columns, high, first in kinds:
            for half in range(2):
                for tile, column in enumerate(columns[half]):
                    rows = slice(row + tile * high, row + (tile + 1) * high)
                    value = packed[gradient][half, :, rows, :].reshape(plane * high, TILE)
                    out_ref[first : first + plane * high, column : column + TILE] = value


def place_sums(gradients, shapes, matrices):
    sources = [source for group, _ in gradients for source in group]
    plane = sources[0].shape[0]
    scalars = [v for _, places in gradients for place in places for v in place]
    where = jnp.stack([jnp.asarray(v, jnp.int32) for v in scalars])
    return pl.pallas_call(
        functools.partial(place_kernel, matrices, len(gradients)),
        in_specs=[pl.BlockSpec(memory_space=pltpu.SMEM)]
        + [pl.BlockSpec(memory_space=pl.ANY)] * len(sources),
        out_specs=[pl.BlockSpec(memory_space=pltpu.VMEM)] * len(shapes),
        out_shape=[jax.ShapeDtypeStruct(shape, jnp.bfloat16) for shape in shapes],
        scratch_shapes=[
            pltpu.VMEM((2, plane) + group[0].shape[1:], jnp.bfloat16) for group, _ in gradients
        ]
        + [pltpu.SemaphoreType.DMA((len(sources) * plane,))],
        compiler_params=compiler(32),
        cost_estimate=cost(0, 4 * sum(rows * columns for rows, columns in shapes)),
        name="place_sums",
    )(where, *sources)


def tile_of(packed_ref, half, row, high):
    part = packed_ref[half, :, pl.ds(row, high), :]
    return part.reshape(ROW_BLOCKS * high, TILE)


def normal_of(rows):
    centre = jnp.mean(rows, axis=1, keepdims=True)
    centred = rows - centre
    spread = jnp.mean(centred * centred, axis=1, keepdims=True)
    ratio = lax.rsqrt(spread + NORM_EPS)
    return centred * ratio, ratio


def normal_back(normal, ratio, scaled):
    along = jnp.mean(scaled * normal, axis=1, keepdims=True)
    return ratio * (scaled - jnp.mean(scaled, axis=1, keepdims=True) - normal * along)


def project_kernel(group, where_ref, tokens_ref, params_ref, *refs):
    pieces, (out_ref, turned_ref, packed_ref, sems) = refs[:-4], refs[-4:]
    slots, width = tokens_ref.shape
    high = width // ROW_BLOCKS
    copies = start_pieces(where_ref, pieces, group, packed_ref, sems)
    lows = []
    for first in range(0, slots, CHUNK):
        normal, _ = normal_of(tokens_ref[first : first + CHUNK, :].astype(jnp.float32))
        low = (normal * params_ref[0:1, :] + params_ref[1:2, :]).astype(jnp.bfloat16)
        turned_ref[:, first : first + CHUNK] = low.T
        lows.append(low)
    for copy in copies:
        copy.wait()
    for part in range(3):
        weight = jnp.concatenate(
            [tile_of(packed_ref, t // 3, t % 3 * high, high) for t in (2 * part, 2 * part + 1)], axis=1
        )
        for number, low in enumerate(lows):
            value = dot(low, weight)
            if part != 1:
                row = 4 if part == 0 else 5
                value = value + params_ref[row : row + 1, :]
            out_ref[number * CHUNK : (number + 1) * CHUNK, part * width : (part + 1) * width] = (
                value.astype(jnp.bfloat16)
            )


def project_rows(tokens, params, sources, where, group):
    slots, width = tokens.shape
    high = width // ROW_BLOCKS
    vmem = pl.BlockSpec(memory_space=pltpu.VMEM)
    return pl.pallas_call(
        functools.partial(project_kernel, group),
        in_specs=[pl.BlockSpec(memory_space=pltpu.SMEM), vmem, vmem]
        + [pl.BlockSpec(memory_space=pl.ANY)] * len(sources),
        out_specs=[vmem] * 3,
        out_shape=[
            jax.ShapeDtypeStruct((slots, 3 * width), jnp.bfloat16),
            jax.ShapeDtypeStruct((width, slots), jnp.bfloat16),
            jax.ShapeDtypeStruct((2, ROW_BLOCKS, 3 * high, TILE), jnp.bfloat16),
        ],
        scratch_shapes=[pltpu.SemaphoreType.DMA((copy_count(sources, group),))],
        compiler_params=compiler(40),
        cost_estimate=cost(6 * slots * width * width, 16 * slots * width),
        name="project_rows",
    )(where, tokens, params, *sources)


def tail_of(values):
    size = jnp.abs(values) * (0.5**0.5)
    bell = jnp.exp(-0.5 * values * values)
    t = 1.0 / (1.0 + 0.5 * size)
    series = jnp.full_like(t, 0.17087277)
    for c in (
        -0.82215223, 1.48851587, -1.13520398, 0.27886807, -0.18628806, 0.09678418, 0.37409196, 1.00002368, -1.26551223,
    ):
        series = series * t + c
    tail = 0.5 * t * bell * jnp.exp(series)
    return bell, jnp.where(values > 0, 1.0 - tail, tail)


def halves_out(scratch_ref, core, kept_ref, sent_ref, sems):
    copies = [
        pltpu.make_async_copy(scratch_ref.at[core], kept_ref, sems.at[0]),
        pltpu.make_async_copy(scratch_ref.at[1 - core], sent_ref, sems.at[1]),
    ]
    for copy in copies:
        copy.start()
    return copies


def feed(parity, packed_ref, params_ref, low_ref, turned_ref, back_ref, total_ref, two_ref, act_ref, pre_ref, bias_ref, grad_ref):
    slots, width = low_ref.shape
    high = width // ROW_BLOCKS
    deep = slice(2 * high, 4 * high)

    def step(number, carry):
        wide = jnp.concatenate(
            [tile_of(packed_ref, number, tile * high, high) for tile in range(2)], axis=1
        )
        blocks = pl.ds(number * (ROW_BLOCKS // 2), ROW_BLOCKS // 2)
        deep_weight = jnp.concatenate(
            [packed_ref[side, blocks, deep, :].reshape(width, TILE) for side in range(2)], axis=1
        )
        bias = params_ref[pl.ds(8 + 2 * parity + number, 1), :]
        bias_sum = jnp.zeros((1, width), jnp.float32)
        for first in range(0, slots, CHUNK):
            here = slice(first, first + CHUNK)
            pre = dot(low_ref[here, :], wide) + bias
            bell, below = tail_of(pre)
            act = (pre * below).astype(jnp.bfloat16)
            act_ref[here, :] = act
            slope = below + pre * bell * 0.3989422804014327
            grad = (dot(back_ref[here, :], deep_weight, NT) * slope).astype(jnp.bfloat16)
            pre_ref[here, :] = grad
            bias_sum = bias_sum + jnp.sum(grad.astype(jnp.float32), axis=0, keepdims=True)
            total_ref[here, :] += dot(act, deep_weight)
            two_ref[here, :] += dot(grad, wide, NT)
        bias_ref[pl.ds(number, 1), :] = bias_sum
        expand_grad = dot(turned_ref[...], pre_ref[...]).astype(jnp.bfloat16)
        project_grad = dot(act_ref[...], back_ref[...], TN).astype(jnp.bfloat16)
        for side in range(2):
            here = slice(side * TILE, (side + 1) * TILE)
            grad_ref[number, :, side * high : (side + 1) * high, :] = expand_grad[:, here].reshape(
                ROW_BLOCKS, high, TILE
            )
            grad_ref[side, blocks, deep, :] = project_grad[:, here].reshape(
                ROW_BLOCKS // 2, 2 * high, TILE
            )
        return carry

    lax.fori_loop(0, 2, step, 0)


def first_kernel(group, count, where_ref, tokens_ref, cotangent_ref, live_ref, params_ref, *refs):
    mixed_parts, pieces = refs[:count], refs[count:-17]
    (resid_ref, total_ref, two_ref, back_ref, outer_ref, kept_ref, sent_ref, sums_ref) = refs[-17:-9]
    (packed_ref, grad_ref, low_ref, turned_ref, act_ref, pre_ref, bias_ref, sems, out_sems) = refs[-9:]
    slots, width = tokens_ref.shape
    high = width // ROW_BLOCKS
    copies = start_pieces(where_ref, pieces, group, packed_ref, sems)
    sums_ref[...] = jnp.zeros_like(sums_ref)
    for first in range(0, slots, CHUNK):
        here = slice(first, first + CHUNK)
        back_ref[here, :] = (cotangent_ref[here, :].astype(jnp.float32) * live_ref[here, :]).astype(
            jnp.bfloat16
        )
    for copy in copies:
        copy.wait()
    weight = jnp.concatenate([tile_of(packed_ref, half, 4 * high, high) for half in range(2)], axis=1)
    outer_ref[...] = weight
    for first in range(0, slots, CHUNK):
        here = slice(first, first + CHUNK)
        mixed = jnp.concatenate([ref[here, :] for ref in mixed_parts], axis=1)
        resid = tokens_ref[here, :].astype(jnp.float32) + (dot(mixed, weight) + params_ref[6:7, :])
        normal, _ = normal_of(resid)
        low = (normal * params_ref[2:3, :] + params_ref[3:4, :]).astype(jnp.bfloat16)
        low_ref[here, :] = low
        turned_ref[:, here] = low.T
        resid_ref[here, :] = resid
        total_ref[here, :] = resid + params_ref[7:8, :]
        two_ref[here, :] = jnp.zeros((CHUNK, width), jnp.float32)
    feed(0, packed_ref, params_ref, low_ref, turned_ref, back_ref, total_ref, two_ref, act_ref, pre_ref, bias_ref, grad_ref)
    sums_ref[8:10, :] = bias_ref[0:2, :]
    for copy in halves_out(grad_ref, where_ref[where_ref.shape[0] - 1], kept_ref, sent_ref, out_sems):
        copy.wait()


def second_kernel(group, count, where_ref, live_ref, params_ref, resid_in, total_in, two_in, back_ref, outer_ref, *refs):
    mixed_parts, pieces = refs[:count], refs[count:-18]
    (out_ref, resid_ref, mixed_grad_ref, kept_ref, sent_ref, sums_ref) = refs[-18:-12]
    (packed_ref, grad_ref, low_ref, turned_ref, total_ref, two_ref, act_ref, pre_ref, bias_ref, ratio_ref, sems, out_sems) = refs[-12:]
    slots, width = resid_in.shape
    high = width // ROW_BLOCKS
    copies = start_pieces(where_ref, pieces, group, packed_ref, sems)
    sums_ref[...] = jnp.zeros_like(sums_ref)
    for first in range(0, slots, CHUNK):
        here = slice(first, first + CHUNK)
        normal, ratio = normal_of(resid_in[here, :])
        low = (normal * params_ref[2:3, :] + params_ref[3:4, :]).astype(jnp.bfloat16)
        low_ref[here, :] = low
        turned_ref[:, here] = low.T
        resid_ref[here, :] = normal
        ratio_ref[here, :] = ratio
        total_ref[here, :] = total_in[here, :]
        two_ref[here, :] = two_in[here, :]
    for copy in copies:
        copy.wait()
    feed(1, packed_ref, params_ref, low_ref, turned_ref, back_ref, total_ref, two_ref, act_ref, pre_ref, bias_ref, grad_ref)
    sums_ref[10:12, :] = bias_ref[0:2, :]
    weight = outer_ref[...]
    for first in range(0, slots, CHUNK):
        here = slice(first, first + CHUNK)
        normal = resid_ref[here, :]
        two = two_ref[here, :]
        back = back_ref[here, :].astype(jnp.float32)
        grad = back + normal_back(normal, ratio_ref[here, :], two * params_ref[2:3, :])
        low = grad.astype(jnp.bfloat16)
        sums_ref[2:3, :] += jnp.sum(two * normal, axis=0, keepdims=True)
        sums_ref[3:4, :] += jnp.sum(two, axis=0, keepdims=True)
        sums_ref[6:7, :] += jnp.sum(low.astype(jnp.float32), axis=0, keepdims=True)
        sums_ref[7:8, :] += jnp.sum(back, axis=0, keepdims=True)
        resid_ref[here, :] = grad
        act_ref[here, :] = low
        mixed_grad_ref[here, :] = dot(low, weight, NT).astype(jnp.bfloat16)
        out_ref[here, :] = (total_ref[here, :] * live_ref[here, :]).astype(jnp.bfloat16)
    mixed = jnp.concatenate([ref[...] for ref in mixed_parts], axis=1)
    outer_grad = dot(mixed, act_ref[...], TN).astype(jnp.bfloat16)
    for side in range(2):
        grad_ref[side, :, 4 * high : 5 * high, :] = outer_grad[
            :, side * TILE : (side + 1) * TILE
        ].reshape(ROW_BLOCKS, high, TILE)
    for copy in halves_out(grad_ref, where_ref[where_ref.shape[0] - 1], kept_ref, sent_ref, out_sems):
        copy.wait()


def middle(kernel, name, in_vmem, mixed, sources, where, outs, rows, weight_rows, extra, group):
    slots, width = mixed[0].shape[0], in_vmem[1].shape[1]
    vmem, anywhere = pl.BlockSpec(memory_space=pltpu.VMEM), pl.BlockSpec(memory_space=pl.ANY)
    half = jax.ShapeDtypeStruct((ROW_BLOCKS, rows, TILE), jnp.bfloat16)
    low = pltpu.VMEM((slots, width), jnp.bfloat16)
    return pl.pallas_call(
        functools.partial(kernel, group, len(mixed)),
        in_specs=[pl.BlockSpec(memory_space=pltpu.SMEM)]
        + [vmem] * (len(in_vmem) + len(mixed))
        + [anywhere] * len(sources),
        out_specs=[vmem] * len(outs) + [anywhere] * 2 + [vmem],
        out_shape=outs + [half, half, jax.ShapeDtypeStruct((16, width), jnp.float32)],
        scratch_shapes=[
            pltpu.VMEM((2, ROW_BLOCKS, weight_rows, TILE), jnp.bfloat16),
            pltpu.VMEM((2, ROW_BLOCKS, rows, TILE), jnp.bfloat16),
            low,
            pltpu.VMEM((width, slots), jnp.bfloat16),
        ]
        + [pltpu.VMEM((slots, width), jnp.float32)] * extra
        + [low, low, pltpu.VMEM((8, width), jnp.float32)]
        + [pltpu.VMEM((slots, 1), jnp.float32)] * (extra // 2)
        + [
            pltpu.SemaphoreType.DMA((copy_count(sources, group),)),
            pltpu.SemaphoreType.DMA((2,)),
        ],
        compiler_params=compiler(60),
        cost_estimate=cost(27 * slots * width * width, 40 * slots * width),
        name=name,
    )(where, *in_vmem, *mixed, *sources)


def inner_kernel(where_ref, turned_ref, *refs):
    grads, (kept_ref, sent_ref, sums_ref, grad_ref, sems) = refs[:-5], refs[-5:]
    width = turned_ref.shape[0]
    high = width // ROW_BLOCKS
    turned = turned_ref[...]
    sums_ref[...] = jnp.zeros_like(sums_ref)
    for part in range(3):
        values = jnp.concatenate([ref[part] for ref in grads], axis=1)
        grad = dot(turned, values).astype(jnp.bfloat16)
        for side in range(2):
            t = 2 * part + side
            grad_ref[t // 3, :, t % 3 * high : (t % 3 + 1) * high, :] = grad[
                :, side * TILE : (side + 1) * TILE
            ].reshape(ROW_BLOCKS, high, TILE)
        if part != 1:
            row = 4 if part == 0 else 5
            sums_ref[row : row + 1, :] = jnp.sum(values.astype(jnp.float32), axis=0, keepdims=True)
    for copy in halves_out(grad_ref, where_ref[where_ref.shape[0] - 1], kept_ref, sent_ref, sems):
        copy.wait()


def inner_gradient(where, turned, grads):
    width, slots = turned.shape
    rows = 3 * (width // ROW_BLOCKS)
    vmem, anywhere = pl.BlockSpec(memory_space=pltpu.VMEM), pl.BlockSpec(memory_space=pl.ANY)
    half = jax.ShapeDtypeStruct((ROW_BLOCKS, rows, TILE), jnp.bfloat16)
    return pl.pallas_call(
        inner_kernel,
        in_specs=[pl.BlockSpec(memory_space=pltpu.SMEM)] + [vmem] * (1 + len(grads)),
        out_specs=[anywhere, anywhere, vmem],
        out_shape=[half, half, jax.ShapeDtypeStruct((16, width), jnp.float32)],
        scratch_shapes=[
            pltpu.VMEM((2, ROW_BLOCKS, rows, TILE), jnp.bfloat16),
            pltpu.SemaphoreType.DMA((2,)),
        ],
        compiler_params=compiler(40),
        cost_estimate=cost(6 * slots * width * width, 8 * slots * width),
        name="inner_gradient",
    )(where, turned, *grads)


def input_kernel(tokens_ref, params_ref, packed_ref, resid_ref, *refs):
    grads, (out_ref, sums_ref) = refs[:-2], refs[-2:]
    slots, width = tokens_ref.shape
    high = width // ROW_BLOCKS
    sums_ref[...] = jnp.zeros_like(sums_ref)
    weights = [
        jnp.concatenate(
            [tile_of(packed_ref, t // 3, t % 3 * high, high) for t in (2 * part, 2 * part + 1)], axis=1
        )
        for part in range(3)
    ]
    for first in range(0, slots, CHUNK):
        here = slice(first, first + CHUNK)
        grad = jnp.zeros((CHUNK, width), jnp.float32)
        for part in range(3):
            values = jnp.concatenate([ref[part, here, :] for ref in grads], axis=1)
            grad = grad + dot(values, weights[part], NT)
        normal, ratio = normal_of(tokens_ref[here, :].astype(jnp.float32))
        sums_ref[0:1, :] += jnp.sum(grad * normal, axis=0, keepdims=True)
        sums_ref[1:2, :] += jnp.sum(grad, axis=0, keepdims=True)
        out_ref[here, :] = resid_ref[here, :] + normal_back(normal, ratio, grad * params_ref[0:1, :])


def input_gradient(tokens, params, packed, grads, resid):
    slots, width = tokens.shape
    vmem = pl.BlockSpec(memory_space=pltpu.VMEM)
    return pl.pallas_call(
        input_kernel,
        in_specs=[vmem] * (4 + len(grads)),
        out_specs=[vmem] * 2,
        out_shape=[
            jax.ShapeDtypeStruct((slots, width), jnp.float32),
            jax.ShapeDtypeStruct((16, width), jnp.float32),
        ],
        compiler_params=compiler(48),
        cost_estimate=cost(6 * slots * width * width, 16 * slots * width),
        name="input_gradient",
    )(tokens, params, packed, resid, *grads)


def gather_vector(master, ring):
    own = master.astype(jnp.bfloat16)
    group = ring.group
    parts = [own] + [ring.send_shard(own, step) for step in range(1, group)]
    stacked = jnp.stack(parts)
    order = (ring.z - jnp.arange(group)) % group
    return jnp.take(stacked, order, axis=0).reshape(group * own.shape[0], own.shape[1])


class VectorSum:
    def __init__(self, grad, ring):
        self.grad, self.ring = grad, ring
        self.flat = grad.reshape(ring.group, -1, 128) if ring.staged() else None

    def hop(self, bit):
        pairs = [(i, i ^ bit) for i in range(self.ring.data)]
        self.got = lax.ppermute(self.flat, "dp", pairs)

    def add(self, *others):
        self.flat = after(self.flat + after(self.got, *others))
        return self.flat

    def shards(self):
        ring = self.ring

        def shard_of(step):
            return lax.dynamic_index_in_dim(
                self.flat, (ring.z + step) % ring.group, 0, keepdims=False
            )

        self.arrived = [ring.send_shard(shard_of(step), step) for step in range(1, ring.group)]
        self.flat = shard_of(0)

    def finish(self, *others):
        if not self.ring.staged():
            whole = lax.psum_scatter(self.grad, "shard", scatter_dimension=0, tiled=True)
            return lax.psum(whole, "dp")
        arrived = lax.optimization_barrier((*self.arrived, *others))[: len(self.arrived)]
        done = self.flat
        for value in arrived:
            done = done + value
        return done.reshape(self.grad.shape[0] // self.ring.group, self.grad.shape[1])


def on_device(
    tokens,
    cotangent,
    seq_lengths,
    seq_owner,
    attend_master,
    expand_master,
    project_master,
    vector_master,
    attend_mean,
    expand_mean,
    project_mean,
    vector_mean,
    attend_square,
    expand_square,
    project_square,
    vector_square,
):
    ring = Ring()
    slots, width = tokens.shape
    high = width // ROW_BLOCKS
    staged = ring.staged()
    masters = (attend_master, expand_master, project_master)
    if not staged:
        masters = tuple(
            lax.all_gather(m.astype(jnp.bfloat16), "shard", axis=0, tiled=True) for m in masters
        )
    tall = masters[0].shape[0]

    def pack_group(parity, tie):
        attend, expand, project = lax.optimization_barrier((*masters, tie))[:3] if staged else masters
        parts = [
            (expand, hidden_of(parity), high, [0], tall),
            (project, halves_of(0, 1), 2 * high, starts_of(project.shape[0], parity), TILE),
        ]
        if parity == 0:
            parts.append((attend, halves_of(3 * width, 1), high, [0], tall))
        return pack(parts)

    own_inner = pack([(masters[0], halves_of(0, 3), high, [0], tall)])
    vector = gather_vector(vector_master, ring).astype(jnp.float32)
    device = lax.axis_index("dp") * ring.group + ring.z
    segment = slot_segments(seq_lengths, seq_owner, device, slots)
    live = (segment >= 0).astype(jnp.float32)[:, None]
    hidden_bias = vector[:, 8:].reshape(2, 2, 2, TILE).transpose(2, 0, 1, 3).reshape(4, width)
    params = jnp.concatenate(
        [vector[:, :8].T, hidden_bias, jnp.zeros((4, width), jnp.float32)]
    )
    rows = tokens
    if staged:
        inner_part = Gather(own_inner, ring)
        far = inner_part.foreign()
        inner_part.plane(True)
        even_part = Gather(pack_group(0, far), ring)
        inner_part.cores()
        far = even_part.foreign(*inner_part.other)
        even_part.plane(False)
        odd_part = Gather(pack_group(1, far), ring)
        rows = after(tokens, far)
        inner_sources = inner_part.sources()
        inner_where = where_array(inner_part.places(), ring)
    else:
        inner_sources, inner_where = [own_inner], where_array([(None, 0)], ring)
    projected, turned, inner = project_rows(rows, params, inner_sources, inner_where, ring.group)
    if staged:
        projected = after(projected, even_part.mine[2])
    half = HEADS // 4
    mixed, logs = [None, None], [None, None]
    mixed[0], logs[0] = attention(projected, segment, 0, half)
    later = projected
    if staged:
        even_part.cores(mixed[0])
        far = odd_part.foreign(mixed[0])
        odd_part.plane(False)
        later = after(projected, *even_part.mine, far)
    mixed[1], logs[1] = attention(later, segment, half, half)
    if staged:
        odd_part.cores(mixed[1])
        even_sources, even_where = even_part.sources(), where_array(even_part.places(), ring)
        odd_sources, odd_where = odd_part.sources(), where_array(odd_part.places(), ring)
        mixed[0] = after(mixed[0], *odd_part.mine)
    else:
        even_sources, even_where = [pack_group(0, None)], inner_where
        odd_sources, odd_where = [pack_group(1, None)], inner_where
    low = jax.ShapeDtypeStruct((slots, width), jnp.bfloat16)
    wide = jax.ShapeDtypeStruct((slots, width), jnp.float32)
    square = jax.ShapeDtypeStruct((width, width), jnp.bfloat16)
    resid, total, two, back, outer, *even_halves, even_sums = middle(
        first_kernel,
        "first_half",
        [tokens, cotangent, live, params],
        mixed,
        even_sources,
        even_where,
        [wide, wide, wide, low, square],
        4 * high,
        5 * high,
        0,
        ring.group,
    )
    if staged:
        even = Sum(*even_halves, ring)
    layer_output, grad_resid, grad_mixed, *odd_halves, odd_sums = middle(
        second_kernel,
        "second_half",
        [live, params, resid, total, two, back, outer],
        mixed,
        odd_sources,
        odd_where,
        [low, wide, low],
        5 * high,
        4 * high,
        2,
        ring.group,
    )
    if staged:
        odd = Sum(*odd_halves, ring)
        level = even.chip(False, grad_mixed)
        grad_mixed = after(grad_mixed, level)
    part = HEADS // 6
    grads = [attention_back(projected, grad_mixed, logs[0], 0, segment, 0, part)]
    back_logs = jnp.concatenate([logs[0][part:], logs[1][: 2 * part - half]])
    if staged:
        level = even.halfway(grads[0])
        grad_mixed = after(grad_mixed, odd.chip(False, grads[0], level))
    grads.append(attention_back(projected, grad_mixed, back_logs, 0, segment, part, part))
    if staged:
        level = even.plane(grads[1])
        grad_mixed = after(grad_mixed, level, odd.halfway(grads[1]))
    grads.append(attention_back(projected, grad_mixed, logs[1], 2 * part - half, segment, 2 * part, part))
    if staged:
        even_done = even.finish(grads[2])
        turned = after(turned, even_done, odd.plane(grads[2]))
    *inner_halves, inner_sums = inner_gradient(inner_where, turned, grads)
    last = grads
    if staged:
        tail = Sum(*inner_halves, ring)
        last = grads[:2] + [after(grads[2], inner_sums)]
    input_grad, input_sums = input_gradient(tokens, params, inner, last, grad_resid)
    sums = even_sums + odd_sums + inner_sums + input_sums
    hidden_sum = sums[8:12].reshape(2, 2, 2, TILE).transpose(1, 2, 0, 3).reshape(width, 4)
    vector_grad = jnp.concatenate([sums[:8].T, hidden_sum], axis=1)
    vector_part = VectorSum(vector_grad, ring)
    if staged:
        vector_part.hop(1)
        level = tail.chip(True, input_sums)
        odd_done = odd.finish(level)
        level = vector_part.add(odd_done)
        vector_part.hop(2)
        level = tail.plane(level)
        rest_part = Spread(after(jnp.concatenate([even_done, odd_done]), level), ring, False)
        tail_done = tail.finish(vector_part.add(rest_part.mine[0]))
        tail_part = Spread(tail_done, ring, True)
        rest_sum = rest_part.cores(tail_part.mine[0])
        vector_part.flat = after(vector_part.flat, rest_sum[1])
        vector_part.hop(4)
        expand_sum, project_sum = place_sums(
            [rest_sum],
            [expand_master.shape, project_master.shape],
            [
                [(0, 4 * high * parity, hidden_of(parity), high, 0) for parity in range(2)],
                [
                    (0, 4 * high * parity + 2 * high, halves_of(0, 1), 2 * high, parity * TILE)
                    for parity in range(2)
                ],
            ],
        )
        vector_part.add(expand_sum)
        vector_part.shards()
        expand_state = adam(
            expand_master,
            expand_mean,
            expand_square,
            expand_sum.astype(jnp.float32),
            RATE_MATRIX,
            DECAY_MATRIX,
        )
        tail_sum = tail_part.cores(expand_state[0])
        (attend_sum,) = place_sums(
            [tail_sum, rest_sum],
            [attend_master.shape],
            [
                [
                    (0, 0, halves_of(0, 3), high, 0),
                    (1, 8 * high, halves_of(3 * width, 1), high, 0),
                ]
            ],
        )
    else:
        plain = plain_gradients(even_halves, odd_halves, inner_halves, ring.core, high)
        attend_sum, expand_sum, project_sum = (
            lax.psum(lax.psum_scatter(g, "shard", scatter_dimension=0, tiled=True), "dp")
            for g in plain
        )
        expand_state = adam(
            expand_master, expand_mean, expand_square, expand_sum, RATE_MATRIX, DECAY_MATRIX
        )
    attend_sum, project_sum = attend_sum.astype(jnp.float32), project_sum.astype(jnp.float32)
    attend_state = adam(
        attend_master, attend_mean, attend_square, attend_sum, RATE_MATRIX, DECAY_MATRIX
    )
    project_state = adam(
        project_master, project_mean, project_square, project_sum, RATE_MATRIX, DECAY_MATRIX
    )
    vector_sum = vector_part.finish(expand_state[0])
    vector_state = adam(vector_master, vector_mean, vector_square, vector_sum, RATE_VECTOR, 0.0)
    return (
        layer_output,
        input_grad,
        attend_state[0],
        expand_state[0],
        project_state[0],
        vector_state[0],
        attend_state[1],
        expand_state[1],
        project_state[1],
        vector_state[1],
        attend_state[2],
        expand_state[2],
        project_state[2],
        vector_state[2],
    )


def solution(mesh):
    return jax.shard_map(
        on_device,
        mesh=mesh,
        in_specs=(
            P(("dp", "shard"), None),
            P(("dp", "shard"), None),
            P(),
            P(),
            P("shard", None),
            P("shard", None),
            P("shard", None),
            P("shard", None),
            P("shard", None),
            P("shard", None),
            P("shard", None),
            P("shard", None),
            P("shard", None),
            P("shard", None),
            P("shard", None),
            P("shard", None),
        ),
        out_specs=(
            P(("dp", "shard"), None),
            P(("dp", "shard"), None),
            P("shard", None),
            P("shard", None),
            P("shard", None),
            P("shard", None),
            P("shard", None),
            P("shard", None),
            P("shard", None),
            P("shard", None),
            P("shard", None),
            P("shard", None),
            P("shard", None),
            P("shard", None),
        ),
        check_vma=False,
    )
```
